32 devices in a mesh: dp: 8 (over z, y), vocab: 4 (over x, core).
Axes of the slice: x: 2, y: 2, z: 4, core: 2. Of those that a mesh axis runs over, the one named last changes fastest.
Arguments:
- hidden: bfloat16 [1024, 4096], P('dp', 'vocab')
- weight: bfloat16 [4096, 16384], P(None, ('dp', 'vocab'))
- loss_mask: int32 [1024], P('dp'), may hold values from 0 to 1, as said below
- target_ids: int32 [1024], P('dp'), may hold values from 0 to 16383
- turn_ids: int32 [1024], P('dp'), may hold values from 0 to 31, never falling along the last dimension, each value on 1 to 128 neighbouring positions
- advantages: float32 [32], replicated, may hold values from -4 to 4
Outputs:
- loss_value: float32 [], replicated
- hidden_grad: bfloat16 [1024, 4096], P('dp', 'vocab')
- weight_grad: bfloat16 [4096, 16384], P(None, ('dp', 'vocab'))
The draws below stay inside these ranges and needn't reach their ends.
Inputs may be any that keep to these rules, and one draw needn't show every extreme that they name: `loss_mask`: of the 128 tokens of one index of dp at most 32 bear loss, and some index has exactly 32.
All inputs are finite; a program needn't handle non-finite values.
Results may differ from the reference program's by a relative error of at most 0.0051.
Values may be sent and summed in bfloat16 or wider, within the bound.
No kernel may reach another device: no remote copies, remote signals or barrier semaphores. Data moves between devices by JAX's collectives and lax.ppermute only.
A program may use at most 128 MiB of HBM per device.

```python
import math
import jax
import jax.numpy as jnp
import numpy as np
from jax import lax

D = 4096
TOK_DEV = 128
CAP = 32
VOCAB = 16384
TOKENS = 1024
TURNS = 32


def shared_columns(key):
    head_key = jax.random.fold_in(key, 11)
    return jnp.clip(jax.random.normal(head_key, (D, 128), jnp.float32), -6.0, 6.0)


def draw_weight(key, part):
    head = shared_columns(key)
    key = jax.random.fold_in(key, 1)
    others = jnp.clip(jax.random.normal(key, (D, VOCAB - 128), jnp.float32), -6.0, 6.0)
    return (jnp.concatenate([head, others], axis=1) / math.sqrt(D)).astype(jnp.bfloat16)


def draw_hidden(key, part):
    key = jax.random.fold_in(key, 2)
    base_key = jax.random.fold_in(key, 1)
    values = jnp.clip(jax.random.normal(base_key, (TOKENS, D), jnp.float32) * 3.0, -18.0, 18.0)
    return values.astype(jnp.bfloat16)


def draw_loss_mask(key, part):
    key = jax.random.fold_in(key, 3)
    flip_key, order_key = jax.random.split(key, 2)
    groups = TOKENS // TOK_DEV
    lowest = CAP // 3
    ranks = jnp.arange(groups, dtype=jnp.int32)
    flipped = jax.random.randint(flip_key, (), 0, 2)
    ranks = jnp.where(flipped == 1, groups - 1 - ranks, ranks)
    counts = lowest + (CAP - lowest) * ranks // max(groups - 1, 1)
    orders = jax.vmap(lambda single: jax.random.permutation(single, TOK_DEV))(jax.random.split(order_key, groups))
    return (orders < counts[:, None]).astype(jnp.int32).reshape(TOKENS)


def plant(result, stream_key, smallest, high):
    place = [jax.random.randint(jax.random.fold_in(stream_key, axis), (), 0, length) for axis, length in enumerate(result.shape)]
    main_axis = result.shape.index(max(result.shape))
    neighbour = place[:main_axis] + [(place[main_axis] + 1) % result.shape[main_axis]] + place[main_axis + 1:]
    return result.at[tuple(place)].set(smallest).at[tuple(neighbour)].set(high)


def rank_bounds(amount, skew):
    loads = [(1 << 20) // math.isqrt(standing ** skew) + 1 for standing in range(1, amount + 1)]
    scale = 1 + sum(loads) // (1 << 30)
    return np.cumsum(np.array([max(1, weight // scale) for weight in loads]))


def skewed_ids(own_key, shape, number_of, slope):
    listing = rank_bounds(number_of, slope)
    ticket = jax.random.randint(jax.random.fold_in(own_key, 1), shape, 0, int(listing[number_of - 1]))
    grade = jnp.searchsorted(jnp.asarray(listing, jnp.int32), ticket, side="right")
    return jax.random.permutation(jax.random.fold_in(own_key, 2), number_of)[grade].astype(jnp.int32)


def profile(amount, total, bound, slope):
    portions = [(1 << 20) // math.isqrt(grade ** slope) + 1 for grade in range(2, amount + 1)]
    rest, given = total - bound - (amount - 1), [1] * (amount - 1)
    while rest > 0:
        free = [i for i in range(amount - 1) if given[i] < bound]
        pool, left = sum([portions[i] for i in free]), rest
        for i in free:
            addition = min(bound - given[i], max(1, left * portions[i] // pool), rest)
            given[i] = given[i] + addition
            rest = rest - addition
    return np.array([bound] + given)


def uneven_parts(own_key, count, total, most, skew):
    if count == 2:
        one = jax.random.randint(own_key, (), max(1, total - most), min(most, total - 1) + 1)
        return jnp.stack([one, total - one])
    sizes = jnp.asarray(profile(count, total, most, skew), jnp.int32)
    couples = (count - 1) // 2
    giver, sink = sizes[1:1 + 2 * couples:2], sizes[2:2 + 2 * couples:2]
    room = jnp.minimum(giver - 1, most - sink)
    passed = jax.random.randint(jax.random.fold_in(own_key, 1), (couples,), 0, 1 << 20) % (room + 1)
    sizes = sizes.at[1:1 + 2 * couples:2].set(giver - passed).at[2:2 + 2 * couples:2].set(sink + passed)
    return sizes[jax.random.permutation(jax.random.fold_in(own_key, 2), count)]


def normal_values(own_key, dims, scale, limit, kind=jnp.bfloat16):
    entries = jax.random.normal(own_key, dims, jnp.float32) * scale
    return jnp.minimum(jnp.maximum(entries, -limit), limit).astype(kind)


def setup_inputs(seed: int = 0) -> dict:
    key_of = jax.random.split(jax.random.key(seed), 7)
    return {
        "hidden": draw_hidden(jax.random.fold_in(key_of[6], 71), 0),
        "weight": draw_weight(jax.random.fold_in(key_of[6], 71), 0),
        "loss_mask": draw_loss_mask(jax.random.fold_in(key_of[6], 71), 0),
        "target_ids": plant(skewed_ids(key_of[3], (TOKENS,), VOCAB, 2), jax.random.fold_in(key_of[3], 3), 0, VOCAB - 1).astype(jnp.int32),
        "turn_ids": jnp.searchsorted(jnp.cumsum(uneven_parts(key_of[4], TURNS, TOKENS, TOK_DEV, 2)), jnp.arange(TOKENS), side="right").astype(jnp.int32),
        "advantages": normal_values(key_of[5], (TURNS,), 1.0, 4.0, jnp.float32),
    }


grad_scale = 16384.0


def reference(hidden, weight, loss_mask, target_ids, turn_ids, advantages):
    groups = TOKENS // TOK_DEV
    mask_grid = loss_mask.reshape(groups, TOK_DEV)
    row_slot = jnp.cumsum(mask_grid, axis=1, dtype=jnp.int32) - 1
    slot_ids = jnp.arange(CAP, dtype=jnp.int32)
    chosen = (row_slot[:, None, :] == slot_ids[None, :, None]) & (mask_grid[:, None, :] == 1)
    chosen_float = chosen.astype(jnp.float32)
    packed = jnp.einsum("gct,gtd->gcd", chosen_float, hidden.reshape(groups, TOK_DEV, D).astype(jnp.float32), precision=lax.Precision.HIGHEST)
    packed = packed.astype(jnp.bfloat16).reshape(groups * CAP, D)

    def pack_ints(values):
        picked = jnp.where(chosen, values.reshape(groups, 1, TOK_DEV), 0)
        return jnp.sum(picked, axis=2).astype(jnp.int32).reshape(groups * CAP)

    targets = pack_ints(target_ids)
    turn_rows = pack_ints(turn_ids)
    is_valid = pack_ints(loss_mask).astype(jnp.float32)
    logits = jnp.dot(packed, weight, preferred_element_type=jnp.float32)
    row_peak = jnp.max(logits, axis=1)
    row_total = jnp.sum(jnp.exp(logits - row_peak[:, None]), axis=1)
    log_total = row_peak + jnp.log(row_total)
    target_logit = jnp.take_along_axis(logits, targets[:, None], axis=1)[:, 0]
    row_advantage = advantages[turn_rows]
    row_weight = is_valid * row_advantage / jnp.sum(is_valid)
    loss_value = -jnp.sum(row_weight * (target_logit - log_total))
    is_target = jnp.arange(VOCAB, dtype=jnp.int32)[None, :] == targets[:, None]
    logit_grad = (grad_scale * row_weight[:, None] * (jnp.exp(logits - log_total[:, None]) - is_target.astype(jnp.float32))).astype(jnp.bfloat16)
    weight_grad = jnp.dot(packed.T, logit_grad, preferred_element_type=jnp.float32).astype(jnp.bfloat16)
    packed_grad = jnp.dot(logit_grad, weight.T, preferred_element_type=jnp.float32)
    hidden_grad = jnp.einsum("gct,gcd->gtd", chosen_float, packed_grad.reshape(groups, CAP, D), precision=lax.Precision.HIGHEST)
    return loss_value, hidden_grad.reshape(TOKENS, D).astype(jnp.bfloat16), weight_grad
```

```python
import functools

import jax
import jax.numpy as jnp
from jax import lax
from jax.experimental import pallas as pl
from jax.experimental.pallas import tpu as pltpu
from jax.sharding import PartitionSpec as P

CAP = 32
grad_scale = 16384.0
VMEM_BYTES = 56 * 1024 * 1024
AXES = ("dp", "vocab")


def params():
    return pltpu.CompilerParams(vmem_limit_bytes=VMEM_BYTES)


def vmem(count):
    return [pl.BlockSpec(memory_space=pltpu.VMEM)] * count


def choose(mask):
    tokens = mask.shape[1]
    wide = jnp.broadcast_to(mask.astype(jnp.float32), (8, tokens))
    before = lax.broadcasted_iota(jnp.int32, (tokens, tokens), 0)
    after = lax.broadcasted_iota(jnp.int32, (tokens, tokens), 1)
    upto = (before <= after).astype(jnp.float32)
    slot = jnp.dot(
        wide.astype(jnp.bfloat16), upto.astype(jnp.bfloat16), preferred_element_type=jnp.float32
    )[0:1]
    grid = lax.broadcasted_iota(jnp.int32, (CAP, tokens), 0) + 1
    return (slot.astype(jnp.int32) == grid) & (mask == 1)


def pack_kernel(hidden, mask, target, turn, rows, ids):
    chosen = choose(mask[...])
    rows[...] = jnp.dot(
        chosen.astype(jnp.float32).astype(jnp.bfloat16),
        hidden[...],
        preferred_element_type=jnp.float32,
    ).astype(jnp.bfloat16)
    lane = lax.broadcasted_iota(jnp.int32, ids.shape, 1)
    table = jnp.zeros(ids.shape, jnp.float32)
    for place, field in enumerate((mask, turn, target)):
        picked = jnp.where(chosen, field[...].astype(jnp.float32), 0.0)
        table = jnp.where(lane == place, jnp.sum(picked, axis=1, keepdims=True), table)
    ids[...] = table


def info_kernel(own, other, advantages, info):
    table = jnp.concatenate([own[...], other[...]], axis=0)
    valid, turn, target = table[:, 0:1], table[:, 1:2], table[:, 2:3]
    turns = advantages.shape[1]
    spot = lax.broadcasted_iota(jnp.int32, (table.shape[0], turns), 1)
    gain = jnp.sum(
        jnp.where(spot == turn.astype(jnp.int32), advantages[...], 0.0), axis=1, keepdims=True
    )
    weight = valid * gain / jnp.sum(valid)
    lane = lax.broadcasted_iota(jnp.int32, info.shape, 1)
    info[...] = jnp.where(lane == 0, weight, jnp.where(lane == 1, target, 0.0))


def reorder(stats, position, groups):
    lanes = stats.shape[1]
    lane = lax.broadcasted_iota(jnp.int32, stats.shape, 1)
    bit = 1
    while bit < groups:
        size = CAP * bit
        swapped = jnp.where(
            (lane & size) != 0,
            pltpu.roll(stats, size, 1),
            pltpu.roll(stats, lanes - size, 1),
        )
        stats = jnp.where((position & bit) != 0, swapped, stats)
        bit *= 2
    return stats


def load_rows(pieces, rows, sems):
    copies = {}
    for number, (block, start, ref) in enumerate(pieces):
        height, width = ref.shape
        copy = pltpu.make_async_copy(
            ref,
            rows.at[pl.ds(start, height), pl.ds(block * width, width)],
            sems.at[number],
        )
        copy.start()
        copies.setdefault(block, []).append(copy)
    return copies


def load_weight(weight, held, sems, vocab_rank, blocks):
    copies = []
    width = weight.shape[0] // blocks
    for block in range(blocks):
        start = pl.multiple_of((vocab_rank ^ block) * width, width)
        copy = pltpu.make_async_copy(
            weight.at[pl.ds(start, width)],
            held.at[pl.ds(block * width, width)],
            sems.at[block],
        )
        copy.start()
        copies.append(copy)
    return copies


def logits_kernel(places, blocks, groups, where, info, weight, *refs):
    count = len(places)
    pieces = [(b, s, r) for (b, s), r in zip(places, refs[:count])]
    logits, stats, rows, held, row_sems, weight_sems = refs[count:]
    rank, position, shard = where[0], where[1], where[2]
    weight_copies = load_weight(weight, held, weight_sems, rank, blocks)
    row_copies = load_rows(pieces, rows, row_sems)
    width = weight.shape[0] // blocks
    total = None
    for block in range(blocks):
        weight_copies[block].wait()
        for copy in row_copies[block]:
            copy.wait()
        part = jnp.dot(
            rows[:, block * width:(block + 1) * width],
            held[block * width:(block + 1) * width],
            preferred_element_type=jnp.float32,
        )
        total = part if total is None else total + part
    logits[...] = total
    height, columns = total.shape
    target = info[:, 1:2].astype(jnp.int32) - shard * columns
    column = lax.broadcasted_iota(jnp.int32, total.shape, 1)
    hit = jnp.sum(jnp.where(column == target, total, 0.0), axis=1, keepdims=True)
    peak = jnp.max(total, axis=1, keepdims=True)
    mass = jnp.sum(jnp.exp(total - peak), axis=1, keepdims=True)
    lane = lax.broadcasted_iota(jnp.int32, (height, 128), 1)
    table = jnp.where(lane == 0, peak, jnp.where(lane == 1, mass, jnp.where(lane == 2, hit, 0.0)))
    stats[...] = reorder(jnp.transpose(table)[0:8], position, groups)


def merge(tables):
    peak = functools.reduce(jnp.maximum, [table[0:1] for table in tables])
    mass = sum(table[1:2] * jnp.exp(table[0:1] - peak) for table in tables)
    hit = sum(table[2:3] for table in tables)
    return peak, mass, hit


def merge_kernel(*refs):
    out = refs[-1]
    peak, mass, hit = merge([ref[...] for ref in refs[:-1]])
    row = lax.broadcasted_iota(jnp.int32, out.shape, 0)
    out[...] = jnp.where(row == 0, peak, jnp.where(row == 1, mass, jnp.where(row == 2, hit, 0.0)))


def grad_kernel(count, blocks, groups, where, info, logits, weight, *refs):
    tables = [ref[...] for ref in refs[:count]]
    outs = refs[count:count + 2 * blocks]
    logit_grad, loss, held, weight_sems = refs[count + 2 * blocks:]
    rank, position, shard = where[0], where[1], where[2]
    copies = load_weight(weight, held, weight_sems, rank, blocks)
    peak, mass, hit = merge(tables)
    lanes = peak.shape[1]
    row = lax.broadcasted_iota(jnp.int32, (8, lanes), 0)
    both = jnp.where(row == 0, peak + jnp.log(mass), jnp.where(row == 1, hit, 0.0))
    both = reorder(both, position, groups)
    both = jnp.transpose(jnp.concatenate([both] * 16, axis=0))
    log_total, target_logit = both[:, 0:1], both[:, 1:2]
    row_weight = info[:, 0:1]
    loss[0, 0] = -jnp.sum(row_weight * (target_logit - log_total))
    columns = logits.shape[1]
    target = info[:, 1:2].astype(jnp.int32) - shard * columns
    column = lax.broadcasted_iota(jnp.int32, logits.shape, 1)
    probability = jnp.exp(logits[...] - log_total)
    grad = (
        grad_scale * row_weight * (probability - (column == target).astype(jnp.float32))
    ).astype(jnp.bfloat16)
    logit_grad[...] = grad
    width = weight.shape[0] // blocks
    half = logits.shape[0] // 2
    order = [b for b in range(blocks) if b % 2] + [b for b in range(blocks) if not b % 2]
    for copy in copies:
        copy.wait()
    for block in order:
        part = lax.dot_general(
            grad,
            held[block * width:(block + 1) * width],
            (((1,), (1,)), ((), ())),
            preferred_element_type=jnp.float32,
        )
        for side in range(2):
            out = outs[2 * block + side]
            out[...] = part[side * half:(side + 1) * half].astype(out.dtype)


def weight_kernel(places, blocks, where, logit_grad, *refs):
    count = len(places)
    pieces = [(b, s, r) for (b, s), r in zip(places, refs[:count])]
    out, rows, done, row_sems, out_sems = refs[count:]
    rank = where[0]
    row_copies = load_rows(pieces, rows, row_sems)
    width = rows.shape[1] // blocks
    out_copies = []
    for block in range(blocks):
        for copy in row_copies[block]:
            copy.wait()
        done[block * width:(block + 1) * width] = lax.dot_general(
            rows[:, block * width:(block + 1) * width],
            logit_grad[...],
            (((0,), (0,)), ((), ())),
            preferred_element_type=jnp.float32,
        ).astype(jnp.bfloat16)
        start = pl.multiple_of((rank ^ block) * width, width)
        copy = pltpu.make_async_copy(
            done.at[pl.ds(block * width, width)], out.at[pl.ds(start, width)], out_sems.at[block]
        )
        copy.start()
        out_copies.append(copy)
    for copy in out_copies:
        copy.wait()


def unpack_kernel(*refs):
    mask, out = refs[0], refs[-1]
    total = sum(ref[...].astype(jnp.float32) for ref in refs[1:-1])
    chosen = choose(mask[...])
    out[...] = lax.dot_general(
        chosen.astype(jnp.float32).astype(jnp.bfloat16),
        total.astype(jnp.bfloat16),
        (((0,), (0,)), ((), ())),
        preferred_element_type=jnp.float32,
    ).astype(jnp.bfloat16)


def body(dps, ranks, hidden, weight, loss_mask, target_ids, turn_ids, advantages):
    tokens, width = hidden.shape
    columns = weight.shape[1]
    zs, xs = dps // 2, ranks // 2
    height = zs * CAP
    half = height // 2
    total_rows = dps * CAP
    bf16, f32 = jnp.bfloat16, jnp.float32
    shape = jax.ShapeDtypeStruct

    def send(value, z, y, x, core):
        far, near = 2 * z + y, 2 * x + core
        pairs = [
            (d * ranks + v, (d ^ far) * ranks + (v ^ near))
            for d in range(dps)
            for v in range(ranks)
        ]
        return lax.ppermute(value, AXES, pairs)

    group, rank = lax.axis_index("dp"), lax.axis_index("vocab")
    position = (group & 1) * zs + (group >> 1)
    where = jnp.stack([rank, position, group * ranks + rank]).astype(jnp.int32)
    mask = loss_mask.reshape(1, tokens)

    packed, ids = pl.pallas_call(
        pack_kernel,
        out_shape=(shape((CAP, width), bf16), shape((CAP, 128), f32)),
        in_specs=vmem(4),
        out_specs=tuple(vmem(2)),
        compiler_params=params(),
    )(hidden, mask, target_ids.reshape(1, tokens), turn_ids.reshape(1, tokens))

    own = jnp.concatenate([packed] + [send(packed, z, 0, 0, 0) for z in range(1, zs)], axis=0)
    own_ids = jnp.concatenate([ids] + [send(ids, z, 0, 0, 0) for z in range(1, zs)], axis=0)
    across = send(own, 0, 1, 0, 0)
    other_ids = send(own_ids, 0, 1, 0, 0)
    pieces = [(0, 0, own), (0, height, across)]
    for x in range(1, xs):
        beside = send(own, 0, 0, x, 0)
        upper = send(beside[:half], 0, 1, 0, 0)
        lower = send(across[half:], 0, 0, x, 0)
        pieces += [(2 * x, 0, beside), (2 * x, height, upper), (2 * x, height + half, lower)]
    pieces += [(b + 1, start, send(piece, 0, 0, 0, 1)) for b, start, piece in pieces]
    places = [(b, start) for b, start, _ in pieces]
    arrays = [piece for _, _, piece in pieces]

    info = pl.pallas_call(
        info_kernel,
        out_shape=shape((total_rows, 128), f32),
        in_specs=vmem(3),
        out_specs=vmem(1)[0],
        compiler_params=params(),
    )(own_ids, other_ids, advantages.reshape(1, -1))

    smem = pl.BlockSpec(memory_space=pltpu.SMEM)
    hbm = pl.BlockSpec(memory_space=pl.ANY)
    depth = weight.shape[0]
    logits, stats = pl.pallas_call(
        functools.partial(logits_kernel, places, ranks, dps),
        out_shape=(shape((total_rows, columns), f32), shape((8, total_rows), f32)),
        in_specs=[smem] + vmem(1) + [hbm] * (1 + len(arrays)),
        out_specs=tuple(vmem(2)),
        scratch_shapes=[
            pltpu.VMEM((total_rows, depth), bf16),
            pltpu.VMEM((depth, columns), bf16),
            pltpu.SemaphoreType.DMA((len(arrays),)),
            pltpu.SemaphoreType.DMA((ranks,)),
        ],
        compiler_params=params(),
    )(where, info, weight, *arrays)

    near = [stats] + [
        send(stats, 0, y, x, core)
        for y in range(2)
        for x in range(xs)
        for core in range(2)
        if y + x + core
    ]
    stats = pl.pallas_call(
        merge_kernel,
        out_shape=shape((8, total_rows), f32),
        in_specs=vmem(len(near)),
        out_specs=vmem(1)[0],
        compiler_params=params(),
    )(*near)
    tables = [stats] + [send(stats, z, 0, 0, 0) for z in range(1, zs)]

    outs = []
    for b in range(ranks):
        outs += [shape((height, width), bf16 if b % 2 else f32)] * 2
    *parts, logit_grad, loss = pl.pallas_call(
        functools.partial(grad_kernel, len(tables), ranks, dps),
        out_shape=tuple(outs) + (shape((total_rows, columns), bf16), shape((1, 1), f32)),
        in_specs=[smem] + vmem(2) + [hbm] + vmem(len(tables)),
        out_specs=tuple(vmem(len(outs) + 1)) + (smem,),
        scratch_shapes=[
            pltpu.VMEM((depth, columns), bf16),
            pltpu.SemaphoreType.DMA((ranks,)),
        ],
        compiler_params=params(),
    )(where, info, logits, weight, *tables)

    def back(x, side):
        return parts[4 * x + side] + send(parts[4 * x + 2 + side], 0, 0, 0, 1).astype(f32)

    corner = [back(x, 1) for x in range(1, xs)]
    across, beside, own = back(0, 1), [back(x, 0) for x in range(1, xs)], back(0, 0)
    across_low, across_high = across[half:], across[:half]
    own = own + jnp.concatenate(
        [jnp.zeros((half, width), f32), send(across_low.astype(bf16), 0, 1, 0, 0).astype(f32)]
    )
    for x in range(1, xs):
        diagonal = corner[x - 1].astype(bf16)
        across_high = across_high + send(diagonal[:half], 0, 0, x, 0).astype(f32)
        low = beside[x - 1][half:] + send(diagonal[half:], 0, 1, 0, 0).astype(f32)
        high = beside[x - 1][:half]
        own = own + jnp.concatenate(
            [send(high.astype(bf16), 0, 0, x, 0), send(low.astype(bf16), 0, 0, x, 0)]
        ).astype(f32)
    own = own + jnp.concatenate(
        [send(across_high.astype(bf16), 0, 1, 0, 0).astype(f32), jnp.zeros((half, width), f32)]
    )
    sums = [own[:CAP]] + [
        send(own[z * CAP:(z + 1) * CAP].astype(bf16), z, 0, 0, 0) for z in range(1, zs)
    ]

    weight_grad = pl.pallas_call(
        functools.partial(weight_kernel, places, ranks),
        out_shape=shape((depth, columns), bf16),
        in_specs=[smem] + vmem(1) + [hbm] * len(arrays),
        out_specs=hbm,
        scratch_shapes=[
            pltpu.VMEM((total_rows, depth), bf16),
            pltpu.VMEM((depth, columns), bf16),
            pltpu.SemaphoreType.DMA((len(arrays),)),
            pltpu.SemaphoreType.DMA((ranks,)),
        ],
        compiler_params=params(),
        cost_estimate=pl.CostEstimate(
            flops=2 * total_rows * depth * columns,
            bytes_accessed=2 * depth * (columns + total_rows),
            transcendentals=0,
        ),
    )(where, logit_grad, *arrays)

    hidden_grad = pl.pallas_call(
        unpack_kernel,
        out_shape=shape((tokens, width), bf16),
        in_specs=vmem(1 + len(sums)),
        out_specs=vmem(1)[0],
        compiler_params=params(),
    )(mask, *sums)
    return loss[0, 0], hidden_grad, weight_grad


def solution(mesh):
    return jax.shard_map(
        functools.partial(body, mesh.shape["dp"], mesh.shape["vocab"]),
        mesh=mesh,
        in_specs=(P("dp", "vocab"), P(None, AXES), P("dp"), P("dp"), P("dp"), P()),
        out_specs=(P(), P("dp", "vocab"), P(None, AXES)),
        check_vma=False,
    )
```

```python
import functools
import math

import jax
import jax.numpy as jnp
from jax import lax
from jax.experimental import pallas as pl
from jax.experimental.pallas import tpu as pltpu
from jax.sharding import PartitionSpec as P

CAP = 32
IDS = 128
grad_scale = 16384.0
AXES = ("dp", "vocab")
SMEM = pl.BlockSpec(memory_space=pltpu.SMEM)
VMEM = pl.BlockSpec(memory_space=pltpu.VMEM)
HBM = pl.BlockSpec(memory_space=pl.ANY)


def size_of(value):
    return math.prod(value.shape) * jnp.dtype(value.dtype).itemsize


def call(kernel, operands, in_specs, out_shape, out_specs, scratch=(), spare=4, flops=0):
    outs = jax.tree.leaves(out_shape)
    sized = [v for v, s in zip(operands, in_specs) if s is VMEM]
    sized += [v for v, s in zip(outs, jax.tree.leaves(out_specs)) if s is VMEM]
    held = [s for s in scratch if s.memory_space == pltpu.VMEM]
    total = sum(size_of(v) for v in sized) + sum(size_of(s) for s in held)
    return pl.pallas_call(
        kernel,
        out_shape=out_shape,
        in_specs=in_specs,
        out_specs=out_specs,
        scratch_shapes=scratch,
        compiler_params=pltpu.CompilerParams(vmem_limit_bytes=total + spare * 1024 * 1024),
        cost_estimate=pl.CostEstimate(
            flops=flops,
            bytes_accessed=sum(size_of(v) for v in list(operands) + outs),
            transcendentals=0,
        ),
    )(*operands)


def choose(mask):
    tokens = mask.shape[1]
    wide = jnp.broadcast_to(mask.astype(jnp.float32), (8, tokens))
    before = lax.broadcasted_iota(jnp.int32, (tokens, tokens), 0)
    after = lax.broadcasted_iota(jnp.int32, (tokens, tokens), 1)
    upto = (before <= after).astype(jnp.float32)
    slot = jnp.dot(
        wide.astype(jnp.bfloat16), upto.astype(jnp.bfloat16), preferred_element_type=jnp.float32
    )[0:1]
    grid = lax.broadcasted_iota(jnp.int32, (CAP, tokens), 0) + 1
    return (slot.astype(jnp.int32) == grid) & (mask == 1)


def pack_kernel(hidden, mask, target, turn, rows, chosen_out):
    width = hidden.shape[1]
    chosen = choose(mask[...])
    one_hot = chosen.astype(jnp.float32).astype(jnp.bfloat16)
    chosen_out[...] = one_hot
    packed = jnp.dot(one_hot, hidden[...], preferred_element_type=jnp.float32)
    packed = packed.astype(jnp.bfloat16)
    turns, targets = turn[...], target[...]
    fields = (
        mask[...],
        turns & 255,
        turns >> 8,
        targets & 255,
        (targets >> 8) & 255,
        targets >> 16,
    )
    lane = lax.broadcasted_iota(jnp.int32, (CAP, IDS), 1)
    table = jnp.zeros((CAP, IDS), jnp.float32)
    for place, field in enumerate(fields):
        picked = jnp.where(chosen, field.astype(jnp.float32), 0.0)
        table = jnp.where(lane == place, jnp.sum(picked, axis=1, keepdims=True), table)
    table = table.astype(jnp.bfloat16)
    for copy in range(rows.shape[0]):
        rows[copy, :, :width] = packed
        rows[copy, :, width:] = table


def info_kernel(where, own, other, advantages, info, held):
    half = own.shape[0]
    side = where[1]
    held[pl.ds(pl.multiple_of(side * half, half), half)] = own[...].astype(jnp.float32)
    held[pl.ds(pl.multiple_of((1 - side) * half, half), half)] = other[...].astype(jnp.float32)
    table = held[...]
    valid = table[:, 0:1]
    turn = table[:, 1:2] + 256.0 * table[:, 2:3]
    target = table[:, 3:4] + 256.0 * table[:, 4:5] + 65536.0 * table[:, 5:6]
    turns = advantages.shape[1]
    spot = lax.broadcasted_iota(jnp.int32, (table.shape[0], turns), 1)
    gain = jnp.sum(
        jnp.where(spot == turn.astype(jnp.int32), advantages[...], 0.0), axis=1, keepdims=True
    )
    weight = valid * gain / jnp.sum(valid)
    lane = lax.broadcasted_iota(jnp.int32, info.shape, 1)
    info[...] = jnp.where(lane == 0, weight, jnp.where(lane == 1, target, 0.0))


def logits_kernel(blocks, where, info, weight, *refs):
    pieces, (logits, stats) = refs[:2 * blocks], refs[2 * blocks:]
    rank, side, shard = where[0], where[1], where[2]
    width = weight.shape[0] // blocks
    total = None
    for block in range(blocks):
        start = pl.multiple_of((rank ^ block) * width, width)
        part = jnp.dot(
            jnp.concatenate([pieces[2 * block][...], pieces[2 * block + 1][...]], axis=0),
            weight[pl.ds(start, width), :],
            preferred_element_type=jnp.float32,
        )
        total = part if total is None else total + part
    half = total.shape[0] // 2
    logits[pl.ds(pl.multiple_of(side * half, half), half)] = total[:half]
    logits[pl.ds(pl.multiple_of((1 - side) * half, half), half)] = total[half:]
    total = logits[...]
    height, columns = total.shape
    target = info[:, 1:2].astype(jnp.int32) - shard * columns
    column = lax.broadcasted_iota(jnp.int32, total.shape, 1)
    hit = jnp.sum(jnp.where(column == target, total, 0.0), axis=1, keepdims=True)
    hit = jnp.sum(hit * info[:, 0:1])
    peak = jnp.max(total, axis=1, keepdims=True)
    mass = jnp.sum(jnp.exp(total - peak), axis=1, keepdims=True)
    lane = lax.broadcasted_iota(jnp.int32, (height, 128), 1)
    table = jnp.transpose(jnp.where(lane == 0, peak, mass))
    whole = (stats.shape[0], 1, height)
    stats[:, :, :height] = jnp.broadcast_to(table[0:1][None], whole)
    stats[:, :, height:2 * height] = jnp.broadcast_to(table[1:2][None], whole)
    stats[:, :, 2 * height:] = jnp.full((stats.shape[0], 1, 128), hit, jnp.float32)


def grad_kernel(blocks, where, info, logits, weight, stats, *refs):
    outs = refs[:2 * blocks]
    logit_grad, loss = refs[2 * blocks:]
    rank, side, shard = where[0], where[1], where[2]
    height, columns = logits.shape
    peaks, masses = stats[:, :, :height], stats[:, :, height:2 * height]
    peak = jnp.max(peaks, axis=0)
    mass = jnp.sum(masses * jnp.exp(peaks - peak[None]), axis=0)
    log_total = jnp.broadcast_to(peak + jnp.log(mass), (128, height))
    log_total = jnp.transpose(log_total)[:, 0:1]
    row_weight = info[:, 0:1]
    hit = jnp.sum(stats[:, :, 2 * height:], axis=0)[0, 0]
    loss[0, 0] = jnp.sum(row_weight * log_total) - hit
    target = info[:, 1:2].astype(jnp.int32) - shard * columns
    column = lax.broadcasted_iota(jnp.int32, logits.shape, 1)
    probability = jnp.exp(logits[...] - log_total)
    grad = (
        grad_scale * row_weight * (probability - (column == target).astype(jnp.float32))
    ).astype(jnp.bfloat16)
    half = height // 2
    logit_grad[pl.ds(pl.multiple_of(side * half, half), half)] = grad[:half]
    logit_grad[pl.ds(pl.multiple_of((1 - side) * half, half), half)] = grad[half:]
    grad = logit_grad[...]
    width = weight.shape[0] // blocks
    order = [b for b in range(blocks) if b % 2] + [b for b in range(blocks) if not b % 2]
    for block in order:
        start = pl.multiple_of((rank ^ block) * width, width)
        part = lax.dot_general(
            grad,
            weight[pl.ds(start, width), :],
            (((1,), (1,)), ((), ())),
            preferred_element_type=jnp.float32,
        )
        for y in range(2):
            out = outs[2 * block + y]
            out[...] = part[y * half:(y + 1) * half].astype(out.dtype)


def weight_kernel(blocks, where, logit_grad, *refs):
    pieces, (out, done, sems) = refs[:2 * blocks], refs[2 * blocks:]
    rank = where[0]
    width = pieces[0].shape[1]
    copies = []
    for block in range(blocks):
        done[block * width:(block + 1) * width] = lax.dot_general(
            jnp.concatenate([pieces[2 * block][...], pieces[2 * block + 1][...]], axis=0),
            logit_grad[...],
            (((0,), (0,)), ((), ())),
            preferred_element_type=jnp.float32,
        ).astype(jnp.bfloat16)
        start = pl.multiple_of((rank ^ block) * width, width)
        copy = pltpu.make_async_copy(
            done.at[pl.ds(block * width, width)], out.at[pl.ds(start, width)], sems.at[block]
        )
        copy.start()
        copies.append(copy)
    for copy in copies:
        copy.wait()


def unpack_kernel(chosen, parts, out):
    total = jnp.sum(parts[...].astype(jnp.float32), axis=0)
    out[...] = lax.dot_general(
        chosen[...],
        total.astype(jnp.bfloat16),
        (((0,), (0,)), ((), ())),
        preferred_element_type=jnp.float32,
    ).astype(jnp.bfloat16)


def body(dps, ranks, hidden, weight, loss_mask, target_ids, turn_ids, advantages):
    tokens, width = hidden.shape
    depth, columns = weight.shape
    zs, xs = dps // 2, ranks // 2
    half, total_rows = zs * CAP, dps * CAP
    bf16, f32 = jnp.bfloat16, jnp.float32
    shape = jax.ShapeDtypeStruct
    lines = [[2 * z + y for z in range(zs)] for y in range(2)]

    def send(value, y, x, core):
        near = 2 * x + core
        pairs = [
            (d * ranks + v, (d ^ y) * ranks + (v ^ near))
            for d in range(dps)
            for v in range(ranks)
        ]
        return lax.ppermute(value, AXES, pairs)

    def spread(value):
        return lax.all_to_all(value, "dp", 0, 0, axis_index_groups=lines)

    group, rank = lax.axis_index("dp"), lax.axis_index("vocab")
    where = jnp.stack([rank, group & 1, group * ranks + rank]).astype(jnp.int32)

    packed, chosen = call(
        pack_kernel,
        (
            hidden,
            loss_mask.reshape(1, tokens),
            target_ids.reshape(1, tokens),
            turn_ids.reshape(1, tokens),
        ),
        [VMEM] * 4,
        (shape((zs, CAP, width + IDS), bf16), shape((CAP, tokens), bf16)),
        (VMEM, VMEM),
    )

    line = spread(packed).reshape(half, width + IDS)
    own, own_ids = line[:, :width], line[:, width:]
    pieces = {(0, 0): own}
    for x in reversed(range(xs)):
        for y in (1, 0):
            if x or y:
                pieces[2 * x, y] = send(own, y, x, 0)
    other_ids = send(own_ids, 1, 0, 0)
    for b, y in list(pieces):
        pieces[b + 1, y] = send(pieces[b, y], 0, 0, 1)
    rows = [pieces[b, y] for b in range(ranks) for y in range(2)]

    info = call(
        info_kernel,
        (where, own_ids, other_ids, advantages.reshape(1, -1)),
        [SMEM] + [VMEM] * 3,
        shape((total_rows, 128), f32),
        VMEM,
        [pltpu.VMEM((total_rows, IDS), f32)],
    )
    flops = 2 * total_rows * depth * columns
    logits, stats = call(
        functools.partial(logits_kernel, ranks),
        (where, info, weight, *rows),
        [SMEM] + [VMEM] * (2 + len(rows)),
        (shape((total_rows, columns), f32), shape((dps * ranks, 1, 2 * total_rows + 128), f32)),
        (VMEM, VMEM),
        flops=flops,
    )

    stats = lax.all_to_all(stats, AXES, 0, 0)

    outs = [
        shape((half, width), bf16 if b % 2 else f32) for b in range(ranks) for y in range(2)
    ]
    *parts, logit_grad, loss = call(
        functools.partial(grad_kernel, ranks),
        (where, info, logits, weight, stats),
        [SMEM] + [VMEM] * 4,
        tuple(outs) + (shape((total_rows, columns), bf16), shape((1, 1), f32)),
        (VMEM,) * (len(outs) + 1) + (SMEM,),
        flops=flops,
    )

    sums = {}
    for x in reversed(range(xs)):
        for y in (1, 0):
            beside = send(parts[4 * x + 2 + y], 0, 0, 1)
            sums[x, y] = parts[4 * x + y] + beside.astype(f32)
    total = sums[0, 0]
    for x, y in sums:
        if x or y:
            total = total + send(sums[x, y].astype(bf16), y, x, 0).astype(f32)
    line = spread(total.astype(bf16).reshape(zs, CAP, width))

    weight_grad = call(
        functools.partial(weight_kernel, ranks),
        (where, logit_grad, *rows),
        [SMEM] + [VMEM] * (1 + len(rows)),
        shape((depth, columns), bf16),
        HBM,
        [pltpu.VMEM((depth, columns), bf16), pltpu.SemaphoreType.DMA((ranks,))],
        flops=flops,
    )
    hidden_grad = call(
        unpack_kernel, (chosen, line), [VMEM, VMEM], shape((tokens, width), bf16), VMEM
    )
    return loss[0, 0], hidden_grad, weight_grad


def solution(mesh):
    return jax.shard_map(
        functools.partial(body, mesh.shape["dp"], mesh.shape["vocab"]),
        mesh=mesh,
        in_specs=(P("dp", "vocab"), P(None, AXES), P("dp"), P("dp"), P("dp"), P()),
        out_specs=(P(), P("dp", "vocab"), P(None, AXES)),
        check_vma=False,
    )
```

```python
import functools
import math

import jax
import jax.numpy as jnp
from jax import lax
from jax.experimental import pallas as pl
from jax.experimental.pallas import tpu as pltpu
from jax.sharding import PartitionSpec as P

CAP = 32
MOST_VMEM = 56 * 1024 * 1024
IDS = 128
grad_scale = 16384.0
AXES = ("dp", "vocab")
SMEM = pl.BlockSpec(memory_space=pltpu.SMEM)
VMEM = pl.BlockSpec(memory_space=pltpu.VMEM)
HBM = pl.BlockSpec(memory_space=pltpu.HBM)
ANY = pl.BlockSpec(memory_space=pl.ANY)


def size_of(value):
    return math.prod(value.shape) * jnp.dtype(value.dtype).itemsize


def call(kernel, operands, in_specs, out_shape, out_specs, scratch=(), spare=4, flops=0):
    outs = jax.tree.leaves(out_shape)
    sized = [v for v, s in zip(operands, in_specs) if s is VMEM]
    sized += [v for v, s in zip(outs, jax.tree.leaves(out_specs)) if s is VMEM]
    held = [s for s in scratch if getattr(s, "memory_space", None) == pltpu.VMEM]
    total = sum(size_of(v) for v in sized) + sum(size_of(s) for s in held)
    return pl.pallas_call(
        kernel,
        out_shape=out_shape,
        in_specs=in_specs,
        out_specs=out_specs,
        scratch_shapes=scratch,
        compiler_params=pltpu.CompilerParams(vmem_limit_bytes=min(total + spare * 1024 * 1024, MOST_VMEM)),
        cost_estimate=pl.CostEstimate(
            flops=flops,
            bytes_accessed=sum(size_of(v) for v in list(operands) + outs),
            transcendentals=0,
        ),
    )(*operands)


def in_hbm(value):
    return pltpu.with_memory_space_constraint(value, pltpu.HBM)


def choose(mask):
    tokens = mask.shape[1]
    wide = jnp.broadcast_to(mask.astype(jnp.float32), (8, tokens))
    before = lax.broadcasted_iota(jnp.int32, (tokens, tokens), 0)
    after = lax.broadcasted_iota(jnp.int32, (tokens, tokens), 1)
    upto = (before <= after).astype(jnp.float32)
    slot = jnp.dot(
        wide.astype(jnp.bfloat16), upto.astype(jnp.bfloat16), preferred_element_type=jnp.float32
    )[0:1]
    grid = lax.broadcasted_iota(jnp.int32, (CAP, tokens), 0) + 1
    return (slot.astype(jnp.int32) == grid) & (mask == 1)


def pack_kernel(hidden_hbm, mask_hbm, target_hbm, turn_hbm, rows, chosen_out, *scratch):
    hidden, mask, target, turn, sems = scratch
    copies = []
    for place, (source, held) in enumerate(
        ((mask_hbm, mask), (target_hbm, target), (turn_hbm, turn), (hidden_hbm, hidden))
    ):
        copy = pltpu.make_async_copy(source, held, sems.at[place])
        copy.start()
        copies.append(copy)
    for copy in copies[:3]:
        copy.wait()
    width = hidden.shape[1]
    chosen = choose(mask[...])
    one_hot = chosen.astype(jnp.float32).astype(jnp.bfloat16)
    chosen_out[...] = one_hot
    turns, targets = turn[...], target[...]
    fields = (
        mask[...],
        turns & 255,
        turns >> 8,
        targets & 255,
        (targets >> 8) & 255,
        targets >> 16,
    )
    lane = lax.broadcasted_iota(jnp.int32, (CAP, IDS), 1)
    table = jnp.zeros((CAP, IDS), jnp.float32)
    for place, field in enumerate(fields):
        picked = jnp.where(chosen, field.astype(jnp.float32), 0.0)
        table = jnp.where(lane == place, jnp.sum(picked, axis=1, keepdims=True), table)
    rows[:, width:] = table.astype(jnp.bfloat16)
    copies[3].wait()
    packed = jnp.dot(one_hot, hidden[...], preferred_element_type=jnp.float32)
    rows[:, :width] = packed.astype(jnp.bfloat16)


def stage_kernel(after, weight, held, sem):
    copy = pltpu.make_async_copy(weight, held, sem)
    copy.start()
    copy.wait()


def info_kernel(own, other, advantages, info):
    start = own.shape[1] - IDS
    table = jnp.concatenate([own[:, start:], other[:, start:]], axis=0).astype(jnp.float32)
    valid = table[:, 0:1]
    turn = table[:, 1:2] + 256.0 * table[:, 2:3]
    target = table[:, 3:4] + 256.0 * table[:, 4:5] + 65536.0 * table[:, 5:6]
    turns = advantages.shape[1]
    spot = lax.broadcasted_iota(jnp.int32, (table.shape[0], turns), 1)
    gain = jnp.sum(
        jnp.where(spot == turn.astype(jnp.int32), advantages[...], 0.0), axis=1, keepdims=True
    )
    weight = valid * gain / jnp.sum(valid)
    lane = lax.broadcasted_iota(jnp.int32, info.shape, 1)
    info[...] = jnp.where(lane == 0, weight, jnp.where(lane == 1, target, 0.0))


def reorder(stats, position, groups):
    lanes = stats.shape[1]
    lane = lax.broadcasted_iota(jnp.int32, stats.shape, 1)
    bit = 1
    while bit < groups:
        size = CAP * bit
        swapped = jnp.where(
            (lane & size) != 0,
            pltpu.roll(stats, size, 1),
            pltpu.roll(stats, lanes - size, 1),
        )
        stats = jnp.where((position & bit) != 0, swapped, stats)
        bit *= 2
    return stats


def both_sides(pieces, block, width):
    pair = [pieces[2 * block + y][:, :width] for y in range(2)]
    return jnp.concatenate(pair, axis=0)


def logits_kernel(blocks, groups, where, info, weight, *refs):
    pieces, (logits, stats) = refs[:2 * blocks], refs[2 * blocks:]
    rank, position, shard = where[0], where[1], where[2]
    width = weight.shape[0] // blocks
    total = None
    for block in range(blocks):
        start = pl.multiple_of((rank ^ block) * width, width)
        part = jnp.dot(
            both_sides(pieces, block, width),
            weight[pl.ds(start, width), :],
            preferred_element_type=jnp.float32,
        )
        total = part if total is None else total + part
    logits[...] = total
    height, columns = total.shape
    target = info[:, 1:2].astype(jnp.int32) - shard * columns
    column = lax.broadcasted_iota(jnp.int32, total.shape, 1)
    hit = jnp.sum(jnp.where(column == target, total, 0.0), axis=1, keepdims=True)
    hit = jnp.sum(hit * info[:, 0:1])
    peak = jnp.max(total, axis=1, keepdims=True)
    mass = jnp.sum(jnp.exp(total - peak), axis=1, keepdims=True)
    lane = lax.broadcasted_iota(jnp.int32, (height, 128), 1)
    table = jnp.where(lane == 0, peak, jnp.where(lane == 1, mass, hit))
    stats[...] = reorder(jnp.transpose(table)[0:8], position, groups)


def merge(tables):
    peak = functools.reduce(jnp.maximum, [table[0:1] for table in tables])
    mass = sum(table[1:2] * jnp.exp(table[0:1] - peak) for table in tables)
    hit = sum(table[2:3] for table in tables)
    return peak, mass, hit


def merge_kernel(*refs):
    out = refs[-1]
    peak, mass, hit = merge([ref[...] for ref in refs[:-1]])
    row = lax.broadcasted_iota(jnp.int32, out.shape, 0)
    out[...] = jnp.where(row == 0, peak, jnp.where(row == 1, mass, hit))


def grad_kernel(count, blocks, groups, where, info, logits, weight, *refs):
    tables = [ref[...] for ref in refs[:count]]
    outs = refs[count:count + 2 * blocks]
    logit_grad, loss = refs[count + 2 * blocks:]
    rank, position, shard = where[0], where[1], where[2]
    height, columns = logits.shape
    peak, mass, hit = merge(tables)
    log_total = jnp.broadcast_to(peak + jnp.log(mass), (8, height))
    log_total = reorder(log_total, position, groups)
    log_total = jnp.transpose(jnp.concatenate([log_total] * 16, axis=0))[:, 0:1]
    row_weight = info[:, 0:1]
    loss[0, 0] = jnp.sum(row_weight * log_total) - hit[0, 0]
    target = info[:, 1:2].astype(jnp.int32) - shard * columns
    column = lax.broadcasted_iota(jnp.int32, logits.shape, 1)
    probability = jnp.exp(logits[...] - log_total)
    grad = (
        grad_scale * row_weight * (probability - (column == target).astype(jnp.float32))
    ).astype(jnp.bfloat16)
    logit_grad[...] = grad
    half = height // 2
    width = weight.shape[0] // blocks
    order = [b for b in range(blocks) if b % 2] + [b for b in range(blocks) if not b % 2]
    for block in order:
        start = pl.multiple_of((rank ^ block) * width, width)
        part = lax.dot_general(
            grad,
            weight[pl.ds(start, width), :],
            (((1,), (1,)), ((), ())),
            preferred_element_type=jnp.float32,
        )
        for y in range(2):
            out = outs[2 * block + y]
            out[...] = part[y * half:(y + 1) * half].astype(out.dtype)


def weight_kernel(blocks, where, after, logit_grad, *refs):
    pieces, (out, token, done, sems) = refs[:2 * blocks], refs[2 * blocks:]
    rank = where[0]
    width = done.shape[0] // blocks
    copies = []
    for block in range(blocks):
        done[block * width:(block + 1) * width] = lax.dot_general(
            both_sides(pieces, block, width),
            logit_grad[...],
            (((0,), (0,)), ((), ())),
            preferred_element_type=jnp.float32,
        ).astype(jnp.bfloat16)
        start = pl.multiple_of((rank ^ block) * width, width)
        copy = pltpu.make_async_copy(
            done.at[pl.ds(block * width, width)], out.at[pl.ds(start, width)], sems.at[block]
        )
        copy.start()
        copies.append(copy)
    for copy in copies:
        copy.wait()
    token[0, 0] = rank


def corner_kernel(count, token, kept, *refs):
    total = kept[...]
    for ref in refs[:count]:
        total = total + ref[...].astype(jnp.float32)
    for z, out in enumerate(refs[count:]):
        out[...] = total[z * CAP:(z + 1) * CAP].astype(out.dtype)


def unpack_kernel(chosen, *refs):
    out = refs[-1]
    total = sum(ref[...].astype(jnp.float32) for ref in refs[:-1])
    out[...] = lax.dot_general(
        chosen[...],
        total.astype(jnp.bfloat16),
        (((0,), (0,)), ((), ())),
        preferred_element_type=jnp.float32,
    ).astype(jnp.bfloat16)


def body(dps, ranks, hidden, weight, loss_mask, target_ids, turn_ids, advantages):
    tokens, width = hidden.shape
    depth, columns = weight.shape
    zs, xs = dps // 2, ranks // 2
    half, total_rows = zs * CAP, dps * CAP
    bf16, f32, i32 = jnp.bfloat16, jnp.float32, jnp.int32
    shape = jax.ShapeDtypeStruct
    square = [(y, x) for x in reversed(range(xs)) for y in (1, 0) if x or y]
    flops = 2 * total_rows * depth * columns

    def send(value, z=0, y=0, x=0, core=0):
        far, near = 2 * z + y, 2 * x + core
        pairs = [
            (d * ranks + v, (d ^ far) * ranks + (v ^ near))
            for d in range(dps)
            for v in range(ranks)
        ]
        return lax.ppermute(value, AXES, pairs)

    group, rank = lax.axis_index("dp"), lax.axis_index("vocab")
    position = (group & 1) * zs + (group >> 1)
    where = jnp.stack([rank, position, group * ranks + rank]).astype(i32)

    packed, chosen = call(
        pack_kernel,
        (
            in_hbm(hidden),
            in_hbm(loss_mask.reshape(1, tokens)),
            in_hbm(target_ids.reshape(1, tokens)),
            in_hbm(turn_ids.reshape(1, tokens)),
        ),
        [HBM] * 4,
        (shape((CAP, width + IDS), bf16), shape((CAP, tokens), bf16)),
        (VMEM, VMEM),
        [pltpu.VMEM((tokens, width), bf16)]
        + [pltpu.VMEM((1, tokens), i32)] * 3
        + [pltpu.SemaphoreType.DMA((4,))],
    )

    line = jnp.concatenate([packed] + [send(packed, z=z) for z in range(1, zs)], axis=0)
    own = line[:, :width]
    pieces = {(0, 0): line, (0, 1): send(line, y=1)}
    for y, x in square:
        if x:
            pieces[2 * x, y] = send(own, y=y, x=x)
    for b, y in list(pieces):
        pieces[b + 1, y] = send(pieces[b, y], core=1)
    rows = [pieces[b, y] for b in range(ranks) for y in range(2)]

    held = call(
        stage_kernel,
        (line, in_hbm(weight)),
        [ANY, HBM],
        shape((depth, columns), bf16),
        VMEM,
        [pltpu.SemaphoreType.DMA],
    )
    info = call(
        info_kernel,
        (pieces[0, 0], pieces[0, 1], advantages.reshape(1, -1)),
        [VMEM] * 3,
        shape((total_rows, 128), f32),
        VMEM,
    )
    logits, stats = call(
        functools.partial(logits_kernel, ranks, dps),
        (where, info, held, *rows),
        [SMEM] + [VMEM] * (2 + len(rows)),
        (shape((total_rows, columns), f32), shape((8, total_rows), f32)),
        (VMEM, VMEM),
        flops=flops,
    )

    for hops in ([{"core": 1}], [{"y": y, "x": x} for y, x in square]):
        tables = [stats] + [send(stats, **hop) for hop in hops]
        stats = call(
            merge_kernel, tables, [VMEM] * len(tables), shape((8, total_rows), f32), VMEM
        )
    tables = [stats] + [send(stats, z=z) for z in range(1, zs)]

    outs = [
        shape((half, width), bf16 if b % 2 else f32) for b in range(ranks) for y in range(2)
    ]
    *parts, logit_grad, loss = call(
        functools.partial(grad_kernel, len(tables), ranks, dps),
        (where, info, logits, held, *tables),
        [SMEM] + [VMEM] * (3 + len(tables)),
        tuple(outs) + (shape((total_rows, columns), bf16), shape((1, 1), f32)),
        (VMEM,) * (len(outs) + 1) + (SMEM,),
        flops=flops,
    )

    arrived, last = [], None
    for y, x in square:
        beside = send(parts[4 * x + 2 + y], core=1)
        last = (parts[4 * x + y] + beside.astype(f32)).astype(bf16)
        arrived.append(send(last, y=y, x=x))
    beside = send(parts[2], core=1)

    weight_grad, token = call(
        functools.partial(weight_kernel, ranks),
        (where, last, logit_grad, *rows),
        [SMEM, ANY] + [VMEM] * (1 + len(rows)),
        (shape((depth, columns), bf16), shape((1, 1), i32)),
        (HBM, SMEM),
        [pltpu.VMEM((depth, columns), bf16), pltpu.SemaphoreType.DMA((ranks,))],
        flops=flops,
    )
    ends = call(
        functools.partial(corner_kernel, 1 + len(arrived)),
        (token, parts[0], beside, *arrived),
        [SMEM] + [VMEM] * (2 + len(arrived)),
        tuple(shape((CAP, width), bf16 if z else f32) for z in range(zs)),
        (VMEM,) * zs,
    )
    ends = [ends[0]] + [send(ends[z], z=z) for z in range(1, zs)]
    hidden_grad = call(
        unpack_kernel,
        (chosen, *ends),
        [VMEM] * (1 + len(ends)),
        shape((tokens, width), bf16),
        VMEM,
    )
    return loss[0, 0], hidden_grad, weight_grad


def solution(mesh):
    return jax.shard_map(
        functools.partial(body, mesh.shape["dp"], mesh.shape["vocab"]),
        mesh=mesh,
        in_specs=(P("dp", "vocab"), P(None, AXES), P("dp"), P("dp"), P("dp"), P()),
        out_specs=(P(), P("dp", "vocab"), P(None, AXES)),
        check_vma=False,
    )
```

```python
import functools
import math

import jax
import jax.numpy as jnp
from jax import lax
from jax.experimental import pallas as pl
from jax.experimental.pallas import tpu as pltpu
from jax.sharding import PartitionSpec as P

CAP = 32
MOST_VMEM = 56 * 1024 * 1024
IDS = 128
grad_scale = 16384.0
AXES = ("dp", "vocab")
SMEM = pl.BlockSpec(memory_space=pltpu.SMEM)
VMEM = pl.BlockSpec(memory_space=pltpu.VMEM)
HBM = pl.BlockSpec(memory_space=pltpu.HBM)
ANY = pl.BlockSpec(memory_space=pl.ANY)


def size_of(value):
    return math.prod(value.shape) * jnp.dtype(value.dtype).itemsize


def call(kernel, operands, in_specs, out_shape, out_specs, scratch=(), spare=4, flops=0):
    outs = jax.tree.leaves(out_shape)
    sized = [v for v, s in zip(operands, in_specs) if s is VMEM]
    sized += [v for v, s in zip(outs, jax.tree.leaves(out_specs)) if s is VMEM]
    held = [s for s in scratch if getattr(s, "memory_space", None) == pltpu.VMEM]
    total = sum(size_of(v) for v in sized) + sum(size_of(s) for s in held)
    return pl.pallas_call(
        kernel,
        out_shape=out_shape,
        in_specs=in_specs,
        out_specs=out_specs,
        scratch_shapes=scratch,
        compiler_params=pltpu.CompilerParams(vmem_limit_bytes=min(total + spare * 1024 * 1024, MOST_VMEM)),
        cost_estimate=pl.CostEstimate(
            flops=flops,
            bytes_accessed=sum(size_of(v) for v in list(operands) + outs),
            transcendentals=0,
        ),
    )(*operands)


def in_hbm(value):
    return pltpu.with_memory_space_constraint(value, pltpu.HBM)


def choose(mask):
    tokens = mask.shape[1]
    wide = jnp.broadcast_to(mask.astype(jnp.float32), (8, tokens))
    before = lax.broadcasted_iota(jnp.int32, (tokens, tokens), 0)
    after = lax.broadcasted_iota(jnp.int32, (tokens, tokens), 1)
    upto = (before <= after).astype(jnp.float32)
    slot = jnp.dot(
        wide.astype(jnp.bfloat16), upto.astype(jnp.bfloat16), preferred_element_type=jnp.float32
    )[0:1]
    grid = lax.broadcasted_iota(jnp.int32, (CAP, tokens), 0) + 1
    return (slot.astype(jnp.int32) == grid) & (mask == 1)


def pack_kernel(hidden_hbm, mask_hbm, target_hbm, turn_hbm, rows, chosen_out, *scratch):
    hidden, mask, target, turn, sems = scratch
    copies = []
    for place, (source, held) in enumerate(
        ((mask_hbm, mask), (target_hbm, target), (turn_hbm, turn), (hidden_hbm, hidden))
    ):
        copy = pltpu.make_async_copy(source, held, sems.at[place])
        copy.start()
        copies.append(copy)
    for copy in copies[:3]:
        copy.wait()
    width = hidden.shape[1]
    chosen = choose(mask[...])
    one_hot = chosen.astype(jnp.float32).astype(jnp.bfloat16)
    chosen_out[...] = one_hot
    turns, targets = turn[...], target[...]
    fields = (
        mask[...],
        turns & 255,
        turns >> 8,
        targets & 255,
        (targets >> 8) & 255,
        targets >> 16,
    )
    lane = lax.broadcasted_iota(jnp.int32, (CAP, IDS), 1)
    table = jnp.zeros((CAP, IDS), jnp.float32)
    for place, field in enumerate(fields):
        picked = jnp.where(chosen, field.astype(jnp.float32), 0.0)
        table = jnp.where(lane == place, jnp.sum(picked, axis=1, keepdims=True), table)
    rows[:, width:] = table.astype(jnp.bfloat16)
    copies[3].wait()
    packed = jnp.dot(one_hot, hidden[...], preferred_element_type=jnp.float32)
    rows[:, :width] = packed.astype(jnp.bfloat16)


def join_kernel(token, *refs):
    blocks, (line, own, again) = refs[:-3], refs[-3:]
    width, start = own.shape[1], 0
    skip = line.shape[0] - own.shape[0]
    for block in blocks:
        end = start + block.shape[0]
        line[start:end] = block[...]
        if start >= skip:
            own[start - skip:end - skip] = block[:, :width]
        start = end
    again[...] = line[:CAP]


def stage_kernel(after, weight, held, token, sems):
    count = sems.shape[0]
    height = weight.shape[0] // count
    copies = []
    for place in range(count):
        part = pl.ds(place * height, height)
        copy = pltpu.make_async_copy(weight.at[part], held.at[part], sems.at[place])
        copy.start()
        copies.append(copy)
    for copy in copies:
        copy.wait()
    token[0, 0] = 0


def info_kernel(*refs):
    advantages, info = refs[-2:]
    start = refs[0].shape[1] - IDS
    table = jnp.concatenate([ref[:, start:] for ref in refs[:-2]], axis=0).astype(jnp.float32)
    valid = table[:, 0:1]
    turn = table[:, 1:2] + 256.0 * table[:, 2:3]
    target = table[:, 3:4] + 256.0 * table[:, 4:5] + 65536.0 * table[:, 5:6]
    turns = advantages.shape[1]
    spot = lax.broadcasted_iota(jnp.int32, (table.shape[0], turns), 1)
    gain = jnp.sum(
        jnp.where(spot == turn.astype(jnp.int32), advantages[...], 0.0), axis=1, keepdims=True
    )
    weight = valid * gain / jnp.sum(valid)
    lane = lax.broadcasted_iota(jnp.int32, info.shape, 1)
    info[...] = jnp.where(lane == 0, weight, jnp.where(lane == 1, target, 0.0))


def reorder(stats, position, groups):
    lanes = stats.shape[1]
    lane = lax.broadcasted_iota(jnp.int32, stats.shape, 1)
    bit = 1
    while bit < groups:
        size = CAP * bit
        swapped = jnp.where(
            (lane & size) != 0,
            pltpu.roll(stats, size, 1),
            pltpu.roll(stats, lanes - size, 1),
        )
        stats = jnp.where((position & bit) != 0, swapped, stats)
        bit *= 2
    return stats


def all_rows(pieces, counts, block, width):
    start = sum(counts[:block])
    return jnp.concatenate(
        [ref[:, :width] for ref in pieces[start:start + counts[block]]], axis=0
    )


def logits_kernel(counts, groups, where, info, weight, *refs):
    blocks = len(counts)
    pieces, (logits, stats) = refs[:-2], refs[-2:]
    rank, position, shard = where[0], where[1], where[2]
    width = weight.shape[0] // blocks
    total = None
    for block in range(blocks):
        start = pl.multiple_of((rank ^ block) * width, width)
        part = jnp.dot(
            all_rows(pieces, counts, block, width),
            weight[pl.ds(start, width), :],
            preferred_element_type=jnp.float32,
        )
        total = part if total is None else total + part
    logits[...] = total
    height, columns = total.shape
    target = info[:, 1:2].astype(jnp.int32) - shard * columns
    column = lax.broadcasted_iota(jnp.int32, total.shape, 1)
    hit = jnp.sum(jnp.where(column == target, total, 0.0), axis=1, keepdims=True)
    hit = jnp.sum(hit * info[:, 0:1])
    peak = jnp.max(total, axis=1, keepdims=True)
    mass = jnp.sum(jnp.exp(total - peak), axis=1, keepdims=True)
    lane = lax.broadcasted_iota(jnp.int32, (height, 128), 1)
    table = jnp.where(lane == 0, peak, jnp.where(lane == 1, mass, hit))
    stats[...] = reorder(jnp.transpose(table)[0:8], position, groups)


def merge(tables):
    peak = functools.reduce(jnp.maximum, [table[0:1] for table in tables])
    mass = sum(table[1:2] * jnp.exp(table[0:1] - peak) for table in tables)
    hit = sum(table[2:3] for table in tables)
    return peak, mass, hit


def merge_kernel(*refs):
    out = refs[-1]
    peak, mass, hit = merge([ref[...] for ref in refs[:-1]])
    row = lax.broadcasted_iota(jnp.int32, out.shape, 0)
    out[...] = jnp.where(row == 0, peak, jnp.where(row == 1, mass, hit))


def grad_kernel(count, blocks, groups, where, info, logits, weight, *refs):
    tables = [ref[...] for ref in refs[:count]]
    away, kept, logit_grad, loss = refs[count:count + 2], refs[count + 2:count + 4], *refs[count + 4:]
    rank, position, shard = where[0], where[1], where[2]
    height, columns = logits.shape
    peak, mass, hit = merge(tables)
    log_total = jnp.broadcast_to(peak + jnp.log(mass), (8, height))
    log_total = reorder(log_total, position, groups)
    log_total = jnp.transpose(jnp.concatenate([log_total] * 16, axis=0))[:, 0:1]
    row_weight = info[:, 0:1]
    loss[0, 0] = jnp.sum(row_weight * log_total) - hit[0, 0]
    target = info[:, 1:2].astype(jnp.int32) - shard * columns
    column = lax.broadcasted_iota(jnp.int32, logits.shape, 1)
    probability = jnp.exp(logits[...] - log_total)
    grad = (
        grad_scale * row_weight * (probability - (column == target).astype(jnp.float32))
    ).astype(jnp.bfloat16)
    logit_grad[...] = grad
    part_rows = height // 4
    width = weight.shape[0] // blocks
    order = [b for b in range(blocks) if b % 2] + [b for b in range(blocks) if not b % 2]
    for block in order:
        start = pl.multiple_of((rank ^ block) * width, width)
        part = lax.dot_general(
            grad,
            weight[pl.ds(start, width), :],
            (((1,), (1,)), ((), ())),
            preferred_element_type=jnp.float32,
        )
        outs = away if block % 2 else kept
        for quarter in range(4):
            side, chunk = quarter // 2, quarter % 2
            out = outs[chunk]
            piece = part[quarter * part_rows:(quarter + 1) * part_rows]
            out[block // 2 * 2 + side] = piece.astype(out.dtype)


def weight_kernel(counts, where, after, logit_grad, *refs):
    blocks = len(counts)
    pieces, (out, token, done, sems) = refs[:-4], refs[-4:]
    rank = where[0]
    width = done.shape[0] // blocks
    copies = []
    for block in range(blocks):
        done[block * width:(block + 1) * width] = lax.dot_general(
            all_rows(pieces, counts, block, width),
            logit_grad[...],
            (((0,), (0,)), ((), ())),
            preferred_element_type=jnp.float32,
        ).astype(jnp.bfloat16)
        start = pl.multiple_of((rank ^ block) * width, width)
        copy = pltpu.make_async_copy(
            done.at[pl.ds(block * width, width)], out.at[pl.ds(start, width)], sems.at[block]
        )
        copy.start()
        copies.append(copy)
    for copy in copies:
        copy.wait()
    token[0, 0] = rank


def pair_kernel(kept, beside, *outs):
    for place, out in enumerate(reversed(outs)):
        total = kept[place] + beside[place].astype(jnp.float32)
        out[...] = total.astype(out.dtype)


def corner_kernel(count, token, kept, *refs):
    total = kept[...]
    for ref in refs[:count]:
        total = total + ref[...].astype(jnp.float32)
    for place, out in enumerate(refs[count:]):
        out[...] = total[place * CAP:(place + 1) * CAP].astype(out.dtype)


def unpack_kernel(chosen, *refs):
    out = refs[-1]
    total = sum(ref[...].astype(jnp.float32) for ref in refs[:-1])
    out[...] = lax.dot_general(
        chosen[...],
        total.astype(jnp.bfloat16),
        (((0,), (0,)), ((), ())),
        preferred_element_type=jnp.float32,
    ).astype(jnp.bfloat16)


def body(dps, ranks, hidden, weight, loss_mask, target_ids, turn_ids, advantages):
    tokens, width = hidden.shape
    depth, columns = weight.shape
    zs, xs = dps // 2, ranks // 2
    total_rows = dps * CAP
    bf16, f32, i32 = jnp.bfloat16, jnp.float32, jnp.int32
    shape = jax.ShapeDtypeStruct
    square = [(y, x) for x in reversed(range(xs)) for y in (1, 0) if x or y]
    flops = 2 * total_rows * depth * columns

    def send(value, z=0, y=0, x=0, core=0):
        far, near = 2 * z + y, 2 * x + core
        pairs = [
            (d * ranks + v, (d ^ far) * ranks + (v ^ near))
            for d in range(dps)
            for v in range(ranks)
        ]
        return lax.ppermute(value, AXES, pairs)

    group, rank = lax.axis_index("dp"), lax.axis_index("vocab")
    position = (group & 1) * zs + (group >> 1)
    where = jnp.stack([rank, position, group * ranks + rank]).astype(i32)

    packed, chosen = call(
        pack_kernel,
        (
            in_hbm(hidden),
            in_hbm(loss_mask.reshape(1, tokens)),
            in_hbm(target_ids.reshape(1, tokens)),
            in_hbm(turn_ids.reshape(1, tokens)),
        ),
        [HBM] * 4,
        (shape((CAP, width + IDS), bf16), shape((CAP, tokens), bf16)),
        (VMEM, VMEM),
        [pltpu.VMEM((tokens, width), bf16)]
        + [pltpu.VMEM((1, tokens), i32)] * 3
        + [pltpu.SemaphoreType.DMA((4,))],
    )

    held, token = call(
        stage_kernel,
        (packed, in_hbm(weight)),
        [ANY, HBM],
        (shape((depth, columns), bf16), shape((1, 1), i32)),
        (VMEM, SMEM),
        [pltpu.SemaphoreType.DMA((4,))],
    )
    pieces, before, again = {}, [], packed
    for chunk in range(2):
        near = range(chunk * zs // 2, (chunk + 1) * zs // 2)
        blocks = [send(again, z=z) if z else packed for z in near]
        line, own, again = call(
            join_kernel,
            (token, *before, *blocks),
            [SMEM] + [VMEM] * len(before + blocks),
            (
                shape(((chunk + 1) * zs // 2 * CAP, width + IDS), bf16),
                shape((zs // 2 * CAP, width), bf16),
                shape((CAP, width + IDS), bf16),
            ),
            (VMEM,) * 3,
        )
        before = [line]
        pieces[0, 1, chunk] = send(line[chunk * zs // 2 * CAP:], y=1)
        for y, x in square:
            if x:
                pieces[2 * x, y, chunk] = send(own, y=y, x=x)
    pieces[0, 0, 0] = line
    for b, y, chunk in list(pieces):
        pieces[b + 1, y, chunk] = send(pieces[b, y, chunk], core=1)
    parted = [[pieces[k] for k in sorted(pieces) if k[0] == b] for b in range(ranks)]
    counts = [len(part) for part in parted]
    rows = [piece for part in parted for piece in part]

    info = call(
        info_kernel,
        (*parted[0], advantages.reshape(1, -1)),
        [VMEM] * (counts[0] + 1),
        shape((total_rows, 128), f32),
        VMEM,
    )
    logits, stats = call(
        functools.partial(logits_kernel, counts, dps),
        (where, info, held, *rows),
        [SMEM] + [VMEM] * (2 + len(rows)),
        (shape((total_rows, columns), f32), shape((8, total_rows), f32)),
        (VMEM, VMEM),
        flops=flops,
    )

    for hops in ([{"core": 1}], [{"y": y, "x": x} for y, x in square]):
        tables = [stats] + [send(stats, **hop) for hop in hops]
        stats = call(
            merge_kernel, tables, [VMEM] * len(tables), shape((8, total_rows), f32), VMEM
        )
    tables = [stats] + [send(stats, z=z) for z in range(1, zs)]

    rows_part = total_rows // 4
    whole = (ranks, rows_part, width)
    outs = [shape(whole, bf16)] * 2 + [shape(whole, f32)] * 2
    *parts, logit_grad, loss = call(
        functools.partial(grad_kernel, len(tables), ranks, dps),
        (where, info, logits, held, *tables),
        [SMEM] + [VMEM] * (3 + len(tables)),
        tuple(outs) + (shape((total_rows, columns), bf16), shape((1, 1), f32)),
        (VMEM,) * (len(outs) + 1) + (SMEM,),
        flops=flops,
    )

    ends, token = [None] * zs, jnp.zeros((1, 1), i32)
    besides = [None, None]
    for chunk in (1, 0):
        besides[chunk] = send(parts[chunk], core=1)
    sums = [None, None]
    for chunk in (1, 0):
        small = shape((rows_part, width), bf16)
        *going, corner = call(
            pair_kernel,
            (parts[2 + chunk], besides[chunk]),
            [VMEM, VMEM],
            (small,) * (ranks - 1) + (shape((rows_part, width), f32),),
            (VMEM,) * ranks,
        )
        arrived = []
        for place, value in enumerate(going):
            x, y = divmod(ranks - 1 - place, 2)
            arrived.append(send(value, y=y, x=x))
        sums[chunk] = (corner, *arrived)
    for chunk in (1, 0):
        near = chunk * zs // 2
        parts_z = call(
            functools.partial(corner_kernel, ranks - 1),
            (token, *sums[chunk]),
            [SMEM] + [VMEM] * ranks,
            tuple(shape((CAP, width), bf16 if near + z else f32) for z in range(zs // 2)),
            (VMEM,) * (zs // 2),
        )
        for z, value in enumerate(parts_z):
            ends[near + z] = send(value, z=near + z) if near + z else value
        if chunk:
            weight_grad, token = call(
                functools.partial(weight_kernel, counts),
                (where, parts_z[0], logit_grad, *rows),
                [SMEM, ANY] + [VMEM] * (1 + len(rows)),
                (shape((depth, columns), bf16), shape((1, 1), i32)),
                (HBM, SMEM),
                [pltpu.VMEM((depth, columns), bf16), pltpu.SemaphoreType.DMA((ranks,))],
                flops=flops,
            )
    hidden_grad = call(
        unpack_kernel,
        (chosen, *ends),
        [VMEM] * (1 + len(ends)),
        shape((tokens, width), bf16),
        VMEM,
    )
    return loss[0, 0], hidden_grad, weight_grad


def solution(mesh):
    return jax.shard_map(
        functools.partial(body, mesh.shape["dp"], mesh.shape["vocab"]),
        mesh=mesh,
        in_specs=(P("dp", "vocab"), P(None, AXES), P("dp"), P("dp"), P("dp"), P()),
        out_specs=(P(), P("dp", "vocab"), P(None, AXES)),
        check_vma=False,
    )
```

```python
import functools
import math

import jax
import jax.numpy as jnp
from jax import lax
from jax.experimental import pallas as pl
from jax.experimental.pallas import tpu as pltpu
from jax.sharding import PartitionSpec as P

CAP = 32
MOST_VMEM = 56 * 1024 * 1024
IDS = 128
grad_scale = 16384.0
AXES = ("dp", "vocab")
SMEM = pl.BlockSpec(memory_space=pltpu.SMEM)
VMEM = pl.BlockSpec(memory_space=pltpu.VMEM)
HBM = pl.BlockSpec(memory_space=pltpu.HBM)
ANY = pl.BlockSpec(memory_space=pl.ANY)


def size_of(value):
    return math.prod(value.shape) * jnp.dtype(value.dtype).itemsize


def call(kernel, operands, in_specs, out_shape, out_specs, scratch=(), spare=4, flops=0):
    outs = jax.tree.leaves(out_shape)
    sized = [v for v, s in zip(operands, in_specs) if s is VMEM]
    sized += [v for v, s in zip(outs, jax.tree.leaves(out_specs)) if s is VMEM]
    held = [s for s in scratch if getattr(s, "memory_space", None) == pltpu.VMEM]
    total = sum(size_of(v) for v in sized) + sum(size_of(s) for s in held)
    return pl.pallas_call(
        kernel,
        out_shape=out_shape,
        in_specs=in_specs,
        out_specs=out_specs,
        scratch_shapes=scratch,
        compiler_params=pltpu.CompilerParams(vmem_limit_bytes=min(total + spare * 1024 * 1024, MOST_VMEM)),
        cost_estimate=pl.CostEstimate(
            flops=flops,
            bytes_accessed=sum(size_of(v) for v in list(operands) + outs),
            transcendentals=0,
        ),
    )(*operands)


def in_hbm(value):
    return pltpu.with_memory_space_constraint(value, pltpu.HBM)


def choose(mask):
    tokens = mask.shape[1]
    wide = jnp.broadcast_to(mask.astype(jnp.float32), (8, tokens))
    before = lax.broadcasted_iota(jnp.int32, (tokens, tokens), 0)
    after = lax.broadcasted_iota(jnp.int32, (tokens, tokens), 1)
    upto = (before <= after).astype(jnp.float32)
    slot = jnp.dot(
        wide.astype(jnp.bfloat16), upto.astype(jnp.bfloat16), preferred_element_type=jnp.float32
    )[0:1]
    grid = lax.broadcasted_iota(jnp.int32, (CAP, tokens), 0) + 1
    return (slot.astype(jnp.int32) == grid) & (mask == 1)


def pack_kernel(where, hidden_hbm, mask_hbm, target_hbm, turn_hbm, rows, plain, chosen_out, *scratch):
    hidden, mask, target, turn, sems = scratch
    copies = []
    for place, (source, held) in enumerate(
        ((mask_hbm, mask), (target_hbm, target), (turn_hbm, turn), (hidden_hbm, hidden))
    ):
        copy = pltpu.make_async_copy(source, held, sems.at[place])
        copy.start()
        copies.append(copy)
    for copy in copies[:3]:
        copy.wait()
    width = hidden.shape[1]
    chosen = choose(mask[...])
    one_hot = chosen.astype(jnp.float32).astype(jnp.bfloat16)
    chosen_out[...] = one_hot
    turns, targets = turn[...], target[...]
    fields = (
        mask[...],
        turns & 255,
        turns >> 8,
        targets & 255,
        (targets >> 8) & 255,
        targets >> 16,
    )
    lane = lax.broadcasted_iota(jnp.int32, (CAP, IDS), 1)
    table = jnp.zeros((CAP, IDS), jnp.float32)
    for place, field in enumerate(fields):
        picked = jnp.where(chosen, field.astype(jnp.float32), 0.0)
        table = jnp.where(lane == place, jnp.sum(picked, axis=1, keepdims=True), table)
    rows[:, width:] = table.astype(jnp.bfloat16)
    copies[3].wait()
    packed = jnp.dot(one_hot, hidden[...], preferred_element_type=jnp.float32)
    packed = packed.astype(jnp.bfloat16)
    rows[:, :width] = packed
    plain[...] = packed


def join_kernel(skipped, *refs):
    blocks, line, plain = refs[skipped:-2], refs[-2], refs[-1]
    start = 0
    for block in blocks:
        end = start + block.shape[0]
        line[start:end] = block[...]
        plain[start:end] = block[:, :plain.shape[1]]
        start = end


def stack_kernel(*refs):
    out, start = refs[-1], 0
    for block in refs[:-1]:
        out[start:start + block.shape[0]] = block[...]
        start += block.shape[0]


def stage_kernel(line, weight, held, same, sems):
    count = sems.shape[0]
    height = weight.shape[0] // count
    copies = []
    for place in range(count):
        part = pl.ds(place * height, height)
        copy = pltpu.make_async_copy(weight.at[part], held.at[part], sems.at[place])
        copy.start()
        copies.append(copy)
    same[...] = line[...]
    for copy in copies:
        copy.wait()


def info_kernel(*refs):
    advantages, info = refs[-2:]
    start = refs[0].shape[1] - IDS
    table = jnp.concatenate([ref[:, start:] for ref in refs[:-2]], axis=0).astype(jnp.float32)
    valid = table[:, 0:1]
    turn = table[:, 1:2] + 256.0 * table[:, 2:3]
    target = table[:, 3:4] + 256.0 * table[:, 4:5] + 65536.0 * table[:, 5:6]
    turns = advantages.shape[1]
    spot = lax.broadcasted_iota(jnp.int32, (table.shape[0], turns), 1)
    gain = jnp.sum(
        jnp.where(spot == turn.astype(jnp.int32), advantages[...], 0.0), axis=1, keepdims=True
    )
    weight = valid * gain / jnp.sum(valid)
    lane = lax.broadcasted_iota(jnp.int32, info.shape, 1)
    info[...] = jnp.where(lane == 0, weight, jnp.where(lane == 1, target, 0.0))


def reorder(stats, position, groups):
    lanes = stats.shape[1]
    lane = lax.broadcasted_iota(jnp.int32, stats.shape, 1)
    bit = 1
    while bit < groups:
        size = CAP * bit
        swapped = jnp.where(
            (lane & size) != 0,
            pltpu.roll(stats, size, 1),
            pltpu.roll(stats, lanes - size, 1),
        )
        stats = jnp.where((position & bit) != 0, swapped, stats)
        bit *= 2
    return stats


def all_rows(pieces, block, width):
    return jnp.concatenate([ref[:, :width] for ref in pieces[2 * block:2 * block + 2]], axis=0)


def logits_kernel(blocks, groups, where, info, weight, *refs):
    pieces, (logits, stats) = refs[:-2], refs[-2:]
    rank, position, shard = where[0], where[1], where[2]
    width = weight.shape[0] // blocks
    total = None
    for block in range(blocks):
        start = pl.multiple_of((rank ^ block) * width, width)
        part = jnp.dot(
            all_rows(pieces, block, width),
            weight[pl.ds(start, width), :],
            preferred_element_type=jnp.float32,
        )
        total = part if total is None else total + part
    logits[...] = total
    height, columns = total.shape
    target = info[:, 1:2].astype(jnp.int32) - shard * columns
    column = lax.broadcasted_iota(jnp.int32, total.shape, 1)
    hit = jnp.sum(jnp.where(column == target, total, 0.0), axis=1, keepdims=True)
    hit = jnp.sum(hit * info[:, 0:1])
    peak = jnp.max(total, axis=1, keepdims=True)
    mass = jnp.sum(jnp.exp(total - peak), axis=1, keepdims=True)
    lane = lax.broadcasted_iota(jnp.int32, (height, 128), 1)
    table = jnp.where(lane == 0, peak, jnp.where(lane == 1, mass, hit))
    stats[...] = reorder(jnp.transpose(table)[0:8], position, groups)


def merge(tables):
    peak = functools.reduce(jnp.maximum, [table[0:1] for table in tables])
    mass = sum(table[1:2] * jnp.exp(table[0:1] - peak) for table in tables)
    hit = sum(table[2:3] for table in tables)
    return peak, mass, hit


def merge_kernel(*refs):
    out = refs[-1]
    peak, mass, hit = merge([ref[...] for ref in refs[:-1]])
    row = lax.broadcasted_iota(jnp.int32, out.shape, 0)
    out[...] = jnp.where(row == 0, peak, jnp.where(row == 1, mass, hit))


def block_grads(blocks, rank, first, grad, weight, outs):
    height = grad.shape[0] // 4
    width = weight.shape[0] // blocks
    for block in range(first, blocks, 2):
        start = pl.multiple_of((rank ^ block) * width, width)
        part = lax.dot_general(
            grad,
            weight[pl.ds(start, width), :],
            (((1,), (1,)), ((), ())),
            preferred_element_type=jnp.float32,
        )
        for quarter in range(4):
            side, out = quarter // 2, outs[quarter % 2]
            piece = part[quarter * height:(quarter + 1) * height]
            out[block // 2 * 2 + side] = piece.astype(out.dtype)


def grad_kernel(blocks, groups, where, info, logits, weight, mine, theirs, *refs):
    away, (logit_grad, loss) = refs[:2], refs[2:]
    rank, position, shard = where[0], where[1], where[2]
    height, columns = logits.shape
    peak, mass, hit = merge([mine[...], theirs[...]])
    log_total = jnp.broadcast_to(peak + jnp.log(mass), (8, height))
    log_total = reorder(log_total, position, groups)
    log_total = jnp.transpose(jnp.concatenate([log_total] * 16, axis=0))[:, 0:1]
    row_weight = info[:, 0:1]
    loss[0, 0] = jnp.sum(row_weight * log_total) - hit[0, 0]
    target = info[:, 1:2].astype(jnp.int32) - shard * columns
    column = lax.broadcasted_iota(jnp.int32, logits.shape, 1)
    probability = jnp.exp(logits[...] - log_total)
    grad = (
        grad_scale * row_weight * (probability - (column == target).astype(jnp.float32))
    ).astype(jnp.bfloat16)
    logit_grad[...] = grad
    block_grads(blocks, rank, 1, grad, weight, away)


def kept_kernel(blocks, where, logit_grad, weight, *kept):
    block_grads(blocks, where[0], 0, logit_grad[...], weight, kept)


def weight_kernel(blocks, where, after, logit_grad, *refs):
    pieces, (out, token, done, sems) = refs[:-4], refs[-4:]
    rank = where[0]
    width = done.shape[0] // blocks
    copies = []
    for block in range(blocks):
        done[block * width:(block + 1) * width] = lax.dot_general(
            all_rows(pieces, block, width),
            logit_grad[...],
            (((0,), (0,)), ((), ())),
            preferred_element_type=jnp.float32,
        ).astype(jnp.bfloat16)
        start = pl.multiple_of((rank ^ block) * width, width)
        copy = pltpu.make_async_copy(
            done.at[pl.ds(block * width, width)], out.at[pl.ds(start, width)], sems.at[block]
        )
        copy.start()
        copies.append(copy)
    for copy in copies:
        copy.wait()
    token[0, 0] = rank


def pair_kernel(kept, beside, *outs):
    for place, out in enumerate(reversed(outs)):
        total = kept[place] + beside[place].astype(jnp.float32)
        out[...] = total.astype(out.dtype)


def corner_kernel(count, token, kept, *refs):
    total = kept[...]
    for ref in refs[:count]:
        total = total + ref[...].astype(jnp.float32)
    for place, out in enumerate(refs[count:]):
        out[...] = total[place * CAP:(place + 1) * CAP].astype(out.dtype)


def unpack_kernel(chosen, *refs):
    out = refs[-1]
    total = sum(ref[...].astype(jnp.float32) for ref in refs[:-1])
    out[...] = lax.dot_general(
        chosen[...],
        total.astype(jnp.bfloat16),
        (((0,), (0,)), ((), ())),
        preferred_element_type=jnp.float32,
    ).astype(jnp.bfloat16)


def body(dps, ranks, hidden, weight, loss_mask, target_ids, turn_ids, advantages):
    tokens, width = hidden.shape
    depth, columns = weight.shape
    zs, xs = dps // 2, ranks // 2
    total_rows = dps * CAP
    bf16, f32, i32 = jnp.bfloat16, jnp.float32, jnp.int32
    shape = jax.ShapeDtypeStruct
    square = [(y, x) for x in reversed(range(xs)) for y in (1, 0) if x or y]
    flops = 2 * total_rows * depth * columns

    def send(value, z=0, y=0, x=0, core=0):
        far, near = 2 * z + y, 2 * x + core
        pairs = [
            (d * ranks + v, (d ^ far) * ranks + (v ^ near))
            for d in range(dps)
            for v in range(ranks)
        ]
        return lax.ppermute(value, AXES, pairs)

    group, rank = lax.axis_index("dp"), lax.axis_index("vocab")
    position = (group & 1) * zs + (group >> 1)
    where = jnp.stack([rank, position, group * ranks + rank]).astype(i32)

    packed, plain, chosen = call(
        pack_kernel,
        (
            where,
            in_hbm(hidden),
            in_hbm(loss_mask.reshape(1, tokens)),
            in_hbm(target_ids.reshape(1, tokens)),
            in_hbm(turn_ids.reshape(1, tokens)),
        ),
        [SMEM] + [HBM] * 4,
        (
            shape((CAP, width + IDS), bf16),
            shape((CAP, width), bf16),
            shape((CAP, tokens), bf16),
        ),
        (VMEM,) * 3,
        [pltpu.VMEM((tokens, width), bf16)]
        + [pltpu.VMEM((1, tokens), i32)] * 3
        + [pltpu.SemaphoreType.DMA((4,))],
    )

    far = [send(packed, z=z) for z in range(1, zs)]
    small = {(y, x): send(plain if x else packed, y=y, x=x) for y, x in square}
    far_rows = (zs - 1) * CAP
    line, line_plain = call(
        functools.partial(join_kernel, len(small)),
        (*small.values(), *far),
        [ANY] * len(small) + [VMEM] * len(far),
        (shape((far_rows, width + IDS), bf16), shape((far_rows, width), bf16)),
        (VMEM, VMEM),
    )
    large = {(y, x): send(line_plain if x else line, y=y, x=x) for y, x in square}
    held, same = call(
        stage_kernel,
        (line, in_hbm(weight)),
        [VMEM, HBM],
        (shape((depth, columns), bf16), shape(line.shape, bf16)),
        (VMEM, VMEM),
        [pltpu.SemaphoreType.DMA((4,))],
    )
    small[0, 0], large[0, 0] = packed, same
    pieces = {}
    for y, x in [(0, 0)] + square:
        piece = call(
            stack_kernel,
            (small[y, x], large[y, x]),
            [VMEM, VMEM],
            shape((zs * CAP, small[y, x].shape[1]), bf16),
            VMEM,
        )
        pieces[2 * x, y], pieces[2 * x + 1, y] = piece, send(piece, core=1)
    rows = [pieces[b, y] for b in range(ranks) for y in range(2)]

    info = call(
        info_kernel,
        (*rows[:2], advantages.reshape(1, -1)),
        [VMEM] * 3,
        shape((total_rows, 128), f32),
        VMEM,
    )
    logits, stats = call(
        functools.partial(logits_kernel, ranks, dps),
        (where, info, held, *rows),
        [SMEM] + [VMEM] * (2 + len(rows)),
        (shape((total_rows, columns), f32), shape((8, total_rows), f32)),
        (VMEM, VMEM),
        flops=flops,
    )

    hops = [{"core": 1}]
    hops += [{"x": 1 << bit} for bit in range((xs - 1).bit_length())] + [{"y": 1}]
    hops += [{"z": 1 << bit} for bit in range((zs - 1).bit_length())]
    for place, hop in enumerate(hops):
        theirs = send(stats, **hop)
        if place + 1 < len(hops):
            stats = call(
                merge_kernel, (stats, theirs), [VMEM] * 2, shape((8, total_rows), f32), VMEM
            )

    rows_part = total_rows // 4
    whole = (ranks, rows_part, width)
    *away, logit_grad, loss = call(
        functools.partial(grad_kernel, ranks, dps),
        (where, info, logits, held, stats, theirs),
        [SMEM] + [VMEM] * 5,
        (shape(whole, bf16),) * 2 + (shape((total_rows, columns), bf16), shape((1, 1), f32)),
        (VMEM,) * 3 + (SMEM,),
        flops=flops // 2,
    )
    kept = call(
        functools.partial(kept_kernel, ranks),
        (where, logit_grad, held),
        [SMEM] + [VMEM] * 2,
        (shape(whole, f32),) * 2,
        (VMEM,) * 2,
        flops=flops // 2,
    )

    ends, token = [None] * zs, jnp.zeros((1, 1), i32)
    besides = [None, None]
    for chunk in (1, 0):
        besides[chunk] = send(away[chunk], core=1)
    sums = [None, None]
    for chunk in (1, 0):
        part = shape((rows_part, width), bf16)
        *going, corner = call(
            pair_kernel,
            (kept[chunk], besides[chunk]),
            [VMEM, VMEM],
            (part,) * (ranks - 1) + (shape((rows_part, width), f32),),
            (VMEM,) * ranks,
        )
        arrived = []
        for place, value in enumerate(going):
            x, y = divmod(ranks - 1 - place, 2)
            arrived.append(send(value, y=y, x=x))
        sums[chunk] = (corner, *arrived)
    weight_grad, last_token = call(
        functools.partial(weight_kernel, ranks),
        (where, sums[0][0], logit_grad, *rows),
        [SMEM, ANY] + [VMEM] * (1 + len(rows)),
        (shape((depth, columns), bf16), shape((1, 1), i32)),
        (HBM, SMEM),
        [pltpu.VMEM((depth, columns), bf16), pltpu.SemaphoreType.DMA((ranks,))],
        flops=flops,
    )
    for chunk in (1, 0):
        near = chunk * zs // 2
        parts_z = call(
            functools.partial(corner_kernel, ranks - 1),
            (token if chunk else last_token, *sums[chunk]),
            [SMEM] + [VMEM] * ranks,
            tuple(shape((CAP, width), bf16 if near + z else f32) for z in range(zs // 2)),
            (VMEM,) * (zs // 2),
        )
        for z, value in enumerate(parts_z):
            ends[near + z] = send(value, z=near + z) if near + z else value
    hidden_grad = call(
        unpack_kernel,
        (chosen, *ends),
        [VMEM] * (1 + len(ends)),
        shape((tokens, width), bf16),
        VMEM,
    )
    return loss[0, 0], hidden_grad, weight_grad


def solution(mesh):
    return jax.shard_map(
        functools.partial(body, mesh.shape["dp"], mesh.shape["vocab"]),
        mesh=mesh,
        in_specs=(P("dp", "vocab"), P(None, AXES), P("dp"), P("dp"), P("dp"), P()),
        out_specs=(P(), P("dp", "vocab"), P(None, AXES)),
        check_vma=False,
    )
```

```python
import functools
import math

import jax
import jax.numpy as jnp
from jax import lax
from jax.experimental import pallas as pl
from jax.experimental.pallas import tpu as pltpu
from jax.sharding import PartitionSpec as P

CAP = 32
MOST_VMEM = 56 * 1024 * 1024
IDS = 128
grad_scale = 16384.0
AXES = ("dp", "vocab")
SMEM = pl.BlockSpec(memory_space=pltpu.SMEM)
VMEM = pl.BlockSpec(memory_space=pltpu.VMEM)
HBM = pl.BlockSpec(memory_space=pltpu.HBM)
ANY = pl.BlockSpec(memory_space=pl.ANY)


def size_of(value):
    return math.prod(value.shape) * jnp.dtype(value.dtype).itemsize


def call(kernel, operands, in_specs, out_shape, out_specs, scratch=(), spare=4, flops=0, aliases={}):
    outs = jax.tree.leaves(out_shape)
    sized = [v for v, s in zip(operands, in_specs) if s is VMEM]
    sized += [v for v, s in zip(outs, jax.tree.leaves(out_specs)) if s is VMEM]
    held = [s for s in scratch if getattr(s, "memory_space", None) == pltpu.VMEM]
    total = sum(size_of(v) for v in sized) + sum(size_of(s) for s in held)
    return pl.pallas_call(
        kernel,
        out_shape=out_shape,
        in_specs=in_specs,
        out_specs=out_specs,
        scratch_shapes=scratch,
        input_output_aliases=aliases,
        compiler_params=pltpu.CompilerParams(vmem_limit_bytes=min(total + spare * 1024 * 1024, MOST_VMEM)),
        cost_estimate=pl.CostEstimate(
            flops=flops,
            bytes_accessed=sum(size_of(v) for v in list(operands) + outs),
            transcendentals=0,
        ),
    )(*operands)


def in_hbm(value):
    return pltpu.with_memory_space_constraint(value, pltpu.HBM)


def choose(mask):
    tokens = mask.shape[1]
    wide = jnp.broadcast_to(mask.astype(jnp.float32), (8, tokens))
    before = lax.broadcasted_iota(jnp.int32, (tokens, tokens), 0)
    after = lax.broadcasted_iota(jnp.int32, (tokens, tokens), 1)
    upto = (before <= after).astype(jnp.float32)
    slot = jnp.dot(
        wide.astype(jnp.bfloat16), upto.astype(jnp.bfloat16), preferred_element_type=jnp.float32
    )[0:1]
    grid = lax.broadcasted_iota(jnp.int32, (CAP, tokens), 0) + 1
    return (slot.astype(jnp.int32) == grid) & (mask == 1)


def pack_kernel(where, hidden_hbm, mask_hbm, target_hbm, turn_hbm, rows, chosen_out, *scratch):
    hidden, mask, target, turn, sems = scratch
    copies = []
    for place, (source, held) in enumerate(
        ((mask_hbm, mask), (target_hbm, target), (turn_hbm, turn), (hidden_hbm, hidden))
    ):
        copy = pltpu.make_async_copy(source, held, sems.at[place])
        copy.start()
        copies.append(copy)
    for copy in copies[:3]:
        copy.wait()
    width = hidden.shape[1]
    chosen = choose(mask[...])
    one_hot = chosen.astype(jnp.float32).astype(jnp.bfloat16)
    chosen_out[...] = one_hot
    turns, targets = turn[...], target[...]
    fields = (
        mask[...],
        turns & 255,
        turns >> 8,
        targets & 255,
        (targets >> 8) & 255,
        targets >> 16,
    )
    lane = lax.broadcasted_iota(jnp.int32, (CAP, IDS), 1)
    table = jnp.zeros((CAP, IDS), jnp.float32)
    for place, field in enumerate(fields):
        picked = jnp.where(chosen, field.astype(jnp.float32), 0.0)
        table = jnp.where(lane == place, jnp.sum(picked, axis=1, keepdims=True), table)
    rows[:, width:] = table.astype(jnp.bfloat16)
    copies[3].wait()
    packed = jnp.dot(one_hot, hidden[...], preferred_element_type=jnp.float32)
    rows[:, :width] = packed.astype(jnp.bfloat16)


def join_kernel(*refs):
    blocks, line, plain = refs[:-2], refs[-2], refs[-1]
    start = 0
    for block in blocks:
        end = start + block.shape[0]
        line[start:end] = block[...]
        plain[start:end] = block[:, :plain.shape[1]]
        start = end


def stage_kernel(line, weight, held, same, sems):
    count = sems.shape[0]
    height = weight.shape[0] // count
    copies = []
    for place in range(count):
        part = pl.ds(place * height, height)
        copy = pltpu.make_async_copy(weight.at[part], held.at[part], sems.at[place])
        copy.start()
        copies.append(copy)
    same[...] = line[...]
    for copy in copies:
        copy.wait()


def info_kernel(*refs):
    advantages, info = refs[-2:]
    start = refs[0].shape[1] - IDS
    table = jnp.concatenate([ref[:, start:] for ref in refs[:-2]], axis=0).astype(jnp.float32)
    valid = table[:, 0:1]
    turn = table[:, 1:2] + 256.0 * table[:, 2:3]
    target = table[:, 3:4] + 256.0 * table[:, 4:5] + 65536.0 * table[:, 5:6]
    turns = advantages.shape[1]
    spot = lax.broadcasted_iota(jnp.int32, (table.shape[0], turns), 1)
    gain = jnp.sum(
        jnp.where(spot == turn.astype(jnp.int32), advantages[...], 0.0), axis=1, keepdims=True
    )
    weight = valid * gain / jnp.sum(valid)
    lane = lax.broadcasted_iota(jnp.int32, info.shape, 1)
    info[...] = jnp.where(lane == 0, weight, jnp.where(lane == 1, target, 0.0))


def reorder(stats, position, groups):
    lanes = stats.shape[1]
    lane = lax.broadcasted_iota(jnp.int32, stats.shape, 1)
    bit = 1
    while bit < groups:
        size = CAP * bit
        swapped = jnp.where(
            (lane & size) != 0,
            pltpu.roll(stats, size, 1),
            pltpu.roll(stats, lanes - size, 1),
        )
        stats = jnp.where((position & bit) != 0, swapped, stats)
        bit *= 2
    return stats


def all_rows(pieces, block, width):
    return jnp.concatenate([ref[:, :width] for ref in pieces[2 * block:2 * block + 2]], axis=0)


def logits_kernel(blocks, groups, where, info, weight, *refs):
    pieces, (logits, stats) = refs[:-2], refs[-2:]
    rank, position, shard = where[0], where[1], where[2]
    width = weight.shape[0] // blocks
    total = None
    for block in range(blocks):
        start = pl.multiple_of((rank ^ block) * width, width)
        part = jnp.dot(
            all_rows(pieces, block, width),
            weight[pl.ds(start, width), :],
            preferred_element_type=jnp.float32,
        )
        total = part if total is None else total + part
    logits[...] = total
    height, columns = total.shape
    target = info[:, 1:2].astype(jnp.int32) - shard * columns
    column = lax.broadcasted_iota(jnp.int32, total.shape, 1)
    hit = jnp.sum(jnp.where(column == target, total, 0.0), axis=1, keepdims=True)
    hit = jnp.sum(hit * info[:, 0:1])
    peak = jnp.max(total, axis=1, keepdims=True)
    mass = jnp.sum(jnp.exp(total - peak), axis=1, keepdims=True)
    lane = lax.broadcasted_iota(jnp.int32, (height, 128), 1)
    table = jnp.where(lane == 0, peak, jnp.where(lane == 1, mass, hit))
    stats[...] = reorder(jnp.transpose(table)[0:8], position, groups)


def merge(tables):
    peak = functools.reduce(jnp.maximum, [table[0:1] for table in tables])
    mass = sum(table[1:2] * jnp.exp(table[0:1] - peak) for table in tables)
    hit = sum(table[2:3] for table in tables)
    return peak, mass, hit


def merge_kernel(*refs):
    out = refs[-1]
    peak, mass, hit = merge([ref[...] for ref in refs[:-1]])
    row = lax.broadcasted_iota(jnp.int32, out.shape, 0)
    out[...] = jnp.where(row == 0, peak, jnp.where(row == 1, mass, hit))


def block_grads(blocks, rank, first, grad, weight, outs):
    height = grad.shape[0] // 4
    width = weight.shape[0] // blocks
    for block in range(first, blocks, 2):
        start = pl.multiple_of((rank ^ block) * width, width)
        part = lax.dot_general(
            grad,
            weight[pl.ds(start, width), :],
            (((1,), (1,)), ((), ())),
            preferred_element_type=jnp.float32,
        )
        for quarter in range(4):
            side, out = quarter // 2, outs[quarter % 2]
            piece = part[quarter * height:(quarter + 1) * height]
            out[block // 2 * 2 + side] = piece.astype(out.dtype)


def grad_kernel(blocks, groups, where, info, logits, weight, mine, handed, *refs):
    away, (logit_grad, loss) = refs[:2], refs[2:]
    rank, position, shard = where[0], where[1], where[2]
    height, columns = logits.shape
    table = jnp.where(rank % 2 == 1, mine[...], handed[...])
    peak, mass, hit = table[0:1], table[1:2], table[2:3]
    log_total = jnp.broadcast_to(peak + jnp.log(mass), (8, height))
    log_total = reorder(log_total, position, groups)
    log_total = jnp.transpose(jnp.concatenate([log_total] * 16, axis=0))[:, 0:1]
    row_weight = info[:, 0:1]
    loss[0, 0] = jnp.sum(row_weight * log_total) - hit[0, 0]
    target = info[:, 1:2].astype(jnp.int32) - shard * columns
    column = lax.broadcasted_iota(jnp.int32, logits.shape, 1)
    probability = jnp.exp(logits[...] - log_total)
    grad = (
        grad_scale * row_weight * (probability - (column == target).astype(jnp.float32))
    ).astype(jnp.bfloat16)
    logit_grad[...] = grad
    block_grads(blocks, rank, 1, grad, weight, away)


def kept_kernel(blocks, where, logit_grad, weight, *kept):
    block_grads(blocks, where[0], 0, logit_grad[...], weight, kept)


def weight_kernel(blocks, skipped, where, after, logit_grad, *refs):
    out, token, done, sems = refs[-4:]
    pieces = refs[skipped:-4]
    rank = where[0]
    width = done.shape[0] // len(blocks)
    copies = []
    for place, block in enumerate(blocks):
        done[place * width:(place + 1) * width] = lax.dot_general(
            all_rows(pieces, place, width),
            logit_grad[...],
            (((0,), (0,)), ((), ())),
            preferred_element_type=jnp.float32,
        ).astype(jnp.bfloat16)
        start = pl.multiple_of((rank ^ block) * width, width)
        copy = pltpu.make_async_copy(
            done.at[pl.ds(place * width, width)], out.at[pl.ds(start, width)], sems.at[place]
        )
        copy.start()
        copies.append(copy)
    for copy in copies:
        copy.wait()
    token[0, 0] = rank


def pair_kernel(kept, beside, *outs):
    for place, out in enumerate(reversed(outs)):
        total = kept[place] + beside[place].astype(jnp.float32)
        out[...] = total.astype(out.dtype)


def corner_kernel(count, token, kept, *refs):
    total = kept[...]
    for ref in refs[:count]:
        total = total + ref[...].astype(jnp.float32)
    for place, out in enumerate(refs[count:]):
        out[...] = total[place * CAP:(place + 1) * CAP].astype(out.dtype)


def unpack_kernel(token, chosen, *refs):
    out = refs[-1]
    total = sum(ref[...].astype(jnp.float32) for ref in refs[:-1])
    out[...] = lax.dot_general(
        chosen[...],
        total.astype(jnp.bfloat16),
        (((0,), (0,)), ((), ())),
        preferred_element_type=jnp.float32,
    ).astype(jnp.bfloat16)


def body(dps, ranks, hidden, weight, loss_mask, target_ids, turn_ids, advantages):
    tokens, width = hidden.shape
    depth, columns = weight.shape
    zs, xs = dps // 2, ranks // 2
    total_rows = dps * CAP
    bf16, f32, i32 = jnp.bfloat16, jnp.float32, jnp.int32
    shape = jax.ShapeDtypeStruct
    square = [(y, x) for x in reversed(range(xs)) for y in (1, 0) if x or y]
    flops = 2 * total_rows * depth * columns

    def send(value, z=0, y=0, x=0, core=0, sources=(0, 1)):
        far, near = 2 * z + y, 2 * x + core
        pairs = [
            (d * ranks + v, (d ^ far) * ranks + (v ^ near))
            for d in range(dps)
            for v in range(ranks)
            if v % 2 in sources
        ]
        return lax.ppermute(value, AXES, pairs)

    group, rank = lax.axis_index("dp"), lax.axis_index("vocab")
    position = (group & 1) * zs + (group >> 1)
    where = jnp.stack([rank, position, group * ranks + rank]).astype(i32)

    packed, chosen = call(
        pack_kernel,
        (
            where,
            in_hbm(hidden),
            in_hbm(loss_mask.reshape(1, tokens)),
            in_hbm(target_ids.reshape(1, tokens)),
            in_hbm(turn_ids.reshape(1, tokens)),
        ),
        [SMEM] + [HBM] * 4,
        (
            shape((CAP, width + IDS), bf16),
            shape((CAP, tokens), bf16),
        ),
        (VMEM,) * 2,
        [pltpu.VMEM((tokens, width), bf16)]
        + [pltpu.VMEM((1, tokens), i32)] * 3
        + [pltpu.SemaphoreType.DMA((4,))],
    )

    blocks = [packed] + [send(packed, z=z) for z in range(1, zs)]
    line_rows = zs * CAP
    line, line_plain = call(
        join_kernel,
        blocks,
        [VMEM] * zs,
        (shape((line_rows, width + IDS), bf16), shape((line_rows, width), bf16)),
        (VMEM, VMEM),
    )
    pieces = {(2 * x, y): send(line_plain if x else line, y=y, x=x) for y, x in square}
    held, same = call(
        stage_kernel,
        (line, in_hbm(weight)),
        [VMEM, HBM],
        (shape((depth, columns), bf16), shape(line.shape, bf16)),
        (VMEM, VMEM),
        [pltpu.SemaphoreType.DMA((4,))],
    )
    pieces[0, 0] = same
    for b, y in list(pieces):
        pieces[b + 1, y] = send(pieces[b, y], core=1)
    rows = [pieces[b, y] for b in range(ranks) for y in range(2)]

    info = call(
        info_kernel,
        (*rows[:2], advantages.reshape(1, -1)),
        [VMEM] * 3,
        shape((total_rows, 128), f32),
        VMEM,
    )
    logits, stats = call(
        functools.partial(logits_kernel, ranks, dps),
        (where, info, held, *rows),
        [SMEM] + [VMEM] * (2 + len(rows)),
        (shape((total_rows, columns), f32), shape((8, total_rows), f32)),
        (VMEM, VMEM),
        flops=flops,
    )

    def combine(*tables):
        return call(
            merge_kernel, tables, [VMEM] * len(tables), shape((8, total_rows), f32), VMEM
        )

    stats = combine(stats, send(stats, core=1, sources=(0,)))
    for bit in range((xs - 1).bit_length()):
        stats = combine(stats, send(stats, x=1 << bit, sources=(1,)))
    stats = combine(stats, send(stats, y=1, sources=(1,)))
    stats = combine(stats, *[send(stats, z=z, sources=(1,)) for z in range(1, zs)])
    handed = send(stats, core=1, sources=(1,))

    rows_part = total_rows // 4
    whole = (ranks, rows_part, width)
    *away, logit_grad, loss = call(
        functools.partial(grad_kernel, ranks, dps),
        (where, info, logits, held, stats, handed),
        [SMEM] + [VMEM] * 5,
        (shape(whole, bf16),) * 2 + (shape((total_rows, columns), bf16), shape((1, 1), f32)),
        (VMEM,) * 3 + (SMEM,),
        flops=flops // 2,
    )
    kept = call(
        functools.partial(kept_kernel, ranks),
        (where, logit_grad, held),
        [SMEM] + [VMEM] * 2,
        (shape(whole, f32),) * 2,
        (VMEM,) * 2,
        flops=flops // 2,
    )

    ends = [None] * zs
    besides = [None, None]
    for chunk in (1, 0):
        besides[chunk] = send(away[chunk], core=1)
    sums = [None, None]
    for chunk in (1, 0):
        part = shape((rows_part, width), bf16)
        *going, corner = call(
            pair_kernel,
            (kept[chunk], besides[chunk]),
            [VMEM, VMEM],
            (part,) * (ranks - 1) + (shape((rows_part, width), f32),),
            (VMEM,) * ranks,
        )
        arrived = []
        for place, value in enumerate(going):
            x, y = divmod(ranks - 1 - place, 2)
            arrived.append(send(value, y=y, x=x))
        sums[chunk] = (corner, *arrived)
    weight_half = ranks // 2

    def weight_part(first, after, partial):
        blocks = range(first, first + weight_half)
        chosen_rows = rows[2 * first:2 * (first + weight_half)]
        return call(
            functools.partial(weight_kernel, blocks, len(partial)),
            (where, after, logit_grad, *partial, *chosen_rows),
            [SMEM, ANY, VMEM] + [HBM] * len(partial) + [VMEM] * len(chosen_rows),
            (shape((depth, columns), bf16), shape((1, 1), i32)),
            (HBM, SMEM),
            [
                pltpu.VMEM((depth // 2, columns), bf16),
                pltpu.SemaphoreType.DMA((weight_half,)),
            ],
            flops=flops // 2,
            aliases={3: 0} if partial else {},
        )

    weight_grad, token = weight_part(0, sums[0][0], ())
    for chunk in (1, 0):
        near = chunk * zs // 2
        parts_z = call(
            functools.partial(corner_kernel, ranks - 1),
            (token, *sums[chunk]),
            [SMEM] + [VMEM] * ranks,
            tuple(shape((CAP, width), bf16 if near + z else f32) for z in range(zs // 2)),
            (VMEM,) * (zs // 2),
        )
        for z, value in enumerate(parts_z):
            ends[near + z] = send(value, z=near + z) if near + z else value
    weight_grad, token = weight_part(weight_half, parts_z[0], (weight_grad,))
    hidden_grad = call(
        unpack_kernel,
        (token, chosen, *ends),
        [SMEM] + [VMEM] * (1 + len(ends)),
        shape((tokens, width), bf16),
        VMEM,
    )
    return loss[0, 0], hidden_grad, weight_grad


def solution(mesh):
    return jax.shard_map(
        functools.partial(body, mesh.shape["dp"], mesh.shape["vocab"]),
        mesh=mesh,
        in_specs=(P("dp", "vocab"), P(None, AXES), P("dp"), P("dp"), P("dp"), P()),
        out_specs=(P(), P("dp", "vocab"), P(None, AXES)),
        check_vma=False,
    )
```

```python
import functools
import math

import jax
import jax.numpy as jnp
from jax import lax
from jax.experimental import pallas as pl
from jax.experimental.pallas import tpu as pltpu
from jax.sharding import PartitionSpec as P

CAP = 32
MOST_VMEM = 56 * 1024 * 1024
IDS = 128
grad_scale = 16384.0
AXES = ("dp", "vocab")
SMEM = pl.BlockSpec(memory_space=pltpu.SMEM)
VMEM = pl.BlockSpec(memory_space=pltpu.VMEM)
HBM = pl.BlockSpec(memory_space=pltpu.HBM)
ANY = pl.BlockSpec(memory_space=pl.ANY)


def size_of(value):
    return math.prod(value.shape) * jnp.dtype(value.dtype).itemsize


def call(kernel, operands, in_specs, out_shape, out_specs, scratch=(), spare=4, flops=0, aliases={}):
    outs = jax.tree.leaves(out_shape)
    sized = [v for v, s in zip(operands, in_specs) if s is VMEM]
    sized += [v for v, s in zip(outs, jax.tree.leaves(out_specs)) if s is VMEM]
    held = [s for s in scratch if getattr(s, "memory_space", None) == pltpu.VMEM]
    total = sum(size_of(v) for v in sized) + sum(size_of(s) for s in held)
    return pl.pallas_call(
        kernel,
        out_shape=out_shape,
        in_specs=in_specs,
        out_specs=out_specs,
        scratch_shapes=scratch,
        input_output_aliases=aliases,
        compiler_params=pltpu.CompilerParams(vmem_limit_bytes=min(total + spare * 1024 * 1024, MOST_VMEM)),
        cost_estimate=pl.CostEstimate(
            flops=flops,
            bytes_accessed=sum(size_of(v) for v in list(operands) + outs),
            transcendentals=0,
        ),
    )(*operands)


def in_hbm(value):
    return pltpu.with_memory_space_constraint(value, pltpu.HBM)


def coordinates():
    group, rank = lax.axis_index("dp"), lax.axis_index("vocab")
    groups, ranks = lax.axis_size("dp"), lax.axis_size("vocab")
    position = group % 2 * (groups // 2) + group // 2
    return rank, position, group * ranks + rank


def choose(mask):
    tokens = mask.shape[1]
    wide = jnp.broadcast_to(mask.astype(jnp.float32), (8, tokens))
    before = lax.broadcasted_iota(jnp.int32, (tokens, tokens), 0)
    after = lax.broadcasted_iota(jnp.int32, (tokens, tokens), 1)
    upto = (before <= after).astype(jnp.float32)
    slot = jnp.dot(
        wide.astype(jnp.bfloat16), upto.astype(jnp.bfloat16), preferred_element_type=jnp.float32
    )[0:1]
    grid = lax.broadcasted_iota(jnp.int32, (CAP, tokens), 0) + 1
    return (slot.astype(jnp.int32) == grid) & (mask == 1)


def pack_kernel(hidden_hbm, mask_hbm, target_hbm, turn_hbm, rows, chosen_out, *scratch):
    hidden, mask, target, turn, sems = scratch
    copies = []
    for place, (source, held) in enumerate(
        ((mask_hbm, mask), (target_hbm, target), (turn_hbm, turn), (hidden_hbm, hidden))
    ):
        copy = pltpu.make_async_copy(source, held, sems.at[place])
        copy.start()
        copies.append(copy)
    for copy in copies[:3]:
        copy.wait()
    width = hidden.shape[1]
    chosen = choose(mask[...])
    one_hot = chosen.astype(jnp.float32).astype(jnp.bfloat16)
    chosen_out[...] = one_hot
    turns, targets = turn[...], target[...]
    fields = (
        mask[...],
        turns & 255,
        turns >> 8,
        targets & 255,
        (targets >> 8) & 255,
        targets >> 16,
    )
    lane = lax.broadcasted_iota(jnp.int32, (CAP, IDS), 1)
    table = jnp.zeros((CAP, IDS), jnp.float32)
    for place, field in enumerate(fields):
        picked = jnp.where(chosen, field.astype(jnp.float32), 0.0)
        table = jnp.where(lane == place, jnp.sum(picked, axis=1, keepdims=True), table)
    rows[:, width:] = table.astype(jnp.bfloat16)
    copies[3].wait()
    packed = jnp.dot(one_hot, hidden[...], preferred_element_type=jnp.float32)
    rows[:, :width] = packed.astype(jnp.bfloat16)


def join_kernel(*refs):
    blocks, line, plain = refs[:-2], refs[-2], refs[-1]
    start = 0
    for block in blocks:
        end = start + block.shape[0]
        line[start:end] = block[...]
        plain[start:end] = block[:, :plain.shape[1]]
        start = end


def stage_kernel(line, weight, held, same, sems):
    count = sems.shape[0]
    height = weight.shape[0] // count
    copies = []
    for place in range(count):
        part = pl.ds(place * height, height)
        copy = pltpu.make_async_copy(weight.at[part], held.at[part], sems.at[place])
        copy.start()
        copies.append(copy)
    same[...] = line[...]
    for copy in copies:
        copy.wait()


def info_kernel(*refs):
    advantages, info = refs[-2:]
    start = refs[0].shape[1] - IDS
    table = jnp.concatenate([ref[:, start:] for ref in refs[:-2]], axis=0).astype(jnp.float32)
    valid = table[:, 0:1]
    turn = table[:, 1:2] + 256.0 * table[:, 2:3]
    target = table[:, 3:4] + 256.0 * table[:, 4:5] + 65536.0 * table[:, 5:6]
    turns = advantages.shape[1]
    spot = lax.broadcasted_iota(jnp.int32, (table.shape[0], turns), 1)
    gain = jnp.sum(
        jnp.where(spot == turn.astype(jnp.int32), advantages[...], 0.0), axis=1, keepdims=True
    )
    weight = valid * gain / jnp.sum(valid)
    lane = lax.broadcasted_iota(jnp.int32, info.shape, 1)
    info[...] = jnp.where(lane == 0, weight, jnp.where(lane == 1, target, 0.0))


def reorder(stats, position, groups):
    lanes = stats.shape[1]
    lane = lax.broadcasted_iota(jnp.int32, stats.shape, 1)
    bit = 1
    while bit < groups:
        size = CAP * bit
        swapped = jnp.where(
            (lane & size) != 0,
            pltpu.roll(stats, size, 1),
            pltpu.roll(stats, lanes - size, 1),
        )
        stats = jnp.where((position & bit) != 0, swapped, stats)
        bit *= 2
    return stats


def all_rows(pieces, block, width):
    return jnp.concatenate([ref[:, :width] for ref in pieces[2 * block:2 * block + 2]], axis=0)


def logits_kernel(blocks, groups, info, weight, *refs):
    pieces, (logits, stats) = refs[:-2], refs[-2:]
    rank, position, shard = coordinates()
    width = weight.shape[0] // blocks
    total = None
    for block in range(blocks):
        start = pl.multiple_of((rank ^ block) * width, width)
        part = jnp.dot(
            all_rows(pieces, block, width),
            weight[pl.ds(start, width), :],
            preferred_element_type=jnp.float32,
        )
        total = part if total is None else total + part
    logits[...] = total
    height, columns = total.shape
    target = info[:, 1:2].astype(jnp.int32) - shard * columns
    column = lax.broadcasted_iota(jnp.int32, total.shape, 1)
    hit = jnp.sum(jnp.where(column == target, total, 0.0), axis=1, keepdims=True)
    hit = jnp.sum(hit * info[:, 0:1])
    peak = jnp.max(total, axis=1, keepdims=True)
    mass = jnp.sum(jnp.exp(total - peak), axis=1, keepdims=True)
    lane = lax.broadcasted_iota(jnp.int32, (height, 128), 1)
    table = jnp.where(lane == 0, peak, jnp.where(lane == 1, mass, hit))
    stats[...] = reorder(jnp.transpose(table)[0:8], position, groups)


def merge(tables):
    peak = functools.reduce(jnp.maximum, [table[0:1] for table in tables])
    mass = sum(table[1:2] * jnp.exp(table[0:1] - peak) for table in tables)
    hit = sum(table[2:3] for table in tables)
    return peak, mass, hit


def merge_kernel(*refs):
    out = refs[-1]
    peak, mass, hit = merge([ref[...] for ref in refs[:-1]])
    row = lax.broadcasted_iota(jnp.int32, out.shape, 0)
    out[...] = jnp.where(row == 0, peak, jnp.where(row == 1, mass, hit))


def block_grads(blocks, rank, first, grad, weight, outs):
    height = grad.shape[0] // 4
    width = weight.shape[0] // blocks
    for block in range(first, blocks, 2):
        start = pl.multiple_of((rank ^ block) * width, width)
        part = lax.dot_general(
            grad,
            weight[pl.ds(start, width), :],
            (((1,), (1,)), ((), ())),
            preferred_element_type=jnp.float32,
        )
        for quarter in range(4):
            side, out = quarter // 2, outs[quarter % 2]
            piece = part[quarter * height:(quarter + 1) * height]
            out[block // 2 * 2 + side] = piece.astype(out.dtype)


def grad_kernel(blocks, groups, info, logits, weight, mine, handed, *refs):
    away, (logit_grad, loss) = refs[:2], refs[2:]
    rank, position, shard = coordinates()
    height, columns = logits.shape
    table = jnp.where(rank % 2 == 1, mine[...], handed[...])
    peak, mass, hit = table[0:1], table[1:2], table[2:3]
    log_total = jnp.broadcast_to(peak + jnp.log(mass), (8, height))
    log_total = reorder(log_total, position, groups)
    log_total = jnp.transpose(jnp.concatenate([log_total] * 16, axis=0))[:, 0:1]
    row_weight = info[:, 0:1]
    loss[0, 0] = jnp.sum(row_weight * log_total) - hit[0, 0]
    target = info[:, 1:2].astype(jnp.int32) - shard * columns
    column = lax.broadcasted_iota(jnp.int32, logits.shape, 1)
    probability = jnp.exp(logits[...] - log_total)
    grad = (
        grad_scale * row_weight * (probability - (column == target).astype(jnp.float32))
    ).astype(jnp.bfloat16)
    logit_grad[...] = grad
    block_grads(blocks, rank, 1, grad, weight, away)


def kept_kernel(blocks, logit_grad, weight, *kept):
    block_grads(blocks, coordinates()[0], 0, logit_grad[...], weight, kept)


def weight_kernel(blocks, after, logit_grad, *refs):
    pieces, (out, finished, done, sems) = refs[:-4], refs[-4:]
    rank = coordinates()[0]
    finished[...] = jnp.zeros_like(finished)
    width = done.shape[0] // blocks
    copies = []
    for block in range(blocks):
        done[block * width:(block + 1) * width] = lax.dot_general(
            all_rows(pieces, block, width),
            logit_grad[...],
            (((0,), (0,)), ((), ())),
            preferred_element_type=jnp.float32,
        ).astype(jnp.bfloat16)
        start = pl.multiple_of((rank ^ block) * width, width)
        copy = pltpu.make_async_copy(
            done.at[pl.ds(block * width, width)], out.at[pl.ds(start, width)], sems.at[block]
        )
        copy.start()
        copies.append(copy)
    for copy in copies:
        copy.wait()


def pair_kernel(kept, beside, *outs):
    for place, out in enumerate(reversed(outs)):
        total = kept[place] + beside[place].astype(jnp.float32)
        out[...] = total.astype(out.dtype)


def corner_kernel(count, after, kept, *refs):
    total = kept[...]
    for ref in refs[:count]:
        total = total + ref[...].astype(jnp.float32)
    for place, out in enumerate(refs[count:]):
        out[...] = total[place * CAP:(place + 1) * CAP].astype(out.dtype)


def unpack_kernel(chosen, *refs):
    out = refs[-1]
    total = sum(ref[...].astype(jnp.float32) for ref in refs[:-1])
    out[...] = lax.dot_general(
        chosen[...],
        total.astype(jnp.bfloat16),
        (((0,), (0,)), ((), ())),
        preferred_element_type=jnp.float32,
    ).astype(jnp.bfloat16)


def body(dps, ranks, hidden, weight, loss_mask, target_ids, turn_ids, advantages):
    tokens, width = hidden.shape
    depth, columns = weight.shape
    zs, xs = dps // 2, ranks // 2
    total_rows = dps * CAP
    bf16, f32, i32 = jnp.bfloat16, jnp.float32, jnp.int32
    shape = jax.ShapeDtypeStruct
    square = [(y, x) for x in reversed(range(xs)) for y in (1, 0) if x or y]
    flops = 2 * total_rows * depth * columns

    def send(value, z=0, y=0, x=0, core=0, cores=(0, 1)):
        far, near = 2 * z + y, 2 * x + core
        pairs = [
            (d * ranks + v, (d ^ far) * ranks + (v ^ near) if v % 2 in cores else d * ranks + v)
            for d in range(dps)
            for v in range(ranks)
        ]
        return lax.ppermute(value, AXES, pairs)

    packed, chosen = call(
        pack_kernel,
        (
            in_hbm(hidden),
            in_hbm(loss_mask.reshape(1, tokens)),
            in_hbm(target_ids.reshape(1, tokens)),
            in_hbm(turn_ids.reshape(1, tokens)),
        ),
        [HBM] * 4,
        (
            shape((CAP, width + IDS), bf16),
            shape((CAP, tokens), bf16),
        ),
        (VMEM,) * 2,
        [pltpu.VMEM((tokens, width), bf16)]
        + [pltpu.VMEM((1, tokens), i32)] * 3
        + [pltpu.SemaphoreType.DMA((4,))],
    )

    blocks = [packed] + [send(packed, z=z) for z in range(1, zs)]
    line_rows = zs * CAP
    line, line_plain = call(
        join_kernel,
        blocks,
        [VMEM] * zs,
        (shape((line_rows, width + IDS), bf16), shape((line_rows, width), bf16)),
        (VMEM, VMEM),
    )
    pieces = {(2 * x, y): send(line_plain if x else line, y=y, x=x) for y, x in square}
    held, same = call(
        stage_kernel,
        (line, in_hbm(weight)),
        [VMEM, HBM],
        (shape((depth, columns), bf16), shape(line.shape, bf16)),
        (VMEM, VMEM),
        [pltpu.SemaphoreType.DMA((4,))],
    )
    pieces[0, 0] = same
    for b, y in list(pieces):
        pieces[b + 1, y] = send(pieces[b, y], core=1)
    rows = [pieces[b, y] for b in range(ranks) for y in range(2)]

    info = call(
        info_kernel,
        (*rows[:2], advantages.reshape(1, -1)),
        [VMEM] * 3,
        shape((total_rows, 128), f32),
        VMEM,
    )
    logits, stats = call(
        functools.partial(logits_kernel, ranks, dps),
        (info, held, *rows),
        [VMEM] * (2 + len(rows)),
        (shape((total_rows, columns), f32), shape((8, total_rows), f32)),
        (VMEM, VMEM),
        flops=flops,
    )

    def combine(*tables):
        return call(
            merge_kernel, tables, [VMEM] * len(tables), shape((8, total_rows), f32), VMEM
        )

    stats = combine(stats, send(stats, core=1))
    for bit in range((xs - 1).bit_length()):
        stats = combine(stats, send(stats, x=1 << bit, cores=(1,)))
    stats = combine(stats, send(stats, y=1, cores=(1,)))
    stats = combine(stats, *[send(stats, z=z, cores=(1,)) for z in range(1, zs)])
    handed = send(stats, core=1)

    rows_part = total_rows // 4
    whole = (ranks, rows_part, width)
    *away, logit_grad, loss = call(
        functools.partial(grad_kernel, ranks, dps),
        (info, logits, held, stats, handed),
        [VMEM] * 5,
        (shape(whole, bf16),) * 2 + (shape((total_rows, columns), bf16), shape((1, 1), f32)),
        (VMEM,) * 3 + (SMEM,),
        flops=flops // 2,
    )
    kept = call(
        functools.partial(kept_kernel, ranks),
        (logit_grad, held),
        [VMEM] * 2,
        (shape(whole, f32),) * 2,
        (VMEM,) * 2,
        flops=flops // 2,
    )

    ends = [None] * zs
    besides = [None, None]
    for chunk in (1, 0):
        besides[chunk] = send(away[chunk], core=1)
    sums = [None, None]
    for chunk in (1, 0):
        part = shape((rows_part, width), bf16)
        *going, corner = call(
            pair_kernel,
            (kept[chunk], besides[chunk]),
            [VMEM, VMEM],
            (part,) * (ranks - 1) + (shape((rows_part, width), f32),),
            (VMEM,) * ranks,
        )
        arrived = []
        for place, value in enumerate(going):
            x, y = divmod(ranks - 1 - place, 2)
            arrived.append(send(value, y=y, x=x))
        sums[chunk] = (corner, *arrived)
    weight_grad, finished = call(
        functools.partial(weight_kernel, ranks),
        (sums[0][0], logit_grad, *rows),
        [ANY] + [VMEM] * (1 + len(rows)),
        (shape((depth, columns), bf16), shape((8, 128), f32)),
        (HBM, VMEM),
        [pltpu.VMEM((depth, columns), bf16), pltpu.SemaphoreType.DMA((ranks,))],
        flops=flops,
    )
    for chunk in (1, 0):
        near = chunk * zs // 2
        parts_z = call(
            functools.partial(corner_kernel, ranks - 1),
            (logit_grad if chunk else finished, *sums[chunk]),
            [ANY] + [VMEM] * ranks,
            tuple(shape((CAP, width), bf16 if near + z else f32) for z in range(zs // 2)),
            (VMEM,) * (zs // 2),
        )
        for z, value in enumerate(parts_z):
            ends[near + z] = send(value, z=near + z) if near + z else value
    hidden_grad = call(
        unpack_kernel,
        (chosen, *ends),
        [VMEM] * (1 + len(ends)),
        shape((tokens, width), bf16),
        VMEM,
    )
    return loss[0, 0], hidden_grad, weight_grad


def solution(mesh):
    return jax.shard_map(
        functools.partial(body, mesh.shape["dp"], mesh.shape["vocab"]),
        mesh=mesh,
        in_specs=(P("dp", "vocab"), P(None, AXES), P("dp"), P("dp"), P("dp"), P()),
        out_specs=(P(), P("dp", "vocab"), P(None, AXES)),
        check_vma=False,
    )
```

```python
import functools
import math

import jax
import jax.numpy as jnp
from jax import lax
from jax.experimental import pallas as pl
from jax.experimental.pallas import tpu as pltpu
from jax.sharding import PartitionSpec as P

CAP = 32
MOST_VMEM = 56 * 1024 * 1024
IDS = 128
grad_scale = 16384.0
AXES = ("dp", "vocab")
SMEM = pl.BlockSpec(memory_space=pltpu.SMEM)
VMEM = pl.BlockSpec(memory_space=pltpu.VMEM)
HBM = pl.BlockSpec(memory_space=pltpu.HBM)
ANY = pl.BlockSpec(memory_space=pl.ANY)


def size_of(value):
    return math.prod(value.shape) * jnp.dtype(value.dtype).itemsize


def call(kernel, operands, in_specs, out_shape, out_specs, scratch=(), spare=4, flops=0, aliases={}):
    outs = jax.tree.leaves(out_shape)
    sized = [v for v, s in zip(operands, in_specs) if s is VMEM]
    sized += [v for v, s in zip(outs, jax.tree.leaves(out_specs)) if s is VMEM]
    held = [s for s in scratch if getattr(s, "memory_space", None) == pltpu.VMEM]
    total = sum(size_of(v) for v in sized) + sum(size_of(s) for s in held)
    return pl.pallas_call(
        kernel,
        out_shape=out_shape,
        in_specs=in_specs,
        out_specs=out_specs,
        scratch_shapes=scratch,
        input_output_aliases=aliases,
        compiler_params=pltpu.CompilerParams(vmem_limit_bytes=min(total + spare * 1024 * 1024, MOST_VMEM)),
        cost_estimate=pl.CostEstimate(
            flops=flops,
            bytes_accessed=sum(size_of(v) for v in list(operands) + outs),
            transcendentals=0,
        ),
    )(*operands)


def in_hbm(value):
    return pltpu.with_memory_space_constraint(value, pltpu.HBM)


def coordinates():
    group, rank = lax.axis_index("dp"), lax.axis_index("vocab")
    groups, ranks = lax.axis_size("dp"), lax.axis_size("vocab")
    position = group % 2 * (groups // 2) + group // 2
    return rank, position, group * ranks + rank


def choose(mask):
    tokens = mask.shape[1]
    wide = jnp.broadcast_to(mask.astype(jnp.float32), (8, tokens))
    before = lax.broadcasted_iota(jnp.int32, (tokens, tokens), 0)
    after = lax.broadcasted_iota(jnp.int32, (tokens, tokens), 1)
    upto = (before <= after).astype(jnp.float32)
    slot = jnp.dot(
        wide.astype(jnp.bfloat16), upto.astype(jnp.bfloat16), preferred_element_type=jnp.float32
    )[0:1]
    grid = lax.broadcasted_iota(jnp.int32, (CAP, tokens), 0) + 1
    return (slot.astype(jnp.int32) == grid) & (mask == 1)


def pack_kernel(hidden_hbm, mask_hbm, target_hbm, turn_hbm, rows, chosen_out, *scratch):
    hidden, mask, target, turn, sems = scratch
    copies = []
    for place, (source, held) in enumerate(
        ((mask_hbm, mask), (target_hbm, target), (turn_hbm, turn), (hidden_hbm, hidden))
    ):
        copy = pltpu.make_async_copy(source, held, sems.at[place])
        copy.start()
        copies.append(copy)
    for copy in copies[:3]:
        copy.wait()
    width = hidden.shape[1]
    chosen = choose(mask[...])
    one_hot = chosen.astype(jnp.float32).astype(jnp.bfloat16)
    chosen_out[...] = one_hot
    turns, targets = turn[...], target[...]
    fields = (
        mask[...],
        turns & 255,
        turns >> 8,
        targets & 255,
        (targets >> 8) & 255,
        targets >> 16,
    )
    lane = lax.broadcasted_iota(jnp.int32, (CAP, IDS), 1)
    table = jnp.zeros((CAP, IDS), jnp.float32)
    for place, field in enumerate(fields):
        picked = jnp.where(chosen, field.astype(jnp.float32), 0.0)
        table = jnp.where(lane == place, jnp.sum(picked, axis=1, keepdims=True), table)
    rows[:, width:] = table.astype(jnp.bfloat16)
    copies[3].wait()
    packed = jnp.dot(one_hot, hidden[...], preferred_element_type=jnp.float32)
    rows[:, :width] = packed.astype(jnp.bfloat16)


def join_kernel(*refs):
    blocks, line, plain = refs[:-2], refs[-2], refs[-1]
    start = 0
    for block in blocks:
        end = start + block.shape[0]
        line[start:end] = block[...]
        plain[start:end] = block[:, :plain.shape[1]]
        start = end


def stage_kernel(line, weight, held, same, sems):
    count = sems.shape[0]
    height = weight.shape[0] // count
    copies = []
    for place in range(count):
        part = pl.ds(place * height, height)
        copy = pltpu.make_async_copy(weight.at[part], held.at[part], sems.at[place])
        copy.start()
        copies.append(copy)
    same[...] = line[...]
    for copy in copies:
        copy.wait()


def info_kernel(*refs):
    advantages, info = refs[-2:]
    start = refs[0].shape[1] - IDS
    table = jnp.concatenate([ref[:, start:] for ref in refs[:-2]], axis=0).astype(jnp.float32)
    valid = table[:, 0:1]
    turn = table[:, 1:2] + 256.0 * table[:, 2:3]
    target = table[:, 3:4] + 256.0 * table[:, 4:5] + 65536.0 * table[:, 5:6]
    turns = advantages.shape[1]
    spot = lax.broadcasted_iota(jnp.int32, (table.shape[0], turns), 1)
    gain = jnp.sum(
        jnp.where(spot == turn.astype(jnp.int32), advantages[...], 0.0), axis=1, keepdims=True
    )
    weight = valid * gain / jnp.sum(valid)
    lane = lax.broadcasted_iota(jnp.int32, info.shape, 1)
    info[...] = jnp.where(lane == 0, weight, jnp.where(lane == 1, target, 0.0))


def reorder(stats, position, groups):
    lanes = stats.shape[1]
    lane = lax.broadcasted_iota(jnp.int32, stats.shape, 1)
    bit = 1
    while bit < groups:
        size = CAP * bit
        swapped = jnp.where(
            (lane & size) != 0,
            pltpu.roll(stats, size, 1),
            pltpu.roll(stats, lanes - size, 1),
        )
        stats = jnp.where((position & bit) != 0, swapped, stats)
        bit *= 2
    return stats


def all_rows(pieces, block, width):
    return jnp.concatenate([ref[:, :width] for ref in pieces[2 * block:2 * block + 2]], axis=0)


def logits_kernel(blocks, groups, info, weight, *refs):
    pieces, (logits, stats) = refs[:-2], refs[-2:]
    rank, position, shard = coordinates()
    width = weight.shape[0] // blocks
    total = None
    for block in range(blocks):
        start = pl.multiple_of((rank ^ block) * width, width)
        part = jnp.dot(
            all_rows(pieces, block, width),
            weight[pl.ds(start, width), :],
            preferred_element_type=jnp.float32,
        )
        total = part if total is None else total + part
    logits[...] = total
    height, columns = total.shape
    target = info[:, 1:2].astype(jnp.int32) - shard * columns
    column = lax.broadcasted_iota(jnp.int32, total.shape, 1)
    hit = jnp.sum(jnp.where(column == target, total, 0.0), axis=1, keepdims=True)
    hit = jnp.sum(hit * info[:, 0:1])
    peak = jnp.max(total, axis=1, keepdims=True)
    mass = jnp.sum(jnp.exp(total - peak), axis=1, keepdims=True)
    lane = lax.broadcasted_iota(jnp.int32, (height, 128), 1)
    table = jnp.where(lane == 0, peak, jnp.where(lane == 1, mass, hit))
    stats[...] = reorder(jnp.transpose(table)[0:8], position, groups)


def merge(tables):
    peak = functools.reduce(jnp.maximum, [table[0:1] for table in tables])
    mass = sum(table[1:2] * jnp.exp(table[0:1] - peak) for table in tables)
    hit = sum(table[2:3] for table in tables)
    return peak, mass, hit


def merge_kernel(mine, theirs, out):
    peak, mass, hit = merge([mine[...], theirs[...]])
    line = jnp.concatenate([peak, mass, hit[:, :128]], axis=1)
    out[...] = jnp.broadcast_to(line[None], out.shape)


def block_grads(blocks, rank, first, grad, weight, outs):
    height = grad.shape[0] // 4
    width = weight.shape[0] // blocks
    for block in range(first, blocks, 2):
        start = pl.multiple_of((rank ^ block) * width, width)
        part = lax.dot_general(
            grad,
            weight[pl.ds(start, width), :],
            (((1,), (1,)), ((), ())),
            preferred_element_type=jnp.float32,
        )
        for quarter in range(4):
            side, out = quarter // 2, outs[quarter % 2]
            piece = part[quarter * height:(quarter + 1) * height]
            out[block // 2 * 2 + side] = piece.astype(out.dtype)


def grad_kernel(blocks, groups, info, logits, weight, stats, *refs):
    away, (logit_grad, loss) = refs[:2], refs[2:]
    rank, position, shard = coordinates()
    height, columns = logits.shape
    peaks, masses = stats[:, :, :height], stats[:, :, height:2 * height]
    peak = jnp.max(peaks, axis=0)
    mass = jnp.sum(masses * jnp.exp(peaks - peak[None]), axis=0)
    hit = jnp.sum(stats[:, :, 2 * height:], axis=0)
    log_total = jnp.broadcast_to(peak + jnp.log(mass), (8, height))
    log_total = reorder(log_total, position, groups)
    log_total = jnp.transpose(jnp.concatenate([log_total] * 16, axis=0))[:, 0:1]
    row_weight = info[:, 0:1]
    loss[0, 0] = jnp.sum(row_weight * log_total) - hit[0, 0]
    target = info[:, 1:2].astype(jnp.int32) - shard * columns
    column = lax.broadcasted_iota(jnp.int32, logits.shape, 1)
    probability = jnp.exp(logits[...] - log_total)
    grad = (
        grad_scale * row_weight * (probability - (column == target).astype(jnp.float32))
    ).astype(jnp.bfloat16)
    logit_grad[...] = grad
    block_grads(blocks, rank, 1, grad, weight, away)


def kept_kernel(blocks, logit_grad, weight, *kept):
    block_grads(blocks, coordinates()[0], 0, logit_grad[...], weight, kept)


def weight_kernel(blocks, after, logit_grad, *refs):
    pieces, (out, finished, done, sems) = refs[:-4], refs[-4:]
    rank = coordinates()[0]
    finished[...] = jnp.zeros_like(finished)
    width = done.shape[0] // blocks
    copies = []
    for block in range(blocks):
        done[block * width:(block + 1) * width] = lax.dot_general(
            all_rows(pieces, block, width),
            logit_grad[...],
            (((0,), (0,)), ((), ())),
            preferred_element_type=jnp.float32,
        ).astype(jnp.bfloat16)
        start = pl.multiple_of((rank ^ block) * width, width)
        copy = pltpu.make_async_copy(
            done.at[pl.ds(block * width, width)], out.at[pl.ds(start, width)], sems.at[block]
        )
        copy.start()
        copies.append(copy)
    for copy in copies:
        copy.wait()


def pair_kernel(order, kept, beside, *outs):
    for place, out in zip(order, outs):
        total = kept[place] + beside[place].astype(jnp.float32)
        out[...] = total.astype(out.dtype)


def corner_kernel(count, after, kept, *refs):
    total = kept[...]
    for ref in refs[:count]:
        total = total + ref[...].astype(jnp.float32)
    for place, out in enumerate(refs[count:]):
        out[...] = total[place * CAP:(place + 1) * CAP].astype(out.dtype)


def unpack_kernel(chosen, *refs):
    out = refs[-1]
    total = sum(ref[...].astype(jnp.float32) for ref in refs[:-1])
    out[...] = lax.dot_general(
        chosen[...],
        total.astype(jnp.bfloat16),
        (((0,), (0,)), ((), ())),
        preferred_element_type=jnp.float32,
    ).astype(jnp.bfloat16)


def body(dps, ranks, hidden, weight, loss_mask, target_ids, turn_ids, advantages):
    tokens, width = hidden.shape
    depth, columns = weight.shape
    zs, xs = dps // 2, ranks // 2
    total_rows = dps * CAP
    bf16, f32, i32 = jnp.bfloat16, jnp.float32, jnp.int32
    shape = jax.ShapeDtypeStruct
    square = [(y, x) for x in reversed(range(xs)) for y in (1, 0) if x or y]
    flops = 2 * total_rows * depth * columns

    def send(value, z=0, y=0, x=0, core=0):
        far, near = 2 * z + y, 2 * x + core
        pairs = [
            (d * ranks + v, (d ^ far) * ranks + (v ^ near))
            for d in range(dps)
            for v in range(ranks)
        ]
        return lax.ppermute(value, AXES, pairs)

    packed, chosen = call(
        pack_kernel,
        (
            in_hbm(hidden),
            in_hbm(loss_mask.reshape(1, tokens)),
            in_hbm(target_ids.reshape(1, tokens)),
            in_hbm(turn_ids.reshape(1, tokens)),
        ),
        [HBM] * 4,
        (
            shape((CAP, width + IDS), bf16),
            shape((CAP, tokens), bf16),
        ),
        (VMEM,) * 2,
        [pltpu.VMEM((tokens, width), bf16)]
        + [pltpu.VMEM((1, tokens), i32)] * 3
        + [pltpu.SemaphoreType.DMA((4,))],
    )

    blocks = [packed] + [send(packed, z=z) for z in range(1, zs)]
    line_rows = zs * CAP
    line, line_plain = call(
        join_kernel,
        blocks,
        [VMEM] * zs,
        (shape((line_rows, width + IDS), bf16), shape((line_rows, width), bf16)),
        (VMEM, VMEM),
    )
    pieces = {(2 * x, y): send(line_plain if x else line, y=y, x=x) for y, x in square}
    held, same = call(
        stage_kernel,
        (line, in_hbm(weight)),
        [VMEM, HBM],
        (shape((depth, columns), bf16), shape(line.shape, bf16)),
        (VMEM, VMEM),
        [pltpu.SemaphoreType.DMA((4,))],
    )
    pieces[0, 0] = same
    for b, y in list(pieces):
        pieces[b + 1, y] = send(pieces[b, y], core=1)
    rows = [pieces[b, y] for b in range(ranks) for y in range(2)]

    info = call(
        info_kernel,
        (*rows[:2], advantages.reshape(1, -1)),
        [VMEM] * 3,
        shape((total_rows, 128), f32),
        VMEM,
    )
    logits, stats = call(
        functools.partial(logits_kernel, ranks, dps),
        (info, held, *rows),
        [VMEM] * (2 + len(rows)),
        (shape((total_rows, columns), f32), shape((8, total_rows), f32)),
        (VMEM, VMEM),
        flops=flops,
    )

    stats = call(
        merge_kernel,
        (stats, send(stats, core=1)),
        [VMEM] * 2,
        shape((dps * xs, 1, 2 * total_rows + 128), f32),
        VMEM,
    )
    chips = [
        [d * ranks + v for d in range(dps) for v in range(core, ranks, 2)] for core in range(2)
    ]
    stats = lax.all_to_all(stats, AXES, 0, 0, axis_index_groups=chips)

    rows_part = total_rows // 4
    whole = (ranks, rows_part, width)
    *away, logit_grad, loss = call(
        functools.partial(grad_kernel, ranks, dps),
        (info, logits, held, stats),
        [VMEM] * 4,
        (shape(whole, bf16),) * 2 + (shape((total_rows, columns), bf16), shape((1, 1), f32)),
        (VMEM,) * 3 + (SMEM,),
        flops=flops // 2,
    )
    kept = call(
        functools.partial(kept_kernel, ranks),
        (logit_grad, held),
        [VMEM] * 2,
        (shape(whole, f32),) * 2,
        (VMEM,) * 2,
        flops=flops // 2,
    )

    ends = [None] * zs
    besides = [None, None]
    order = sorted(range(1, ranks), key=lambda place: (place % 2 + (place > 1), place))
    for chunk in (1, 0):
        besides[chunk] = send(away[chunk], core=1)
    sums = [None, None]
    for chunk in (1, 0):
        part = shape((rows_part, width), bf16)
        *going, corner = call(
            functools.partial(pair_kernel, order + [0]),
            (kept[chunk], besides[chunk]),
            [VMEM, VMEM],
            (part,) * (ranks - 1) + (shape((rows_part, width), f32),),
            (VMEM,) * ranks,
        )
        arrived = []
        for place, value in zip(order, going):
            arrived.append(send(value, y=place % 2, x=place // 2))
        sums[chunk] = (corner, *arrived)
    weight_grad, finished = call(
        functools.partial(weight_kernel, ranks),
        (sums[0][0], logit_grad, *rows),
        [ANY] + [VMEM] * (1 + len(rows)),
        (shape((depth, columns), bf16), shape((8, 128), f32)),
        (HBM, VMEM),
        [pltpu.VMEM((depth, columns), bf16), pltpu.SemaphoreType.DMA((ranks,))],
        flops=flops,
    )
    for chunk in (1, 0):
        near = chunk * zs // 2
        parts_z = call(
            functools.partial(corner_kernel, ranks - 1),
            (logit_grad if chunk else finished, *sums[chunk]),
            [ANY] + [VMEM] * ranks,
            tuple(shape((CAP, width), bf16 if near + z else f32) for z in range(zs // 2)),
            (VMEM,) * (zs // 2),
        )
        for z, value in enumerate(parts_z):
            ends[near + z] = send(value, z=near + z) if near + z else value
    hidden_grad = call(
        unpack_kernel,
        (chosen, *ends),
        [VMEM] * (1 + len(ends)),
        shape((tokens, width), bf16),
        VMEM,
    )
    return loss[0, 0], hidden_grad, weight_grad


def solution(mesh):
    return jax.shard_map(
        functools.partial(body, mesh.shape["dp"], mesh.shape["vocab"]),
        mesh=mesh,
        in_specs=(P("dp", "vocab"), P(None, AXES), P("dp"), P("dp"), P("dp"), P()),
        out_specs=(P(), P("dp", "vocab"), P(None, AXES)),
        check_vma=False,
    )
```

```python
import functools
import math

import jax
import jax.numpy as jnp
from jax import lax
from jax.experimental import pallas as pl
from jax.experimental.pallas import tpu as pltpu
from jax.sharding import PartitionSpec as P

CAP = 32
MOST_VMEM = 56 * 1024 * 1024
IDS = 128
grad_scale = 16384.0
AXES = ("dp", "vocab")
SMEM = pl.BlockSpec(memory_space=pltpu.SMEM)
VMEM = pl.BlockSpec(memory_space=pltpu.VMEM)
HBM = pl.BlockSpec(memory_space=pltpu.HBM)
ANY = pl.BlockSpec(memory_space=pl.ANY)


def size_of(value):
    return math.prod(value.shape) * jnp.dtype(value.dtype).itemsize


def call(kernel, operands, in_specs, out_shape, out_specs, scratch=(), spare=4, flops=0, aliases={}):
    outs = jax.tree.leaves(out_shape)
    sized = [v for v, s in zip(operands, in_specs) if s is VMEM]
    sized += [v for v, s in zip(outs, jax.tree.leaves(out_specs)) if s is VMEM]
    held = [s for s in scratch if getattr(s, "memory_space", None) == pltpu.VMEM]
    total = sum(size_of(v) for v in sized) + sum(size_of(s) for s in held)
    return pl.pallas_call(
        kernel,
        out_shape=out_shape,
        in_specs=in_specs,
        out_specs=out_specs,
        scratch_shapes=scratch,
        input_output_aliases=aliases,
        compiler_params=pltpu.CompilerParams(vmem_limit_bytes=min(total + spare * 1024 * 1024, MOST_VMEM)),
        cost_estimate=pl.CostEstimate(
            flops=flops,
            bytes_accessed=sum(size_of(v) for v in list(operands) + outs),
            transcendentals=0,
        ),
    )(*operands)


def in_hbm(value):
    return pltpu.with_memory_space_constraint(value, pltpu.HBM)


def coordinates():
    group, rank = lax.axis_index("dp"), lax.axis_index("vocab")
    groups, ranks = lax.axis_size("dp"), lax.axis_size("vocab")
    position = group % 2 * (groups // 2) + group // 2
    return rank, position, group * ranks + rank


def choose(mask):
    tokens = mask.shape[1]
    wide = jnp.broadcast_to(mask.astype(jnp.float32), (8, tokens))
    before = lax.broadcasted_iota(jnp.int32, (tokens, tokens), 0)
    after = lax.broadcasted_iota(jnp.int32, (tokens, tokens), 1)
    upto = (before <= after).astype(jnp.float32)
    slot = jnp.dot(
        wide.astype(jnp.bfloat16), upto.astype(jnp.bfloat16), preferred_element_type=jnp.float32
    )[0:1]
    grid = lax.broadcasted_iota(jnp.int32, (CAP, tokens), 0) + 1
    return (slot.astype(jnp.int32) == grid) & (mask == 1)


def pack_kernel(hidden_hbm, mask_hbm, target_hbm, turn_hbm, rows, chosen_out, *scratch):
    hidden, mask, target, turn, sems = scratch
    copies = []
    for place, (source, held) in enumerate(
        ((mask_hbm, mask), (target_hbm, target), (turn_hbm, turn), (hidden_hbm, hidden))
    ):
        copy = pltpu.make_async_copy(source, held, sems.at[place])
        copy.start()
        copies.append(copy)
    for copy in copies[:3]:
        copy.wait()
    width = hidden.shape[1]
    chosen = choose(mask[...])
    one_hot = chosen.astype(jnp.float32).astype(jnp.bfloat16)
    chosen_out[...] = one_hot
    turns, targets = turn[...], target[...]
    fields = (
        mask[...],
        turns & 255,
        turns >> 8,
        targets & 255,
        (targets >> 8) & 255,
        targets >> 16,
    )
    lane = lax.broadcasted_iota(jnp.int32, (CAP, IDS), 1)
    table = jnp.zeros((CAP, IDS), jnp.float32)
    for place, field in enumerate(fields):
        picked = jnp.where(chosen, field.astype(jnp.float32), 0.0)
        table = jnp.where(lane == place, jnp.sum(picked, axis=1, keepdims=True), table)
    rows[:, width:] = table.astype(jnp.bfloat16)
    copies[3].wait()
    packed = jnp.dot(one_hot, hidden[...], preferred_element_type=jnp.float32)
    rows[:, :width] = packed.astype(jnp.bfloat16)


def join_kernel(order, *refs):
    blocks, line, plain = refs[:-2], refs[-2], refs[-1]
    for place, block in zip(order, blocks):
        line[place * CAP:(place + 1) * CAP] = block[...]
        plain[place * CAP:(place + 1) * CAP] = block[:, :plain.shape[1]]


def stage_kernel(line, weight, held, same, sems):
    count = sems.shape[0]
    height = weight.shape[0] // count
    copies = []
    for place in range(count):
        part = pl.ds(place * height, height)
        copy = pltpu.make_async_copy(weight.at[part], held.at[part], sems.at[place])
        copy.start()
        copies.append(copy)
    same[...] = line[...]
    for copy in copies:
        copy.wait()


def info_kernel(*refs):
    advantages, info = refs[-2:]
    start = refs[0].shape[1] - IDS
    table = jnp.concatenate([ref[:, start:] for ref in refs[:-2]], axis=0).astype(jnp.float32)
    valid = table[:, 0:1]
    turn = table[:, 1:2] + 256.0 * table[:, 2:3]
    target = table[:, 3:4] + 256.0 * table[:, 4:5] + 65536.0 * table[:, 5:6]
    turns = advantages.shape[1]
    spot = lax.broadcasted_iota(jnp.int32, (table.shape[0], turns), 1)
    gain = jnp.sum(
        jnp.where(spot == turn.astype(jnp.int32), advantages[...], 0.0), axis=1, keepdims=True
    )
    weight = valid * gain / jnp.sum(valid)
    lane = lax.broadcasted_iota(jnp.int32, info.shape, 1)
    info[...] = jnp.where(lane == 0, weight, jnp.where(lane == 1, target, 0.0))


def reorder(stats, position, groups):
    lanes = stats.shape[1]
    lane = lax.broadcasted_iota(jnp.int32, stats.shape, 1)
    bit = 1
    while bit < groups:
        size = CAP * bit
        swapped = jnp.where(
            (lane & size) != 0,
            pltpu.roll(stats, size, 1),
            pltpu.roll(stats, lanes - size, 1),
        )
        stats = jnp.where((position & bit) != 0, swapped, stats)
        bit *= 2
    return stats


def all_rows(pieces, block, width):
    return jnp.concatenate([ref[:, :width] for ref in pieces[2 * block:2 * block + 2]], axis=0)


def some_logits(blocks, first, pieces, weight):
    width = weight.shape[0] // blocks
    rank, total = coordinates()[0], None
    for place, block in enumerate(range(first, blocks, 2)):
        start = pl.multiple_of((rank ^ block) * width, width)
        part = jnp.dot(
            all_rows(pieces, place, width),
            weight[pl.ds(start, width), :],
            preferred_element_type=jnp.float32,
        )
        total = part if total is None else total + part
    return total


def first_kernel(blocks, weight, *refs):
    refs[-1][...] = some_logits(blocks, 0, refs[:-1], weight)


def logits_kernel(blocks, groups, info, partial, weight, *refs):
    pieces, (logits, stats) = refs[:-2], refs[-2:]
    _, position, shard = coordinates()
    total = partial[...] + some_logits(blocks, 1, pieces, weight)
    logits[...] = total
    height, columns = total.shape
    target = info[:, 1:2].astype(jnp.int32) - shard * columns
    column = lax.broadcasted_iota(jnp.int32, total.shape, 1)
    hit = jnp.sum(jnp.where(column == target, total, 0.0), axis=1, keepdims=True)
    hit = jnp.sum(hit * info[:, 0:1])
    peak = jnp.max(total, axis=1, keepdims=True)
    mass = jnp.sum(jnp.exp(total - peak), axis=1, keepdims=True)
    lane = lax.broadcasted_iota(jnp.int32, (height, 128), 1)
    table = jnp.where(lane == 0, peak, jnp.where(lane == 1, mass, hit))
    table = reorder(jnp.transpose(table)[0:8], position, groups)
    line = jnp.concatenate([table[0:1], table[1:2], table[2:3, :128]], axis=1)
    stats[...] = jnp.broadcast_to(line[None], stats.shape)


def block_grads(blocks, rank, first, grad, weight, outs):
    height = grad.shape[0] // 4
    width = weight.shape[0] // blocks
    for block in range(first, blocks, 2):
        start = pl.multiple_of((rank ^ block) * width, width)
        part = lax.dot_general(
            grad,
            weight[pl.ds(start, width), :],
            (((1,), (1,)), ((), ())),
            preferred_element_type=jnp.float32,
        )
        for quarter in range(4):
            side, out = quarter // 2, outs[quarter % 2]
            piece = part[quarter * height:(quarter + 1) * height]
            out[block // 2 * 2 + side] = piece.astype(out.dtype)


def grad_kernel(blocks, groups, info, logits, weight, stats, *refs):
    away, (logit_grad, loss) = refs[:2], refs[2:]
    rank, position, shard = coordinates()
    height, columns = logits.shape
    peaks, masses = stats[:, :, :height], stats[:, :, height:2 * height]
    peak = jnp.max(peaks, axis=0)
    mass = jnp.sum(masses * jnp.exp(peaks - peak[None]), axis=0)
    hit = jnp.sum(stats[:, :, 2 * height:], axis=0)
    log_total = jnp.broadcast_to(peak + jnp.log(mass), (8, height))
    log_total = reorder(log_total, position, groups)
    log_total = jnp.transpose(jnp.concatenate([log_total] * 16, axis=0))[:, 0:1]
    row_weight = info[:, 0:1]
    loss[0, 0] = jnp.sum(row_weight * log_total) - hit[0, 0]
    target = info[:, 1:2].astype(jnp.int32) - shard * columns
    column = lax.broadcasted_iota(jnp.int32, logits.shape, 1)
    probability = jnp.exp(logits[...] - log_total)
    grad = (
        grad_scale * row_weight * (probability - (column == target).astype(jnp.float32))
    ).astype(jnp.bfloat16)
    logit_grad[...] = grad
    block_grads(blocks, rank, 1, grad, weight, away)


def kept_kernel(blocks, logit_grad, weight, *kept):
    block_grads(blocks, coordinates()[0], 0, logit_grad[...], weight, kept)


def weight_kernel(blocks, after, logit_grad, *refs):
    pieces, (out, finished, done, sems) = refs[:-4], refs[-4:]
    rank = coordinates()[0]
    finished[...] = jnp.zeros_like(finished)
    width = done.shape[0] // blocks
    copies = []
    for block in range(blocks):
        done[block * width:(block + 1) * width] = lax.dot_general(
            all_rows(pieces, block, width),
            logit_grad[...],
            (((0,), (0,)), ((), ())),
            preferred_element_type=jnp.float32,
        ).astype(jnp.bfloat16)
        start = pl.multiple_of((rank ^ block) * width, width)
        copy = pltpu.make_async_copy(
            done.at[pl.ds(block * width, width)], out.at[pl.ds(start, width)], sems.at[block]
        )
        copy.start()
        copies.append(copy)
    for copy in copies:
        copy.wait()


def pair_kernel(order, kept, beside, *outs):
    for place, out in zip(order, outs):
        total = kept[place] + beside[place].astype(jnp.float32)
        out[...] = total.astype(out.dtype)


def corner_kernel(count, after, kept, *refs):
    total = kept[...]
    for ref in refs[:count]:
        total = total + ref[...].astype(jnp.float32)
    for place, out in enumerate(refs[count:]):
        out[...] = total[place * CAP:(place + 1) * CAP].astype(out.dtype)


def unpack_kernel(chosen, *refs):
    out = refs[-1]
    total = sum(ref[...].astype(jnp.float32) for ref in refs[:-1])
    out[...] = lax.dot_general(
        chosen[...],
        total.astype(jnp.bfloat16),
        (((0,), (0,)), ((), ())),
        preferred_element_type=jnp.float32,
    ).astype(jnp.bfloat16)


def body(dps, ranks, hidden, weight, loss_mask, target_ids, turn_ids, advantages):
    tokens, width = hidden.shape
    depth, columns = weight.shape
    zs, xs = dps // 2, ranks // 2
    total_rows = dps * CAP
    bf16, f32, i32 = jnp.bfloat16, jnp.float32, jnp.int32
    shape = jax.ShapeDtypeStruct
    square = [(y, x) for x in reversed(range(xs)) for y in (1, 0) if x or y]
    flops = 2 * total_rows * depth * columns

    def send(value, z=0, y=0, x=0, core=0):
        far, near = 2 * z + y, 2 * x + core
        pairs = [
            (d * ranks + v, (d ^ far) * ranks + (v ^ near))
            for d in range(dps)
            for v in range(ranks)
        ]
        return lax.ppermute(value, AXES, pairs)

    packed, chosen = call(
        pack_kernel,
        (
            in_hbm(hidden),
            in_hbm(loss_mask.reshape(1, tokens)),
            in_hbm(target_ids.reshape(1, tokens)),
            in_hbm(turn_ids.reshape(1, tokens)),
        ),
        [HBM] * 4,
        (
            shape((CAP, width + IDS), bf16),
            shape((CAP, tokens), bf16),
        ),
        (VMEM,) * 2,
        [pltpu.VMEM((tokens, width), bf16)]
        + [pltpu.VMEM((1, tokens), i32)] * 3
        + [pltpu.SemaphoreType.DMA((4,))],
    )

    line_order = [0, 1] + list(range(zs - 1, 1, -1))
    blocks = [send(packed, z=z) if z else packed for z in line_order]
    line_rows = zs * CAP
    line, line_plain = call(
        functools.partial(join_kernel, line_order),
        blocks,
        [VMEM] * zs,
        (shape((line_rows, width + IDS), bf16), shape((line_rows, width), bf16)),
        (VMEM, VMEM),
    )
    pieces = {(2 * x, y): send(line_plain if x else line, y=y, x=x) for y, x in square}
    held, same = call(
        stage_kernel,
        (line, in_hbm(weight)),
        [VMEM, HBM],
        (shape((depth, columns), bf16), shape(line.shape, bf16)),
        (VMEM, VMEM),
        [pltpu.SemaphoreType.DMA((4,))],
    )
    pieces[0, 0] = same
    for b, y in list(pieces):
        pieces[b + 1, y] = send(pieces[b, y], core=1)
    rows = [pieces[b, y] for b in range(ranks) for y in range(2)]

    info = call(
        info_kernel,
        (*rows[:2], advantages.reshape(1, -1)),
        [VMEM] * 3,
        shape((total_rows, 128), f32),
        VMEM,
    )
    near = [pieces[b, y] for b in range(0, ranks, 2) for y in range(2)]
    partial = call(
        functools.partial(first_kernel, ranks),
        (held, *near),
        [VMEM] * (1 + len(near)),
        shape((total_rows, columns), f32),
        VMEM,
        flops=flops // 2,
    )
    beside = [pieces[b, y] for b in range(1, ranks, 2) for y in range(2)]
    logits, stats = call(
        functools.partial(logits_kernel, ranks, dps),
        (info, partial, held, *beside),
        [VMEM] * (3 + len(beside)),
        (
            shape((total_rows, columns), f32),
            shape((dps * ranks, 1, 2 * total_rows + 128), f32),
        ),
        (VMEM, VMEM),
        flops=flops // 2,
    )
    stats = lax.all_to_all(stats, AXES, 0, 0)

    rows_part = total_rows // 4
    whole = (ranks, rows_part, width)
    *away, logit_grad, loss = call(
        functools.partial(grad_kernel, ranks, dps),
        (info, logits, held, stats),
        [VMEM] * 4,
        (shape(whole, bf16),) * 2 + (shape((total_rows, columns), bf16), shape((1, 1), f32)),
        (VMEM,) * 3 + (SMEM,),
        flops=flops // 2,
    )
    kept = call(
        functools.partial(kept_kernel, ranks),
        (logit_grad, held),
        [VMEM] * 2,
        (shape(whole, f32),) * 2,
        (VMEM,) * 2,
        flops=flops // 2,
    )

    ends = [None] * zs
    besides = [None, None]
    order = sorted(range(1, ranks), key=lambda place: (place % 2 + (place > 1), place))
    for chunk in (1, 0):
        besides[chunk] = send(away[chunk], core=1)
    sums = [None, None]
    for chunk in (1, 0):
        part = shape((rows_part, width), bf16)
        *going, corner = call(
            functools.partial(pair_kernel, order + [0]),
            (kept[chunk], besides[chunk]),
            [VMEM, VMEM],
            (part,) * (ranks - 1) + (shape((rows_part, width), f32),),
            (VMEM,) * ranks,
        )
        arrived = []
        for place, value in zip(order, going):
            arrived.append(send(value, y=place % 2, x=place // 2))
        sums[chunk] = (corner, *arrived)
    weight_grad, finished = call(
        functools.partial(weight_kernel, ranks),
        (sums[0][0], logit_grad, *rows),
        [ANY] + [VMEM] * (1 + len(rows)),
        (shape((depth, columns), bf16), shape((8, 128), f32)),
        (HBM, VMEM),
        [pltpu.VMEM((depth, columns), bf16), pltpu.SemaphoreType.DMA((ranks,))],
        flops=flops,
    )
    for chunk in (1, 0):
        near = chunk * zs // 2
        parts_z = call(
            functools.partial(corner_kernel, ranks - 1),
            (logit_grad if chunk else finished, *sums[chunk]),
            [ANY] + [VMEM] * ranks,
            tuple(shape((CAP, width), bf16 if near + z else f32) for z in range(zs // 2)),
            (VMEM,) * (zs // 2),
        )
        for z, value in enumerate(parts_z):
            ends[near + z] = send(value, z=near + z) if near + z else value
    hidden_grad = call(
        unpack_kernel,
        (chosen, *ends),
        [VMEM] * (1 + len(ends)),
        shape((tokens, width), bf16),
        VMEM,
    )
    return loss[0, 0], hidden_grad, weight_grad


def solution(mesh):
    return jax.shard_map(
        functools.partial(body, mesh.shape["dp"], mesh.shape["vocab"]),
        mesh=mesh,
        in_specs=(P("dp", "vocab"), P(None, AXES), P("dp"), P("dp"), P("dp"), P()),
        out_specs=(P(), P("dp", "vocab"), P(None, AXES)),
        check_vma=False,
    )
```

```python
import functools
import math

import jax
import jax.numpy as jnp
from jax import lax
from jax.experimental import pallas as pl
from jax.experimental.pallas import tpu as pltpu
from jax.sharding import PartitionSpec as P

CAP = 32
MOST_VMEM = 56 * 1024 * 1024
IDS = 128
grad_scale = 16384.0
AXES = ("dp", "vocab")
SMEM = pl.BlockSpec(memory_space=pltpu.SMEM)
VMEM = pl.BlockSpec(memory_space=pltpu.VMEM)
HBM = pl.BlockSpec(memory_space=pltpu.HBM)
ANY = pl.BlockSpec(memory_space=pl.ANY)


def size_of(value):
    return math.prod(value.shape) * jnp.dtype(value.dtype).itemsize


def call(kernel, operands, in_specs, out_shape, out_specs, scratch=(), spare=4, flops=0, aliases={}):
    outs = jax.tree.leaves(out_shape)
    sized = [v for v, s in zip(operands, in_specs) if s is VMEM]
    sized += [v for v, s in zip(outs, jax.tree.leaves(out_specs)) if s is VMEM]
    held = [s for s in scratch if getattr(s, "memory_space", None) == pltpu.VMEM]
    total = sum(size_of(v) for v in sized) + sum(size_of(s) for s in held)
    return pl.pallas_call(
        kernel,
        out_shape=out_shape,
        in_specs=in_specs,
        out_specs=out_specs,
        scratch_shapes=scratch,
        input_output_aliases=aliases,
        compiler_params=pltpu.CompilerParams(vmem_limit_bytes=min(total + spare * 1024 * 1024, MOST_VMEM)),
        cost_estimate=pl.CostEstimate(
            flops=flops,
            bytes_accessed=sum(size_of(v) for v in list(operands) + outs),
            transcendentals=0,
        ),
    )(*operands)


def in_hbm(value):
    return pltpu.with_memory_space_constraint(value, pltpu.HBM)


def coordinates():
    group, rank = lax.axis_index("dp"), lax.axis_index("vocab")
    groups, ranks = lax.axis_size("dp"), lax.axis_size("vocab")
    position = group % 2 * (groups // 2) + group // 2
    return rank, position, group * ranks + rank


def choose(mask):
    tokens = mask.shape[1]
    wide = jnp.broadcast_to(mask.astype(jnp.float32), (8, tokens))
    before = lax.broadcasted_iota(jnp.int32, (tokens, tokens), 0)
    after = lax.broadcasted_iota(jnp.int32, (tokens, tokens), 1)
    upto = (before <= after).astype(jnp.float32)
    slot = jnp.dot(
        wide.astype(jnp.bfloat16), upto.astype(jnp.bfloat16), preferred_element_type=jnp.float32
    )[0:1]
    grid = lax.broadcasted_iota(jnp.int32, (CAP, tokens), 0) + 1
    return (slot.astype(jnp.int32) == grid) & (mask == 1)


def pack_kernel(hidden_hbm, mask_hbm, target_hbm, turn_hbm, rows, chosen_out, *scratch):
    hidden, mask, target, turn, sems = scratch
    copies = []
    for place, (source, held) in enumerate(
        ((mask_hbm, mask), (target_hbm, target), (turn_hbm, turn), (hidden_hbm, hidden))
    ):
        copy = pltpu.make_async_copy(source, held, sems.at[place])
        copy.start()
        copies.append(copy)
    for copy in copies[:3]:
        copy.wait()
    width = hidden.shape[1]
    chosen = choose(mask[...])
    one_hot = chosen.astype(jnp.float32).astype(jnp.bfloat16)
    chosen_out[...] = one_hot
    turns, targets = turn[...], target[...]
    fields = (
        mask[...],
        turns & 255,
        turns >> 8,
        targets & 255,
        (targets >> 8) & 255,
        targets >> 16,
    )
    lane = lax.broadcasted_iota(jnp.int32, (CAP, IDS), 1)
    table = jnp.zeros((CAP, IDS), jnp.float32)
    for place, field in enumerate(fields):
        picked = jnp.where(chosen, field.astype(jnp.float32), 0.0)
        table = jnp.where(lane == place, jnp.sum(picked, axis=1, keepdims=True), table)
    rows[:, width:] = table.astype(jnp.bfloat16)
    copies[3].wait()
    packed = jnp.dot(one_hot, hidden[...], preferred_element_type=jnp.float32)
    rows[:, :width] = packed.astype(jnp.bfloat16)


def join_kernel(order, after, *refs):
    blocks, line, plain = refs[:-2], refs[-2], refs[-1]
    for place, block in zip(order, blocks):
        line[place * CAP:(place + 1) * CAP] = block[...]
        plain[place * CAP:(place + 1) * CAP] = block[:, :plain.shape[1]]


def stage_kernel(blocks, after, weight, held, away, finished, sems):
    rank = coordinates()[0]
    width = weight.shape[0] // blocks
    copies = []
    for block in list(range(1, blocks, 2)) + list(range(0, blocks, 2)):
        start = pl.multiple_of((rank ^ block) * width, width)
        targets = [held.at[pl.ds(start, width)]]
        if block % 2:
            targets.append(away.at[pl.ds(block // 2 * width, width)])
        for target in targets:
            copy = pltpu.make_async_copy(
                weight.at[pl.ds(start, width)], target, sems.at[len(copies)]
            )
            copy.start()
            copies.append(copy)
    finished[...] = jnp.zeros_like(finished)
    for copy in copies:
        copy.wait()


def info_kernel(*refs):
    advantages, info = refs[-2:]
    start = refs[0].shape[1] - IDS
    table = jnp.concatenate([ref[:, start:] for ref in refs[:-2]], axis=0).astype(jnp.float32)
    valid = table[:, 0:1]
    turn = table[:, 1:2] + 256.0 * table[:, 2:3]
    target = table[:, 3:4] + 256.0 * table[:, 4:5] + 65536.0 * table[:, 5:6]
    turns = advantages.shape[1]
    spot = lax.broadcasted_iota(jnp.int32, (table.shape[0], turns), 1)
    gain = jnp.sum(
        jnp.where(spot == turn.astype(jnp.int32), advantages[...], 0.0), axis=1, keepdims=True
    )
    weight = valid * gain / jnp.sum(valid)
    lane = lax.broadcasted_iota(jnp.int32, info.shape, 1)
    info[...] = jnp.where(lane == 0, weight, jnp.where(lane == 1, target, 0.0))


def reorder(stats, position, groups):
    lanes = stats.shape[1]
    lane = lax.broadcasted_iota(jnp.int32, stats.shape, 1)
    bit = 1
    while bit < groups:
        size = CAP * bit
        swapped = jnp.where(
            (lane & size) != 0,
            pltpu.roll(stats, size, 1),
            pltpu.roll(stats, lanes - size, 1),
        )
        stats = jnp.where((position & bit) != 0, swapped, stats)
        bit *= 2
    return stats


def all_rows(pieces, block, width):
    return jnp.concatenate([ref[:, :width] for ref in pieces[2 * block:2 * block + 2]], axis=0)


def some_logits(blocks, first, pieces, weight):
    width = weight.shape[0] // blocks
    rank, total = coordinates()[0], None
    for place, block in enumerate(range(first, blocks, 2)):
        start = pl.multiple_of((rank ^ block) * width, width)
        part = jnp.dot(
            all_rows(pieces, place, width),
            weight[pl.ds(start, width), :],
            preferred_element_type=jnp.float32,
        )
        total = part if total is None else total + part
    return total


def first_kernel(blocks, weight, *refs):
    refs[-1][...] = some_logits(blocks, 0, refs[:-1], weight)


def logits_kernel(blocks, groups, info, partial, weight, *refs):
    pieces, (logits, stats) = refs[:-2], refs[-2:]
    _, position, shard = coordinates()
    total = partial[...] + some_logits(blocks, 1, pieces, weight)
    logits[...] = total
    height, columns = total.shape
    target = info[:, 1:2].astype(jnp.int32) - shard * columns
    column = lax.broadcasted_iota(jnp.int32, total.shape, 1)
    hit = jnp.sum(jnp.where(column == target, total, 0.0), axis=1, keepdims=True)
    hit = jnp.sum(hit * info[:, 0:1])
    peak = jnp.max(total, axis=1, keepdims=True)
    mass = jnp.sum(jnp.exp(total - peak), axis=1, keepdims=True)
    lane = lax.broadcasted_iota(jnp.int32, (height, 128), 1)
    table = jnp.where(lane == 0, peak, jnp.where(lane == 1, mass, hit))
    table = reorder(jnp.transpose(table)[0:8], position, groups)
    line = jnp.concatenate([table[0:1], table[1:2], table[2:3, :128]], axis=1)
    stats[...] = jnp.broadcast_to(line[None], stats.shape)


def log_totals_kernel(groups, info, stats, columns, loss):
    position = coordinates()[1]
    height = info.shape[0]
    peaks, masses = stats[:, :, :height], stats[:, :, height:2 * height]
    peak = jnp.max(peaks, axis=0)
    mass = jnp.sum(masses * jnp.exp(peaks - peak[None]), axis=0)
    hit = jnp.sum(stats[:, :, 2 * height:], axis=0)
    log_total = jnp.broadcast_to(peak + jnp.log(mass), (8, height))
    log_total = reorder(log_total, position, groups)
    log_total = jnp.transpose(jnp.concatenate([log_total] * 16, axis=0))
    loss[0, 0] = jnp.sum(info[:, 0:1] * log_total[:, 0:1]) - hit[0, 0]
    columns[...] = log_total


def grad_kernel(chunk, order, info, mine, theirs, weight, other_weight, table, *refs):
    logit_grad, outs = refs[0], refs[1:]
    rank, _, shard = coordinates()
    height, columns = mine.shape
    part = height // 4
    quarters = [chunk, 2 + chunk]

    def rows_of(ref):
        return jnp.concatenate([ref[q * part:(q + 1) * part] for q in quarters], axis=0)

    rows_info = rows_of(info)
    log_total = rows_of(table)[:, 0:1]
    row_weight, target = rows_info[:, 0:1], rows_info[:, 1:2].astype(jnp.int32)

    def grad_of(logits, shard):
        column = lax.broadcasted_iota(jnp.int32, (2 * part, columns), 1) + shard * columns
        probability = jnp.exp(rows_of(logits) - log_total)
        return (
            grad_scale * row_weight * (probability - (column == target).astype(jnp.float32))
        ).astype(jnp.bfloat16)

    grad = grad_of(mine, shard)
    logit_grad[...] = grad
    grads = (grad, grad_of(theirs, shard ^ 1))
    width = outs[0].shape[1]
    for x in reversed(range(len(outs) // 2)):
        start = pl.multiple_of((rank ^ 2 * x) * width, width)
        weights = (weight[pl.ds(start, width), :], other_weight[x * width:(x + 1) * width, :])
        total = sum(
            lax.dot_general(g, w, (((1,), (1,)), ((), ())), preferred_element_type=jnp.float32)
            for g, w in zip(grads, weights)
        )
        for y in range(2):
            out = outs[order.index(2 * x + y)]
            out[...] = total[y * part:(y + 1) * part].astype(out.dtype)


def weight_kernel(blocks, after, near_grad, far_grad, *refs):
    pieces, (out, finished, done, sems) = refs[:-4], refs[-4:]
    rank = coordinates()[0]
    finished[...] = jnp.zeros_like(finished)
    part = near_grad.shape[0] // 2
    logit_grad = jnp.concatenate(
        [ref[y * part:(y + 1) * part] for y in range(2) for ref in (near_grad, far_grad)], axis=0
    )
    width = done.shape[0] // blocks
    copies = []
    for block in range(blocks):
        done[block * width:(block + 1) * width] = lax.dot_general(
            all_rows(pieces, block, width),
            logit_grad,
            (((0,), (0,)), ((), ())),
            preferred_element_type=jnp.float32,
        ).astype(jnp.bfloat16)
        start = pl.multiple_of((rank ^ block) * width, width)
        copy = pltpu.make_async_copy(
            done.at[pl.ds(block * width, width)], out.at[pl.ds(start, width)], sems.at[block]
        )
        copy.start()
        copies.append(copy)
    for copy in copies:
        copy.wait()


def corner_kernel(count, after, kept, *refs):
    total = kept[...]
    for ref in refs[:count]:
        total = total + ref[...].astype(jnp.float32)
    for place, out in enumerate(refs[count:]):
        out[...] = total[place * CAP:(place + 1) * CAP].astype(out.dtype)


def unpack_kernel(chosen, *refs):
    out = refs[-1]
    total = sum(ref[...].astype(jnp.float32) for ref in refs[:-1])
    out[...] = lax.dot_general(
        chosen[...],
        total.astype(jnp.bfloat16),
        (((0,), (0,)), ((), ())),
        preferred_element_type=jnp.float32,
    ).astype(jnp.bfloat16)


def body(dps, ranks, hidden, weight, loss_mask, target_ids, turn_ids, advantages):
    tokens, width = hidden.shape
    depth, columns = weight.shape
    zs, xs = dps // 2, ranks // 2
    total_rows = dps * CAP
    bf16, f32, i32 = jnp.bfloat16, jnp.float32, jnp.int32
    shape = jax.ShapeDtypeStruct
    square = [(y, x) for x in reversed(range(xs)) for y in (1, 0) if x or y]
    flops = 2 * total_rows * depth * columns

    def send(value, z=0, y=0, x=0, core=0):
        far, near = 2 * z + y, 2 * x + core
        pairs = [
            (d * ranks + v, (d ^ far) * ranks + (v ^ near))
            for d in range(dps)
            for v in range(ranks)
        ]
        return lax.ppermute(value, AXES, pairs)

    packed, chosen = call(
        pack_kernel,
        (
            in_hbm(hidden),
            in_hbm(loss_mask.reshape(1, tokens)),
            in_hbm(target_ids.reshape(1, tokens)),
            in_hbm(turn_ids.reshape(1, tokens)),
        ),
        [HBM] * 4,
        (
            shape((CAP, width + IDS), bf16),
            shape((CAP, tokens), bf16),
        ),
        (VMEM,) * 2,
        [pltpu.VMEM((tokens, width), bf16)]
        + [pltpu.VMEM((1, tokens), i32)] * 3
        + [pltpu.SemaphoreType.DMA((4,))],
    )

    line_order = [0, 1] + list(range(zs - 1, 1, -1))
    blocks = [send(packed, z=z) if z else packed for z in line_order]
    held, away, finished = call(
        functools.partial(stage_kernel, ranks),
        (blocks[1], in_hbm(weight)),
        [ANY, HBM],
        (
            shape((depth, columns), bf16),
            shape((depth // 2, columns), bf16),
            shape((8, 128), f32),
        ),
        (VMEM,) * 3,
        [pltpu.SemaphoreType.DMA((ranks + xs,))],
    )
    other_held = send(away, core=1)
    line_rows = zs * CAP
    line, line_plain = call(
        functools.partial(join_kernel, line_order),
        (finished, *blocks),
        [ANY] + [VMEM] * zs,
        (shape((line_rows, width + IDS), bf16), shape((line_rows, width), bf16)),
        (VMEM, VMEM),
    )
    pieces = {(2 * x, y): send(line_plain if x else line, y=y, x=x) for y, x in square}
    pieces[0, 0] = line
    for b, y in list(pieces):
        pieces[b + 1, y] = send(pieces[b, y], core=1)
    rows = [pieces[b, y] for b in range(ranks) for y in range(2)]

    info = call(
        info_kernel,
        (*rows[:2], advantages.reshape(1, -1)),
        [VMEM] * 3,
        shape((total_rows, 128), f32),
        VMEM,
    )
    near = [pieces[b, y] for b in range(0, ranks, 2) for y in range(2)]
    partial = call(
        functools.partial(first_kernel, ranks),
        (held, *near),
        [VMEM] * (1 + len(near)),
        shape((total_rows, columns), f32),
        VMEM,
        flops=flops // 2,
    )
    beside = [pieces[b, y] for b in range(1, ranks, 2) for y in range(2)]
    logits, stats = call(
        functools.partial(logits_kernel, ranks, dps),
        (info, partial, held, *beside),
        [VMEM] * (3 + len(beside)),
        (
            shape((total_rows, columns), f32),
            shape((dps * ranks, 1, 2 * total_rows + 128), f32),
        ),
        (VMEM, VMEM),
        flops=flops // 2,
    )
    other_logits = send(logits, core=1)
    stats = lax.all_to_all(stats, AXES, 0, 0)
    table, loss = call(
        functools.partial(log_totals_kernel, dps),
        (info, stats),
        [VMEM] * 2,
        (shape((total_rows, 128), f32), shape((1, 1), f32)),
        (VMEM, SMEM),
    )

    rows_part = total_rows // 4
    order = sorted(range(1, ranks), key=lambda place: (place % 2 + (place > 1), place)) + [0]
    ends, sums, grads = [None] * zs, [None, None], [None, None]
    for chunk in (1, 0):
        grads[chunk], *going = call(
            functools.partial(grad_kernel, chunk, order),
            (info, logits, other_logits, held, other_held, table),
            [VMEM] * 6,
            (shape((total_rows // 2, columns), bf16),)
            + (shape((rows_part, width), bf16),) * (ranks - 1)
            + (shape((rows_part, width), f32),),
            (VMEM,) * (ranks + 1),
            flops=flops // 2,
        )
        sums[chunk] = [going[-1]]
        for place, value in zip(order, going[:-1]):
            sums[chunk].append(send(value, y=place % 2, x=place // 2))
    weight_grad, finished = call(
        functools.partial(weight_kernel, ranks),
        (sums[0][0], *grads, *rows),
        [ANY] + [VMEM] * (2 + len(rows)),
        (shape((depth, columns), bf16), shape((8, 128), f32)),
        (HBM, VMEM),
        [pltpu.VMEM((depth, columns), bf16), pltpu.SemaphoreType.DMA((ranks,))],
        flops=flops,
    )
    for chunk in (1, 0):
        near = chunk * zs // 2
        parts_z = call(
            functools.partial(corner_kernel, ranks - 1),
            (table if chunk else finished, *sums[chunk]),
            [ANY] + [VMEM] * ranks,
            tuple(shape((CAP, width), bf16 if near + z else f32) for z in range(zs // 2)),
            (VMEM,) * (zs // 2),
        )
        for z, value in enumerate(parts_z):
            ends[near + z] = send(value, z=near + z) if near + z else value
    hidden_grad = call(
        unpack_kernel,
        (chosen, *ends),
        [VMEM] * (1 + len(ends)),
        shape((tokens, width), bf16),
        VMEM,
    )
    return loss[0, 0], hidden_grad, weight_grad


def solution(mesh):
    return jax.shard_map(
        functools.partial(body, mesh.shape["dp"], mesh.shape["vocab"]),
        mesh=mesh,
        in_specs=(P("dp", "vocab"), P(None, AXES), P("dp"), P("dp"), P("dp"), P()),
        out_specs=(P(), P("dp", "vocab"), P(None, AXES)),
        check_vma=False,
    )
```

```python
import functools
import math

import jax
import jax.numpy as jnp
from jax import lax
from jax.experimental import pallas as pl
from jax.experimental.pallas import tpu as pltpu
from jax.sharding import PartitionSpec as P

CAP = 32
MOST_VMEM = 56 * 1024 * 1024
IDS = 128
grad_scale = 16384.0
AXES = ("dp", "vocab")
SMEM = pl.BlockSpec(memory_space=pltpu.SMEM)
VMEM = pl.BlockSpec(memory_space=pltpu.VMEM)
HBM = pl.BlockSpec(memory_space=pltpu.HBM)
ANY = pl.BlockSpec(memory_space=pl.ANY)


def size_of(value):
    return math.prod(value.shape) * jnp.dtype(value.dtype).itemsize


def call(kernel, operands, in_specs, out_shape, out_specs, scratch=(), spare=4, flops=0, aliases={}):
    outs = jax.tree.leaves(out_shape)
    sized = [v for v, s in zip(operands, in_specs) if s is VMEM]
    sized += [v for v, s in zip(outs, jax.tree.leaves(out_specs)) if s is VMEM]
    held = [s for s in scratch if getattr(s, "memory_space", None) == pltpu.VMEM]
    total = sum(size_of(v) for v in sized) + sum(size_of(s) for s in held)
    return pl.pallas_call(
        kernel,
        out_shape=out_shape,
        in_specs=in_specs,
        out_specs=out_specs,
        scratch_shapes=scratch,
        input_output_aliases=aliases,
        compiler_params=pltpu.CompilerParams(vmem_limit_bytes=min(total + spare * 1024 * 1024, MOST_VMEM)),
        cost_estimate=pl.CostEstimate(
            flops=flops,
            bytes_accessed=sum(size_of(v) for v in list(operands) + outs),
            transcendentals=0,
        ),
    )(*operands)


def in_hbm(value):
    return pltpu.with_memory_space_constraint(value, pltpu.HBM)


def coordinates():
    group, rank = lax.axis_index("dp"), lax.axis_index("vocab")
    groups, ranks = lax.axis_size("dp"), lax.axis_size("vocab")
    position = group % 2 * (groups // 2) + group // 2
    return rank, position, group * ranks + rank


def choose(mask):
    tokens = mask.shape[1]
    wide = jnp.broadcast_to(mask.astype(jnp.float32), (8, tokens))
    before = lax.broadcasted_iota(jnp.int32, (tokens, tokens), 0)
    after = lax.broadcasted_iota(jnp.int32, (tokens, tokens), 1)
    upto = (before <= after).astype(jnp.float32)
    slot = jnp.dot(
        wide.astype(jnp.bfloat16), upto.astype(jnp.bfloat16), preferred_element_type=jnp.float32
    )[0:1]
    grid = lax.broadcasted_iota(jnp.int32, (CAP, tokens), 0) + 1
    return (slot.astype(jnp.int32) == grid) & (mask == 1)


def pack_kernel(hidden_hbm, mask_hbm, target_hbm, turn_hbm, rows, chosen_out, *scratch):
    hidden, mask, target, turn, sems = scratch
    copies = []
    for place, (source, held) in enumerate(
        ((mask_hbm, mask), (target_hbm, target), (turn_hbm, turn), (hidden_hbm, hidden))
    ):
        copy = pltpu.make_async_copy(source, held, sems.at[place])
        copy.start()
        copies.append(copy)
    for copy in copies[:3]:
        copy.wait()
    width = hidden.shape[1]
    chosen = choose(mask[...])
    one_hot = chosen.astype(jnp.float32).astype(jnp.bfloat16)
    chosen_out[...] = one_hot
    turns, targets = turn[...], target[...]
    fields = (
        mask[...],
        turns & 255,
        turns >> 8,
        targets & 255,
        (targets >> 8) & 255,
        targets >> 16,
    )
    lane = lax.broadcasted_iota(jnp.int32, (CAP, IDS), 1)
    table = jnp.zeros((CAP, IDS), jnp.float32)
    for place, field in enumerate(fields):
        picked = jnp.where(chosen, field.astype(jnp.float32), 0.0)
        table = jnp.where(lane == place, jnp.sum(picked, axis=1, keepdims=True), table)
    rows[:, width:] = table.astype(jnp.bfloat16)
    copies[3].wait()
    packed = jnp.dot(one_hot, hidden[...], preferred_element_type=jnp.float32)
    rows[:, :width] = packed.astype(jnp.bfloat16)


def join_kernel(order, *refs):
    blocks, line, plain = refs[:-2], refs[-2], refs[-1]
    for place, block in zip(order, blocks):
        line[place * CAP:(place + 1) * CAP] = block[...]
        plain[place * CAP:(place + 1) * CAP] = block[:, :plain.shape[1]]


def stage_kernel(blocks, line, weight, held, away, same, sems):
    rank = coordinates()[0]
    width = weight.shape[0] // blocks
    copies = []
    for block in list(range(1, blocks, 2)) + list(range(0, blocks, 2)):
        start = pl.multiple_of((rank ^ block) * width, width)
        targets = [held.at[pl.ds(start, width)]]
        if block % 2:
            targets.append(away.at[pl.ds(block // 2 * width, width)])
        for target in targets:
            copy = pltpu.make_async_copy(
                weight.at[pl.ds(start, width)], target, sems.at[len(copies)]
            )
            copy.start()
            copies.append(copy)
    same[...] = line[...]
    for copy in copies:
        copy.wait()


def gate_kernel(value, after, same):
    pass


def info_kernel(*refs):
    advantages, info = refs[-2:]
    start = refs[0].shape[1] - IDS
    table = jnp.concatenate([ref[:, start:] for ref in refs[:-2]], axis=0).astype(jnp.float32)
    valid = table[:, 0:1]
    turn = table[:, 1:2] + 256.0 * table[:, 2:3]
    target = table[:, 3:4] + 256.0 * table[:, 4:5] + 65536.0 * table[:, 5:6]
    turns = advantages.shape[1]
    spot = lax.broadcasted_iota(jnp.int32, (table.shape[0], turns), 1)
    gain = jnp.sum(
        jnp.where(spot == turn.astype(jnp.int32), advantages[...], 0.0), axis=1, keepdims=True
    )
    weight = valid * gain / jnp.sum(valid)
    lane = lax.broadcasted_iota(jnp.int32, info.shape, 1)
    info[...] = jnp.where(lane == 0, weight, jnp.where(lane == 1, target, 0.0))


def reorder(stats, position, groups):
    lanes = stats.shape[1]
    lane = lax.broadcasted_iota(jnp.int32, stats.shape, 1)
    bit = 1
    while bit < groups:
        size = CAP * bit
        swapped = jnp.where(
            (lane & size) != 0,
            pltpu.roll(stats, size, 1),
            pltpu.roll(stats, lanes - size, 1),
        )
        stats = jnp.where((position & bit) != 0, swapped, stats)
        bit *= 2
    return stats


def all_rows(pieces, block, width):
    return jnp.concatenate([ref[:, :width] for ref in pieces[2 * block:2 * block + 2]], axis=0)


def some_logits(blocks, first, pieces, weight):
    width = weight.shape[0] // blocks
    rank, total = coordinates()[0], None
    for place, block in enumerate(range(first, blocks, 2)):
        start = pl.multiple_of((rank ^ block) * width, width)
        part = jnp.dot(
            all_rows(pieces, place, width),
            weight[pl.ds(start, width), :],
            preferred_element_type=jnp.float32,
        )
        total = part if total is None else total + part
    return total


def first_kernel(blocks, weight, *refs):
    refs[-1][...] = some_logits(blocks, 0, refs[:-1], weight)


def logits_kernel(blocks, groups, info, partial, weight, *refs):
    pieces, (logits, stats) = refs[:-2], refs[-2:]
    _, position, shard = coordinates()
    total = partial[...] + some_logits(blocks, 1, pieces, weight)
    logits[...] = total
    height, columns = total.shape
    target = info[:, 1:2].astype(jnp.int32) - shard * columns
    column = lax.broadcasted_iota(jnp.int32, total.shape, 1)
    hit = jnp.sum(jnp.where(column == target, total, 0.0), axis=1, keepdims=True)
    hit = jnp.sum(hit * info[:, 0:1])
    peak = jnp.max(total, axis=1, keepdims=True)
    mass = jnp.sum(jnp.exp(total - peak), axis=1, keepdims=True)
    lane = lax.broadcasted_iota(jnp.int32, (height, 128), 1)
    table = jnp.where(lane == 0, peak, jnp.where(lane == 1, mass, hit))
    table = reorder(jnp.transpose(table)[0:8], position, groups)
    line = jnp.concatenate([table[0:1], table[1:2], table[2:3, :128]], axis=1)
    stats[...] = jnp.broadcast_to(line[None], stats.shape)


def log_totals(groups, stats, height):
    peaks, masses = stats[:, :, :height], stats[:, :, height:2 * height]
    peak = jnp.max(peaks, axis=0)
    mass = jnp.sum(masses * jnp.exp(peaks - peak[None]), axis=0)
    line = jnp.broadcast_to(peak + jnp.log(mass), (8, height))
    line = reorder(line, coordinates()[1], groups)
    return jnp.transpose(jnp.concatenate([line] * 16, axis=0))


def grad_kernel(chunk, order, groups, info, mine, theirs, weight, other_weight, stats, *refs):
    logit_grad, outs = refs[0], refs[1:len(order) + 1]
    rank, _, shard = coordinates()
    height, columns = mine.shape
    part = height // 4
    quarters = [chunk, 2 + chunk]

    def rows_of(value):
        return jnp.concatenate([value[q * part:(q + 1) * part] for q in quarters], axis=0)

    if chunk:
        table = log_totals(groups, stats, height)
        refs[-1][...] = table
    else:
        table = stats[...]
    log_total = rows_of(table)[:, 0:1]
    rows_info = rows_of(info)
    row_weight, target = rows_info[:, 0:1], rows_info[:, 1:2].astype(jnp.int32)

    def grad_of(logits, shard):
        column = lax.broadcasted_iota(jnp.int32, (2 * part, columns), 1) + shard * columns
        probability = jnp.exp(rows_of(logits) - log_total)
        return (
            grad_scale * row_weight * (probability - (column == target).astype(jnp.float32))
        ).astype(jnp.bfloat16)

    grad = grad_of(mine, shard)
    logit_grad[...] = grad
    grads = (grad, grad_of(theirs, shard ^ 1))
    width = outs[0].shape[1]
    for x in reversed(range(len(outs) // 2)):
        start = pl.multiple_of((rank ^ 2 * x) * width, width)
        weights = (weight[pl.ds(start, width), :], other_weight[x * width:(x + 1) * width, :])
        total = sum(
            lax.dot_general(g, w, (((1,), (1,)), ((), ())), preferred_element_type=jnp.float32)
            for g, w in zip(grads, weights)
        )
        for y in range(2):
            out = outs[order.index(2 * x + y)]
            out[...] = total[y * part:(y + 1) * part].astype(out.dtype)


def weight_kernel(blocks, skipped, after, near_grad, far_grad, *refs):
    pieces, (out, last, done, sems) = refs[skipped:-4], refs[-4:]
    rank = coordinates()[0]
    part = near_grad.shape[0] // 2
    logit_grad = jnp.concatenate(
        [ref[y * part:(y + 1) * part] for y in range(2) for ref in (near_grad, far_grad)], axis=0
    )
    width = done.shape[0] // len(blocks)
    copies = []
    for place, block in enumerate(blocks):
        done[place * width:(place + 1) * width] = lax.dot_general(
            all_rows(pieces, place, width),
            logit_grad,
            (((0,), (0,)), ((), ())),
            preferred_element_type=jnp.float32,
        ).astype(jnp.bfloat16)
        start = pl.multiple_of((rank ^ block) * width, width)
        copy = pltpu.make_async_copy(
            done.at[pl.ds(place * width, width)], out.at[pl.ds(start, width)], sems.at[place]
        )
        copy.start()
        copies.append(copy)
    if skipped:
        info, table, stats = refs[1:4]
        hits = jnp.sum(stats[:, :, 2 * info.shape[0]:], axis=0)
        loss = jnp.sum(info[:, 0:1] * table[:, 0:1]) - hits[0, 0]
        last[...] = jnp.full(last.shape, loss, jnp.float32)
    else:
        last[...] = jnp.zeros_like(last)
    for copy in copies:
        copy.wait()


def corner_kernel(count, after, kept, *refs):
    total = kept[...]
    for ref in refs[:count]:
        total = total + ref[...].astype(jnp.float32)
    for place, out in enumerate(refs[count:]):
        out[...] = total[place * CAP:(place + 1) * CAP].astype(out.dtype)


def unpack_kernel(last, chosen, *refs):
    out, loss = refs[-2:]
    loss[0, 0] = last[0, 0]
    total = sum(ref[...].astype(jnp.float32) for ref in refs[:-2])
    out[...] = lax.dot_general(
        chosen[...],
        total.astype(jnp.bfloat16),
        (((0,), (0,)), ((), ())),
        preferred_element_type=jnp.float32,
    ).astype(jnp.bfloat16)


def body(dps, ranks, hidden, weight, loss_mask, target_ids, turn_ids, advantages):
    tokens, width = hidden.shape
    depth, columns = weight.shape
    zs, xs = dps // 2, ranks // 2
    total_rows = dps * CAP
    bf16, f32, i32 = jnp.bfloat16, jnp.float32, jnp.int32
    shape = jax.ShapeDtypeStruct
    square = [(y, x) for x in reversed(range(xs)) for y in (1, 0) if x or y]
    flops = 2 * total_rows * depth * columns

    def send(value, z=0, y=0, x=0, core=0):
        far, near = 2 * z + y, 2 * x + core
        pairs = [
            (d * ranks + v, (d ^ far) * ranks + (v ^ near))
            for d in range(dps)
            for v in range(ranks)
        ]
        return lax.ppermute(value, AXES, pairs)

    packed, chosen = call(
        pack_kernel,
        (
            in_hbm(hidden),
            in_hbm(loss_mask.reshape(1, tokens)),
            in_hbm(target_ids.reshape(1, tokens)),
            in_hbm(turn_ids.reshape(1, tokens)),
        ),
        [HBM] * 4,
        (
            shape((CAP, width + IDS), bf16),
            shape((CAP, tokens), bf16),
        ),
        (VMEM,) * 2,
        [pltpu.VMEM((tokens, width), bf16)]
        + [pltpu.VMEM((1, tokens), i32)] * 3
        + [pltpu.SemaphoreType.DMA((4,))],
    )

    line_order = [0, *range(2, zs), 1]
    blocks = [send(packed, z=z) if z else packed for z in line_order]
    line_rows = zs * CAP
    line, line_plain = call(
        functools.partial(join_kernel, line_order),
        blocks,
        [VMEM] * zs,
        (shape((line_rows, width + IDS), bf16), shape((line_rows, width), bf16)),
        (VMEM, VMEM),
    )
    pieces = {(2 * x, y): send(line_plain if x else line, y=y, x=x) for y, x in square}
    held, away, same = call(
        functools.partial(stage_kernel, ranks),
        (line, in_hbm(weight)),
        [VMEM, HBM],
        (
            shape((depth, columns), bf16),
            shape((depth // 2, columns), bf16),
            shape(line.shape, bf16),
        ),
        (VMEM,) * 3,
        [pltpu.SemaphoreType.DMA((ranks + xs,))],
    )
    pieces[0, 0] = same
    for b, y in list(pieces):
        pieces[b + 1, y] = send(pieces[b, y], core=1)
    rows = [pieces[b, y] for b in range(ranks) for y in range(2)]

    info = call(
        info_kernel,
        (*rows[:2], advantages.reshape(1, -1)),
        [VMEM] * 3,
        shape((total_rows, 128), f32),
        VMEM,
    )
    near = [pieces[b, y] for b in range(0, ranks, 2) for y in range(2)]
    partial = call(
        functools.partial(first_kernel, ranks),
        (held, *near),
        [VMEM] * (1 + len(near)),
        shape((total_rows, columns), f32),
        VMEM,
        flops=flops // 2,
    )
    beside = [pieces[b, y] for b in range(1, ranks, 2) for y in range(2)]
    logits, stats = call(
        functools.partial(logits_kernel, ranks, dps),
        (info, partial, held, *beside),
        [VMEM] * (3 + len(beside)),
        (
            shape((total_rows, columns), f32),
            shape((dps * ranks, 1, 2 * total_rows + 128), f32),
        ),
        (VMEM, VMEM),
        flops=flops // 2,
    )
    other_logits = send(logits, core=1)
    away = call(
        gate_kernel, (away, stats), [ANY, ANY], shape(away.shape, bf16), ANY, aliases={0: 0}
    )
    other_held = send(away, core=1)
    stats = lax.all_to_all(stats, AXES, 0, 0)
    rows_part = total_rows // 4
    order = sorted(range(1, ranks), key=lambda place: (place % 2 + (place > 1), place)) + [0]
    ends, sums, grads = [None] * zs, [None, None], [None, None]
    for chunk in (1, 0):
        outs = (shape((total_rows // 2, columns), bf16),)
        outs += (shape((rows_part, width), bf16),) * (ranks - 1) + (shape((rows_part, width), f32),)
        if chunk:
            outs += (shape((total_rows, 128), f32),)
        grads[chunk], *going = call(
            functools.partial(grad_kernel, chunk, order, dps),
            (info, logits, other_logits, held, other_held, stats if chunk else table),
            [VMEM] * 6,
            outs,
            (VMEM,) * len(outs),
            flops=flops // 2,
        )
        if chunk:
            table = going.pop()
        sums[chunk] = [going[-1]]
        for place, value in zip(order, going[:-1]):
            sums[chunk].append(send(value, y=place % 2, x=place // 2))

    def weight_part(first, after, *extra):
        blocks = range(first, first + ranks // 2)
        chosen_rows = rows[2 * first:2 * first + ranks]
        return call(
            functools.partial(weight_kernel, blocks, len(extra)),
            (after, *grads, *extra, *chosen_rows),
            [ANY] + [VMEM] * 2 + [HBM] * (len(extra) > 0)
            + [VMEM] * (max(len(extra) - 1, 0) + len(chosen_rows)),
            (shape((depth, columns), bf16), shape((8, 128), f32)),
            (HBM, VMEM),
            [
                pltpu.VMEM((depth // 2, columns), bf16),
                pltpu.SemaphoreType.DMA((ranks // 2,)),
            ],
            flops=flops // 2,
            aliases={3: 0} if extra else {},
        )

    weight_grad, finished = weight_part(0, sums[0][0])
    for chunk in (1, 0):
        near = chunk * zs // 2
        parts_z = call(
            functools.partial(corner_kernel, ranks - 1),
            (table if chunk else finished, *sums[chunk]),
            [ANY] + [VMEM] * ranks,
            tuple(shape((CAP, width), bf16 if near + z else f32) for z in range(zs // 2)),
            (VMEM,) * (zs // 2),
        )
        for z, value in enumerate(parts_z):
            ends[near + z] = send(value, z=near + z) if near + z else value
    weight_grad, last = weight_part(ranks // 2, parts_z[0], weight_grad, info, table, stats)
    hidden_grad, loss = call(
        unpack_kernel,
        (last, chosen, *ends),
        [VMEM] * (2 + len(ends)),
        (shape((tokens, width), bf16), shape((1, 1), f32)),
        (VMEM, SMEM),
    )
    return loss[0, 0], hidden_grad, weight_grad


def solution(mesh):
    return jax.shard_map(
        functools.partial(body, mesh.shape["dp"], mesh.shape["vocab"]),
        mesh=mesh,
        in_specs=(P("dp", "vocab"), P(None, AXES), P("dp"), P("dp"), P("dp"), P()),
        out_specs=(P(), P("dp", "vocab"), P(None, AXES)),
        check_vma=False,
    )
```

```python
import functools
import math

import jax
import jax.numpy as jnp
from jax import lax
from jax.experimental import pallas as pl
from jax.experimental.pallas import tpu as pltpu
from jax.sharding import PartitionSpec as P

CAP = 32
MOST_VMEM = 56 * 1024 * 1024
IDS = 128
grad_scale = 16384.0
AXES = ("dp", "vocab")
SMEM = pl.BlockSpec(memory_space=pltpu.SMEM)
VMEM = pl.BlockSpec(memory_space=pltpu.VMEM)
HBM = pl.BlockSpec(memory_space=pltpu.HBM)
ANY = pl.BlockSpec(memory_space=pl.ANY)


def size_of(value):
    return math.prod(value.shape) * jnp.dtype(value.dtype).itemsize


def call(kernel, operands, in_specs, out_shape, out_specs, scratch=(), spare=4, flops=0, aliases={}):
    outs = jax.tree.leaves(out_shape)
    sized = [v for v, s in zip(operands, in_specs) if s is VMEM]
    sized += [v for v, s in zip(outs, jax.tree.leaves(out_specs)) if s is VMEM]
    held = [s for s in scratch if getattr(s, "memory_space", None) == pltpu.VMEM]
    total = sum(size_of(v) for v in sized) + sum(size_of(s) for s in held)
    return pl.pallas_call(
        kernel,
        out_shape=out_shape,
        in_specs=in_specs,
        out_specs=out_specs,
        scratch_shapes=scratch,
        input_output_aliases=aliases,
        compiler_params=pltpu.CompilerParams(vmem_limit_bytes=min(total + spare * 1024 * 1024, MOST_VMEM)),
        cost_estimate=pl.CostEstimate(
            flops=flops,
            bytes_accessed=sum(size_of(v) for v in list(operands) + outs),
            transcendentals=0,
        ),
    )(*operands)


def in_hbm(value):
    return pltpu.with_memory_space_constraint(value, pltpu.HBM)


def coordinates():
    group, rank = lax.axis_index("dp"), lax.axis_index("vocab")
    groups, ranks = lax.axis_size("dp"), lax.axis_size("vocab")
    position = group % 2 * (groups // 2) + group // 2
    return rank, position, group * ranks + rank


def choose(mask):
    tokens = mask.shape[1]
    wide = jnp.broadcast_to(mask.astype(jnp.float32), (8, tokens))
    before = lax.broadcasted_iota(jnp.int32, (tokens, tokens), 0)
    after = lax.broadcasted_iota(jnp.int32, (tokens, tokens), 1)
    upto = (before <= after).astype(jnp.float32)
    slot = jnp.dot(
        wide.astype(jnp.bfloat16), upto.astype(jnp.bfloat16), preferred_element_type=jnp.float32
    )[0:1]
    grid = lax.broadcasted_iota(jnp.int32, (CAP, tokens), 0) + 1
    return (slot.astype(jnp.int32) == grid) & (mask == 1)


def pack_kernel(hidden_hbm, mask_hbm, target_hbm, turn_hbm, rows, chosen_out, *scratch):
    hidden, mask, target, turn, sems = scratch
    copies = []
    for place, (source, held) in enumerate(
        ((mask_hbm, mask), (target_hbm, target), (turn_hbm, turn), (hidden_hbm, hidden))
    ):
        copy = pltpu.make_async_copy(source, held, sems.at[place])
        copy.start()
        copies.append(copy)
    for copy in copies[:3]:
        copy.wait()
    width = hidden.shape[1]
    chosen = choose(mask[...])
    one_hot = chosen.astype(jnp.float32).astype(jnp.bfloat16)
    chosen_out[...] = one_hot
    turns, targets = turn[...], target[...]
    fields = (
        mask[...],
        turns & 255,
        turns >> 8,
        targets & 255,
        (targets >> 8) & 255,
        targets >> 16,
    )
    lane = lax.broadcasted_iota(jnp.int32, (CAP, IDS), 1)
    table = jnp.zeros((CAP, IDS), jnp.float32)
    for place, field in enumerate(fields):
        picked = jnp.where(chosen, field.astype(jnp.float32), 0.0)
        table = jnp.where(lane == place, jnp.sum(picked, axis=1, keepdims=True), table)
    rows[:, width:] = table.astype(jnp.bfloat16)
    copies[3].wait()
    packed = jnp.dot(one_hot, hidden[...], preferred_element_type=jnp.float32)
    rows[:, :width] = packed.astype(jnp.bfloat16)


def join_kernel(order, *refs):
    blocks, line, plain = refs[:-2], refs[-2], refs[-1]
    for place, block in zip(order, blocks):
        line[place * CAP:(place + 1) * CAP] = block[...]
        plain[place * CAP:(place + 1) * CAP] = block[:, :plain.shape[1]]


def stage_kernel(blocks, line, weight, held, away, same, sems):
    rank = coordinates()[0]
    width = weight.shape[0] // blocks
    copies = []
    for block in list(range(1, blocks, 2)) + list(range(0, blocks, 2)):
        start = pl.multiple_of((rank ^ block) * width, width)
        targets = [held.at[pl.ds(start, width)]]
        if block % 2:
            targets.append(away.at[pl.ds(block // 2 * width, width)])
        for target in targets:
            copy = pltpu.make_async_copy(
                weight.at[pl.ds(start, width)], target, sems.at[len(copies)]
            )
            copy.start()
            copies.append(copy)
    same[...] = line[...]
    for copy in copies:
        copy.wait()


def gate_kernel(value, after, same):
    pass


def info_kernel(*refs):
    advantages, info = refs[-2:]
    start = refs[0].shape[1] - IDS
    table = jnp.concatenate([ref[:, start:] for ref in refs[:-2]], axis=0).astype(jnp.float32)
    valid = table[:, 0:1]
    turn = table[:, 1:2] + 256.0 * table[:, 2:3]
    target = table[:, 3:4] + 256.0 * table[:, 4:5] + 65536.0 * table[:, 5:6]
    turns = advantages.shape[1]
    spot = lax.broadcasted_iota(jnp.int32, (table.shape[0], turns), 1)
    gain = jnp.sum(
        jnp.where(spot == turn.astype(jnp.int32), advantages[...], 0.0), axis=1, keepdims=True
    )
    weight = valid * gain / jnp.sum(valid)
    lane = lax.broadcasted_iota(jnp.int32, info.shape, 1)
    info[...] = jnp.where(lane == 0, weight, jnp.where(lane == 1, target, 0.0))


def reorder(stats, position, groups):
    lanes = stats.shape[1]
    lane = lax.broadcasted_iota(jnp.int32, stats.shape, 1)
    bit = 1
    while bit < groups:
        size = CAP * bit
        swapped = jnp.where(
            (lane & size) != 0,
            pltpu.roll(stats, size, 1),
            pltpu.roll(stats, lanes - size, 1),
        )
        stats = jnp.where((position & bit) != 0, swapped, stats)
        bit *= 2
    return stats


def all_rows(pieces, block, width):
    return jnp.concatenate([ref[:, :width] for ref in pieces[2 * block:2 * block + 2]], axis=0)


def some_logits(blocks, first, pieces, weight):
    width = weight.shape[0] // blocks
    rank, total = coordinates()[0], None
    for place, block in enumerate(range(first, blocks, 2)):
        start = pl.multiple_of((rank ^ block) * width, width)
        part = jnp.dot(
            all_rows(pieces, place, width),
            weight[pl.ds(start, width), :],
            preferred_element_type=jnp.float32,
        )
        total = part if total is None else total + part
    return total


def first_kernel(blocks, weight, *refs):
    refs[-1][...] = some_logits(blocks, 0, refs[:-1], weight)


def logits_kernel(blocks, groups, info, partial, weight, *refs):
    pieces, (logits, stats) = refs[:-2], refs[-2:]
    _, position, shard = coordinates()
    total = partial[...] + some_logits(blocks, 1, pieces, weight)
    logits[...] = total
    height, columns = total.shape
    target = info[:, 1:2].astype(jnp.int32) - shard * columns
    column = lax.broadcasted_iota(jnp.int32, total.shape, 1)
    hit = jnp.sum(jnp.where(column == target, total, 0.0), axis=1, keepdims=True)
    hit = jnp.sum(hit * info[:, 0:1])
    peak = jnp.max(total, axis=1, keepdims=True)
    mass = jnp.sum(jnp.exp(total - peak), axis=1, keepdims=True)
    lane = lax.broadcasted_iota(jnp.int32, (height, 128), 1)
    table = jnp.where(lane == 0, peak, jnp.where(lane == 1, mass, hit))
    table = reorder(jnp.transpose(table)[0:8], position, groups)
    line = jnp.concatenate([table[0:1], table[1:2], table[2:3, :128]], axis=1)
    stats[...] = jnp.broadcast_to(line[None], stats.shape)


def log_totals(groups, stats, height):
    peaks, masses = stats[:, :, :height], stats[:, :, height:2 * height]
    peak = jnp.max(peaks, axis=0)
    mass = jnp.sum(masses * jnp.exp(peaks - peak[None]), axis=0)
    line = jnp.broadcast_to(peak + jnp.log(mass), (8, height))
    line = reorder(line, coordinates()[1], groups)
    return jnp.transpose(jnp.concatenate([line] * 16, axis=0))


def products_kernel(info, mine, theirs, weight, other_weight, columns, *refs):
    sums, picks = refs[:2], refs[2:]
    rank, _, shard = coordinates()
    height, width_v = mine.shape
    part = height // 4
    target = info[:, 1:2].astype(jnp.int32)
    logits = (mine[...], theirs[...])
    hits = [
        lax.broadcasted_iota(jnp.int32, mine.shape, 1) + place * width_v == target
        for place in (shard, shard ^ 1)
    ]
    peak = functools.reduce(
        jnp.maximum, [jnp.max(value, axis=1, keepdims=True) for value in logits]
    )
    hit = sum(
        jnp.sum(jnp.where(chosen, value - peak, 0.0), axis=1, keepdims=True)
        for chosen, value in zip(hits, logits)
    )
    lane = lax.broadcasted_iota(jnp.int32, columns.shape, 1)
    columns[...] = jnp.where(lane == 0, peak, hit + peak)
    factors = [
        jnp.where(chosen, 0.0, jnp.exp(value - peak)).astype(jnp.bfloat16)
        for chosen, value in zip(hits, logits)
    ]
    one_hots = [chosen.astype(jnp.float32).astype(jnp.bfloat16) for chosen in hits]
    width = sums[0].shape[2]
    for x in range(sums[0].shape[0] // 2):
        start = pl.multiple_of((rank ^ 2 * x) * width, width)
        weights = (weight[pl.ds(start, width), :], other_weight[x * width:(x + 1) * width, :])
        for lefts, outs in ((factors, sums), (one_hots, picks)):
            total = sum(
                lax.dot_general(
                    left, right, (((1,), (1,)), ((), ())), preferred_element_type=jnp.float32
                )
                for left, right in zip(lefts, weights)
            )
            for quarter in range(4):
                out = outs[quarter % 2]
                piece = total[quarter * part:(quarter + 1) * part]
                out[2 * x + quarter // 2] = piece.astype(out.dtype)


def chunk_grads(chunk, order, info, columns, log_total, sums, picks, outs):
    part = sums.shape[1]
    for place, out in zip(order, outs):
        quarter = place % 2 * 2 + chunk
        rows = slice(quarter * part, (quarter + 1) * part)
        scale = grad_scale * info[rows, 0:1]
        many = scale * jnp.exp(columns[rows, 0:1] - log_total[rows])
        one = scale * (jnp.exp(columns[rows, 1:2] - log_total[rows]) - 1.0)
        total = many * sums[place] + one * picks[place].astype(jnp.float32)
        out[...] = total.astype(out.dtype)


def far_kernel(order, groups, info, columns, stats, sums, picks, table, *outs):
    log_total = log_totals(groups, stats, info.shape[0])
    table[...] = log_total
    chunk_grads(1, order, info, columns, log_total[:, 0:1], sums, picks, outs)


def near_kernel(order, info, columns, table, sums, picks, logits, logit_grad, *outs):
    log_total = table[:, 0:1]
    chunk_grads(0, order, info, columns, log_total, sums, picks, outs)
    target = info[:, 1:2].astype(jnp.int32) - coordinates()[2] * logits.shape[1]
    column = lax.broadcasted_iota(jnp.int32, logits.shape, 1)
    probability = jnp.exp(logits[...] - log_total)
    logit_grad[...] = (
        grad_scale * info[:, 0:1] * (probability - (column == target).astype(jnp.float32))
    ).astype(jnp.bfloat16)


def weight_kernel(blocks, skipped, after, logit_grad, *refs):
    pieces, (out, last, done, sems) = refs[skipped:-4], refs[-4:]
    rank = coordinates()[0]
    width = done.shape[0] // len(blocks)
    copies = []
    for place, block in enumerate(blocks):
        done[place * width:(place + 1) * width] = lax.dot_general(
            all_rows(pieces, place, width),
            logit_grad[...],
            (((0,), (0,)), ((), ())),
            preferred_element_type=jnp.float32,
        ).astype(jnp.bfloat16)
        start = pl.multiple_of((rank ^ block) * width, width)
        copy = pltpu.make_async_copy(
            done.at[pl.ds(place * width, width)], out.at[pl.ds(start, width)], sems.at[place]
        )
        copy.start()
        copies.append(copy)
    if skipped:
        info, table, stats = refs[1:4]
        hits = jnp.sum(stats[:, :, 2 * info.shape[0]:], axis=0)
        loss = jnp.sum(info[:, 0:1] * table[:, 0:1]) - hits[0, 0]
        last[...] = jnp.full(last.shape, loss, jnp.float32)
    else:
        last[...] = jnp.zeros_like(last)
    for copy in copies:
        copy.wait()


def corner_kernel(count, after, kept, *refs):
    total = kept[...]
    for ref in refs[:count]:
        total = total + ref[...].astype(jnp.float32)
    for place, out in enumerate(refs[count:]):
        out[...] = total[place * CAP:(place + 1) * CAP].astype(out.dtype)


def unpack_kernel(last, chosen, *refs):
    out, loss = refs[-2:]
    loss[0, 0] = last[0, 0]
    total = sum(ref[...].astype(jnp.float32) for ref in refs[:-2])
    out[...] = lax.dot_general(
        chosen[...],
        total.astype(jnp.bfloat16),
        (((0,), (0,)), ((), ())),
        preferred_element_type=jnp.float32,
    ).astype(jnp.bfloat16)


def body(dps, ranks, hidden, weight, loss_mask, target_ids, turn_ids, advantages):
    tokens, width = hidden.shape
    depth, columns = weight.shape
    zs, xs = dps // 2, ranks // 2
    total_rows = dps * CAP
    bf16, f32, i32 = jnp.bfloat16, jnp.float32, jnp.int32
    shape = jax.ShapeDtypeStruct
    square = [(y, x) for x in reversed(range(xs)) for y in (1, 0) if x or y]
    flops = 2 * total_rows * depth * columns

    def send(value, z=0, y=0, x=0, core=0):
        far, near = 2 * z + y, 2 * x + core
        pairs = [
            (d * ranks + v, (d ^ far) * ranks + (v ^ near))
            for d in range(dps)
            for v in range(ranks)
        ]
        return lax.ppermute(value, AXES, pairs)

    packed, chosen = call(
        pack_kernel,
        (
            in_hbm(hidden),
            in_hbm(loss_mask.reshape(1, tokens)),
            in_hbm(target_ids.reshape(1, tokens)),
            in_hbm(turn_ids.reshape(1, tokens)),
        ),
        [HBM] * 4,
        (
            shape((CAP, width + IDS), bf16),
            shape((CAP, tokens), bf16),
        ),
        (VMEM,) * 2,
        [pltpu.VMEM((tokens, width), bf16)]
        + [pltpu.VMEM((1, tokens), i32)] * 3
        + [pltpu.SemaphoreType.DMA((4,))],
    )

    line_order = [0, *range(2, zs), 1]
    blocks = [send(packed, z=z) if z else packed for z in line_order]
    line_rows = zs * CAP
    line, line_plain = call(
        functools.partial(join_kernel, line_order),
        blocks,
        [VMEM] * zs,
        (shape((line_rows, width + IDS), bf16), shape((line_rows, width), bf16)),
        (VMEM, VMEM),
    )
    pieces = {(2 * x, y): send(line_plain if x else line, y=y, x=x) for y, x in square}
    held, away, same = call(
        functools.partial(stage_kernel, ranks),
        (line, in_hbm(weight)),
        [VMEM, HBM],
        (
            shape((depth, columns), bf16),
            shape((depth // 2, columns), bf16),
            shape(line.shape, bf16),
        ),
        (VMEM,) * 3,
        [pltpu.SemaphoreType.DMA((ranks + xs,))],
    )
    pieces[0, 0] = same
    for b, y in list(pieces):
        pieces[b + 1, y] = send(pieces[b, y], core=1)
    rows = [pieces[b, y] for b in range(ranks) for y in range(2)]

    info = call(
        info_kernel,
        (*rows[:2], advantages.reshape(1, -1)),
        [VMEM] * 3,
        shape((total_rows, 128), f32),
        VMEM,
    )
    near = [pieces[b, y] for b in range(0, ranks, 2) for y in range(2)]
    partial = call(
        functools.partial(first_kernel, ranks),
        (held, *near),
        [VMEM] * (1 + len(near)),
        shape((total_rows, columns), f32),
        VMEM,
        flops=flops // 2,
    )
    beside = [pieces[b, y] for b in range(1, ranks, 2) for y in range(2)]
    logits, stats = call(
        functools.partial(logits_kernel, ranks, dps),
        (info, partial, held, *beside),
        [VMEM] * (3 + len(beside)),
        (
            shape((total_rows, columns), f32),
            shape((dps * ranks, 1, 2 * total_rows + 128), f32),
        ),
        (VMEM, VMEM),
        flops=flops // 2,
    )
    other_logits = send(logits, core=1)
    away = call(
        gate_kernel, (away, stats), [ANY, ANY], shape(away.shape, bf16), ANY, aliases={0: 0}
    )
    other_held = send(away, core=1)
    stats = lax.all_to_all(stats, AXES, 0, 0)
    rows_part = total_rows // 4
    whole = (ranks, rows_part, width)
    columns_shape = shape((total_rows, 128), f32)
    pair_columns, *products = call(
        products_kernel,
        (info, logits, other_logits, held, other_held),
        [VMEM] * 5,
        (columns_shape,) + (shape(whole, f32),) * 2 + (shape(whole, bf16),) * 2,
        (VMEM,) * 5,
        flops=2 * flops,
    )

    order = sorted(range(1, ranks), key=lambda place: (place % 2 + (place > 1), place)) + [0]
    outs = (shape((rows_part, width), bf16),) * (ranks - 1) + (shape((rows_part, width), f32),)
    ends, sums = [None] * zs, [None, None]
    table, *going_far = call(
        functools.partial(far_kernel, order, dps),
        (info, pair_columns, stats, products[1], products[3]),
        [VMEM] * 5,
        (columns_shape, *outs),
        (VMEM,) * (1 + ranks),
    )
    logit_grad, *going_near = call(
        functools.partial(near_kernel, order),
        (info, pair_columns, table, products[0], products[2], logits),
        [VMEM] * 6,
        (shape((total_rows, columns), bf16), *outs),
        (VMEM,) * (1 + ranks),
    )
    for chunk, going in ((1, going_far), (0, going_near)):
        sums[chunk] = [going[-1]]
        for place, value in zip(order, going[:-1]):
            sums[chunk].append(send(value, y=place % 2, x=place // 2))

    def weight_part(first, after, *extra):
        blocks = range(first, first + ranks // 2)
        chosen_rows = rows[2 * first:2 * first + ranks]
        return call(
            functools.partial(weight_kernel, blocks, len(extra)),
            (after, logit_grad, *extra, *chosen_rows),
            [ANY, VMEM] + [HBM] * (len(extra) > 0)
            + [VMEM] * (max(len(extra) - 1, 0) + len(chosen_rows)),
            (shape((depth, columns), bf16), shape((8, 128), f32)),
            (HBM, VMEM),
            [
                pltpu.VMEM((depth // 2, columns), bf16),
                pltpu.SemaphoreType.DMA((ranks // 2,)),
            ],
            flops=flops // 2,
            aliases={2: 0} if extra else {},
        )

    weight_grad, finished = weight_part(0, sums[0][0])
    for chunk in (1, 0):
        near = chunk * zs // 2
        parts_z = call(
            functools.partial(corner_kernel, ranks - 1),
            (table if chunk else finished, *sums[chunk]),
            [ANY] + [VMEM] * ranks,
            tuple(shape((CAP, width), bf16 if near + z else f32) for z in range(zs // 2)),
            (VMEM,) * (zs // 2),
        )
        for z, value in enumerate(parts_z):
            ends[near + z] = send(value, z=near + z) if near + z else value
    weight_grad, last = weight_part(ranks // 2, parts_z[0], weight_grad, info, table, stats)
    hidden_grad, loss = call(
        unpack_kernel,
        (last, chosen, *ends),
        [VMEM] * (2 + len(ends)),
        (shape((tokens, width), bf16), shape((1, 1), f32)),
        (VMEM, SMEM),
    )
    return loss[0, 0], hidden_grad, weight_grad


def solution(mesh):
    return jax.shard_map(
        functools.partial(body, mesh.shape["dp"], mesh.shape["vocab"]),
        mesh=mesh,
        in_specs=(P("dp", "vocab"), P(None, AXES), P("dp"), P("dp"), P("dp"), P()),
        out_specs=(P(), P("dp", "vocab"), P(None, AXES)),
        check_vma=False,
    )
```

```python
import functools
import math

import jax
import jax.numpy as jnp
from jax import lax
from jax.experimental import pallas as pl
from jax.experimental.pallas import tpu as pltpu
from jax.sharding import PartitionSpec as P

CAP = 32
MOST_VMEM = 56 * 1024 * 1024
IDS = 128
grad_scale = 16384.0
AXES = ("dp", "vocab")
SMEM = pl.BlockSpec(memory_space=pltpu.SMEM)
VMEM = pl.BlockSpec(memory_space=pltpu.VMEM)
HBM = pl.BlockSpec(memory_space=pltpu.HBM)
ANY = pl.BlockSpec(memory_space=pl.ANY)


def size_of(value):
    return math.prod(value.shape) * jnp.dtype(value.dtype).itemsize


def call(kernel, operands, in_specs, out_shape, out_specs, scratch=(), spare=4, flops=0, aliases={}):
    outs = jax.tree.leaves(out_shape)
    sized = [v for v, s in zip(operands, in_specs) if s is VMEM]
    sized += [v for v, s in zip(outs, jax.tree.leaves(out_specs)) if s is VMEM]
    held = [s for s in scratch if getattr(s, "memory_space", None) == pltpu.VMEM]
    total = sum(size_of(v) for v in sized) + sum(size_of(s) for s in held)
    return pl.pallas_call(
        kernel,
        out_shape=out_shape,
        in_specs=in_specs,
        out_specs=out_specs,
        scratch_shapes=scratch,
        input_output_aliases=aliases,
        compiler_params=pltpu.CompilerParams(vmem_limit_bytes=min(total + spare * 1024 * 1024, MOST_VMEM)),
        cost_estimate=pl.CostEstimate(
            flops=flops,
            bytes_accessed=sum(size_of(v) for v in list(operands) + outs),
            transcendentals=0,
        ),
    )(*operands)


def in_hbm(value):
    return pltpu.with_memory_space_constraint(value, pltpu.HBM)


def coordinates():
    group, rank = lax.axis_index("dp"), lax.axis_index("vocab")
    groups, ranks = lax.axis_size("dp"), lax.axis_size("vocab")
    position = group % 2 * (groups // 2) + group // 2
    return rank, position, group * ranks + rank


def choose(mask):
    tokens = mask.shape[1]
    wide = jnp.broadcast_to(mask.astype(jnp.float32), (8, tokens))
    before = lax.broadcasted_iota(jnp.int32, (tokens, tokens), 0)
    after = lax.broadcasted_iota(jnp.int32, (tokens, tokens), 1)
    upto = (before <= after).astype(jnp.float32)
    slot = jnp.dot(
        wide.astype(jnp.bfloat16), upto.astype(jnp.bfloat16), preferred_element_type=jnp.float32
    )[0:1]
    grid = lax.broadcasted_iota(jnp.int32, (CAP, tokens), 0) + 1
    return (slot.astype(jnp.int32) == grid) & (mask == 1)


def pack_kernel(hidden_hbm, mask_hbm, target_hbm, turn_hbm, rows, chosen_out, *scratch):
    hidden, mask, target, turn, sems = scratch
    copies = []
    for place, (source, held) in enumerate(
        ((mask_hbm, mask), (target_hbm, target), (turn_hbm, turn), (hidden_hbm, hidden))
    ):
        copy = pltpu.make_async_copy(source, held, sems.at[place])
        copy.start()
        copies.append(copy)
    for copy in copies[:3]:
        copy.wait()
    width = hidden.shape[1]
    chosen = choose(mask[...])
    one_hot = chosen.astype(jnp.float32).astype(jnp.bfloat16)
    chosen_out[...] = one_hot
    turns, targets = turn[...], target[...]
    fields = (
        mask[...],
        turns & 255,
        turns >> 8,
        targets & 255,
        (targets >> 8) & 255,
        targets >> 16,
    )
    lane = lax.broadcasted_iota(jnp.int32, (CAP, IDS), 1)
    table = jnp.zeros((CAP, IDS), jnp.float32)
    for place, field in enumerate(fields):
        picked = jnp.where(chosen, field.astype(jnp.float32), 0.0)
        table = jnp.where(lane == place, jnp.sum(picked, axis=1, keepdims=True), table)
    rows[:, width:] = table.astype(jnp.bfloat16)
    copies[3].wait()
    packed = jnp.dot(one_hot, hidden[...], preferred_element_type=jnp.float32)
    rows[:, :width] = packed.astype(jnp.bfloat16)


def join_kernel(order, *refs):
    blocks, line, plain = refs[:-2], refs[-2], refs[-1]
    for place, block in zip(order, blocks):
        line[place * CAP:(place + 1) * CAP] = block[...]
        plain[place * CAP:(place + 1) * CAP] = block[:, :plain.shape[1]]


def stage_kernel(blocks, line, weight, held, away, same, sems):
    rank = coordinates()[0]
    width = weight.shape[0] // blocks
    copies = []
    for block in list(range(1, blocks, 2)) + list(range(0, blocks, 2)):
        start = pl.multiple_of((rank ^ block) * width, width)
        targets = [held.at[pl.ds(start, width)]]
        if block % 2:
            targets.append(away.at[pl.ds(block // 2 * width, width)])
        for target in targets:
            copy = pltpu.make_async_copy(
                weight.at[pl.ds(start, width)], target, sems.at[len(copies)]
            )
            copy.start()
            copies.append(copy)
    same[...] = line[...]
    for copy in copies:
        copy.wait()


def gate_kernel(value, after, same):
    pass


def info_kernel(*refs):
    advantages, info = refs[-2:]
    start = refs[0].shape[1] - IDS
    table = jnp.concatenate([ref[:, start:] for ref in refs[:-2]], axis=0).astype(jnp.float32)
    valid = table[:, 0:1]
    turn = table[:, 1:2] + 256.0 * table[:, 2:3]
    target = table[:, 3:4] + 256.0 * table[:, 4:5] + 65536.0 * table[:, 5:6]
    turns = advantages.shape[1]
    spot = lax.broadcasted_iota(jnp.int32, (table.shape[0], turns), 1)
    gain = jnp.sum(
        jnp.where(spot == turn.astype(jnp.int32), advantages[...], 0.0), axis=1, keepdims=True
    )
    weight = valid * gain / jnp.sum(valid)
    lane = lax.broadcasted_iota(jnp.int32, info.shape, 1)
    info[...] = jnp.where(lane == 0, weight, jnp.where(lane == 1, target, 0.0))


def reorder(stats, position, groups):
    lanes = stats.shape[1]
    lane = lax.broadcasted_iota(jnp.int32, stats.shape, 1)
    bit = 1
    while bit < groups:
        size = CAP * bit
        swapped = jnp.where(
            (lane & size) != 0,
            pltpu.roll(stats, size, 1),
            pltpu.roll(stats, lanes - size, 1),
        )
        stats = jnp.where((position & bit) != 0, swapped, stats)
        bit *= 2
    return stats


def all_rows(pieces, block, width):
    return jnp.concatenate([ref[:, :width] for ref in pieces[2 * block:2 * block + 2]], axis=0)


def some_logits(blocks, first, pieces, weight):
    width = weight.shape[0] // blocks
    rank, total = coordinates()[0], None
    for place, block in enumerate(range(first, blocks, 2)):
        start = pl.multiple_of((rank ^ block) * width, width)
        part = jnp.dot(
            all_rows(pieces, place, width),
            weight[pl.ds(start, width), :],
            preferred_element_type=jnp.float32,
        )
        total = part if total is None else total + part
    return total


def first_kernel(blocks, weight, *refs):
    refs[-1][...] = some_logits(blocks, 0, refs[:-1], weight)


def logits_kernel(blocks, groups, info, partial, weight, *refs):
    pieces, (logits, stats) = refs[:-2], refs[-2:]
    _, position, shard = coordinates()
    total = partial[...] + some_logits(blocks, 1, pieces, weight)
    logits[...] = total
    height, columns = total.shape
    target = info[:, 1:2].astype(jnp.int32) - shard * columns
    column = lax.broadcasted_iota(jnp.int32, total.shape, 1)
    hit = jnp.sum(jnp.where(column == target, total, 0.0), axis=1, keepdims=True)
    hit = jnp.sum(hit * info[:, 0:1])
    peak = jnp.max(total, axis=1, keepdims=True)
    mass = jnp.sum(jnp.exp(total - peak), axis=1, keepdims=True)
    lane = lax.broadcasted_iota(jnp.int32, (height, 128), 1)
    table = jnp.where(lane == 0, peak, jnp.where(lane == 1, mass, hit))
    table = reorder(jnp.transpose(table)[0:8], position, groups)
    line = jnp.concatenate([table[0:1], table[1:2], table[2:3, :128]], axis=1)
    stats[...] = jnp.broadcast_to(line[None], stats.shape)


def log_totals(groups, stats, height):
    peaks, masses = stats[:, :, :height], stats[:, :, height:2 * height]
    peak = jnp.max(peaks, axis=0)
    mass = jnp.sum(masses * jnp.exp(peaks - peak[None]), axis=0)
    line = jnp.broadcast_to(peak + jnp.log(mass), (8, height))
    line = reorder(line, coordinates()[1], groups)
    return jnp.transpose(jnp.concatenate([line] * 16, axis=0))


def grad_kernel(order, groups, info, mine, theirs, weight, other_weight, stats, *refs):
    logit_grad, table, outs = refs[0], refs[1], refs[2:]
    chunks = (outs[len(order):], outs[:len(order)])
    rank, _, shard = coordinates()
    height, columns = mine.shape
    part = height // 4
    table[...] = log_totals(groups, stats, height)
    log_total = table[:, 0:1]
    row_weight, target = info[:, 0:1], info[:, 1:2].astype(jnp.int32)

    def grad_of(logits, shard):
        column = lax.broadcasted_iota(jnp.int32, (height, columns), 1) + shard * columns
        probability = jnp.exp(logits[...] - log_total)
        return (
            grad_scale * row_weight * (probability - (column == target).astype(jnp.float32))
        ).astype(jnp.bfloat16)

    grad = grad_of(mine, shard)
    logit_grad[...] = grad
    grads = (grad, grad_of(theirs, shard ^ 1))
    width = outs[0].shape[1]
    for x in range(len(order) // 2):
        start = pl.multiple_of((rank ^ 2 * x) * width, width)
        weights = (weight[pl.ds(start, width), :], other_weight[x * width:(x + 1) * width, :])
        total = sum(
            lax.dot_general(g, w, (((1,), (1,)), ((), ())), preferred_element_type=jnp.float32)
            for g, w in zip(grads, weights)
        )
        for quarter in range(4):
            out = chunks[quarter % 2][order.index(2 * x + quarter // 2)]
            out[...] = total[quarter * part:(quarter + 1) * part].astype(out.dtype)


def weight_kernel(blocks, skipped, after, logit_grad, *refs):
    pieces, (out, last, done, sems) = refs[skipped:-4], refs[-4:]
    rank = coordinates()[0]
    width = done.shape[0] // len(blocks)
    copies = []
    for place, block in enumerate(blocks):
        done[place * width:(place + 1) * width] = lax.dot_general(
            all_rows(pieces, place, width),
            logit_grad[...],
            (((0,), (0,)), ((), ())),
            preferred_element_type=jnp.float32,
        ).astype(jnp.bfloat16)
        start = pl.multiple_of((rank ^ block) * width, width)
        copy = pltpu.make_async_copy(
            done.at[pl.ds(place * width, width)], out.at[pl.ds(start, width)], sems.at[place]
        )
        copy.start()
        copies.append(copy)
    if skipped:
        info, table, stats = refs[1:4]
        hits = jnp.sum(stats[:, :, 2 * info.shape[0]:], axis=0)
        loss = jnp.sum(info[:, 0:1] * table[:, 0:1]) - hits[0, 0]
        last[...] = jnp.full(last.shape, loss, jnp.float32)
    else:
        last[...] = jnp.zeros_like(last)
    for copy in copies:
        copy.wait()


def corner_kernel(count, after, kept, *refs):
    total = kept[...]
    for ref in refs[:count]:
        total = total + ref[...].astype(jnp.float32)
    for place, out in enumerate(refs[count:]):
        out[...] = total[place * CAP:(place + 1) * CAP].astype(out.dtype)


def unpack_kernel(last, chosen, *refs):
    out, loss = refs[-2:]
    loss[0, 0] = last[0, 0]
    total = sum(ref[...].astype(jnp.float32) for ref in refs[:-2])
    out[...] = lax.dot_general(
        chosen[...],
        total.astype(jnp.bfloat16),
        (((0,), (0,)), ((), ())),
        preferred_element_type=jnp.float32,
    ).astype(jnp.bfloat16)


def body(dps, ranks, hidden, weight, loss_mask, target_ids, turn_ids, advantages):
    tokens, width = hidden.shape
    depth, columns = weight.shape
    zs, xs = dps // 2, ranks // 2
    total_rows = dps * CAP
    bf16, f32, i32 = jnp.bfloat16, jnp.float32, jnp.int32
    shape = jax.ShapeDtypeStruct
    square = [(y, x) for x in reversed(range(xs)) for y in (1, 0) if x or y]
    flops = 2 * total_rows * depth * columns

    def send(value, z=0, y=0, x=0, core=0):
        far, near = 2 * z + y, 2 * x + core
        pairs = [
            (d * ranks + v, (d ^ far) * ranks + (v ^ near))
            for d in range(dps)
            for v in range(ranks)
        ]
        return lax.ppermute(value, AXES, pairs)

    packed, chosen = call(
        pack_kernel,
        (
            in_hbm(hidden),
            in_hbm(loss_mask.reshape(1, tokens)),
            in_hbm(target_ids.reshape(1, tokens)),
            in_hbm(turn_ids.reshape(1, tokens)),
        ),
        [HBM] * 4,
        (
            shape((CAP, width + IDS), bf16),
            shape((CAP, tokens), bf16),
        ),
        (VMEM,) * 2,
        [pltpu.VMEM((tokens, width), bf16)]
        + [pltpu.VMEM((1, tokens), i32)] * 3
        + [pltpu.SemaphoreType.DMA((4,))],
    )

    line_order = [0, *range(2, zs), 1]
    blocks = [send(packed, z=z) if z else packed for z in line_order]
    line_rows = zs * CAP
    line, line_plain = call(
        functools.partial(join_kernel, line_order),
        blocks,
        [VMEM] * zs,
        (shape((line_rows, width + IDS), bf16), shape((line_rows, width), bf16)),
        (VMEM, VMEM),
    )
    pieces = {(2 * x, y): send(line_plain if x else line, y=y, x=x) for y, x in square}
    held, away, same = call(
        functools.partial(stage_kernel, ranks),
        (line, in_hbm(weight)),
        [VMEM, HBM],
        (
            shape((depth, columns), bf16),
            shape((depth // 2, columns), bf16),
            shape(line.shape, bf16),
        ),
        (VMEM,) * 3,
        [pltpu.SemaphoreType.DMA((ranks + xs,))],
    )
    pieces[0, 0] = same
    for b, y in list(pieces):
        pieces[b + 1, y] = send(pieces[b, y], core=1)
    rows = [pieces[b, y] for b in range(ranks) for y in range(2)]

    info = call(
        info_kernel,
        (*rows[:2], advantages.reshape(1, -1)),
        [VMEM] * 3,
        shape((total_rows, 128), f32),
        VMEM,
    )
    near = [pieces[b, y] for b in range(0, ranks, 2) for y in range(2)]
    partial = call(
        functools.partial(first_kernel, ranks),
        (held, *near),
        [VMEM] * (1 + len(near)),
        shape((total_rows, columns), f32),
        VMEM,
        flops=flops // 2,
    )
    beside = [pieces[b, y] for b in range(1, ranks, 2) for y in range(2)]
    logits, stats = call(
        functools.partial(logits_kernel, ranks, dps),
        (info, partial, held, *beside),
        [VMEM] * (3 + len(beside)),
        (
            shape((total_rows, columns), f32),
            shape((dps * ranks, 1, 2 * total_rows + 128), f32),
        ),
        (VMEM, VMEM),
        flops=flops // 2,
    )
    other_logits = send(logits, core=1)
    away = call(
        gate_kernel, (away, stats), [ANY, ANY], shape(away.shape, bf16), ANY, aliases={0: 0}
    )
    other_held = send(away, core=1)
    stats = lax.all_to_all(stats, AXES, 0, 0)
    rows_part = total_rows // 4
    order = sorted(range(1, ranks), key=lambda place: (place % 2 + (place > 1), place)) + [0]
    outs = (shape((rows_part, width), bf16),) * (ranks - 1) + (shape((rows_part, width), f32),)
    logit_grad, table, *going = call(
        functools.partial(grad_kernel, order, dps),
        (info, logits, other_logits, held, other_held, stats),
        [VMEM] * 6,
        (shape((total_rows, columns), bf16), shape((total_rows, 128), f32)) + outs * 2,
        (VMEM,) * (2 + 2 * ranks),
        flops=flops,
    )
    ends, sums = [None] * zs, [None, None]
    for chunk in (1, 0):
        *values, corner = going[(1 - chunk) * ranks:(2 - chunk) * ranks]
        sums[chunk] = [corner]
        for place, value in zip(order, values):
            sums[chunk].append(send(value, y=place % 2, x=place // 2))

    def weight_part(first, after, *extra):
        blocks = range(first, first + ranks // 2)
        chosen_rows = rows[2 * first:2 * first + ranks]
        return call(
            functools.partial(weight_kernel, blocks, len(extra)),
            (after, logit_grad, *extra, *chosen_rows),
            [ANY, VMEM] + [HBM] * (len(extra) > 0)
            + [VMEM] * (max(len(extra) - 1, 0) + len(chosen_rows)),
            (shape((depth, columns), bf16), shape((8, 128), f32)),
            (HBM, VMEM),
            [
                pltpu.VMEM((depth // 2, columns), bf16),
                pltpu.SemaphoreType.DMA((ranks // 2,)),
            ],
            flops=flops // 2,
            aliases={2: 0} if extra else {},
        )

    weight_grad, finished = weight_part(0, sums[0][0])
    for chunk in (1, 0):
        near = chunk * zs // 2
        parts_z = call(
            functools.partial(corner_kernel, ranks - 1),
            (table if chunk else finished, *sums[chunk]),
            [ANY] + [VMEM] * ranks,
            tuple(shape((CAP, width), bf16 if near + z else f32) for z in range(zs // 2)),
            (VMEM,) * (zs // 2),
        )
        for z, value in enumerate(parts_z):
            ends[near + z] = send(value, z=near + z) if near + z else value
    weight_grad, last = weight_part(ranks // 2, parts_z[0], weight_grad, info, table, stats)
    hidden_grad, loss = call(
        unpack_kernel,
        (last, chosen, *ends),
        [VMEM] * (2 + len(ends)),
        (shape((tokens, width), bf16), shape((1, 1), f32)),
        (VMEM, SMEM),
    )
    return loss[0, 0], hidden_grad, weight_grad


def solution(mesh):
    return jax.shard_map(
        functools.partial(body, mesh.shape["dp"], mesh.shape["vocab"]),
        mesh=mesh,
        in_specs=(P("dp", "vocab"), P(None, AXES), P("dp"), P("dp"), P("dp"), P()),
        out_specs=(P(), P("dp", "vocab"), P(None, AXES)),
        check_vma=False,
    )
```

```python
import functools
import math

import jax
import jax.numpy as jnp
from jax import lax
from jax.experimental import pallas as pl
from jax.experimental.pallas import tpu as pltpu
from jax.sharding import PartitionSpec as P

CAP = 32
LANES = 128
SUB = 16
MOST_VMEM = 56 * 1024 * 1024
grad_scale = 16384.0
AXES = ("dp", "vocab")
SMEM = pl.BlockSpec(memory_space=pltpu.SMEM)
VMEM = pl.BlockSpec(memory_space=pltpu.VMEM)
HBM = pl.BlockSpec(memory_space=pltpu.HBM)
ANY = pl.BlockSpec(memory_space=pl.ANY)


def size_of(value):
    return math.prod(value.shape) * jnp.dtype(value.dtype).itemsize


def call(kernel, operands, in_specs, out_shape, out_specs, scratch=(), spare=4, flops=0, aliases={}):
    outs = jax.tree.leaves(out_shape)
    sized = [v for v, s in zip(operands, in_specs) if s is VMEM]
    sized += [v for v, s in zip(outs, jax.tree.leaves(out_specs)) if s is VMEM]
    held = [s for s in scratch if getattr(s, "memory_space", None) == pltpu.VMEM]
    total = sum(size_of(v) for v in sized) + sum(size_of(s) for s in held)
    return pl.pallas_call(
        kernel,
        out_shape=out_shape,
        in_specs=in_specs,
        out_specs=out_specs,
        scratch_shapes=scratch,
        input_output_aliases=aliases,
        compiler_params=pltpu.CompilerParams(vmem_limit_bytes=min(total + spare * 1024 * 1024, MOST_VMEM)),
        cost_estimate=pl.CostEstimate(
            flops=flops,
            bytes_accessed=sum(size_of(v) for v in list(operands) + outs),
            transcendentals=0,
        ),
    )(*operands)


def in_hbm(value):
    return pltpu.with_memory_space_constraint(value, pltpu.HBM)


def coordinates():
    group, rank = lax.axis_index("dp"), lax.axis_index("vocab")
    groups, ranks = lax.axis_size("dp"), lax.axis_size("vocab")
    position = group % 2 * (groups // 2) + group // 2
    return rank, position, group * ranks + rank


def choose(mask):
    tokens = mask.shape[1]
    wide = jnp.broadcast_to(mask.astype(jnp.float32), (8, tokens))
    before = lax.broadcasted_iota(jnp.int32, (tokens, tokens), 0)
    after = lax.broadcasted_iota(jnp.int32, (tokens, tokens), 1)
    upto = (before <= after).astype(jnp.float32)
    slot = jnp.dot(
        wide.astype(jnp.bfloat16), upto.astype(jnp.bfloat16), preferred_element_type=jnp.float32
    )[0:1]
    grid = lax.broadcasted_iota(jnp.int32, (CAP, tokens), 0) + 1
    return (slot.astype(jnp.int32) == grid) & (mask == 1)


def payload_rows(width):
    return CAP * width // LANES + SUB


def tiles(width):
    count = width // LANES
    for high in range(CAP // SUB):
        for low in range(count):
            yield (
                (high * count + low) * SUB,
                slice(high * SUB, (high + 1) * SUB),
                slice(low * LANES, (low + 1) * LANES),
            )


def pack_kernel(hidden_hbm, mask_hbm, target_hbm, turn_hbm, payload, chosen_out, *scratch):
    hidden, mask, target, turn, sems = scratch
    copies = []
    for place, (source, held) in enumerate(
        ((mask_hbm, mask), (target_hbm, target), (turn_hbm, turn), (hidden_hbm, hidden))
    ):
        copy = pltpu.make_async_copy(source, held, sems.at[place])
        copy.start()
        copies.append(copy)
    for copy in copies[:3]:
        copy.wait()
    width = hidden.shape[1]
    one_hot = choose(mask[...]).astype(jnp.float32).astype(jnp.bfloat16)
    chosen_out[...] = one_hot
    turns, targets = turn[...], target[...]
    fields = (
        mask[...],
        turns & 255,
        turns >> 8,
        targets & 255,
        (targets >> 8) & 255,
        targets >> 16,
    )
    fields += (jnp.zeros_like(turns),) * (SUB - len(fields))
    fields = jnp.concatenate([field.astype(jnp.float32) for field in fields], axis=0)
    slots = jnp.concatenate([one_hot] + [jnp.zeros_like(one_hot)] * (LANES // CAP - 1), axis=0)
    ids = lax.dot_general(
        fields.astype(jnp.bfloat16),
        slots,
        (((1,), (1,)), ((), ())),
        preferred_element_type=jnp.float32,
    )
    payload[payload.shape[0] - SUB:] = ids.astype(jnp.bfloat16)
    copies[3].wait()
    packed = jnp.dot(one_hot, hidden[...], preferred_element_type=jnp.float32)
    packed = packed.astype(jnp.bfloat16)
    for start, rows, lanes in tiles(width):
        payload[start:start + SUB] = packed[rows, lanes]


def unroll(payload, first, plain, place):
    for start, rows, lanes in tiles(plain.shape[1]):
        target = slice(place * CAP + rows.start, place * CAP + rows.stop)
        plain[target, lanes] = payload[first + start:first + start + SUB]


def join_kernel(order, *refs):
    blocks, line, plain = refs[:-2], refs[-2], refs[-1]
    for place, block in zip(order, blocks):
        height = block.shape[0]
        line[place * height:(place + 1) * height] = block[...]
        unroll(block, 0, plain, place)


def rows_kernel(after, line, plain):
    height = payload_rows(plain.shape[1])
    for place in range(line.shape[0] // height):
        unroll(line, place * height, plain, place)


def stage_kernel(blocks, line, weight, held, away, same, sems):
    rank = coordinates()[0]
    width = weight.shape[0] // blocks
    copies = []
    for block in list(range(1, blocks, 2)) + list(range(0, blocks, 2)):
        start = pl.multiple_of((rank ^ block) * width, width)
        targets = [held.at[pl.ds(start, width)]]
        if block % 2:
            targets.append(away.at[pl.ds(block // 2 * width, width)])
        for target in targets:
            copy = pltpu.make_async_copy(
                weight.at[pl.ds(start, width)], target, sems.at[len(copies)]
            )
            copy.start()
            copies.append(copy)
    same[...] = line[...]
    for copy in copies:
        copy.wait()


def gate_kernel(value, after, same):
    pass


def info_kernel(height, own, other, advantages, info):
    tables = []
    for line in (own, other):
        for end in range(height, line.shape[0] + 1, height):
            ids = line[end - SUB:end].astype(jnp.float32)
            ids = jnp.concatenate([ids] * (LANES // SUB), axis=0)
            tables.append(jnp.transpose(ids)[:CAP])
    table = jnp.concatenate(tables, axis=0)
    valid = table[:, 0:1]
    turn = table[:, 1:2] + 256.0 * table[:, 2:3]
    target = table[:, 3:4] + 256.0 * table[:, 4:5] + 65536.0 * table[:, 5:6]
    turns = advantages.shape[1]
    spot = lax.broadcasted_iota(jnp.int32, (table.shape[0], turns), 1)
    gain = jnp.sum(
        jnp.where(spot == turn.astype(jnp.int32), advantages[...], 0.0), axis=1, keepdims=True
    )
    weight = valid * gain / jnp.sum(valid)
    lane = lax.broadcasted_iota(jnp.int32, info.shape, 1)
    info[...] = jnp.where(lane == 0, weight, jnp.where(lane == 1, target, 0.0))


def reorder(stats, position, groups):
    lanes = stats.shape[1]
    lane = lax.broadcasted_iota(jnp.int32, stats.shape, 1)
    bit = 1
    while bit < groups:
        size = CAP * bit
        swapped = jnp.where(
            (lane & size) != 0,
            pltpu.roll(stats, size, 1),
            pltpu.roll(stats, lanes - size, 1),
        )
        stats = jnp.where((position & bit) != 0, swapped, stats)
        bit *= 2
    return stats


def all_rows(pieces, block):
    return jnp.concatenate([ref[...] for ref in pieces[2 * block:2 * block + 2]], axis=0)


def some_logits(blocks, first, pieces, weight):
    width = weight.shape[0] // blocks
    rank, total = coordinates()[0], None
    for place, block in enumerate(range(first, blocks, 2)):
        start = pl.multiple_of((rank ^ block) * width, width)
        part = jnp.dot(
            all_rows(pieces, place),
            weight[pl.ds(start, width), :],
            preferred_element_type=jnp.float32,
        )
        total = part if total is None else total + part
    return total


def first_kernel(blocks, weight, *refs):
    refs[-1][...] = some_logits(blocks, 0, refs[:-1], weight)


def logits_kernel(blocks, groups, info, partial, weight, *refs):
    pieces, (logits, stats) = refs[:-2], refs[-2:]
    _, position, shard = coordinates()
    total = partial[...] + some_logits(blocks, 1, pieces, weight)
    logits[...] = total
    height, columns = total.shape
    target = info[:, 1:2].astype(jnp.int32) - shard * columns
    column = lax.broadcasted_iota(jnp.int32, total.shape, 1)
    hit = jnp.sum(jnp.where(column == target, total, 0.0), axis=1, keepdims=True)
    hit = jnp.sum(hit * info[:, 0:1])
    peak = jnp.max(total, axis=1, keepdims=True)
    mass = jnp.sum(jnp.exp(total - peak), axis=1, keepdims=True)
    lane = lax.broadcasted_iota(jnp.int32, (height, 128), 1)
    table = jnp.where(lane == 0, peak, jnp.where(lane == 1, mass, hit))
    table = reorder(jnp.transpose(table)[0:8], position, groups)
    line = jnp.concatenate([table[0:1], table[1:2], table[2:3, :128]], axis=1)
    stats[...] = jnp.broadcast_to(line[None], stats.shape)


def log_totals(groups, stats, height):
    peaks, masses = stats[:, :, :height], stats[:, :, height:2 * height]
    peak = jnp.max(peaks, axis=0)
    mass = jnp.sum(masses * jnp.exp(peaks - peak[None]), axis=0)
    line = jnp.broadcast_to(peak + jnp.log(mass), (8, height))
    line = reorder(line, coordinates()[1], groups)
    return jnp.transpose(jnp.concatenate([line] * 16, axis=0))


def grad_kernel(order, groups, info, mine, theirs, weight, other_weight, stats, *refs):
    logit_grad, table, outs = refs[0], refs[1], refs[2:]
    chunks = (outs[len(order):], outs[:len(order)])
    rank, _, shard = coordinates()
    height, columns = mine.shape
    part = height // 4
    table[...] = log_totals(groups, stats, height)
    log_total = table[:, 0:1]
    row_weight, target = info[:, 0:1], info[:, 1:2].astype(jnp.int32)

    def grad_of(logits, shard):
        column = lax.broadcasted_iota(jnp.int32, (height, columns), 1) + shard * columns
        probability = jnp.exp(logits[...] - log_total)
        return (
            grad_scale * row_weight * (probability - (column == target).astype(jnp.float32))
        ).astype(jnp.bfloat16)

    grad = grad_of(mine, shard)
    logit_grad[...] = grad
    grads = (grad, grad_of(theirs, shard ^ 1))
    width = outs[0].shape[1]
    for x in range(len(order) // 2):
        start = pl.multiple_of((rank ^ 2 * x) * width, width)
        weights = (weight[pl.ds(start, width), :], other_weight[x * width:(x + 1) * width, :])
        total = sum(
            lax.dot_general(g, w, (((1,), (1,)), ((), ())), preferred_element_type=jnp.float32)
            for g, w in zip(grads, weights)
        )
        for quarter in range(4):
            out = chunks[quarter % 2][order.index(2 * x + quarter // 2)]
            out[...] = total[quarter * part:(quarter + 1) * part].astype(out.dtype)


def weight_kernel(blocks, skipped, after, logit_grad, *refs):
    pieces, (out, last, done, sems) = refs[skipped:-4], refs[-4:]
    rank = coordinates()[0]
    width = done.shape[0] // len(blocks)
    copies = []
    for place, block in enumerate(blocks):
        done[place * width:(place + 1) * width] = lax.dot_general(
            all_rows(pieces, place),
            logit_grad[...],
            (((0,), (0,)), ((), ())),
            preferred_element_type=jnp.float32,
        ).astype(jnp.bfloat16)
        start = pl.multiple_of((rank ^ block) * width, width)
        copy = pltpu.make_async_copy(
            done.at[pl.ds(place * width, width)], out.at[pl.ds(start, width)], sems.at[place]
        )
        copy.start()
        copies.append(copy)
    if skipped:
        info, table, stats = refs[1:4]
        hits = jnp.sum(stats[:, :, 2 * info.shape[0]:], axis=0)
        loss = jnp.sum(info[:, 0:1] * table[:, 0:1]) - hits[0, 0]
        last[...] = jnp.full(last.shape, loss, jnp.float32)
    else:
        last[...] = jnp.zeros_like(last)
    for copy in copies:
        copy.wait()


def corner_kernel(count, after, kept, *refs):
    total = kept[...]
    for ref in refs[:count]:
        total = total + ref[...].astype(jnp.float32)
    for place, out in enumerate(refs[count:]):
        out[...] = total[place * CAP:(place + 1) * CAP].astype(out.dtype)


def unpack_kernel(last, chosen, *refs):
    out, loss = refs[-2:]
    loss[0, 0] = last[0, 0]
    total = sum(ref[...].astype(jnp.float32) for ref in refs[:-2])
    out[...] = lax.dot_general(
        chosen[...],
        total.astype(jnp.bfloat16),
        (((0,), (0,)), ((), ())),
        preferred_element_type=jnp.float32,
    ).astype(jnp.bfloat16)


def body(dps, ranks, hidden, weight, loss_mask, target_ids, turn_ids, advantages):
    tokens, width = hidden.shape
    depth, columns = weight.shape
    zs, xs = dps // 2, ranks // 2
    total_rows = dps * CAP
    bf16, f32, i32 = jnp.bfloat16, jnp.float32, jnp.int32
    shape = jax.ShapeDtypeStruct
    square = [(y, x) for x in reversed(range(xs)) for y in (1, 0) if x or y]
    flops = 2 * total_rows * depth * columns

    def send(value, z=0, y=0, x=0, core=0):
        far, near = 2 * z + y, 2 * x + core
        pairs = [
            (d * ranks + v, (d ^ far) * ranks + (v ^ near))
            for d in range(dps)
            for v in range(ranks)
        ]
        return lax.ppermute(value, AXES, pairs)

    packed, chosen = call(
        pack_kernel,
        (
            in_hbm(hidden),
            in_hbm(loss_mask.reshape(1, tokens)),
            in_hbm(target_ids.reshape(1, tokens)),
            in_hbm(turn_ids.reshape(1, tokens)),
        ),
        [HBM] * 4,
        (
            shape((payload_rows(width), LANES), bf16),
            shape((CAP, tokens), bf16),
        ),
        (VMEM,) * 2,
        [pltpu.VMEM((tokens, width), bf16)]
        + [pltpu.VMEM((1, tokens), i32)] * 3
        + [pltpu.SemaphoreType.DMA((4,))],
    )

    line_order = [0, *range(2, zs), 1]
    blocks = [send(packed, z=z) if z else packed for z in line_order]
    height = payload_rows(width)
    line, line_plain = call(
        functools.partial(join_kernel, line_order),
        blocks,
        [VMEM] * zs,
        (shape((zs * height, LANES), bf16), shape((zs * CAP, width), bf16)),
        (VMEM, VMEM),
    )
    pieces = {(2 * x, y): send(line_plain if x else line, y=y, x=x) for y, x in square}
    across = pieces[0, 1]
    held, away, same = call(
        functools.partial(stage_kernel, ranks),
        (line_plain, in_hbm(weight)),
        [VMEM, HBM],
        (
            shape((depth, columns), bf16),
            shape((depth // 2, columns), bf16),
            shape(line_plain.shape, bf16),
        ),
        (VMEM,) * 3,
        [pltpu.SemaphoreType.DMA((ranks + xs,))],
    )
    plain = shape((zs * CAP, width), bf16)
    pieces[0, 1] = call(rows_kernel, (same, across), [ANY, VMEM], plain, VMEM)
    pieces[1, 1] = send(pieces[0, 1], core=1)
    for x in range(1, xs):
        operands = (pieces[2 * x, 1], pieces[1, 1])
        pieces[2 * x, 1] = call(gate_kernel, operands, [ANY] * 2, plain, ANY, aliases={0: 0})
    pieces[0, 0] = same
    for b, y in list(pieces):
        if b % 2 == 0 and (b + 1, y) not in pieces:
            pieces[b + 1, y] = send(pieces[b, y], core=1)
    rows = [pieces[b, y] for b in range(ranks) for y in range(2)]

    info = call(
        functools.partial(info_kernel, height),
        (line, across, advantages.reshape(1, -1)),
        [VMEM] * 3,
        shape((total_rows, 128), f32),
        VMEM,
    )
    near = [pieces[b, y] for b in range(0, ranks, 2) for y in range(2)]
    partial = call(
        functools.partial(first_kernel, ranks),
        (held, *near),
        [VMEM] * (1 + len(near)),
        shape((total_rows, columns), f32),
        VMEM,
        flops=flops // 2,
    )
    beside = [pieces[b, y] for b in range(1, ranks, 2) for y in range(2)]
    logits, stats = call(
        functools.partial(logits_kernel, ranks, dps),
        (info, partial, held, *beside),
        [VMEM] * (3 + len(beside)),
        (
            shape((total_rows, columns), f32),
            shape((dps * ranks, 1, 2 * total_rows + 128), f32),
        ),
        (VMEM, VMEM),
        flops=flops // 2,
    )
    other_logits = send(logits, core=1)
    away = call(
        gate_kernel, (away, stats), [ANY, ANY], shape(away.shape, bf16), ANY, aliases={0: 0}
    )
    other_held = send(away, core=1)
    stats = lax.all_to_all(stats, AXES, 0, 0)
    rows_part = total_rows // 4
    order = sorted(range(1, ranks), key=lambda place: (place % 2 + (place > 1), place)) + [0]
    outs = (shape((rows_part, width), bf16),) * (ranks - 1) + (shape((rows_part, width), f32),)
    logit_grad, table, *going = call(
        functools.partial(grad_kernel, order, dps),
        (info, logits, other_logits, held, other_held, stats),
        [VMEM] * 6,
        (shape((total_rows, columns), bf16), shape((total_rows, 128), f32)) + outs * 2,
        (VMEM,) * (2 + 2 * ranks),
        flops=flops,
    )
    ends, sums = [None] * zs, [None, None]
    for chunk in (1, 0):
        *values, corner = going[(1 - chunk) * ranks:(2 - chunk) * ranks]
        sums[chunk] = [corner]
        for place, value in zip(order, values):
            sums[chunk].append(send(value, y=place % 2, x=place // 2))

    def weight_part(first, after, *extra):
        blocks = range(first, first + ranks // 2)
        chosen_rows = rows[2 * first:2 * first + ranks]
        return call(
            functools.partial(weight_kernel, blocks, len(extra)),
            (after, logit_grad, *extra, *chosen_rows),
            [ANY, VMEM] + [HBM] * (len(extra) > 0)
            + [VMEM] * (max(len(extra) - 1, 0) + len(chosen_rows)),
            (shape((depth, columns), bf16), shape((8, 128), f32)),
            (HBM, VMEM),
            [
                pltpu.VMEM((depth // 2, columns), bf16),
                pltpu.SemaphoreType.DMA((ranks // 2,)),
            ],
            flops=flops // 2,
            aliases={2: 0} if extra else {},
        )

    weight_grad, finished = weight_part(0, sums[0][0])
    for chunk in (1, 0):
        near = chunk * zs // 2
        parts_z = call(
            functools.partial(corner_kernel, ranks - 1),
            (table if chunk else finished, *sums[chunk]),
            [ANY] + [VMEM] * ranks,
            tuple(shape((CAP, width), bf16 if near + z else f32) for z in range(zs // 2)),
            (VMEM,) * (zs // 2),
        )
        for z, value in enumerate(parts_z):
            ends[near + z] = send(value, z=near + z) if near + z else value
    weight_grad, last = weight_part(ranks // 2, parts_z[0], weight_grad, info, table, stats)
    hidden_grad, loss = call(
        unpack_kernel,
        (last, chosen, *ends),
        [VMEM] * (2 + len(ends)),
        (shape((tokens, width), bf16), shape((1, 1), f32)),
        (VMEM, SMEM),
    )
    return loss[0, 0], hidden_grad, weight_grad


def solution(mesh):
    return jax.shard_map(
        functools.partial(body, mesh.shape["dp"], mesh.shape["vocab"]),
        mesh=mesh,
        in_specs=(P("dp", "vocab"), P(None, AXES), P("dp"), P("dp"), P("dp"), P()),
        out_specs=(P(), P("dp", "vocab"), P(None, AXES)),
        check_vma=False,
    )
```

```python
import functools
import math

import jax
import jax.numpy as jnp
from jax import lax
from jax.experimental import pallas as pl
from jax.experimental.pallas import tpu as pltpu
from jax.sharding import PartitionSpec as P

CAP = 32
MOST_VMEM = 56 * 1024 * 1024
IDS = 128
grad_scale = 16384.0
AXES = ("dp", "vocab")
SMEM = pl.BlockSpec(memory_space=pltpu.SMEM)
VMEM = pl.BlockSpec(memory_space=pltpu.VMEM)
HBM = pl.BlockSpec(memory_space=pltpu.HBM)
ANY = pl.BlockSpec(memory_space=pl.ANY)


def size_of(value):
    return math.prod(value.shape) * jnp.dtype(value.dtype).itemsize


def call(kernel, operands, in_specs, out_shape, out_specs, scratch=(), spare=4, flops=0, aliases={}):
    outs = jax.tree.leaves(out_shape)
    sized = [v for v, s in zip(operands, in_specs) if s is VMEM]
    sized += [v for v, s in zip(outs, jax.tree.leaves(out_specs)) if s is VMEM]
    held = [s for s in scratch if getattr(s, "memory_space", None) == pltpu.VMEM]
    total = sum(size_of(v) for v in sized) + sum(size_of(s) for s in held)
    return pl.pallas_call(
        kernel,
        out_shape=out_shape,
        in_specs=in_specs,
        out_specs=out_specs,
        scratch_shapes=scratch,
        input_output_aliases=aliases,
        compiler_params=pltpu.CompilerParams(vmem_limit_bytes=min(total + spare * 1024 * 1024, MOST_VMEM)),
        cost_estimate=pl.CostEstimate(
            flops=flops,
            bytes_accessed=sum(size_of(v) for v in list(operands) + outs),
            transcendentals=0,
        ),
    )(*operands)


def in_hbm(value):
    return pltpu.with_memory_space_constraint(value, pltpu.HBM)


def coordinates():
    group, rank = lax.axis_index("dp"), lax.axis_index("vocab")
    groups, ranks = lax.axis_size("dp"), lax.axis_size("vocab")
    position = group % 2 * (groups // 2) + group // 2
    return rank, position, group * ranks + rank


def choose(mask):
    tokens = mask.shape[1]
    wide = jnp.broadcast_to(mask.astype(jnp.float32), (8, tokens))
    before = lax.broadcasted_iota(jnp.int32, (tokens, tokens), 0)
    after = lax.broadcasted_iota(jnp.int32, (tokens, tokens), 1)
    upto = (before <= after).astype(jnp.float32)
    slot = jnp.dot(
        wide.astype(jnp.bfloat16), upto.astype(jnp.bfloat16), preferred_element_type=jnp.float32
    )[0:1]
    grid = lax.broadcasted_iota(jnp.int32, (CAP, tokens), 0) + 1
    return (slot.astype(jnp.int32) == grid) & (mask == 1)


def pack_kernel(hidden_hbm, mask_hbm, target_hbm, turn_hbm, rows, plain, chosen_out, *scratch):
    hidden, mask, target, turn, sems = scratch
    copies = []
    for place, (source, held) in enumerate(
        ((mask_hbm, mask), (target_hbm, target), (turn_hbm, turn), (hidden_hbm, hidden))
    ):
        copy = pltpu.make_async_copy(source, held, sems.at[place])
        copy.start()
        copies.append(copy)
    for copy in copies[:3]:
        copy.wait()
    width = hidden.shape[1]
    chosen = choose(mask[...])
    one_hot = chosen.astype(jnp.float32).astype(jnp.bfloat16)
    chosen_out[...] = one_hot
    turns, targets = turn[...], target[...]
    fields = (
        mask[...],
        turns & 255,
        turns >> 8,
        targets & 255,
        (targets >> 8) & 255,
        targets >> 16,
    )
    lane = lax.broadcasted_iota(jnp.int32, (CAP, IDS), 1)
    table = jnp.zeros((CAP, IDS), jnp.float32)
    for place, field in enumerate(fields):
        picked = jnp.where(chosen, field.astype(jnp.float32), 0.0)
        table = jnp.where(lane == place, jnp.sum(picked, axis=1, keepdims=True), table)
    rows[:, width:] = table.astype(jnp.bfloat16)
    copies[3].wait()
    packed = jnp.dot(one_hot, hidden[...], preferred_element_type=jnp.float32)
    packed = packed.astype(jnp.bfloat16)
    rows[:, :width] = packed
    plain[...] = packed


def join_kernel(order, *refs):
    blocks, (line, plain, far) = refs[:len(order) - 1] + refs[-4:-3], refs[-3:]
    width = plain.shape[1]
    for place, block in zip(order, blocks):
        rows = slice(place * CAP, (place + 1) * CAP)
        line[rows] = block[...]
        plain[rows] = block[:, :width]
        if place:
            far[(place - 1) * CAP:place * CAP] = block[:, :width]


def stage_kernel(blocks, line, weight, held, away, same, sems):
    rank = coordinates()[0]
    width = weight.shape[0] // blocks
    copies = []
    for block in list(range(1, blocks, 2)) + list(range(0, blocks, 2)):
        start = pl.multiple_of((rank ^ block) * width, width)
        targets = [held.at[pl.ds(start, width)]]
        if block % 2:
            targets.append(away.at[pl.ds(block // 2 * width, width)])
        for target in targets:
            copy = pltpu.make_async_copy(
                weight.at[pl.ds(start, width)], target, sems.at[len(copies)]
            )
            copy.start()
            copies.append(copy)
    same[...] = line[...]
    for copy in copies:
        copy.wait()


def gate_kernel(value, after, same):
    pass


def info_kernel(*refs):
    advantages, info = refs[-2:]
    start = refs[0].shape[1] - IDS
    table = jnp.concatenate([ref[:, start:] for ref in refs[:-2]], axis=0).astype(jnp.float32)
    valid = table[:, 0:1]
    turn = table[:, 1:2] + 256.0 * table[:, 2:3]
    target = table[:, 3:4] + 256.0 * table[:, 4:5] + 65536.0 * table[:, 5:6]
    turns = advantages.shape[1]
    spot = lax.broadcasted_iota(jnp.int32, (table.shape[0], turns), 1)
    gain = jnp.sum(
        jnp.where(spot == turn.astype(jnp.int32), advantages[...], 0.0), axis=1, keepdims=True
    )
    weight = valid * gain / jnp.sum(valid)
    lane = lax.broadcasted_iota(jnp.int32, info.shape, 1)
    info[...] = jnp.where(lane == 0, weight, jnp.where(lane == 1, target, 0.0))


def reorder(stats, position, groups):
    lanes = stats.shape[1]
    lane = lax.broadcasted_iota(jnp.int32, stats.shape, 1)
    bit = 1
    while bit < groups:
        size = CAP * bit
        swapped = jnp.where(
            (lane & size) != 0,
            pltpu.roll(stats, size, 1),
            pltpu.roll(stats, lanes - size, 1),
        )
        stats = jnp.where((position & bit) != 0, swapped, stats)
        bit *= 2
    return stats


def all_rows(pieces, counts, place, width):
    start = sum(counts[:place])
    return jnp.concatenate([ref[:, :width] for ref in pieces[start:start + counts[place]]], axis=0)


def some_logits(counts, first, pieces, weight):
    blocks = 2 * len(counts)
    width = weight.shape[0] // blocks
    rank, total = coordinates()[0], None
    for place, block in enumerate(range(first, blocks, 2)):
        start = pl.multiple_of((rank ^ block) * width, width)
        part = jnp.dot(
            all_rows(pieces, counts, place, width),
            weight[pl.ds(start, width), :],
            preferred_element_type=jnp.float32,
        )
        total = part if total is None else total + part
    return total


def first_kernel(counts, weight, *refs):
    refs[-1][...] = some_logits(counts, 0, refs[:-1], weight)


def logits_kernel(counts, groups, info, partial, weight, *refs):
    pieces, (logits, stats) = refs[:-2], refs[-2:]
    _, position, shard = coordinates()
    total = partial[...] + some_logits(counts, 1, pieces, weight)
    logits[...] = total
    height, columns = total.shape
    target = info[:, 1:2].astype(jnp.int32) - shard * columns
    column = lax.broadcasted_iota(jnp.int32, total.shape, 1)
    hit = jnp.sum(jnp.where(column == target, total, 0.0), axis=1, keepdims=True)
    hit = jnp.sum(hit * info[:, 0:1])
    peak = jnp.max(total, axis=1, keepdims=True)
    mass = jnp.sum(jnp.exp(total - peak), axis=1, keepdims=True)
    lane = lax.broadcasted_iota(jnp.int32, (height, 128), 1)
    table = jnp.where(lane == 0, peak, jnp.where(lane == 1, mass, hit))
    table = reorder(jnp.transpose(table)[0:8], position, groups)
    line = jnp.concatenate([table[0:1], table[1:2], table[2:3, :128]], axis=1)
    stats[...] = jnp.broadcast_to(line[None], stats.shape)


def log_totals(groups, stats, height):
    peaks, masses = stats[:, :, :height], stats[:, :, height:2 * height]
    peak = jnp.max(peaks, axis=0)
    mass = jnp.sum(masses * jnp.exp(peaks - peak[None]), axis=0)
    line = jnp.broadcast_to(peak + jnp.log(mass), (8, height))
    line = reorder(line, coordinates()[1], groups)
    return jnp.transpose(jnp.concatenate([line] * 16, axis=0))


def grad_kernel(order, groups, info, mine, theirs, weight, other_weight, stats, *refs):
    logit_grad, table, outs = refs[0], refs[1], refs[2:]
    chunks = (outs[len(order):], outs[:len(order)])
    rank, _, shard = coordinates()
    height, columns = mine.shape
    part = height // 4
    table[...] = log_totals(groups, stats, height)
    log_total = table[:, 0:1]
    row_weight, target = info[:, 0:1], info[:, 1:2].astype(jnp.int32)

    def grad_of(logits, shard):
        column = lax.broadcasted_iota(jnp.int32, (height, columns), 1) + shard * columns
        probability = jnp.exp(logits[...] - log_total)
        return (
            grad_scale * row_weight * (probability - (column == target).astype(jnp.float32))
        ).astype(jnp.bfloat16)

    grad = grad_of(mine, shard)
    logit_grad[...] = grad
    grads = (grad, grad_of(theirs, shard ^ 1))
    width = outs[0].shape[1]
    for x in range(len(order) // 2):
        start = pl.multiple_of((rank ^ 2 * x) * width, width)
        weights = (weight[pl.ds(start, width), :], other_weight[x * width:(x + 1) * width, :])
        total = sum(
            lax.dot_general(g, w, (((1,), (1,)), ((), ())), preferred_element_type=jnp.float32)
            for g, w in zip(grads, weights)
        )
        for quarter in range(4):
            out = chunks[quarter % 2][order.index(2 * x + quarter // 2)]
            out[...] = total[quarter * part:(quarter + 1) * part].astype(out.dtype)


def weight_kernel(blocks, counts, skipped, after, logit_grad, *refs):
    pieces, (out, last, done, sems) = refs[skipped:-4], refs[-4:]
    rank = coordinates()[0]
    width = done.shape[0] // len(blocks)
    copies = []
    for place, block in enumerate(blocks):
        done[place * width:(place + 1) * width] = lax.dot_general(
            all_rows(pieces, counts, place, width),
            logit_grad[...],
            (((0,), (0,)), ((), ())),
            preferred_element_type=jnp.float32,
        ).astype(jnp.bfloat16)
        start = pl.multiple_of((rank ^ block) * width, width)
        copy = pltpu.make_async_copy(
            done.at[pl.ds(place * width, width)], out.at[pl.ds(start, width)], sems.at[place]
        )
        copy.start()
        copies.append(copy)
    if skipped:
        info, table, stats = refs[1:4]
        hits = jnp.sum(stats[:, :, 2 * info.shape[0]:], axis=0)
        loss = jnp.sum(info[:, 0:1] * table[:, 0:1]) - hits[0, 0]
        last[...] = jnp.full(last.shape, loss, jnp.float32)
    else:
        last[...] = jnp.zeros_like(last)
    for copy in copies:
        copy.wait()


def corner_kernel(count, after, kept, *refs):
    total = kept[...]
    for ref in refs[:count]:
        total = total + ref[...].astype(jnp.float32)
    for place, out in enumerate(refs[count:]):
        out[...] = total[place * CAP:(place + 1) * CAP].astype(out.dtype)


def unpack_kernel(last, chosen, *refs):
    out, loss = refs[-2:]
    loss[0, 0] = last[0, 0]
    total = sum(ref[...].astype(jnp.float32) for ref in refs[:-2])
    out[...] = lax.dot_general(
        chosen[...],
        total.astype(jnp.bfloat16),
        (((0,), (0,)), ((), ())),
        preferred_element_type=jnp.float32,
    ).astype(jnp.bfloat16)


def body(dps, ranks, hidden, weight, loss_mask, target_ids, turn_ids, advantages):
    tokens, width = hidden.shape
    depth, columns = weight.shape
    zs, xs = dps // 2, ranks // 2
    total_rows = dps * CAP
    bf16, f32, i32 = jnp.bfloat16, jnp.float32, jnp.int32
    shape = jax.ShapeDtypeStruct
    flops = 2 * total_rows * depth * columns

    def send(value, z=0, y=0, x=0, core=0):
        far, near = 2 * z + y, 2 * x + core
        pairs = [
            (d * ranks + v, (d ^ far) * ranks + (v ^ near))
            for d in range(dps)
            for v in range(ranks)
        ]
        return lax.ppermute(value, AXES, pairs)

    packed, own, chosen = call(
        pack_kernel,
        (
            in_hbm(hidden),
            in_hbm(loss_mask.reshape(1, tokens)),
            in_hbm(target_ids.reshape(1, tokens)),
            in_hbm(turn_ids.reshape(1, tokens)),
        ),
        [HBM] * 4,
        (
            shape((CAP, width + IDS), bf16),
            shape((CAP, width), bf16),
            shape((CAP, tokens), bf16),
        ),
        (VMEM,) * 3,
        [pltpu.VMEM((tokens, width), bf16)]
        + [pltpu.VMEM((1, tokens), i32)] * 3
        + [pltpu.SemaphoreType.DMA((4,))],
    )

    line_order = [0, *range(2, zs), 1]
    blocks = [send(packed, z=z) if z else packed for z in line_order[:-1]]
    corners = {x: send(own, y=1, x=x) for x in range(1, xs)}
    blocks.append(send(packed, z=1))
    line_rows = zs * CAP
    line, line_plain, far = call(
        functools.partial(join_kernel, line_order),
        (*blocks[:-1], *corners.values(), blocks[-1]),
        [VMEM] * (zs - 1) + [ANY] * len(corners) + [VMEM],
        (
            shape((line_rows, width + IDS), bf16),
            shape((line_rows, width), bf16),
            shape((line_rows - CAP, width), bf16),
        ),
        (VMEM,) * 3,
    )
    pieces = {(0, 1, 0): send(line, y=1)}
    for x in range(1, xs):
        pieces[2 * x, 0, 0] = send(line_plain, x=x)
        pieces[2 * x, 1, 0] = corners[x]
        pieces[2 * x, 1, 1] = send(far, y=1, x=x)
    held, away, same = call(
        functools.partial(stage_kernel, ranks),
        (line, in_hbm(weight)),
        [VMEM, HBM],
        (
            shape((depth, columns), bf16),
            shape((depth // 2, columns), bf16),
            shape(line.shape, bf16),
        ),
        (VMEM,) * 3,
        [pltpu.SemaphoreType.DMA((ranks + xs,))],
    )
    pieces[0, 0, 0] = same
    for b, y, part in list(pieces):
        pieces[b + 1, y, part] = send(pieces[b, y, part], core=1)
    parted = [[pieces[key] for key in sorted(pieces) if key[0] == b] for b in range(ranks)]

    def rows_of(blocks):
        return [piece for b in blocks for piece in parted[b]]

    def counts_of(blocks):
        return [len(parted[b]) for b in blocks]

    info = call(
        info_kernel,
        (*parted[0], advantages.reshape(1, -1)),
        [VMEM] * (1 + len(parted[0])),
        shape((total_rows, 128), f32),
        VMEM,
    )
    near = range(0, ranks, 2)
    partial = call(
        functools.partial(first_kernel, counts_of(near)),
        (held, *rows_of(near)),
        [VMEM] * (1 + sum(counts_of(near))),
        shape((total_rows, columns), f32),
        VMEM,
        flops=flops // 2,
    )
    beside = range(1, ranks, 2)
    logits, stats = call(
        functools.partial(logits_kernel, counts_of(beside), dps),
        (info, partial, held, *rows_of(beside)),
        [VMEM] * (3 + sum(counts_of(beside))),
        (
            shape((total_rows, columns), f32),
            shape((dps * ranks, 1, 2 * total_rows + 128), f32),
        ),
        (VMEM, VMEM),
        flops=flops // 2,
    )
    other_logits = send(logits, core=1)
    away = call(
        gate_kernel, (away, stats), [ANY, ANY], shape(away.shape, bf16), ANY, aliases={0: 0}
    )
    other_held = send(away, core=1)
    stats = lax.all_to_all(stats, AXES, 0, 0)
    rows_part = total_rows // 4
    order = sorted(range(1, ranks), key=lambda place: (place % 2 + (place > 1), place)) + [0]
    outs = (shape((rows_part, width), bf16),) * (ranks - 1) + (shape((rows_part, width), f32),)
    logit_grad, table, *going = call(
        functools.partial(grad_kernel, order, dps),
        (info, logits, other_logits, held, other_held, stats),
        [VMEM] * 6,
        (shape((total_rows, columns), bf16), shape((total_rows, 128), f32)) + outs * 2,
        (VMEM,) * (2 + 2 * ranks),
        flops=flops,
    )
    ends, sums = [None] * zs, [None, None]
    for chunk in (1, 0):
        *values, corner = going[(1 - chunk) * ranks:(2 - chunk) * ranks]
        sums[chunk] = [corner]
        for place, value in zip(order, values):
            sums[chunk].append(send(value, y=place % 2, x=place // 2))

    def weight_part(first, after, *extra):
        blocks = range(first, first + ranks // 2)
        chosen_rows = rows_of(blocks)
        return call(
            functools.partial(weight_kernel, blocks, counts_of(blocks), len(extra)),
            (after, logit_grad, *extra, *chosen_rows),
            [ANY, VMEM] + [HBM] * (len(extra) > 0)
            + [VMEM] * (max(len(extra) - 1, 0) + len(chosen_rows)),
            (shape((depth, columns), bf16), shape((8, 128), f32)),
            (HBM, VMEM),
            [
                pltpu.VMEM((depth // 2, columns), bf16),
                pltpu.SemaphoreType.DMA((ranks // 2,)),
            ],
            flops=flops // 2,
            aliases={2: 0} if extra else {},
        )

    weight_grad, finished = weight_part(0, sums[0][0])
    for chunk in (1, 0):
        near = chunk * zs // 2
        parts_z = call(
            functools.partial(corner_kernel, ranks - 1),
            (table if chunk else finished, *sums[chunk]),
            [ANY] + [VMEM] * ranks,
            tuple(shape((CAP, width), bf16 if near + z else f32) for z in range(zs // 2)),
            (VMEM,) * (zs // 2),
        )
        for z, value in enumerate(parts_z):
            ends[near + z] = send(value, z=near + z) if near + z else value
    weight_grad, last = weight_part(ranks // 2, parts_z[0], weight_grad, info, table, stats)
    hidden_grad, loss = call(
        unpack_kernel,
        (last, chosen, *ends),
        [VMEM] * (2 + len(ends)),
        (shape((tokens, width), bf16), shape((1, 1), f32)),
        (VMEM, SMEM),
    )
    return loss[0, 0], hidden_grad, weight_grad


def solution(mesh):
    return jax.shard_map(
        functools.partial(body, mesh.shape["dp"], mesh.shape["vocab"]),
        mesh=mesh,
        in_specs=(P("dp", "vocab"), P(None, AXES), P("dp"), P("dp"), P("dp"), P()),
        out_specs=(P(), P("dp", "vocab"), P(None, AXES)),
        check_vma=False,
    )
```

```python
import functools
import math

import jax
import jax.numpy as jnp
from jax import lax
from jax.experimental import pallas as pl
from jax.experimental.pallas import tpu as pltpu
from jax.sharding import PartitionSpec as P

CAP = 32
MOST_VMEM = 56 * 1024 * 1024
IDS = 128
LANES = 128
grad_scale = 16384.0
AXES = ("dp", "vocab")
SMEM = pl.BlockSpec(memory_space=pltpu.SMEM)
VMEM = pl.BlockSpec(memory_space=pltpu.VMEM)
HBM = pl.BlockSpec(memory_space=pltpu.HBM)
ANY = pl.BlockSpec(memory_space=pl.ANY)


def size_of(value):
    return math.prod(value.shape) * jnp.dtype(value.dtype).itemsize


def call(kernel, operands, in_specs, out_shape, out_specs, scratch=(), spare=4, flops=0, aliases={}):
    outs = jax.tree.leaves(out_shape)
    sized = [v for v, s in zip(operands, in_specs) if s is VMEM]
    sized += [v for v, s in zip(outs, jax.tree.leaves(out_specs)) if s is VMEM]
    held = [s for s in scratch if getattr(s, "memory_space", None) == pltpu.VMEM]
    total = sum(size_of(v) for v in sized) + sum(size_of(s) for s in held)
    return pl.pallas_call(
        kernel,
        out_shape=out_shape,
        in_specs=in_specs,
        out_specs=out_specs,
        scratch_shapes=scratch,
        input_output_aliases=aliases,
        compiler_params=pltpu.CompilerParams(vmem_limit_bytes=min(total + spare * 1024 * 1024, MOST_VMEM)),
        cost_estimate=pl.CostEstimate(
            flops=flops,
            bytes_accessed=sum(size_of(v) for v in list(operands) + outs),
            transcendentals=0,
        ),
    )(*operands)


def in_hbm(value):
    return pltpu.with_memory_space_constraint(value, pltpu.HBM)


def coordinates():
    group, rank = lax.axis_index("dp"), lax.axis_index("vocab")
    groups, ranks = lax.axis_size("dp"), lax.axis_size("vocab")
    position = group % 2 * (groups // 2) + group // 2
    return rank, position, group * ranks + rank


def choose(mask):
    tokens = mask.shape[1]
    wide = jnp.broadcast_to(mask.astype(jnp.float32), (8, tokens))
    before = lax.broadcasted_iota(jnp.int32, (tokens, tokens), 0)
    after = lax.broadcasted_iota(jnp.int32, (tokens, tokens), 1)
    upto = (before <= after).astype(jnp.float32)
    slot = jnp.dot(
        wide.astype(jnp.bfloat16), upto.astype(jnp.bfloat16), preferred_element_type=jnp.float32
    )[0:1]
    grid = lax.broadcasted_iota(jnp.int32, (CAP, tokens), 0) + 1
    return (slot.astype(jnp.int32) == grid) & (mask == 1)


def pack_kernel(hidden_hbm, mask_hbm, target_hbm, turn_hbm, rows, plain, chosen_out, *scratch):
    hidden, mask, target, turn, sems = scratch
    copies = []
    for place, (source, held) in enumerate(
        ((mask_hbm, mask), (target_hbm, target), (turn_hbm, turn), (hidden_hbm, hidden))
    ):
        copy = pltpu.make_async_copy(source, held, sems.at[place])
        copy.start()
        copies.append(copy)
    for copy in copies[:3]:
        copy.wait()
    width = hidden.shape[1]
    chosen = choose(mask[...])
    one_hot = chosen.astype(jnp.float32).astype(jnp.bfloat16)
    chosen_out[...] = one_hot
    turns, targets = turn[...], target[...]
    fields = (
        mask[...],
        turns & 255,
        turns >> 8,
        targets & 255,
        (targets >> 8) & 255,
        targets >> 16,
    )
    lane = lax.broadcasted_iota(jnp.int32, (CAP, IDS), 1)
    table = jnp.zeros((CAP, IDS), jnp.float32)
    for place, field in enumerate(fields):
        picked = jnp.where(chosen, field.astype(jnp.float32), 0.0)
        table = jnp.where(lane == place, jnp.sum(picked, axis=1, keepdims=True), table)
    rows[:, width:] = table.astype(jnp.bfloat16)
    copies[3].wait()
    packed = jnp.dot(one_hot, hidden[...], preferred_element_type=jnp.float32)
    packed = packed.astype(jnp.bfloat16)
    rows[:, :width] = packed
    plain[...] = packed


def join_kernel(order, *refs):
    blocks, (line, plain, far) = refs[:len(order) - 1] + refs[-4:-3], refs[-3:]
    width = plain.shape[1]
    for place, block in zip(order, blocks):
        rows = slice(place * CAP, (place + 1) * CAP)
        line[rows] = block[...]
        plain[rows] = block[:, :width]
        if place:
            far[(place - 1) * CAP:place * CAP] = block[:, :width]


def stage_kernel(blocks, line, weight, held, away, same, sems):
    rank = coordinates()[0]
    width = weight.shape[0] // blocks
    copies = []
    for block in list(range(1, blocks, 2)) + list(range(0, blocks, 2)):
        start = pl.multiple_of((rank ^ block) * width, width)
        targets = [held.at[pl.ds(start, width)]]
        if block % 2:
            targets.append(away.at[pl.ds(block // 2 * width, width)])
        for target in targets:
            copy = pltpu.make_async_copy(
                weight.at[pl.ds(start, width)], target, sems.at[len(copies)]
            )
            copy.start()
            copies.append(copy)
    same[...] = line[...]
    for copy in copies:
        copy.wait()


def gate_kernel(value, after, same):
    pass


def info_kernel(*refs):
    advantages, info = refs[-2:]
    start = refs[0].shape[1] - IDS
    table = jnp.concatenate([ref[:, start:] for ref in refs[:-2]], axis=0).astype(jnp.float32)
    valid = table[:, 0:1]
    turn = table[:, 1:2] + 256.0 * table[:, 2:3]
    target = table[:, 3:4] + 256.0 * table[:, 4:5] + 65536.0 * table[:, 5:6]
    turns = advantages.shape[1]
    spot = lax.broadcasted_iota(jnp.int32, (table.shape[0], turns), 1)
    gain = jnp.sum(
        jnp.where(spot == turn.astype(jnp.int32), advantages[...], 0.0), axis=1, keepdims=True
    )
    weight = valid * gain / jnp.sum(valid)
    lane = lax.broadcasted_iota(jnp.int32, info.shape, 1)
    info[...] = jnp.where(lane == 0, weight, jnp.where(lane == 1, target, 0.0))


def reorder(stats, position, groups):
    lanes = stats.shape[1]
    lane = lax.broadcasted_iota(jnp.int32, stats.shape, 1)
    bit = 1
    while bit < groups:
        size = CAP * bit
        swapped = jnp.where(
            (lane & size) != 0,
            pltpu.roll(stats, size, 1),
            pltpu.roll(stats, lanes - size, 1),
        )
        stats = jnp.where((position & bit) != 0, swapped, stats)
        bit *= 2
    return stats


def all_rows(pieces, counts, place, width):
    start = sum(counts[:place])
    return jnp.concatenate([ref[:, :width] for ref in pieces[start:start + counts[place]]], axis=0)


def some_logits(counts, first, pieces, weight):
    blocks = 2 * len(counts)
    width = weight.shape[0] // blocks
    rank, total = coordinates()[0], None
    for place, block in enumerate(range(first, blocks, 2)):
        start = pl.multiple_of((rank ^ block) * width, width)
        part = jnp.dot(
            all_rows(pieces, counts, place, width),
            weight[pl.ds(start, width), :],
            preferred_element_type=jnp.float32,
        )
        total = part if total is None else total + part
    return total


def first_kernel(counts, weight, *refs):
    refs[-1][...] = some_logits(counts, 0, refs[:-1], weight)


def logits_kernel(counts, groups, info, partial, weight, *refs):
    pieces, (logits, stats) = refs[:-2], refs[-2:]
    _, position, shard = coordinates()
    total = partial[...] + some_logits(counts, 1, pieces, weight)
    logits[...] = total
    height, columns = total.shape
    target = info[:, 1:2].astype(jnp.int32) - shard * columns
    column = lax.broadcasted_iota(jnp.int32, total.shape, 1)
    hit = jnp.sum(jnp.where(column == target, total, 0.0), axis=1, keepdims=True)
    hit = jnp.sum(hit * info[:, 0:1])
    peak = jnp.max(total, axis=1, keepdims=True)
    mass = jnp.sum(jnp.exp(total - peak), axis=1, keepdims=True)
    lane = lax.broadcasted_iota(jnp.int32, (height, 128), 1)
    table = jnp.where(lane == 0, peak, jnp.where(lane == 1, mass, hit))
    table = reorder(jnp.transpose(table)[0:8], position, groups)
    lines = [
        table[row:row + 1, start:start + LANES]
        for row in range(2)
        for start in range(0, height, LANES)
    ]
    lines.append(table[2:3, :LANES])
    lines += [jnp.zeros_like(lines[0])] * (stats.shape[1] - len(lines))
    stats[...] = jnp.broadcast_to(jnp.concatenate(lines, axis=0)[None], stats.shape)


def log_totals(groups, stats, height):
    count = height // LANES
    peaks, masses = stats[:, :count, :], stats[:, count:2 * count, :]
    peak = jnp.max(peaks, axis=0)
    mass = jnp.sum(masses * jnp.exp(peaks - peak[None]), axis=0)
    total = peak + jnp.log(mass)
    line = jnp.concatenate([total[row:row + 1] for row in range(count)], axis=1)
    line = reorder(jnp.broadcast_to(line, (8, height)), coordinates()[1], groups)
    return jnp.transpose(jnp.concatenate([line] * 16, axis=0))


def grad_kernel(order, groups, info, mine, theirs, weight, other_weight, stats, *refs):
    logit_grad, table, outs = refs[0], refs[1], refs[2:]
    chunks = (outs[len(order):], outs[:len(order)])
    rank, _, shard = coordinates()
    height, columns = mine.shape
    part = height // 4
    table[...] = log_totals(groups, stats, height)
    log_total = table[:, 0:1]
    row_weight, target = info[:, 0:1], info[:, 1:2].astype(jnp.int32)

    def grad_of(logits, shard):
        column = lax.broadcasted_iota(jnp.int32, (height, columns), 1) + shard * columns
        probability = jnp.exp(logits[...] - log_total)
        return (
            grad_scale * row_weight * (probability - (column == target).astype(jnp.float32))
        ).astype(jnp.bfloat16)

    grad = grad_of(mine, shard)
    logit_grad[...] = grad
    grads = (grad, grad_of(theirs, shard ^ 1))
    width = outs[0].shape[1]
    for x in range(len(order) // 2):
        start = pl.multiple_of((rank ^ 2 * x) * width, width)
        weights = (weight[pl.ds(start, width), :], other_weight[x * width:(x + 1) * width, :])
        total = sum(
            lax.dot_general(g, w, (((1,), (1,)), ((), ())), preferred_element_type=jnp.float32)
            for g, w in zip(grads, weights)
        )
        for quarter in range(4):
            out = chunks[quarter % 2][order.index(2 * x + quarter // 2)]
            out[...] = total[quarter * part:(quarter + 1) * part].astype(out.dtype)


def weight_kernel(blocks, counts, skipped, after, logit_grad, *refs):
    pieces, (out, last, done, sems) = refs[skipped:-4], refs[-4:]
    rank = coordinates()[0]
    width = done.shape[0] // len(blocks)
    copies = []
    for place, block in enumerate(blocks):
        done[place * width:(place + 1) * width] = lax.dot_general(
            all_rows(pieces, counts, place, width),
            logit_grad[...],
            (((0,), (0,)), ((), ())),
            preferred_element_type=jnp.float32,
        ).astype(jnp.bfloat16)
        start = pl.multiple_of((rank ^ block) * width, width)
        copy = pltpu.make_async_copy(
            done.at[pl.ds(place * width, width)], out.at[pl.ds(start, width)], sems.at[place]
        )
        copy.start()
        copies.append(copy)
    if skipped:
        info, table, stats = refs[1:4]
        first = 2 * info.shape[0] // LANES
        hits = jnp.sum(stats[:, first:first + 1, :], axis=0)
        loss = jnp.sum(info[:, 0:1] * table[:, 0:1]) - hits[0, 0]
        last[...] = jnp.full(last.shape, loss, jnp.float32)
    else:
        last[...] = jnp.zeros_like(last)
    for copy in copies:
        copy.wait()


def corner_kernel(count, after, kept, *refs):
    total = kept[...]
    for ref in refs[:count]:
        total = total + ref[...].astype(jnp.float32)
    for place, out in enumerate(refs[count:]):
        out[...] = total[place * CAP:(place + 1) * CAP].astype(out.dtype)


def unpack_kernel(last, chosen, *refs):
    out, loss = refs[-2:]
    loss[0, 0] = last[0, 0]
    total = sum(ref[...].astype(jnp.float32) for ref in refs[:-2])
    out[...] = lax.dot_general(
        chosen[...],
        total.astype(jnp.bfloat16),
        (((0,), (0,)), ((), ())),
        preferred_element_type=jnp.float32,
    ).astype(jnp.bfloat16)


def body(dps, ranks, hidden, weight, loss_mask, target_ids, turn_ids, advantages):
    tokens, width = hidden.shape
    depth, columns = weight.shape
    zs, xs = dps // 2, ranks // 2
    total_rows = dps * CAP
    bf16, f32, i32 = jnp.bfloat16, jnp.float32, jnp.int32
    shape = jax.ShapeDtypeStruct
    flops = 2 * total_rows * depth * columns

    def send(value, z=0, y=0, x=0, core=0):
        far, near = 2 * z + y, 2 * x + core
        pairs = [
            (d * ranks + v, (d ^ far) * ranks + (v ^ near))
            for d in range(dps)
            for v in range(ranks)
        ]
        return lax.ppermute(value, AXES, pairs)

    packed, own, chosen = call(
        pack_kernel,
        (
            in_hbm(hidden),
            in_hbm(loss_mask.reshape(1, tokens)),
            in_hbm(target_ids.reshape(1, tokens)),
            in_hbm(turn_ids.reshape(1, tokens)),
        ),
        [HBM] * 4,
        (
            shape((CAP, width + IDS), bf16),
            shape((CAP, width), bf16),
            shape((CAP, tokens), bf16),
        ),
        (VMEM,) * 3,
        [pltpu.VMEM((tokens, width), bf16)]
        + [pltpu.VMEM((1, tokens), i32)] * 3
        + [pltpu.SemaphoreType.DMA((4,))],
    )

    line_order = [0, *range(2, zs), 1]
    blocks = [send(packed, z=z) if z else packed for z in line_order[:-1]]
    corners = {x: send(own, y=1, x=x) for x in range(1, xs)}
    blocks.append(send(packed, z=1))
    line_rows = zs * CAP
    line, line_plain, far = call(
        functools.partial(join_kernel, line_order),
        (*blocks[:-1], *corners.values(), blocks[-1]),
        [VMEM] * (zs - 1) + [ANY] * len(corners) + [VMEM],
        (
            shape((line_rows, width + IDS), bf16),
            shape((line_rows, width), bf16),
            shape((line_rows - CAP, width), bf16),
        ),
        (VMEM,) * 3,
    )
    pieces = {(0, 1, 0): send(line, y=1)}
    for x in range(1, xs):
        pieces[2 * x, 0, 0] = send(line_plain, x=x)
        pieces[2 * x, 1, 0] = corners[x]
        pieces[2 * x, 1, 1] = send(far, y=1, x=x)
    held, away, same = call(
        functools.partial(stage_kernel, ranks),
        (line, in_hbm(weight)),
        [VMEM, HBM],
        (
            shape((depth, columns), bf16),
            shape((depth // 2, columns), bf16),
            shape(line.shape, bf16),
        ),
        (VMEM,) * 3,
        [pltpu.SemaphoreType.DMA((ranks + xs,))],
    )
    pieces[0, 0, 0] = same
    info = call(
        info_kernel,
        (same, pieces[0, 1, 0], advantages.reshape(1, -1)),
        [VMEM] * 3,
        shape((total_rows, 128), f32),
        VMEM,
    )

    def hold(value, after):
        like = shape(value.shape, value.dtype)
        return call(gate_kernel, (value, after), [ANY, ANY], like, ANY, aliases={0: 0})

    for x in range(1, xs):
        pieces[2 * x + 1, 1, 0] = send(pieces[2 * x, 1, 0], core=1)
        pieces[2 * x, 0, 0] = hold(pieces[2 * x, 0, 0], info)
        pieces[2 * x, 1, 1] = hold(pieces[2 * x, 1, 1], pieces[2 * x + 1, 1, 0])
    for b, y, part in list(pieces):
        if b % 2 == 0 and (b + 1, y, part) not in pieces:
            pieces[b + 1, y, part] = send(pieces[b, y, part], core=1)
    parted = [[pieces[key] for key in sorted(pieces) if key[0] == b] for b in range(ranks)]

    def rows_of(blocks):
        return [piece for b in blocks for piece in parted[b]]

    def counts_of(blocks):
        return [len(parted[b]) for b in blocks]

    near = range(0, ranks, 2)
    stat_rows = (2 * total_rows // LANES + 1 + 7) // 8 * 8
    partial = call(
        functools.partial(first_kernel, counts_of(near)),
        (held, *rows_of(near)),
        [VMEM] * (1 + sum(counts_of(near))),
        shape((total_rows, columns), f32),
        VMEM,
        flops=flops // 2,
    )
    beside = range(1, ranks, 2)
    logits, stats = call(
        functools.partial(logits_kernel, counts_of(beside), dps),
        (info, partial, held, *rows_of(beside)),
        [VMEM] * (3 + sum(counts_of(beside))),
        (
            shape((total_rows, columns), f32),
            shape((dps * ranks, stat_rows, LANES), f32),
        ),
        (VMEM, VMEM),
        flops=flops // 2,
    )
    other_logits = send(logits, core=1)
    other_held = send(hold(away, stats), core=1)
    stats = lax.all_to_all(stats, AXES, 0, 0)
    rows_part = total_rows // 4
    order = sorted(range(1, ranks), key=lambda place: (place % 2 + (place > 1), place)) + [0]
    outs = (shape((rows_part, width), bf16),) * (ranks - 1) + (shape((rows_part, width), f32),)
    logit_grad, table, *going = call(
        functools.partial(grad_kernel, order, dps),
        (info, logits, other_logits, held, other_held, stats),
        [VMEM] * 6,
        (shape((total_rows, columns), bf16), shape((total_rows, 128), f32)) + outs * 2,
        (VMEM,) * (2 + 2 * ranks),
        flops=flops,
    )
    ends, sums = [None] * zs, [None, None]
    for chunk in (1, 0):
        *values, corner = going[(1 - chunk) * ranks:(2 - chunk) * ranks]
        sums[chunk] = [corner]
        for place, value in zip(order, values):
            sums[chunk].append(send(value, y=place % 2, x=place // 2))

    def weight_part(first, after, *extra):
        blocks = range(first, first + ranks // 2)
        chosen_rows = rows_of(blocks)
        return call(
            functools.partial(weight_kernel, blocks, counts_of(blocks), len(extra)),
            (after, logit_grad, *extra, *chosen_rows),
            [ANY, VMEM] + [HBM] * (len(extra) > 0)
            + [VMEM] * (max(len(extra) - 1, 0) + len(chosen_rows)),
            (shape((depth, columns), bf16), shape((8, 128), f32)),
            (HBM, VMEM),
            [
                pltpu.VMEM((depth // 2, columns), bf16),
                pltpu.SemaphoreType.DMA((ranks // 2,)),
            ],
            flops=flops // 2,
            aliases={2: 0} if extra else {},
        )

    weight_grad, finished = weight_part(0, sums[0][0])
    for chunk in (1, 0):
        near = chunk * zs // 2
        parts_z = call(
            functools.partial(corner_kernel, ranks - 1),
            (table if chunk else finished, *sums[chunk]),
            [ANY] + [VMEM] * ranks,
            tuple(shape((CAP, width), bf16 if near + z else f32) for z in range(zs // 2)),
            (VMEM,) * (zs // 2),
        )
        for z, value in enumerate(parts_z):
            ends[near + z] = send(value, z=near + z) if near + z else value
    weight_grad, last = weight_part(ranks // 2, parts_z[0], weight_grad, info, table, stats)
    hidden_grad, loss = call(
        unpack_kernel,
        (last, chosen, *ends),
        [VMEM] * (2 + len(ends)),
        (shape((tokens, width), bf16), shape((1, 1), f32)),
        (VMEM, SMEM),
    )
    return loss[0, 0], hidden_grad, weight_grad


def solution(mesh):
    return jax.shard_map(
        functools.partial(body, mesh.shape["dp"], mesh.shape["vocab"]),
        mesh=mesh,
        in_specs=(P("dp", "vocab"), P(None, AXES), P("dp"), P("dp"), P("dp"), P()),
        out_specs=(P(), P("dp", "vocab"), P(None, AXES)),
        check_vma=False,
    )
```

```python
import functools
import math

import jax
import jax.numpy as jnp
from jax import lax
from jax.experimental import pallas as pl
from jax.experimental.pallas import tpu as pltpu
from jax.sharding import PartitionSpec as P

CAP = 32
MOST_VMEM = 56 * 1024 * 1024
IDS = 128
LANES = 128
grad_scale = 16384.0
AXES = ("dp", "vocab")
SMEM = pl.BlockSpec(memory_space=pltpu.SMEM)
VMEM = pl.BlockSpec(memory_space=pltpu.VMEM)
HBM = pl.BlockSpec(memory_space=pltpu.HBM)
ANY = pl.BlockSpec(memory_space=pl.ANY)


def size_of(value):
    return math.prod(value.shape) * jnp.dtype(value.dtype).itemsize


def call(kernel, operands, in_specs, out_shape, out_specs, scratch=(), spare=4, flops=0, aliases={}):
    outs = jax.tree.leaves(out_shape)
    sized = [v for v, s in zip(operands, in_specs) if s is VMEM]
    sized += [v for v, s in zip(outs, jax.tree.leaves(out_specs)) if s is VMEM]
    held = [s for s in scratch if getattr(s, "memory_space", None) == pltpu.VMEM]
    total = sum(size_of(v) for v in sized) + sum(size_of(s) for s in held)
    return pl.pallas_call(
        kernel,
        out_shape=out_shape,
        in_specs=in_specs,
        out_specs=out_specs,
        scratch_shapes=scratch,
        input_output_aliases=aliases,
        compiler_params=pltpu.CompilerParams(vmem_limit_bytes=min(total + spare * 1024 * 1024, MOST_VMEM)),
        cost_estimate=pl.CostEstimate(
            flops=flops,
            bytes_accessed=sum(size_of(v) for v in list(operands) + outs),
            transcendentals=0,
        ),
    )(*operands)


def in_hbm(value):
    return pltpu.with_memory_space_constraint(value, pltpu.HBM)


def coordinates():
    group, rank = lax.axis_index("dp"), lax.axis_index("vocab")
    groups, ranks = lax.axis_size("dp"), lax.axis_size("vocab")
    position = group % 2 * (groups // 2) + group // 2
    return rank, position, group * ranks + rank


def choose(mask):
    tokens = mask.shape[1]
    wide = jnp.broadcast_to(mask.astype(jnp.float32), (8, tokens))
    before = lax.broadcasted_iota(jnp.int32, (tokens, tokens), 0)
    after = lax.broadcasted_iota(jnp.int32, (tokens, tokens), 1)
    upto = (before <= after).astype(jnp.float32)
    slot = jnp.dot(
        wide.astype(jnp.bfloat16), upto.astype(jnp.bfloat16), preferred_element_type=jnp.float32
    )[0:1]
    grid = lax.broadcasted_iota(jnp.int32, (CAP, tokens), 0) + 1
    return (slot.astype(jnp.int32) == grid) & (mask == 1)


def pack_kernel(hidden_hbm, mask_hbm, target_hbm, turn_hbm, rows, plain, chosen_out, *scratch):
    hidden, mask, target, turn, sems = scratch
    copies = []
    for place, (source, held) in enumerate(
        ((mask_hbm, mask), (target_hbm, target), (turn_hbm, turn), (hidden_hbm, hidden))
    ):
        copy = pltpu.make_async_copy(source, held, sems.at[place])
        copy.start()
        copies.append(copy)
    for copy in copies[:3]:
        copy.wait()
    width = hidden.shape[1]
    chosen = choose(mask[...])
    one_hot = chosen.astype(jnp.float32).astype(jnp.bfloat16)
    chosen_out[...] = one_hot
    turns, targets = turn[...], target[...]
    fields = (
        mask[...],
        turns & 255,
        turns >> 8,
        targets & 255,
        (targets >> 8) & 255,
        targets >> 16,
    )
    lane = lax.broadcasted_iota(jnp.int32, (CAP, IDS), 1)
    table = jnp.zeros((CAP, IDS), jnp.float32)
    for place, field in enumerate(fields):
        picked = jnp.where(chosen, field.astype(jnp.float32), 0.0)
        table = jnp.where(lane == place, jnp.sum(picked, axis=1, keepdims=True), table)
    rows[:, width:] = table.astype(jnp.bfloat16)
    copies[3].wait()
    packed = jnp.dot(one_hot, hidden[...], preferred_element_type=jnp.float32)
    packed = packed.astype(jnp.bfloat16)
    rows[:, :width] = packed
    plain[...] = packed


def join_kernel(order, *refs):
    blocks, (line, plain, far) = refs[:len(order) - 1] + refs[-4:-3], refs[-3:]
    width = plain.shape[1]
    for place, block in zip(order, blocks):
        rows = slice(place * CAP, (place + 1) * CAP)
        line[rows] = block[...]
        plain[rows] = block[:, :width]
        if place:
            far[(place - 1) * CAP:place * CAP] = block[:, :width]


def stage_kernel(blocks, line, weight, held, away, same, sems):
    rank = coordinates()[0]
    width = weight.shape[0] // blocks
    copies = []
    for block in list(range(1, blocks, 2)) + list(range(0, blocks, 2)):
        start = pl.multiple_of((rank ^ block) * width, width)
        targets = [held.at[pl.ds(start, width)]]
        if block % 2:
            targets.append(away.at[pl.ds(block // 2 * width, width)])
        for target in targets:
            copy = pltpu.make_async_copy(
                weight.at[pl.ds(start, width)], target, sems.at[len(copies)]
            )
            copy.start()
            copies.append(copy)
    same[...] = line[...]
    for copy in copies:
        copy.wait()


def gate_kernel(value, after, same):
    pass


def info_kernel(*refs):
    advantages, info = refs[-2:]
    start = refs[0].shape[1] - IDS
    table = jnp.concatenate([ref[:, start:] for ref in refs[:-2]], axis=0).astype(jnp.float32)
    valid = table[:, 0:1]
    turn = table[:, 1:2] + 256.0 * table[:, 2:3]
    target = table[:, 3:4] + 256.0 * table[:, 4:5] + 65536.0 * table[:, 5:6]
    turns = advantages.shape[1]
    spot = lax.broadcasted_iota(jnp.int32, (table.shape[0], turns), 1)
    gain = jnp.sum(
        jnp.where(spot == turn.astype(jnp.int32), advantages[...], 0.0), axis=1, keepdims=True
    )
    weight = valid * gain / jnp.sum(valid)
    lane = lax.broadcasted_iota(jnp.int32, info.shape, 1)
    info[...] = jnp.where(lane == 0, weight, jnp.where(lane == 1, target, 0.0))


def reorder(stats, position, groups):
    lanes = stats.shape[1]
    lane = lax.broadcasted_iota(jnp.int32, stats.shape, 1)
    bit = 1
    while bit < groups:
        size = CAP * bit
        swapped = jnp.where(
            (lane & size) != 0,
            pltpu.roll(stats, size, 1),
            pltpu.roll(stats, lanes - size, 1),
        )
        stats = jnp.where((position & bit) != 0, swapped, stats)
        bit *= 2
    return stats


def all_rows(pieces, counts, place, width):
    start = sum(counts[:place])
    return jnp.concatenate([ref[:, :width] for ref in pieces[start:start + counts[place]]], axis=0)


def some_logits(counts, first, pieces, weight):
    blocks = 2 * len(counts)
    width = weight.shape[0] // blocks
    rank, total = coordinates()[0], None
    for place, block in enumerate(range(first, blocks, 2)):
        start = pl.multiple_of((rank ^ block) * width, width)
        part = jnp.dot(
            all_rows(pieces, counts, place, width),
            weight[pl.ds(start, width), :],
            preferred_element_type=jnp.float32,
        )
        total = part if total is None else total + part
    return total


def first_kernel(counts, weight, *refs):
    refs[-1][...] = some_logits(counts, 0, refs[:-1], weight)


def logits_kernel(counts, groups, info, partial, weight, *refs):
    pieces, (logits, stats) = refs[:-2], refs[-2:]
    _, position, shard = coordinates()
    total = partial[...] + some_logits(counts, 1, pieces, weight)
    logits[...] = total
    height, columns = total.shape
    target = info[:, 1:2].astype(jnp.int32) - shard * columns
    column = lax.broadcasted_iota(jnp.int32, total.shape, 1)
    hit = jnp.sum(jnp.where(column == target, total, 0.0), axis=1, keepdims=True)
    hit = jnp.sum(hit * info[:, 0:1])
    peak = jnp.max(total, axis=1, keepdims=True)
    mass = jnp.sum(jnp.exp(total - peak), axis=1, keepdims=True)
    lane = lax.broadcasted_iota(jnp.int32, (height, 128), 1)
    table = jnp.where(lane == 0, peak + jnp.log(mass), hit)
    table = reorder(jnp.transpose(table)[0:8], position, groups)
    line = jnp.concatenate([table[0:1], table[1:2, :LANES]], axis=1)
    stats[...] = jnp.broadcast_to(line[None], stats.shape)


def log_totals(groups, stats, height):
    parts = stats[:, :, :height]
    peak = jnp.max(parts, axis=0)
    line = peak + jnp.log(jnp.sum(jnp.exp(parts - peak[None]), axis=0))
    line = reorder(jnp.broadcast_to(line, (8, height)), coordinates()[1], groups)
    return jnp.transpose(jnp.concatenate([line] * 16, axis=0))


def grad_kernel(order, groups, info, mine, theirs, weight, other_weight, stats, *refs):
    logit_grad, table, outs = refs[0], refs[1], refs[2:]
    chunks = (outs[len(order):], outs[:len(order)])
    rank, _, shard = coordinates()
    height, columns = mine.shape
    part = height // 4
    table[...] = log_totals(groups, stats, height)
    log_total = table[:, 0:1]
    row_weight, target = info[:, 0:1], info[:, 1:2].astype(jnp.int32)

    def grad_of(logits, shard):
        column = lax.broadcasted_iota(jnp.int32, (height, columns), 1) + shard * columns
        probability = jnp.exp(logits[...] - log_total)
        return (
            grad_scale * row_weight * (probability - (column == target).astype(jnp.float32))
        ).astype(jnp.bfloat16)

    grad = grad_of(mine, shard)
    logit_grad[...] = grad
    grads = (grad, grad_of(theirs, shard ^ 1))
    width = outs[0].shape[1]
    for x in range(len(order) // 2):
        start = pl.multiple_of((rank ^ 2 * x) * width, width)
        weights = (weight[pl.ds(start, width), :], other_weight[x * width:(x + 1) * width, :])
        total = sum(
            lax.dot_general(g, w, (((1,), (1,)), ((), ())), preferred_element_type=jnp.float32)
            for g, w in zip(grads, weights)
        )
        for quarter in range(4):
            out = chunks[quarter % 2][order.index(2 * x + quarter // 2)]
            out[...] = total[quarter * part:(quarter + 1) * part].astype(out.dtype)


def weight_kernel(blocks, counts, skipped, after, logit_grad, *refs):
    pieces, (out, last, done, sems) = refs[skipped:-4], refs[-4:]
    rank = coordinates()[0]
    width = done.shape[0] // len(blocks)
    copies = []
    for place, block in enumerate(blocks):
        done[place * width:(place + 1) * width] = lax.dot_general(
            all_rows(pieces, counts, place, width),
            logit_grad[...],
            (((0,), (0,)), ((), ())),
            preferred_element_type=jnp.float32,
        ).astype(jnp.bfloat16)
        start = pl.multiple_of((rank ^ block) * width, width)
        copy = pltpu.make_async_copy(
            done.at[pl.ds(place * width, width)], out.at[pl.ds(start, width)], sems.at[place]
        )
        copy.start()
        copies.append(copy)
    if skipped:
        info, table, stats = refs[1:4]
        hits = jnp.sum(stats[:, :, info.shape[0]:], axis=0)
        loss = jnp.sum(info[:, 0:1] * table[:, 0:1]) - hits[0, 0]
        last[...] = jnp.full(last.shape, loss, jnp.float32)
    else:
        last[...] = jnp.zeros_like(last)
    for copy in copies:
        copy.wait()


def corner_kernel(count, after, kept, *refs):
    total = kept[...]
    for ref in refs[:count]:
        total = total + ref[...].astype(jnp.float32)
    for place, out in enumerate(refs[count:]):
        out[...] = total[place * CAP:(place + 1) * CAP].astype(out.dtype)


def unpack_kernel(last, chosen, *refs):
    out, loss = refs[-2:]
    loss[0, 0] = last[0, 0]
    total = sum(ref[...].astype(jnp.float32) for ref in refs[:-2])
    out[...] = lax.dot_general(
        chosen[...],
        total.astype(jnp.bfloat16),
        (((0,), (0,)), ((), ())),
        preferred_element_type=jnp.float32,
    ).astype(jnp.bfloat16)


def body(dps, ranks, hidden, weight, loss_mask, target_ids, turn_ids, advantages):
    tokens, width = hidden.shape
    depth, columns = weight.shape
    zs, xs = dps // 2, ranks // 2
    total_rows = dps * CAP
    bf16, f32, i32 = jnp.bfloat16, jnp.float32, jnp.int32
    shape = jax.ShapeDtypeStruct
    flops = 2 * total_rows * depth * columns

    def send(value, z=0, y=0, x=0, core=0):
        far, near = 2 * z + y, 2 * x + core
        pairs = [
            (d * ranks + v, (d ^ far) * ranks + (v ^ near))
            for d in range(dps)
            for v in range(ranks)
        ]
        return lax.ppermute(value, AXES, pairs)

    packed, own, chosen = call(
        pack_kernel,
        (
            in_hbm(hidden),
            in_hbm(loss_mask.reshape(1, tokens)),
            in_hbm(target_ids.reshape(1, tokens)),
            in_hbm(turn_ids.reshape(1, tokens)),
        ),
        [HBM] * 4,
        (
            shape((CAP, width + IDS), bf16),
            shape((CAP, width), bf16),
            shape((CAP, tokens), bf16),
        ),
        (VMEM,) * 3,
        [pltpu.VMEM((tokens, width), bf16)]
        + [pltpu.VMEM((1, tokens), i32)] * 3
        + [pltpu.SemaphoreType.DMA((4,))],
    )

    line_order = [0, *range(2, zs), 1]
    blocks = [send(packed, z=z) if z else packed for z in line_order[:-1]]
    corners = {x: send(own, y=1, x=x) for x in range(1, xs)}
    blocks.append(send(packed, z=1))
    line_rows = zs * CAP
    line, line_plain, far = call(
        functools.partial(join_kernel, line_order),
        (*blocks[:-1], *corners.values(), blocks[-1]),
        [VMEM] * (zs - 1) + [ANY] * len(corners) + [VMEM],
        (
            shape((line_rows, width + IDS), bf16),
            shape((line_rows, width), bf16),
            shape((line_rows - CAP, width), bf16),
        ),
        (VMEM,) * 3,
    )
    pieces = {(0, 1, 0): send(line, y=1)}
    for x in range(1, xs):
        pieces[2 * x, 0, 0] = send(line_plain, x=x)
        pieces[2 * x, 1, 0] = corners[x]
        pieces[2 * x, 1, 1] = send(far, y=1, x=x)
    held, away, same = call(
        functools.partial(stage_kernel, ranks),
        (line, in_hbm(weight)),
        [VMEM, HBM],
        (
            shape((depth, columns), bf16),
            shape((depth // 2, columns), bf16),
            shape(line.shape, bf16),
        ),
        (VMEM,) * 3,
        [pltpu.SemaphoreType.DMA((ranks + xs,))],
    )
    pieces[0, 0, 0] = same
    info = call(
        info_kernel,
        (same, pieces[0, 1, 0], advantages.reshape(1, -1)),
        [VMEM] * 3,
        shape((total_rows, 128), f32),
        VMEM,
    )

    def hold(value, after):
        like = shape(value.shape, value.dtype)
        return call(gate_kernel, (value, after), [ANY, ANY], like, ANY, aliases={0: 0})

    for x in range(1, xs):
        pieces[2 * x + 1, 1, 0] = send(pieces[2 * x, 1, 0], core=1)
        pieces[2 * x, 0, 0] = hold(pieces[2 * x, 0, 0], info)
        pieces[2 * x, 1, 1] = hold(pieces[2 * x, 1, 1], pieces[2 * x + 1, 1, 0])
    for b, y, part in list(pieces):
        if b % 2 == 0 and (b + 1, y, part) not in pieces:
            pieces[b + 1, y, part] = send(pieces[b, y, part], core=1)
    parted = [[pieces[key] for key in sorted(pieces) if key[0] == b] for b in range(ranks)]

    def rows_of(blocks):
        return [piece for b in blocks for piece in parted[b]]

    def counts_of(blocks):
        return [len(parted[b]) for b in blocks]

    near = range(0, ranks, 2)
    partial = call(
        functools.partial(first_kernel, counts_of(near)),
        (held, *rows_of(near)),
        [VMEM] * (1 + sum(counts_of(near))),
        shape((total_rows, columns), f32),
        VMEM,
        flops=flops // 2,
    )
    beside = range(1, ranks, 2)
    logits, stats = call(
        functools.partial(logits_kernel, counts_of(beside), dps),
        (info, partial, held, *rows_of(beside)),
        [VMEM] * (3 + sum(counts_of(beside))),
        (
            shape((total_rows, columns), f32),
            shape((dps * ranks, 1, total_rows + LANES), f32),
        ),
        (VMEM, VMEM),
        flops=flops // 2,
    )
    other_logits = send(logits, core=1)
    other_held = send(hold(away, stats), core=1)
    stats = lax.all_to_all(stats, AXES, 0, 0)
    rows_part = total_rows // 4
    order = sorted(range(1, ranks), key=lambda place: (place % 2 + (place > 1), place)) + [0]
    outs = (shape((rows_part, width), bf16),) * (ranks - 1) + (shape((rows_part, width), f32),)
    logit_grad, table, *going = call(
        functools.partial(grad_kernel, order, dps),
        (info, logits, other_logits, held, other_held, stats),
        [VMEM] * 6,
        (shape((total_rows, columns), bf16), shape((total_rows, 128), f32)) + outs * 2,
        (VMEM,) * (2 + 2 * ranks),
        flops=flops,
    )
    ends, sums = [None] * zs, [None, None]
    for chunk in (1, 0):
        *values, corner = going[(1 - chunk) * ranks:(2 - chunk) * ranks]
        sums[chunk] = [corner]
        for place, value in zip(order, values):
            sums[chunk].append(send(value, y=place % 2, x=place // 2))

    def weight_part(first, after, *extra):
        blocks = range(first, first + ranks // 2)
        chosen_rows = rows_of(blocks)
        return call(
            functools.partial(weight_kernel, blocks, counts_of(blocks), len(extra)),
            (after, logit_grad, *extra, *chosen_rows),
            [ANY, VMEM] + [HBM] * (len(extra) > 0)
            + [VMEM] * (max(len(extra) - 1, 0) + len(chosen_rows)),
            (shape((depth, columns), bf16), shape((8, 128), f32)),
            (HBM, VMEM),
            [
                pltpu.VMEM((depth // 2, columns), bf16),
                pltpu.SemaphoreType.DMA((ranks // 2,)),
            ],
            flops=flops // 2,
            aliases={2: 0} if extra else {},
        )

    weight_grad, finished = weight_part(0, sums[0][0])
    for chunk in (1, 0):
        near = chunk * zs // 2
        parts_z = call(
            functools.partial(corner_kernel, ranks - 1),
            (table if chunk else finished, *sums[chunk]),
            [ANY] + [VMEM] * ranks,
            tuple(shape((CAP, width), bf16 if near + z else f32) for z in range(zs // 2)),
            (VMEM,) * (zs // 2),
        )
        for z, value in enumerate(parts_z):
            ends[near + z] = send(value, z=near + z) if near + z else value
    weight_grad, last = weight_part(ranks // 2, parts_z[0], weight_grad, info, table, stats)
    hidden_grad, loss = call(
        unpack_kernel,
        (last, chosen, *ends),
        [VMEM] * (2 + len(ends)),
        (shape((tokens, width), bf16), shape((1, 1), f32)),
        (VMEM, SMEM),
    )
    return loss[0, 0], hidden_grad, weight_grad


def solution(mesh):
    return jax.shard_map(
        functools.partial(body, mesh.shape["dp"], mesh.shape["vocab"]),
        mesh=mesh,
        in_specs=(P("dp", "vocab"), P(None, AXES), P("dp"), P("dp"), P("dp"), P()),
        out_specs=(P(), P("dp", "vocab"), P(None, AXES)),
        check_vma=False,
    )
```

```python
import functools
import math

import jax
import jax.numpy as jnp
from jax import lax
from jax.experimental import pallas as pl
from jax.experimental.pallas import tpu as pltpu
from jax.sharding import PartitionSpec as P

CAP = 32
MOST_VMEM = 56 * 1024 * 1024
LANES = 128
SUB = 16
grad_scale = 16384.0
AXES = ("dp", "vocab")
SMEM = pl.BlockSpec(memory_space=pltpu.SMEM)
VMEM = pl.BlockSpec(memory_space=pltpu.VMEM)
HBM = pl.BlockSpec(memory_space=pltpu.HBM)
ANY = pl.BlockSpec(memory_space=pl.ANY)


def size_of(value):
    return math.prod(value.shape) * jnp.dtype(value.dtype).itemsize


def call(kernel, operands, in_specs, out_shape, out_specs, scratch=(), spare=4, flops=0, aliases={}):
    outs = jax.tree.leaves(out_shape)
    sized = [v for v, s in zip(operands, in_specs) if s is VMEM]
    sized += [v for v, s in zip(outs, jax.tree.leaves(out_specs)) if s is VMEM]
    held = [s for s in scratch if getattr(s, "memory_space", None) == pltpu.VMEM]
    total = sum(size_of(v) for v in sized) + sum(size_of(s) for s in held)
    return pl.pallas_call(
        kernel,
        out_shape=out_shape,
        in_specs=in_specs,
        out_specs=out_specs,
        scratch_shapes=scratch,
        input_output_aliases=aliases,
        compiler_params=pltpu.CompilerParams(vmem_limit_bytes=min(total + spare * 1024 * 1024, MOST_VMEM)),
        cost_estimate=pl.CostEstimate(
            flops=flops,
            bytes_accessed=sum(size_of(v) for v in list(operands) + outs),
            transcendentals=0,
        ),
    )(*operands)


def in_hbm(value):
    return pltpu.with_memory_space_constraint(value, pltpu.HBM)


def coordinates():
    group, rank = lax.axis_index("dp"), lax.axis_index("vocab")
    groups, ranks = lax.axis_size("dp"), lax.axis_size("vocab")
    position = group % 2 * (groups // 2) + group // 2
    return rank, position, group * ranks + rank


def choose(mask):
    tokens = mask.shape[1]
    wide = jnp.broadcast_to(mask.astype(jnp.float32), (8, tokens))
    before = lax.broadcasted_iota(jnp.int32, (tokens, tokens), 0)
    after = lax.broadcasted_iota(jnp.int32, (tokens, tokens), 1)
    upto = (before <= after).astype(jnp.float32)
    slot = jnp.dot(
        wide.astype(jnp.bfloat16), upto.astype(jnp.bfloat16), preferred_element_type=jnp.float32
    )[0:1]
    grid = lax.broadcasted_iota(jnp.int32, (CAP, tokens), 0) + 1
    return (slot.astype(jnp.int32) == grid) & (mask == 1)


def payload_rows(width):
    return CAP * width // LANES + SUB


def tiles(width):
    count = width // LANES
    for high in range(CAP // SUB):
        for low in range(count):
            yield (
                (high * count + low) * SUB,
                slice(high * SUB, (high + 1) * SUB),
                slice(low * LANES, (low + 1) * LANES),
            )


def pack_kernel(hidden_hbm, mask_hbm, target_hbm, turn_hbm, payload, plain, chosen_out, *scratch):
    hidden, mask, target, turn, sems = scratch
    copies = []
    for place, (source, held) in enumerate(
        ((mask_hbm, mask), (target_hbm, target), (turn_hbm, turn), (hidden_hbm, hidden))
    ):
        copy = pltpu.make_async_copy(source, held, sems.at[place])
        copy.start()
        copies.append(copy)
    for copy in copies[:3]:
        copy.wait()
    width = hidden.shape[1]
    one_hot = choose(mask[...]).astype(jnp.float32).astype(jnp.bfloat16)
    chosen_out[...] = one_hot
    turns, targets = turn[...], target[...]
    fields = (
        mask[...],
        turns & 255,
        turns >> 8,
        targets & 255,
        (targets >> 8) & 255,
        targets >> 16,
    )
    fields += (jnp.zeros_like(turns),) * (SUB - len(fields))
    fields = jnp.concatenate([field.astype(jnp.float32) for field in fields], axis=0)
    slots = jnp.concatenate([one_hot] + [jnp.zeros_like(one_hot)] * (LANES // CAP - 1), axis=0)
    ids = lax.dot_general(
        fields.astype(jnp.bfloat16),
        slots,
        (((1,), (1,)), ((), ())),
        preferred_element_type=jnp.float32,
    )
    payload[payload.shape[0] - SUB:] = ids.astype(jnp.bfloat16)
    copies[3].wait()
    packed = jnp.dot(one_hot, hidden[...], preferred_element_type=jnp.float32)
    packed = packed.astype(jnp.bfloat16)
    plain[...] = packed
    for start, rows, lanes in tiles(width):
        payload[start:start + SUB] = packed[rows, lanes]


def unroll(payload, first, plain, place):
    for start, rows, lanes in tiles(plain.shape[1]):
        target = slice(place * CAP + rows.start, place * CAP + rows.stop)
        plain[target, lanes] = payload[first + start:first + start + SUB]


def join_kernel(order, *refs):
    blocks, (line, plain, far) = refs[:len(order) - 1] + refs[-4:-3], refs[-3:]
    for place, block in zip(order, blocks):
        height = block.shape[0]
        line[place * height:(place + 1) * height] = block[...]
        unroll(block, 0, plain, place)
        if place:
            unroll(block, 0, far, place - 1)


def rows_kernel(line, plain):
    height = payload_rows(plain.shape[1])
    for place in range(line.shape[0] // height):
        unroll(line, place * height, plain, place)


def stage_kernel(blocks, line, weight, held, away, same, sems):
    rank = coordinates()[0]
    width = weight.shape[0] // blocks
    copies = []
    for block in list(range(1, blocks, 2)) + list(range(0, blocks, 2)):
        start = pl.multiple_of((rank ^ block) * width, width)
        targets = [held.at[pl.ds(start, width)]]
        if block % 2:
            targets.append(away.at[pl.ds(block // 2 * width, width)])
        for target in targets:
            copy = pltpu.make_async_copy(
                weight.at[pl.ds(start, width)], target, sems.at[len(copies)]
            )
            copy.start()
            copies.append(copy)
    same[...] = line[...]
    for copy in copies:
        copy.wait()


def gate_kernel(value, after, same):
    pass


def info_kernel(height, own, other, advantages, info):
    tables = []
    for line in (own, other):
        for end in range(height, line.shape[0] + 1, height):
            ids = line[end - SUB:end].astype(jnp.float32)
            ids = jnp.concatenate([ids] * (LANES // SUB), axis=0)
            tables.append(jnp.transpose(ids)[:CAP])
    table = jnp.concatenate(tables, axis=0)
    valid = table[:, 0:1]
    turn = table[:, 1:2] + 256.0 * table[:, 2:3]
    target = table[:, 3:4] + 256.0 * table[:, 4:5] + 65536.0 * table[:, 5:6]
    turns = advantages.shape[1]
    spot = lax.broadcasted_iota(jnp.int32, (table.shape[0], turns), 1)
    gain = jnp.sum(
        jnp.where(spot == turn.astype(jnp.int32), advantages[...], 0.0), axis=1, keepdims=True
    )
    weight = valid * gain / jnp.sum(valid)
    lane = lax.broadcasted_iota(jnp.int32, info.shape, 1)
    info[...] = jnp.where(lane == 0, weight, jnp.where(lane == 1, target, 0.0))


def reorder(stats, position, groups):
    lanes = stats.shape[1]
    lane = lax.broadcasted_iota(jnp.int32, stats.shape, 1)
    bit = 1
    while bit < groups:
        size = CAP * bit
        swapped = jnp.where(
            (lane & size) != 0,
            pltpu.roll(stats, size, 1),
            pltpu.roll(stats, lanes - size, 1),
        )
        stats = jnp.where((position & bit) != 0, swapped, stats)
        bit *= 2
    return stats


def all_rows(pieces, counts, place):
    start = sum(counts[:place])
    return jnp.concatenate([ref[...] for ref in pieces[start:start + counts[place]]], axis=0)


def some_logits(counts, first, pieces, weight):
    blocks = 2 * len(counts)
    width = weight.shape[0] // blocks
    rank, total = coordinates()[0], None
    for place, block in enumerate(range(first, blocks, 2)):
        start = pl.multiple_of((rank ^ block) * width, width)
        part = jnp.dot(
            all_rows(pieces, counts, place),
            weight[pl.ds(start, width), :],
            preferred_element_type=jnp.float32,
        )
        total = part if total is None else total + part
    return total


def first_kernel(counts, weight, *refs):
    refs[-1][...] = some_logits(counts, 0, refs[:-1], weight)


def logits_kernel(counts, groups, info, partial, weight, *refs):
    pieces, (logits, stats) = refs[:-2], refs[-2:]
    _, position, shard = coordinates()
    total = partial[...] + some_logits(counts, 1, pieces, weight)
    logits[...] = total
    height, columns = total.shape
    target = info[:, 1:2].astype(jnp.int32) - shard * columns
    column = lax.broadcasted_iota(jnp.int32, total.shape, 1)
    hit = jnp.sum(jnp.where(column == target, total, 0.0), axis=1, keepdims=True)
    hit = jnp.sum(hit * info[:, 0:1])
    peak = jnp.max(total, axis=1, keepdims=True)
    mass = jnp.sum(jnp.exp(total - peak), axis=1, keepdims=True)
    lane = lax.broadcasted_iota(jnp.int32, (height, 128), 1)
    table = jnp.where(lane == 0, peak + jnp.log(mass), hit)
    table = reorder(jnp.transpose(table)[0:8], position, groups)
    line = jnp.concatenate([table[0:1], table[1:2, :LANES]], axis=1)
    stats[...] = jnp.broadcast_to(line[None], stats.shape)


def log_totals(groups, stats, height):
    parts = stats[:, :, :height]
    peak = jnp.max(parts, axis=0)
    line = peak + jnp.log(jnp.sum(jnp.exp(parts - peak[None]), axis=0))
    line = reorder(jnp.broadcast_to(line, (8, height)), coordinates()[1], groups)
    return jnp.transpose(jnp.concatenate([line] * 16, axis=0))


def grad_kernel(order, groups, info, mine, theirs, weight, other_weight, stats, *refs):
    logit_grad, table, outs = refs[0], refs[1], refs[2:]
    chunks = (outs[len(order):], outs[:len(order)])
    rank, _, shard = coordinates()
    height, columns = mine.shape
    part = height // 4
    table[...] = log_totals(groups, stats, height)
    log_total = table[:, 0:1]
    row_weight, target = info[:, 0:1], info[:, 1:2].astype(jnp.int32)

    def grad_of(logits, shard):
        column = lax.broadcasted_iota(jnp.int32, (height, columns), 1) + shard * columns
        probability = jnp.exp(logits[...] - log_total)
        return (
            grad_scale * row_weight * (probability - (column == target).astype(jnp.float32))
        ).astype(jnp.bfloat16)

    grad = grad_of(mine, shard)
    logit_grad[...] = grad
    grads = (grad, grad_of(theirs, shard ^ 1))
    width = outs[0].shape[1]
    for x in range(len(order) // 2):
        start = pl.multiple_of((rank ^ 2 * x) * width, width)
        weights = (weight[pl.ds(start, width), :], other_weight[x * width:(x + 1) * width, :])
        total = sum(
            lax.dot_general(g, w, (((1,), (1,)), ((), ())), preferred_element_type=jnp.float32)
            for g, w in zip(grads, weights)
        )
        for quarter in range(4):
            out = chunks[quarter % 2][order.index(2 * x + quarter // 2)]
            out[...] = total[quarter * part:(quarter + 1) * part].astype(out.dtype)


def weight_kernel(blocks, counts, skipped, after, logit_grad, *refs):
    pieces, (out, last, done, sems) = refs[skipped:-4], refs[-4:]
    rank = coordinates()[0]
    width = done.shape[0] // len(blocks)
    copies = []
    for place, block in enumerate(blocks):
        done[place * width:(place + 1) * width] = lax.dot_general(
            all_rows(pieces, counts, place),
            logit_grad[...],
            (((0,), (0,)), ((), ())),
            preferred_element_type=jnp.float32,
        ).astype(jnp.bfloat16)
        start = pl.multiple_of((rank ^ block) * width, width)
        copy = pltpu.make_async_copy(
            done.at[pl.ds(place * width, width)], out.at[pl.ds(start, width)], sems.at[place]
        )
        copy.start()
        copies.append(copy)
    if skipped:
        info, table, stats = refs[1:4]
        hits = jnp.sum(stats[:, :, info.shape[0]:], axis=0)
        loss = jnp.sum(info[:, 0:1] * table[:, 0:1]) - hits[0, 0]
        last[...] = jnp.full(last.shape, loss, jnp.float32)
    else:
        last[...] = jnp.zeros_like(last)
    for copy in copies:
        copy.wait()


def corner_kernel(count, after, kept, *refs):
    total = kept[...]
    for ref in refs[:count]:
        total = total + ref[...].astype(jnp.float32)
    for place, out in enumerate(refs[count:]):
        out[...] = total[place * CAP:(place + 1) * CAP].astype(out.dtype)


def unpack_kernel(last, chosen, *refs):
    out, loss = refs[-2:]
    loss[0, 0] = last[0, 0]
    total = sum(ref[...].astype(jnp.float32) for ref in refs[:-2])
    out[...] = lax.dot_general(
        chosen[...],
        total.astype(jnp.bfloat16),
        (((0,), (0,)), ((), ())),
        preferred_element_type=jnp.float32,
    ).astype(jnp.bfloat16)


def body(dps, ranks, hidden, weight, loss_mask, target_ids, turn_ids, advantages):
    tokens, width = hidden.shape
    depth, columns = weight.shape
    zs, xs = dps // 2, ranks // 2
    total_rows = dps * CAP
    bf16, f32, i32 = jnp.bfloat16, jnp.float32, jnp.int32
    shape = jax.ShapeDtypeStruct
    flops = 2 * total_rows * depth * columns

    def send(value, z=0, y=0, x=0, core=0):
        far, near = 2 * z + y, 2 * x + core
        pairs = [
            (d * ranks + v, (d ^ far) * ranks + (v ^ near))
            for d in range(dps)
            for v in range(ranks)
        ]
        return lax.ppermute(value, AXES, pairs)

    packed, own, chosen = call(
        pack_kernel,
        (
            in_hbm(hidden),
            in_hbm(loss_mask.reshape(1, tokens)),
            in_hbm(target_ids.reshape(1, tokens)),
            in_hbm(turn_ids.reshape(1, tokens)),
        ),
        [HBM] * 4,
        (
            shape((payload_rows(width), LANES), bf16),
            shape((CAP, width), bf16),
            shape((CAP, tokens), bf16),
        ),
        (VMEM,) * 3,
        [pltpu.VMEM((tokens, width), bf16)]
        + [pltpu.VMEM((1, tokens), i32)] * 3
        + [pltpu.SemaphoreType.DMA((4,))],
    )

    line_order = [0, *range(2, zs), 1]
    blocks = [send(packed, z=z) if z else packed for z in line_order[:-1]]
    corners = {x: send(own, y=1, x=x) for x in range(1, xs)}
    blocks.append(send(packed, z=1))
    line_rows, height = zs * CAP, payload_rows(width)
    line, line_plain, far = call(
        functools.partial(join_kernel, line_order),
        (*blocks[:-1], *corners.values(), blocks[-1]),
        [VMEM] * (zs - 1) + [ANY] * len(corners) + [VMEM],
        (
            shape((zs * height, LANES), bf16),
            shape((line_rows, width), bf16),
            shape((line_rows - CAP, width), bf16),
        ),
        (VMEM,) * 3,
    )
    across = send(line, y=1)
    pieces = {(0, 1, 0): call(rows_kernel, (across,), [VMEM], shape((line_rows, width), bf16), VMEM)}
    for x in range(1, xs):
        pieces[2 * x, 0, 0] = send(line_plain, x=x)
        pieces[2 * x, 1, 0] = corners[x]
        pieces[2 * x, 1, 1] = send(far, y=1, x=x)
    held, away, same = call(
        functools.partial(stage_kernel, ranks),
        (line_plain, in_hbm(weight)),
        [VMEM, HBM],
        (
            shape((depth, columns), bf16),
            shape((depth // 2, columns), bf16),
            shape(line_plain.shape, bf16),
        ),
        (VMEM,) * 3,
        [pltpu.SemaphoreType.DMA((ranks + xs,))],
    )
    pieces[0, 0, 0] = same
    info = call(
        functools.partial(info_kernel, height),
        (line, across, advantages.reshape(1, -1)),
        [VMEM] * 3,
        shape((total_rows, 128), f32),
        VMEM,
    )

    def hold(value, after):
        like = shape(value.shape, value.dtype)
        return call(gate_kernel, (value, after), [ANY, ANY], like, ANY, aliases={0: 0})

    for x in range(1, xs):
        pieces[2 * x + 1, 1, 0] = send(pieces[2 * x, 1, 0], core=1)
        pieces[2 * x, 0, 0] = hold(pieces[2 * x, 0, 0], info)
        pieces[2 * x, 1, 1] = hold(pieces[2 * x, 1, 1], pieces[2 * x + 1, 1, 0])
    for b, y, part in list(pieces):
        if b % 2 == 0 and (b + 1, y, part) not in pieces:
            pieces[b + 1, y, part] = send(pieces[b, y, part], core=1)
    parted = [[pieces[key] for key in sorted(pieces) if key[0] == b] for b in range(ranks)]

    def rows_of(blocks):
        return [piece for b in blocks for piece in parted[b]]

    def counts_of(blocks):
        return [len(parted[b]) for b in blocks]

    near = range(0, ranks, 2)
    partial = call(
        functools.partial(first_kernel, counts_of(near)),
        (held, *rows_of(near)),
        [VMEM] * (1 + sum(counts_of(near))),
        shape((total_rows, columns), f32),
        VMEM,
        flops=flops // 2,
    )
    beside = range(1, ranks, 2)
    logits, stats = call(
        functools.partial(logits_kernel, counts_of(beside), dps),
        (info, partial, held, *rows_of(beside)),
        [VMEM] * (3 + sum(counts_of(beside))),
        (
            shape((total_rows, columns), f32),
            shape((dps * ranks, 1, total_rows + LANES), f32),
        ),
        (VMEM, VMEM),
        flops=flops // 2,
    )
    other_logits = send(logits, core=1)
    other_held = send(hold(away, stats), core=1)
    stats = lax.all_to_all(stats, AXES, 0, 0)
    rows_part = total_rows // 4
    order = sorted(range(1, ranks), key=lambda place: (place % 2 + (place > 1), place)) + [0]
    outs = (shape((rows_part, width), bf16),) * (ranks - 1) + (shape((rows_part, width), f32),)
    logit_grad, table, *going = call(
        functools.partial(grad_kernel, order, dps),
        (info, logits, other_logits, held, other_held, stats),
        [VMEM] * 6,
        (shape((total_rows, columns), bf16), shape((total_rows, 128), f32)) + outs * 2,
        (VMEM,) * (2 + 2 * ranks),
        flops=flops,
    )
    ends, sums = [None] * zs, [None, None]
    for chunk in (1, 0):
        *values, corner = going[(1 - chunk) * ranks:(2 - chunk) * ranks]
        sums[chunk] = [corner]
        for place, value in zip(order, values):
            sums[chunk].append(send(value, y=place % 2, x=place // 2))

    def weight_part(first, after, *extra):
        blocks = range(first, first + ranks // 2)
        chosen_rows = rows_of(blocks)
        return call(
            functools.partial(weight_kernel, blocks, counts_of(blocks), len(extra)),
            (after, logit_grad, *extra, *chosen_rows),
            [ANY, VMEM] + [HBM] * (len(extra) > 0)
            + [VMEM] * (max(len(extra) - 1, 0) + len(chosen_rows)),
            (shape((depth, columns), bf16), shape((8, 128), f32)),
            (HBM, VMEM),
            [
                pltpu.VMEM((depth // 2, columns), bf16),
                pltpu.SemaphoreType.DMA((ranks // 2,)),
            ],
            flops=flops // 2,
            aliases={2: 0} if extra else {},
        )

    weight_grad, finished = weight_part(0, sums[0][0])
    for chunk in (1, 0):
        near = chunk * zs // 2
        parts_z = call(
            functools.partial(corner_kernel, ranks - 1),
            (table if chunk else finished, *sums[chunk]),
            [ANY] + [VMEM] * ranks,
            tuple(shape((CAP, width), bf16 if near + z else f32) for z in range(zs // 2)),
            (VMEM,) * (zs // 2),
        )
        for z, value in enumerate(parts_z):
            ends[near + z] = send(value, z=near + z) if near + z else value
    weight_grad, last = weight_part(ranks // 2, parts_z[0], weight_grad, info, table, stats)
    hidden_grad, loss = call(
        unpack_kernel,
        (last, chosen, *ends),
        [VMEM] * (2 + len(ends)),
        (shape((tokens, width), bf16), shape((1, 1), f32)),
        (VMEM, SMEM),
    )
    return loss[0, 0], hidden_grad, weight_grad


def solution(mesh):
    return jax.shard_map(
        functools.partial(body, mesh.shape["dp"], mesh.shape["vocab"]),
        mesh=mesh,
        in_specs=(P("dp", "vocab"), P(None, AXES), P("dp"), P("dp"), P("dp"), P()),
        out_specs=(P(), P("dp", "vocab"), P(None, AXES)),
        check_vma=False,
    )
```

```python
import functools
import math

import jax
import jax.numpy as jnp
from jax import lax
from jax.experimental import pallas as pl
from jax.experimental.pallas import tpu as pltpu
from jax.sharding import PartitionSpec as P

CAP = 32
MOST_VMEM = 56 * 1024 * 1024
IDS = 128
LANES = 128
grad_scale = 16384.0
AXES = ("dp", "vocab")
SMEM = pl.BlockSpec(memory_space=pltpu.SMEM)
VMEM = pl.BlockSpec(memory_space=pltpu.VMEM)
HBM = pl.BlockSpec(memory_space=pltpu.HBM)
ANY = pl.BlockSpec(memory_space=pl.ANY)


def size_of(value):
    return math.prod(value.shape) * jnp.dtype(value.dtype).itemsize


def call(kernel, operands, in_specs, out_shape, out_specs, scratch=(), spare=4, flops=0, aliases={}):
    outs = jax.tree.leaves(out_shape)
    sized = [v for v, s in zip(operands, in_specs) if s is VMEM]
    sized += [v for v, s in zip(outs, jax.tree.leaves(out_specs)) if s is VMEM]
    held = [s for s in scratch if getattr(s, "memory_space", None) == pltpu.VMEM]
    total = sum(size_of(v) for v in sized) + sum(size_of(s) for s in held)
    return pl.pallas_call(
        kernel,
        out_shape=out_shape,
        in_specs=in_specs,
        out_specs=out_specs,
        scratch_shapes=scratch,
        input_output_aliases=aliases,
        compiler_params=pltpu.CompilerParams(vmem_limit_bytes=min(total + spare * 1024 * 1024, MOST_VMEM)),
        cost_estimate=pl.CostEstimate(
            flops=flops,
            bytes_accessed=sum(size_of(v) for v in list(operands) + outs),
            transcendentals=0,
        ),
    )(*operands)


def in_hbm(value):
    return pltpu.with_memory_space_constraint(value, pltpu.HBM)


def coordinates():
    group, rank = lax.axis_index("dp"), lax.axis_index("vocab")
    groups, ranks = lax.axis_size("dp"), lax.axis_size("vocab")
    position = group % 2 * (groups // 2) + group // 2
    return rank, position, group * ranks + rank


def choose(mask):
    tokens = mask.shape[1]
    wide = jnp.broadcast_to(mask.astype(jnp.float32), (8, tokens))
    before = lax.broadcasted_iota(jnp.int32, (tokens, tokens), 0)
    after = lax.broadcasted_iota(jnp.int32, (tokens, tokens), 1)
    upto = (before <= after).astype(jnp.float32)
    slot = jnp.dot(
        wide.astype(jnp.bfloat16), upto.astype(jnp.bfloat16), preferred_element_type=jnp.float32
    )[0:1]
    grid = lax.broadcasted_iota(jnp.int32, (CAP, tokens), 0) + 1
    return (slot.astype(jnp.int32) == grid) & (mask == 1)


def pack_kernel(hidden_hbm, mask_hbm, target_hbm, turn_hbm, rows, plain, chosen_out, *scratch):
    hidden, mask, target, turn, sems = scratch
    copies = []
    for place, (source, held) in enumerate(
        ((mask_hbm, mask), (target_hbm, target), (turn_hbm, turn), (hidden_hbm, hidden))
    ):
        copy = pltpu.make_async_copy(source, held, sems.at[place])
        copy.start()
        copies.append(copy)
    for copy in copies[:3]:
        copy.wait()
    width = hidden.shape[1]
    chosen = choose(mask[...])
    one_hot = chosen.astype(jnp.float32).astype(jnp.bfloat16)
    chosen_out[...] = one_hot
    turns, targets = turn[...], target[...]
    fields = (
        mask[...],
        turns & 255,
        turns >> 8,
        targets & 255,
        (targets >> 8) & 255,
        targets >> 16,
    )
    lane = lax.broadcasted_iota(jnp.int32, (CAP, IDS), 1)
    table = jnp.zeros((CAP, IDS), jnp.float32)
    for place, field in enumerate(fields):
        picked = jnp.where(chosen, field.astype(jnp.float32), 0.0)
        table = jnp.where(lane == place, jnp.sum(picked, axis=1, keepdims=True), table)
    rows[:, width:] = table.astype(jnp.bfloat16)
    copies[3].wait()
    packed = jnp.dot(one_hot, hidden[...], preferred_element_type=jnp.float32)
    packed = packed.astype(jnp.bfloat16)
    rows[:, :width] = packed
    plain[...] = packed


def join_kernel(order, *refs):
    blocks, (line, plain, far) = refs[:len(order) - 1] + refs[-4:-3], refs[-3:]
    width = plain.shape[1]
    for place, block in zip(order, blocks):
        rows = slice(place * CAP, (place + 1) * CAP)
        line[rows] = block[...]
        plain[rows] = block[:, :width]
        if place:
            far[(place - 1) * CAP:place * CAP] = block[:, :width]


def stage_kernel(blocks, line, weight, held, away, same, sems):
    rank = coordinates()[0]
    width = weight.shape[0] // blocks
    copies = []
    for block in list(range(1, blocks, 2)) + list(range(0, blocks, 2)):
        start = pl.multiple_of((rank ^ block) * width, width)
        targets = [held.at[pl.ds(start, width)]]
        if block % 2:
            targets.append(away.at[pl.ds(block // 2 * width, width)])
        for target in targets:
            copy = pltpu.make_async_copy(
                weight.at[pl.ds(start, width)], target, sems.at[len(copies)]
            )
            copy.start()
            copies.append(copy)
    same[...] = line[...]
    for copy in copies:
        copy.wait()


def gate_kernel(*refs):
    pass


def info_kernel(*refs):
    advantages, info = refs[-2:]
    start = refs[0].shape[1] - IDS
    table = jnp.concatenate([ref[:, start:] for ref in refs[:-2]], axis=0).astype(jnp.float32)
    valid = table[:, 0:1]
    turn = table[:, 1:2] + 256.0 * table[:, 2:3]
    target = table[:, 3:4] + 256.0 * table[:, 4:5] + 65536.0 * table[:, 5:6]
    turns = advantages.shape[1]
    spot = lax.broadcasted_iota(jnp.int32, (table.shape[0], turns), 1)
    gain = jnp.sum(
        jnp.where(spot == turn.astype(jnp.int32), advantages[...], 0.0), axis=1, keepdims=True
    )
    weight = valid * gain / jnp.sum(valid)
    lane = lax.broadcasted_iota(jnp.int32, info.shape, 1)
    info[...] = jnp.where(lane == 0, weight, jnp.where(lane == 1, target, 0.0))


def reorder(stats, position, groups):
    lanes = stats.shape[1]
    lane = lax.broadcasted_iota(jnp.int32, stats.shape, 1)
    bit = 1
    while bit < groups:
        size = CAP * bit
        swapped = jnp.where(
            (lane & size) != 0,
            pltpu.roll(stats, size, 1),
            pltpu.roll(stats, lanes - size, 1),
        )
        stats = jnp.where((position & bit) != 0, swapped, stats)
        bit *= 2
    return stats


def all_rows(pieces, counts, place, width):
    start = sum(counts[:place])
    return jnp.concatenate([ref[:, :width] for ref in pieces[start:start + counts[place]]], axis=0)


def some_logits(counts, first, pieces, weight):
    blocks = 2 * len(counts)
    width = weight.shape[0] // blocks
    rank, total = coordinates()[0], None
    for place, block in enumerate(range(first, blocks, 2)):
        start = pl.multiple_of((rank ^ block) * width, width)
        part = jnp.dot(
            all_rows(pieces, counts, place, width),
            weight[pl.ds(start, width), :],
            preferred_element_type=jnp.float32,
        )
        total = part if total is None else total + part
    return total


def first_kernel(counts, weight, *refs):
    refs[-1][...] = some_logits(counts, 0, refs[:-1], weight)


def logits_kernel(counts, groups, info, partial, weight, *refs):
    pieces, (logits, stats) = refs[:-2], refs[-2:]
    _, position, shard = coordinates()
    total = partial[...] + some_logits(counts, 1, pieces, weight)
    logits[...] = total
    height, columns = total.shape
    target = info[:, 1:2].astype(jnp.int32) - shard * columns
    column = lax.broadcasted_iota(jnp.int32, total.shape, 1)
    hit = jnp.sum(jnp.where(column == target, total, 0.0), axis=1, keepdims=True)
    hit = jnp.sum(hit * info[:, 0:1])
    peak = jnp.max(total, axis=1, keepdims=True)
    mass = jnp.sum(jnp.exp(total - peak), axis=1, keepdims=True)
    lane = lax.broadcasted_iota(jnp.int32, (height, 128), 1)
    table = jnp.where(lane == 0, peak + jnp.log(mass), hit)
    table = reorder(jnp.transpose(table)[0:8], position, groups)
    line = jnp.concatenate([table[0:1], table[1:2, :LANES]], axis=1)
    stats[...] = jnp.broadcast_to(line[None], stats.shape)


def log_totals(groups, stats, height):
    parts = stats[:, :, :height]
    peak = jnp.max(parts, axis=0)
    line = peak + jnp.log(jnp.sum(jnp.exp(parts - peak[None]), axis=0))
    line = reorder(jnp.broadcast_to(line, (8, height)), coordinates()[1], groups)
    return jnp.transpose(jnp.concatenate([line] * 16, axis=0))


def grad_kernel(order, groups, info, mine, theirs, weight, other_weight, stats, *refs):
    logit_grad, table, outs = refs[0], refs[1], refs[2:]
    chunks = (outs[len(order):], outs[:len(order)])
    rank, _, shard = coordinates()
    height, columns = mine.shape
    part = height // 4
    table[...] = log_totals(groups, stats, height)
    log_total = table[:, 0:1]
    row_weight, target = info[:, 0:1], info[:, 1:2].astype(jnp.int32)

    def grad_of(logits, shard):
        column = lax.broadcasted_iota(jnp.int32, (height, columns), 1) + shard * columns
        probability = jnp.exp(logits[...] - log_total)
        return (
            grad_scale * row_weight * (probability - (column == target).astype(jnp.float32))
        ).astype(jnp.bfloat16)

    grad = grad_of(mine, shard)
    logit_grad[...] = grad
    grads = (grad, grad_of(theirs, shard ^ 1))
    width = outs[0].shape[1]
    for x in range(len(order) // 2):
        start = pl.multiple_of((rank ^ 2 * x) * width, width)
        weights = (weight[pl.ds(start, width), :], other_weight[x * width:(x + 1) * width, :])
        total = sum(
            lax.dot_general(g, w, (((1,), (1,)), ((), ())), preferred_element_type=jnp.float32)
            for g, w in zip(grads, weights)
        )
        for quarter in range(4):
            out = chunks[quarter % 2][order.index(2 * x + quarter // 2)]
            out[...] = total[quarter * part:(quarter + 1) * part].astype(out.dtype)


def weight_kernel(blocks, counts, skipped, after, logit_grad, *refs):
    pieces, (out, last, done, sems) = refs[skipped:-4], refs[-4:]
    rank = coordinates()[0]
    width = done.shape[0] // len(blocks)
    copies = []
    for place, block in enumerate(blocks):
        done[place * width:(place + 1) * width] = lax.dot_general(
            all_rows(pieces, counts, place, width),
            logit_grad[...],
            (((0,), (0,)), ((), ())),
            preferred_element_type=jnp.float32,
        ).astype(jnp.bfloat16)
        start = pl.multiple_of((rank ^ block) * width, width)
        copy = pltpu.make_async_copy(
            done.at[pl.ds(place * width, width)], out.at[pl.ds(start, width)], sems.at[place]
        )
        copy.start()
        copies.append(copy)
    if skipped:
        info, table, stats = refs[1:4]
        hits = jnp.sum(stats[:, :, info.shape[0]:], axis=0)
        loss = jnp.sum(info[:, 0:1] * table[:, 0:1]) - hits[0, 0]
        last[...] = jnp.full(last.shape, loss, jnp.float32)
    else:
        last[...] = jnp.zeros_like(last)
    for copy in copies:
        copy.wait()


def corner_kernel(count, after, kept, *refs):
    total = kept[...]
    for ref in refs[:count]:
        total = total + ref[...].astype(jnp.float32)
    for place, out in enumerate(refs[count:]):
        out[...] = total[place * CAP:(place + 1) * CAP].astype(out.dtype)


def unpack_kernel(last, chosen, *refs):
    out, loss = refs[-2:]
    loss[0, 0] = last[0, 0]
    total = sum(ref[...].astype(jnp.float32) for ref in refs[:-2])
    out[...] = lax.dot_general(
        chosen[...],
        total.astype(jnp.bfloat16),
        (((0,), (0,)), ((), ())),
        preferred_element_type=jnp.float32,
    ).astype(jnp.bfloat16)


def body(dps, ranks, hidden, weight, loss_mask, target_ids, turn_ids, advantages):
    tokens, width = hidden.shape
    depth, columns = weight.shape
    zs, xs = dps // 2, ranks // 2
    total_rows = dps * CAP
    bf16, f32, i32 = jnp.bfloat16, jnp.float32, jnp.int32
    shape = jax.ShapeDtypeStruct
    flops = 2 * total_rows * depth * columns

    def send(value, z=0, y=0, x=0, core=0):
        far, near = 2 * z + y, 2 * x + core
        pairs = [
            (d * ranks + v, (d ^ far) * ranks + (v ^ near))
            for d in range(dps)
            for v in range(ranks)
        ]
        return lax.ppermute(value, AXES, pairs)

    packed, own, chosen = call(
        pack_kernel,
        (
            in_hbm(hidden),
            in_hbm(loss_mask.reshape(1, tokens)),
            in_hbm(target_ids.reshape(1, tokens)),
            in_hbm(turn_ids.reshape(1, tokens)),
        ),
        [HBM] * 4,
        (
            shape((CAP, width + IDS), bf16),
            shape((CAP, width), bf16),
            shape((CAP, tokens), bf16),
        ),
        (VMEM,) * 3,
        [pltpu.VMEM((tokens, width), bf16)]
        + [pltpu.VMEM((1, tokens), i32)] * 3
        + [pltpu.SemaphoreType.DMA((4,))],
    )

    line_order = [0, *range(2, zs), 1]
    blocks = [send(packed, z=z) if z else packed for z in line_order[:-1]]
    corners = {x: send(own, y=1, x=x) for x in range(1, xs)}
    blocks.append(send(packed, z=1))
    line_rows = zs * CAP
    line, line_plain, far = call(
        functools.partial(join_kernel, line_order),
        (*blocks[:-1], *corners.values(), blocks[-1]),
        [VMEM] * (zs - 1) + [ANY] * len(corners) + [VMEM],
        (
            shape((line_rows, width + IDS), bf16),
            shape((line_rows, width), bf16),
            shape((line_rows - CAP, width), bf16),
        ),
        (VMEM,) * 3,
    )
    pieces = {(0, 1, 0): send(line, y=1)}
    for x in range(1, xs):
        pieces[2 * x, 0, 0] = send(line_plain, x=x)
        pieces[2 * x, 1, 0] = corners[x]
        pieces[2 * x, 1, 1] = send(far, y=1, x=x)
    held, away, same = call(
        functools.partial(stage_kernel, ranks),
        (line, in_hbm(weight)),
        [VMEM, HBM],
        (
            shape((depth, columns), bf16),
            shape((depth // 2, columns), bf16),
            shape(line.shape, bf16),
        ),
        (VMEM,) * 3,
        [pltpu.SemaphoreType.DMA((ranks + xs,))],
    )
    pieces[0, 0, 0] = same
    info = call(
        info_kernel,
        (same, pieces[0, 1, 0], advantages.reshape(1, -1)),
        [VMEM] * 3,
        shape((total_rows, 128), f32),
        VMEM,
    )

    def hold(value, after):
        like = shape(value.shape, value.dtype)
        return call(gate_kernel, (value, after), [ANY, ANY], like, ANY, aliases={0: 0})

    for x in range(1, xs):
        pieces[2 * x + 1, 1, 0] = send(pieces[2 * x, 1, 0], core=1)
        pieces[2 * x, 0, 0] = hold(pieces[2 * x, 0, 0], info)
        pieces[2 * x, 1, 1] = hold(pieces[2 * x, 1, 1], pieces[2 * x + 1, 1, 0])
    for b, y, part in list(pieces):
        if b % 2 == 0 and (b + 1, y, part) not in pieces:
            pieces[b + 1, y, part] = send(pieces[b, y, part], core=1)
    parted = [[pieces[key] for key in sorted(pieces) if key[0] == b] for b in range(ranks)]

    def rows_of(blocks):
        return [piece for b in blocks for piece in parted[b]]

    def counts_of(blocks):
        return [len(parted[b]) for b in blocks]

    near = range(0, ranks, 2)
    partial = call(
        functools.partial(first_kernel, counts_of(near)),
        (held, *rows_of(near)),
        [VMEM] * (1 + sum(counts_of(near))),
        shape((total_rows, columns), f32),
        VMEM,
        flops=flops // 2,
    )
    beside = range(1, ranks, 2)
    logits, stats = call(
        functools.partial(logits_kernel, counts_of(beside), dps),
        (info, partial, held, *rows_of(beside)),
        [VMEM] * (3 + sum(counts_of(beside))),
        (
            shape((total_rows, columns), f32),
            shape((dps * ranks, 1, total_rows + LANES), f32),
        ),
        (VMEM, VMEM),
        flops=flops // 2,
    )
    other_logits = send(logits, core=1)
    other_held = send(hold(away, stats), core=1)
    stats = lax.all_to_all(stats, AXES, 0, 0)
    rows_part = total_rows // 4
    order = sorted(range(1, ranks), key=lambda place: (place % 2 + (place > 1), place)) + [0]
    outs = (shape((rows_part, width), bf16),) * (ranks - 1) + (shape((rows_part, width), f32),)
    logit_grad, table, *going = call(
        functools.partial(grad_kernel, order, dps),
        (info, logits, other_logits, held, other_held, stats),
        [VMEM] * 6,
        (shape((total_rows, columns), bf16), shape((total_rows, 128), f32)) + outs * 2,
        (VMEM,) * (2 + 2 * ranks),
        flops=flops,
    )
    def weight_part(first, after, *extra):
        blocks = range(first, first + ranks // 2)
        chosen_rows = rows_of(blocks)
        return call(
            functools.partial(weight_kernel, blocks, counts_of(blocks), len(extra)),
            (after, logit_grad, *extra, *chosen_rows),
            [ANY, VMEM] + [HBM] * (len(extra) > 0)
            + [VMEM] * (max(len(extra) - 1, 0) + len(chosen_rows)),
            (shape((depth, columns), bf16), shape((8, 128), f32)),
            (HBM, VMEM),
            [
                pltpu.VMEM((depth // 2, columns), bf16),
                pltpu.SemaphoreType.DMA((ranks // 2,)),
            ],
            flops=flops // 2,
            aliases={2: 0} if extra else {},
        )

    far_values, near_values = list(going[:ranks]), list(going[ranks:])
    weight_grad, finished = weight_part(0, far_values[-1])
    near_values[:-1] = call(
        gate_kernel,
        (*near_values[:-1], finished),
        [ANY] * ranks,
        outs[:-1],
        (ANY,) * (ranks - 1),
        aliases={place: place for place in range(ranks - 1)},
    )
    ends, sums = [None] * zs, [None, None]
    for chunk, values in ((1, far_values), (0, near_values)):
        sums[chunk] = [values[-1]]
        for place, value in zip(order, values):
            if place:
                sums[chunk].append(send(value, y=place % 2, x=place // 2))
    for chunk in (1, 0):
        near = chunk * zs // 2
        parts_z = call(
            functools.partial(corner_kernel, ranks - 1),
            (table, *sums[chunk]),
            [ANY] + [VMEM] * ranks,
            tuple(shape((CAP, width), bf16 if near + z else f32) for z in range(zs // 2)),
            (VMEM,) * (zs // 2),
        )
        for z, value in enumerate(parts_z):
            ends[near + z] = send(value, z=near + z) if near + z else value
    weight_grad, last = weight_part(ranks // 2, parts_z[0], weight_grad, info, table, stats)
    hidden_grad, loss = call(
        unpack_kernel,
        (last, chosen, *ends),
        [VMEM] * (2 + len(ends)),
        (shape((tokens, width), bf16), shape((1, 1), f32)),
        (VMEM, SMEM),
    )
    return loss[0, 0], hidden_grad, weight_grad


def solution(mesh):
    return jax.shard_map(
        functools.partial(body, mesh.shape["dp"], mesh.shape["vocab"]),
        mesh=mesh,
        in_specs=(P("dp", "vocab"), P(None, AXES), P("dp"), P("dp"), P("dp"), P()),
        out_specs=(P(), P("dp", "vocab"), P(None, AXES)),
        check_vma=False,
    )
```

```python
import functools
import math

import jax
import jax.numpy as jnp
from jax import lax
from jax.experimental import pallas as pl
from jax.experimental.pallas import tpu as pltpu
from jax.sharding import PartitionSpec as P

CAP = 32
MOST_VMEM = 56 * 1024 * 1024
IDS = 128
LANES = 128
grad_scale = 16384.0
AXES = ("dp", "vocab")
SMEM = pl.BlockSpec(memory_space=pltpu.SMEM)
VMEM = pl.BlockSpec(memory_space=pltpu.VMEM)
HBM = pl.BlockSpec(memory_space=pltpu.HBM)
ANY = pl.BlockSpec(memory_space=pl.ANY)


def size_of(value):
    return math.prod(value.shape) * jnp.dtype(value.dtype).itemsize


def call(kernel, operands, in_specs, out_shape, out_specs, scratch=(), spare=4, flops=0, aliases={}):
    outs = jax.tree.leaves(out_shape)
    sized = [v for v, s in zip(operands, in_specs) if s is VMEM]
    sized += [v for v, s in zip(outs, jax.tree.leaves(out_specs)) if s is VMEM]
    held = [s for s in scratch if getattr(s, "memory_space", None) == pltpu.VMEM]
    total = sum(size_of(v) for v in sized) + sum(size_of(s) for s in held)
    return pl.pallas_call(
        kernel,
        out_shape=out_shape,
        in_specs=in_specs,
        out_specs=out_specs,
        scratch_shapes=scratch,
        input_output_aliases=aliases,
        compiler_params=pltpu.CompilerParams(vmem_limit_bytes=min(total + spare * 1024 * 1024, MOST_VMEM)),
        cost_estimate=pl.CostEstimate(
            flops=flops,
            bytes_accessed=sum(size_of(v) for v in list(operands) + outs),
            transcendentals=0,
        ),
    )(*operands)


def in_hbm(value):
    return pltpu.with_memory_space_constraint(value, pltpu.HBM)


def coordinates():
    group, rank = lax.axis_index("dp"), lax.axis_index("vocab")
    groups, ranks = lax.axis_size("dp"), lax.axis_size("vocab")
    position = group % 2 * (groups // 2) + group // 2
    return rank, position, group * ranks + rank


def choose(mask):
    tokens = mask.shape[1]
    wide = jnp.broadcast_to(mask.astype(jnp.float32), (8, tokens))
    before = lax.broadcasted_iota(jnp.int32, (tokens, tokens), 0)
    after = lax.broadcasted_iota(jnp.int32, (tokens, tokens), 1)
    upto = (before <= after).astype(jnp.float32)
    slot = jnp.dot(
        wide.astype(jnp.bfloat16), upto.astype(jnp.bfloat16), preferred_element_type=jnp.float32
    )[0:1]
    grid = lax.broadcasted_iota(jnp.int32, (CAP, tokens), 0) + 1
    return (slot.astype(jnp.int32) == grid) & (mask == 1)


def pack_kernel(hidden_hbm, mask_hbm, target_hbm, turn_hbm, rows, plain, chosen_out, *scratch):
    hidden, mask, target, turn, sems = scratch
    copies = []
    for place, (source, held) in enumerate(
        ((mask_hbm, mask), (target_hbm, target), (turn_hbm, turn), (hidden_hbm, hidden))
    ):
        copy = pltpu.make_async_copy(source, held, sems.at[place])
        copy.start()
        copies.append(copy)
    for copy in copies[:3]:
        copy.wait()
    width = hidden.shape[1]
    chosen = choose(mask[...])
    one_hot = chosen.astype(jnp.float32).astype(jnp.bfloat16)
    chosen_out[...] = one_hot
    turns, targets = turn[...], target[...]
    fields = (
        mask[...],
        turns & 255,
        turns >> 8,
        targets & 255,
        (targets >> 8) & 255,
        targets >> 16,
    )
    lane = lax.broadcasted_iota(jnp.int32, (CAP, IDS), 1)
    table = jnp.zeros((CAP, IDS), jnp.float32)
    for place, field in enumerate(fields):
        picked = jnp.where(chosen, field.astype(jnp.float32), 0.0)
        table = jnp.where(lane == place, jnp.sum(picked, axis=1, keepdims=True), table)
    rows[:, width:] = table.astype(jnp.bfloat16)
    copies[3].wait()
    packed = jnp.dot(one_hot, hidden[...], preferred_element_type=jnp.float32)
    packed = packed.astype(jnp.bfloat16)
    rows[:, :width] = packed
    plain[...] = packed


def join_kernel(order, *refs):
    blocks, (line, plain, far) = refs[:len(order) - 1] + refs[-4:-3], refs[-3:]
    width = plain.shape[1]
    for place, block in zip(order, blocks):
        rows = slice(place * CAP, (place + 1) * CAP)
        line[rows] = block[...]
        plain[rows] = block[:, :width]
        if place:
            far[(place - 1) * CAP:place * CAP] = block[:, :width]


def stage_kernel(blocks, line, weight, held, away, same, sems):
    rank = coordinates()[0]
    width = weight.shape[0] // blocks
    copies = []
    for block in list(range(1, blocks, 2)) + list(range(0, blocks, 2)):
        start = pl.multiple_of((rank ^ block) * width, width)
        targets = [held.at[pl.ds(start, width)]]
        if block % 2:
            targets.append(away.at[pl.ds(block // 2 * width, width)])
        for target in targets:
            copy = pltpu.make_async_copy(
                weight.at[pl.ds(start, width)], target, sems.at[len(copies)]
            )
            copy.start()
            copies.append(copy)
    same[...] = line[...]
    for copy in copies:
        copy.wait()


def gate_kernel(*refs):
    pass


def info_kernel(*refs):
    advantages, info = refs[-2:]
    start = refs[0].shape[1] - IDS
    table = jnp.concatenate([ref[:, start:] for ref in refs[:-2]], axis=0).astype(jnp.float32)
    valid = table[:, 0:1]
    turn = table[:, 1:2] + 256.0 * table[:, 2:3]
    target = table[:, 3:4] + 256.0 * table[:, 4:5] + 65536.0 * table[:, 5:6]
    turns = advantages.shape[1]
    spot = lax.broadcasted_iota(jnp.int32, (table.shape[0], turns), 1)
    gain = jnp.sum(
        jnp.where(spot == turn.astype(jnp.int32), advantages[...], 0.0), axis=1, keepdims=True
    )
    weight = valid * gain / jnp.sum(valid)
    lane = lax.broadcasted_iota(jnp.int32, info.shape, 1)
    info[...] = jnp.where(lane == 0, weight, jnp.where(lane == 1, target, 0.0))


def reorder(stats, position, groups):
    lanes = stats.shape[1]
    lane = lax.broadcasted_iota(jnp.int32, stats.shape, 1)
    bit = 1
    while bit < groups:
        size = CAP * bit
        swapped = jnp.where(
            (lane & size) != 0,
            pltpu.roll(stats, size, 1),
            pltpu.roll(stats, lanes - size, 1),
        )
        stats = jnp.where((position & bit) != 0, swapped, stats)
        bit *= 2
    return stats


def all_rows(pieces, counts, place, width):
    start = sum(counts[:place])
    return jnp.concatenate([ref[:, :width] for ref in pieces[start:start + counts[place]]], axis=0)


def some_logits(counts, first, pieces, weight):
    blocks = 2 * len(counts)
    width = weight.shape[0] // blocks
    rank, total = coordinates()[0], None
    for place, block in enumerate(range(first, blocks, 2)):
        start = pl.multiple_of((rank ^ block) * width, width)
        part = jnp.dot(
            all_rows(pieces, counts, place, width),
            weight[pl.ds(start, width), :],
            preferred_element_type=jnp.float32,
        )
        total = part if total is None else total + part
    return total


def first_kernel(counts, weight, *refs):
    refs[-1][...] = some_logits(counts, 0, refs[:-1], weight)


def logits_kernel(counts, groups, info, partial, weight, *refs):
    pieces, (logits, stats) = refs[:-2], refs[-2:]
    _, position, shard = coordinates()
    total = partial[...] + some_logits(counts, 1, pieces, weight)
    logits[...] = total
    height, columns = total.shape
    target = info[:, 1:2].astype(jnp.int32) - shard * columns
    column = lax.broadcasted_iota(jnp.int32, total.shape, 1)
    hit = jnp.sum(jnp.where(column == target, total, 0.0), axis=1, keepdims=True)
    hit = jnp.sum(hit * info[:, 0:1])
    peak = jnp.max(total, axis=1, keepdims=True)
    mass = jnp.sum(jnp.exp(total - peak), axis=1, keepdims=True)
    lane = lax.broadcasted_iota(jnp.int32, (height, 128), 1)
    table = jnp.where(lane == 0, peak + jnp.log(mass), hit)
    table = reorder(jnp.transpose(table)[0:8], position, groups)
    line = jnp.concatenate([table[0:1], table[1:2, :LANES]], axis=1)
    stats[...] = jnp.broadcast_to(line[None], stats.shape)


def log_totals(groups, stats, height):
    parts = stats[:, :, :height]
    peak = jnp.max(parts, axis=0)
    line = peak + jnp.log(jnp.sum(jnp.exp(parts - peak[None]), axis=0))
    line = reorder(jnp.broadcast_to(line, (8, height)), coordinates()[1], groups)
    return jnp.transpose(jnp.concatenate([line] * 16, axis=0))


def grad_kernel(order, groups, info, mine, theirs, weight, other_weight, stats, *refs):
    logit_grad, table, outs = refs[0], refs[1], refs[2:]
    chunks = (outs[len(order):], outs[:len(order)])
    rank, _, shard = coordinates()
    height, columns = mine.shape
    part = height // 4
    table[...] = log_totals(groups, stats, height)
    log_total = table[:, 0:1]
    row_weight, target = info[:, 0:1], info[:, 1:2].astype(jnp.int32)

    def grad_of(logits, shard):
        column = lax.broadcasted_iota(jnp.int32, (height, columns), 1) + shard * columns
        probability = jnp.exp(logits[...] - log_total)
        return (
            grad_scale * row_weight * (probability - (column == target).astype(jnp.float32))
        ).astype(jnp.bfloat16)

    grad = grad_of(mine, shard)
    logit_grad[...] = grad
    grads = (grad, grad_of(theirs, shard ^ 1))
    width = outs[0].shape[1]
    for x in range(len(order) // 2):
        start = pl.multiple_of((rank ^ 2 * x) * width, width)
        weights = (weight[pl.ds(start, width), :], other_weight[x * width:(x + 1) * width, :])
        total = sum(
            lax.dot_general(g, w, (((1,), (1,)), ((), ())), preferred_element_type=jnp.float32)
            for g, w in zip(grads, weights)
        )
        for quarter in range(4):
            out = chunks[quarter % 2][order.index(2 * x + quarter // 2)]
            out[...] = total[quarter * part:(quarter + 1) * part].astype(out.dtype)


def weight_kernel(blocks, counts, skipped, after, logit_grad, *refs):
    pieces, (out, last, done, sems) = refs[skipped:-4], refs[-4:]
    rank = coordinates()[0]
    width = done.shape[0] // len(blocks)
    copies = []
    for place, block in enumerate(blocks):
        done[place * width:(place + 1) * width] = lax.dot_general(
            all_rows(pieces, counts, place, width),
            logit_grad[...],
            (((0,), (0,)), ((), ())),
            preferred_element_type=jnp.float32,
        ).astype(jnp.bfloat16)
        start = pl.multiple_of((rank ^ block) * width, width)
        copy = pltpu.make_async_copy(
            done.at[pl.ds(place * width, width)], out.at[pl.ds(start, width)], sems.at[place]
        )
        copy.start()
        copies.append(copy)
    if skipped:
        info, table, stats = refs[1:4]
        hits = jnp.sum(stats[:, :, info.shape[0]:], axis=0)
        loss = jnp.sum(info[:, 0:1] * table[:, 0:1]) - hits[0, 0]
        last[...] = jnp.full(last.shape, loss, jnp.float32)
    else:
        last[...] = jnp.zeros_like(last)
    for copy in copies:
        copy.wait()


def corner_kernel(count, after, kept, *refs):
    total = kept[...]
    for ref in refs[:count]:
        total = total + ref[...].astype(jnp.float32)
    for place, out in enumerate(refs[count:]):
        out[...] = total[place * CAP:(place + 1) * CAP].astype(out.dtype)


def unpack_kernel(last, chosen, *refs):
    out, loss = refs[-2:]
    loss[0, 0] = last[0, 0]
    total = sum(ref[...].astype(jnp.float32) for ref in refs[:-2])
    out[...] = lax.dot_general(
        chosen[...],
        total.astype(jnp.bfloat16),
        (((0,), (0,)), ((), ())),
        preferred_element_type=jnp.float32,
    ).astype(jnp.bfloat16)


def body(dps, ranks, hidden, weight, loss_mask, target_ids, turn_ids, advantages):
    tokens, width = hidden.shape
    depth, columns = weight.shape
    zs, xs = dps // 2, ranks // 2
    total_rows = dps * CAP
    bf16, f32, i32 = jnp.bfloat16, jnp.float32, jnp.int32
    shape = jax.ShapeDtypeStruct
    flops = 2 * total_rows * depth * columns

    def send(value, z=0, y=0, x=0, core=0):
        far, near = 2 * z + y, 2 * x + core
        pairs = [
            (d * ranks + v, (d ^ far) * ranks + (v ^ near))
            for d in range(dps)
            for v in range(ranks)
        ]
        return lax.ppermute(value, AXES, pairs)

    packed, own, chosen = call(
        pack_kernel,
        (
            in_hbm(hidden),
            in_hbm(loss_mask.reshape(1, tokens)),
            in_hbm(target_ids.reshape(1, tokens)),
            in_hbm(turn_ids.reshape(1, tokens)),
        ),
        [HBM] * 4,
        (
            shape((CAP, width + IDS), bf16),
            shape((CAP, width), bf16),
            shape((CAP, tokens), bf16),
        ),
        (VMEM,) * 3,
        [pltpu.VMEM((tokens, width), bf16)]
        + [pltpu.VMEM((1, tokens), i32)] * 3
        + [pltpu.SemaphoreType.DMA((4,))],
    )

    line_order = [0, *range(2, zs), 1]
    blocks = [send(packed, z=z) if z else packed for z in line_order[:-1]]
    corners = {x: send(own, y=1, x=x) for x in range(1, xs)}
    blocks.append(send(packed, z=1))
    line_rows = zs * CAP
    line, line_plain, far = call(
        functools.partial(join_kernel, line_order),
        (*blocks[:-1], *corners.values(), blocks[-1]),
        [VMEM] * (zs - 1) + [ANY] * len(corners) + [VMEM],
        (
            shape((line_rows, width + IDS), bf16),
            shape((line_rows, width), bf16),
            shape((line_rows - CAP, width), bf16),
        ),
        (VMEM,) * 3,
    )
    pieces = {(0, 1, 0): send(line, y=1)}
    for x in range(1, xs):
        pieces[2 * x, 0, 0] = send(line_plain, x=x)
        pieces[2 * x, 1, 0] = corners[x]
        pieces[2 * x, 1, 1] = send(far, y=1, x=x)
    held, away, same = call(
        functools.partial(stage_kernel, ranks),
        (line, in_hbm(weight)),
        [VMEM, HBM],
        (
            shape((depth, columns), bf16),
            shape((depth // 2, columns), bf16),
            shape(line.shape, bf16),
        ),
        (VMEM,) * 3,
        [pltpu.SemaphoreType.DMA((ranks + xs,))],
    )
    pieces[0, 0, 0] = same
    info = call(
        info_kernel,
        (same, pieces[0, 1, 0], advantages.reshape(1, -1)),
        [VMEM] * 3,
        shape((total_rows, 128), f32),
        VMEM,
    )

    def hold(value, after):
        like = shape(value.shape, value.dtype)
        return call(gate_kernel, (value, after), [ANY, ANY], like, ANY, aliases={0: 0})

    for x in range(1, xs):
        pieces[2 * x + 1, 1, 0] = send(pieces[2 * x, 1, 0], core=1)
        pieces[2 * x, 0, 0] = hold(pieces[2 * x, 0, 0], info)
        pieces[2 * x, 1, 1] = hold(pieces[2 * x, 1, 1], pieces[2 * x + 1, 1, 0])
    for b, y, part in list(pieces):
        if b % 2 == 0 and (b + 1, y, part) not in pieces:
            pieces[b + 1, y, part] = send(pieces[b, y, part], core=1)
    parted = [[pieces[key] for key in sorted(pieces) if key[0] == b] for b in range(ranks)]

    def rows_of(blocks):
        return [piece for b in blocks for piece in parted[b]]

    def counts_of(blocks):
        return [len(parted[b]) for b in blocks]

    near = range(0, ranks, 2)
    partial = call(
        functools.partial(first_kernel, counts_of(near)),
        (held, *rows_of(near)),
        [VMEM] * (1 + sum(counts_of(near))),
        shape((total_rows, columns), f32),
        VMEM,
        flops=flops // 2,
    )
    beside = range(1, ranks, 2)
    logits, stats = call(
        functools.partial(logits_kernel, counts_of(beside), dps),
        (info, partial, held, *rows_of(beside)),
        [VMEM] * (3 + sum(counts_of(beside))),
        (
            shape((total_rows, columns), f32),
            shape((dps * ranks, 1, total_rows + LANES), f32),
        ),
        (VMEM, VMEM),
        flops=flops // 2,
    )
    other_logits = send(logits, core=1)
    other_held = send(hold(away, stats), core=1)
    stats = lax.all_to_all(stats, AXES, 0, 0)
    rows_part = total_rows // 4
    order = sorted(range(1, ranks), key=lambda place: (-(place % 2 + (place > 1)), place)) + [0]
    outs = (shape((rows_part, width), bf16),) * (ranks - 1) + (shape((rows_part, width), f32),)
    logit_grad, table, *going = call(
        functools.partial(grad_kernel, order, dps),
        (info, logits, other_logits, held, other_held, stats),
        [VMEM] * 6,
        (shape((total_rows, columns), bf16), shape((total_rows, 128), f32)) + outs * 2,
        (VMEM,) * (2 + 2 * ranks),
        flops=flops,
    )
    def weight_part(first, after, *extra):
        blocks = range(first, first + ranks // 2)
        chosen_rows = rows_of(blocks)
        return call(
            functools.partial(weight_kernel, blocks, counts_of(blocks), len(extra)),
            (after, logit_grad, *extra, *chosen_rows),
            [ANY, VMEM] + [HBM] * (len(extra) > 0)
            + [VMEM] * (max(len(extra) - 1, 0) + len(chosen_rows)),
            (shape((depth, columns), bf16), shape((8, 128), f32)),
            (HBM, VMEM),
            [
                pltpu.VMEM((depth // 2, columns), bf16),
                pltpu.SemaphoreType.DMA((ranks // 2,)),
            ],
            flops=flops // 2,
            aliases={2: 0} if extra else {},
        )

    far_values, near_values = list(going[:ranks]), list(going[ranks:])
    weight_grad, finished = weight_part(0, far_values[-1])
    near_values[:-1] = call(
        gate_kernel,
        (*near_values[:-1], finished),
        [ANY] * ranks,
        outs[:-1],
        (ANY,) * (ranks - 1),
        aliases={place: place for place in range(ranks - 1)},
    )
    ends, sums = [None] * zs, [None, None]
    for chunk, values in ((1, far_values), (0, near_values)):
        sums[chunk] = [values[-1]]
        for place, value in zip(order, values):
            if place:
                sums[chunk].append(send(value, y=place % 2, x=place // 2))
    for chunk in (1, 0):
        near = chunk * zs // 2
        parts_z = call(
            functools.partial(corner_kernel, ranks - 1),
            (table, *sums[chunk]),
            [ANY] + [VMEM] * ranks,
            tuple(shape((CAP, width), bf16 if near + z else f32) for z in range(zs // 2)),
            (VMEM,) * (zs // 2),
        )
        for z, value in enumerate(parts_z):
            ends[near + z] = send(value, z=near + z) if near + z else value
    weight_grad, last = weight_part(ranks // 2, parts_z[0], weight_grad, info, table, stats)
    hidden_grad, loss = call(
        unpack_kernel,
        (last, chosen, *ends),
        [VMEM] * (2 + len(ends)),
        (shape((tokens, width), bf16), shape((1, 1), f32)),
        (VMEM, SMEM),
    )
    return loss[0, 0], hidden_grad, weight_grad


def solution(mesh):
    return jax.shard_map(
        functools.partial(body, mesh.shape["dp"], mesh.shape["vocab"]),
        mesh=mesh,
        in_specs=(P("dp", "vocab"), P(None, AXES), P("dp"), P("dp"), P("dp"), P()),
        out_specs=(P(), P("dp", "vocab"), P(None, AXES)),
        check_vma=False,
    )
```

```python
import functools
import math

import jax
import jax.numpy as jnp
from jax import lax
from jax.experimental import pallas as pl
from jax.experimental.pallas import tpu as pltpu
from jax.sharding import PartitionSpec as P

CAP = 32
MOST_VMEM = 56 * 1024 * 1024
IDS = 128
LANES = 128
grad_scale = 16384.0
AXES = ("dp", "vocab")
SMEM = pl.BlockSpec(memory_space=pltpu.SMEM)
VMEM = pl.BlockSpec(memory_space=pltpu.VMEM)
HBM = pl.BlockSpec(memory_space=pltpu.HBM)
ANY = pl.BlockSpec(memory_space=pl.ANY)


def size_of(value):
    return math.prod(value.shape) * jnp.dtype(value.dtype).itemsize


def call(kernel, operands, in_specs, out_shape, out_specs, scratch=(), spare=4, flops=0, aliases={}):
    outs = jax.tree.leaves(out_shape)
    sized = [v for v, s in zip(operands, in_specs) if s is VMEM]
    sized += [v for v, s in zip(outs, jax.tree.leaves(out_specs)) if s is VMEM]
    held = [s for s in scratch if getattr(s, "memory_space", None) == pltpu.VMEM]
    total = sum(size_of(v) for v in sized) + sum(size_of(s) for s in held)
    return pl.pallas_call(
        kernel,
        out_shape=out_shape,
        in_specs=in_specs,
        out_specs=out_specs,
        scratch_shapes=scratch,
        input_output_aliases=aliases,
        compiler_params=pltpu.CompilerParams(vmem_limit_bytes=min(total + spare * 1024 * 1024, MOST_VMEM)),
        cost_estimate=pl.CostEstimate(
            flops=flops,
            bytes_accessed=sum(size_of(v) for v in list(operands) + outs),
            transcendentals=0,
        ),
    )(*operands)


def in_hbm(value):
    return pltpu.with_memory_space_constraint(value, pltpu.HBM)


def coordinates():
    group, rank = lax.axis_index("dp"), lax.axis_index("vocab")
    groups, ranks = lax.axis_size("dp"), lax.axis_size("vocab")
    position = group % 2 * (groups // 2) + group // 2
    return rank, position, group * ranks + rank


def choose(mask):
    tokens = mask.shape[1]
    wide = jnp.broadcast_to(mask.astype(jnp.float32), (8, tokens))
    before = lax.broadcasted_iota(jnp.int32, (tokens, tokens), 0)
    after = lax.broadcasted_iota(jnp.int32, (tokens, tokens), 1)
    upto = (before <= after).astype(jnp.float32)
    slot = jnp.dot(
        wide.astype(jnp.bfloat16), upto.astype(jnp.bfloat16), preferred_element_type=jnp.float32
    )[0:1]
    grid = lax.broadcasted_iota(jnp.int32, (CAP, tokens), 0) + 1
    return (slot.astype(jnp.int32) == grid) & (mask == 1)


def pack_kernel(hidden_hbm, mask_hbm, target_hbm, turn_hbm, rows, plain, chosen_out, *scratch):
    hidden, mask, target, turn, sems = scratch
    copies = []
    for place, (source, held) in enumerate(
        ((mask_hbm, mask), (target_hbm, target), (turn_hbm, turn), (hidden_hbm, hidden))
    ):
        copy = pltpu.make_async_copy(source, held, sems.at[place])
        copy.start()
        copies.append(copy)
    for copy in copies[:3]:
        copy.wait()
    width = hidden.shape[1]
    chosen = choose(mask[...])
    one_hot = chosen.astype(jnp.float32).astype(jnp.bfloat16)
    chosen_out[...] = one_hot
    turns, targets = turn[...], target[...]
    fields = (
        mask[...],
        turns & 255,
        turns >> 8,
        targets & 255,
        (targets >> 8) & 255,
        targets >> 16,
    )
    lane = lax.broadcasted_iota(jnp.int32, (CAP, IDS), 1)
    table = jnp.zeros((CAP, IDS), jnp.float32)
    for place, field in enumerate(fields):
        picked = jnp.where(chosen, field.astype(jnp.float32), 0.0)
        table = jnp.where(lane == place, jnp.sum(picked, axis=1, keepdims=True), table)
    rows[:, width:] = table.astype(jnp.bfloat16)
    copies[3].wait()
    packed = jnp.dot(one_hot, hidden[...], preferred_element_type=jnp.float32)
    packed = packed.astype(jnp.bfloat16)
    rows[:, :width] = packed
    plain[...] = packed


def join_kernel(order, *refs):
    blocks, (line, plain, far) = refs[:len(order) - 1] + refs[-4:-3], refs[-3:]
    width = plain.shape[1]
    for place, block in zip(order, blocks):
        rows = slice(place * CAP, (place + 1) * CAP)
        line[rows] = block[...]
        plain[rows] = block[:, :width]
        if place:
            far[(place - 1) * CAP:place * CAP] = block[:, :width]


def stage_kernel(blocks, line, weight, held, away, same, sems):
    rank = coordinates()[0]
    width = weight.shape[0] // blocks
    copies = []
    for block in list(range(1, blocks, 2)) + list(range(0, blocks, 2)):
        start = pl.multiple_of((rank ^ block) * width, width)
        targets = [held.at[pl.ds(start, width)]]
        if block % 2:
            targets.append(away.at[pl.ds(block // 2 * width, width)])
        for target in targets:
            copy = pltpu.make_async_copy(
                weight.at[pl.ds(start, width)], target, sems.at[len(copies)]
            )
            copy.start()
            copies.append(copy)
    same[...] = line[...]
    for copy in copies:
        copy.wait()


def gate_kernel(*refs):
    pass


def info_kernel(*refs):
    advantages, info = refs[-2:]
    start = refs[0].shape[1] - IDS
    table = jnp.concatenate([ref[:, start:] for ref in refs[:-2]], axis=0).astype(jnp.float32)
    valid = table[:, 0:1]
    turn = table[:, 1:2] + 256.0 * table[:, 2:3]
    target = table[:, 3:4] + 256.0 * table[:, 4:5] + 65536.0 * table[:, 5:6]
    turns = advantages.shape[1]
    spot = lax.broadcasted_iota(jnp.int32, (table.shape[0], turns), 1)
    gain = jnp.sum(
        jnp.where(spot == turn.astype(jnp.int32), advantages[...], 0.0), axis=1, keepdims=True
    )
    weight = valid * gain / jnp.sum(valid)
    lane = lax.broadcasted_iota(jnp.int32, info.shape, 1)
    info[...] = jnp.where(lane == 0, weight, jnp.where(lane == 1, target, 0.0))


def reorder(stats, position, groups):
    lanes = stats.shape[1]
    lane = lax.broadcasted_iota(jnp.int32, stats.shape, 1)
    bit = 1
    while bit < groups:
        size = CAP * bit
        swapped = jnp.where(
            (lane & size) != 0,
            pltpu.roll(stats, size, 1),
            pltpu.roll(stats, lanes - size, 1),
        )
        stats = jnp.where((position & bit) != 0, swapped, stats)
        bit *= 2
    return stats


def all_rows(pieces, counts, place, width):
    start = sum(counts[:place])
    return jnp.concatenate([ref[:, :width] for ref in pieces[start:start + counts[place]]], axis=0)


def some_logits(blocks, counts, ranks, pieces, weight):
    width = weight.shape[0] // ranks
    rank, total = coordinates()[0], None
    for place, block in enumerate(blocks):
        start = pl.multiple_of((rank ^ block) * width, width)
        part = jnp.dot(
            all_rows(pieces, counts, place, width),
            weight[pl.ds(start, width), :],
            preferred_element_type=jnp.float32,
        )
        total = part if total is None else total + part
    return total


def first_kernel(blocks, counts, ranks, weight, *refs):
    refs[-1][...] = some_logits(blocks, counts, ranks, refs[:-1], weight)


def logits_kernel(blocks, counts, ranks, groups, info, partial, weight, *refs):
    pieces, (logits, stats) = refs[:-2], refs[-2:]
    _, position, shard = coordinates()
    total = partial[...] + some_logits(blocks, counts, ranks, pieces, weight)
    logits[...] = total
    height, columns = total.shape
    target = info[:, 1:2].astype(jnp.int32) - shard * columns
    column = lax.broadcasted_iota(jnp.int32, total.shape, 1)
    hit = jnp.sum(jnp.where(column == target, total, 0.0), axis=1, keepdims=True)
    hit = jnp.sum(hit * info[:, 0:1])
    peak = jnp.max(total, axis=1, keepdims=True)
    mass = jnp.sum(jnp.exp(total - peak), axis=1, keepdims=True)
    lane = lax.broadcasted_iota(jnp.int32, (height, 128), 1)
    table = jnp.where(lane == 0, peak + jnp.log(mass), hit)
    table = reorder(jnp.transpose(table)[0:8], position, groups)
    line = jnp.concatenate([table[0:1], table[1:2, :LANES]], axis=1)
    stats[...] = jnp.broadcast_to(line[None], stats.shape)


def log_totals(groups, stats, height):
    parts = stats[:, :, :height]
    peak = jnp.max(parts, axis=0)
    line = peak + jnp.log(jnp.sum(jnp.exp(parts - peak[None]), axis=0))
    line = reorder(jnp.broadcast_to(line, (8, height)), coordinates()[1], groups)
    return jnp.transpose(jnp.concatenate([line] * 16, axis=0))


def grad_kernel(order, groups, info, mine, theirs, weight, other_weight, stats, *refs):
    logit_grad, table, outs = refs[0], refs[1], refs[2:]
    chunks = (outs[len(order):], outs[:len(order)])
    rank, _, shard = coordinates()
    height, columns = mine.shape
    part = height // 4
    table[...] = log_totals(groups, stats, height)
    log_total = table[:, 0:1]
    row_weight, target = info[:, 0:1], info[:, 1:2].astype(jnp.int32)

    def grad_of(logits, shard):
        column = lax.broadcasted_iota(jnp.int32, (height, columns), 1) + shard * columns
        probability = jnp.exp(logits[...] - log_total)
        return (
            grad_scale * row_weight * (probability - (column == target).astype(jnp.float32))
        ).astype(jnp.bfloat16)

    grad = grad_of(mine, shard)
    logit_grad[...] = grad
    grads = (grad, grad_of(theirs, shard ^ 1))
    width = outs[0].shape[1]
    for x in range(len(order) // 2):
        start = pl.multiple_of((rank ^ 2 * x) * width, width)
        weights = (weight[pl.ds(start, width), :], other_weight[x * width:(x + 1) * width, :])
        total = sum(
            lax.dot_general(g, w, (((1,), (1,)), ((), ())), preferred_element_type=jnp.float32)
            for g, w in zip(grads, weights)
        )
        for quarter in range(4):
            out = chunks[quarter % 2][order.index(2 * x + quarter // 2)]
            out[...] = total[quarter * part:(quarter + 1) * part].astype(out.dtype)


def weight_kernel(blocks, counts, skipped, after, logit_grad, *refs):
    pieces, (out, last, done, sems) = refs[skipped:-4], refs[-4:]
    rank = coordinates()[0]
    width = done.shape[0] // len(blocks)
    copies = []
    for place, block in enumerate(blocks):
        done[place * width:(place + 1) * width] = lax.dot_general(
            all_rows(pieces, counts, place, width),
            logit_grad[...],
            (((0,), (0,)), ((), ())),
            preferred_element_type=jnp.float32,
        ).astype(jnp.bfloat16)
        start = pl.multiple_of((rank ^ block) * width, width)
        copy = pltpu.make_async_copy(
            done.at[pl.ds(place * width, width)], out.at[pl.ds(start, width)], sems.at[place]
        )
        copy.start()
        copies.append(copy)
    if skipped:
        info, table, stats = refs[1:4]
        hits = jnp.sum(stats[:, :, info.shape[0]:], axis=0)
        loss = jnp.sum(info[:, 0:1] * table[:, 0:1]) - hits[0, 0]
        last[...] = jnp.full(last.shape, loss, jnp.float32)
    else:
        last[...] = jnp.zeros_like(last)
    for copy in copies:
        copy.wait()


def corner_kernel(count, after, kept, *refs):
    total = kept[...]
    for ref in refs[:count]:
        total = total + ref[...].astype(jnp.float32)
    for place, out in enumerate(refs[count:]):
        out[...] = total[place * CAP:(place + 1) * CAP].astype(out.dtype)


def unpack_kernel(last, chosen, *refs):
    out, loss = refs[-2:]
    loss[0, 0] = last[0, 0]
    total = sum(ref[...].astype(jnp.float32) for ref in refs[:-2])
    out[...] = lax.dot_general(
        chosen[...],
        total.astype(jnp.bfloat16),
        (((0,), (0,)), ((), ())),
        preferred_element_type=jnp.float32,
    ).astype(jnp.bfloat16)


def body(dps, ranks, hidden, weight, loss_mask, target_ids, turn_ids, advantages):
    tokens, width = hidden.shape
    depth, columns = weight.shape
    zs, xs = dps // 2, ranks // 2
    total_rows = dps * CAP
    bf16, f32, i32 = jnp.bfloat16, jnp.float32, jnp.int32
    shape = jax.ShapeDtypeStruct
    flops = 2 * total_rows * depth * columns

    def send(value, z=0, y=0, x=0, core=0):
        far, near = 2 * z + y, 2 * x + core
        pairs = [
            (d * ranks + v, (d ^ far) * ranks + (v ^ near))
            for d in range(dps)
            for v in range(ranks)
        ]
        return lax.ppermute(value, AXES, pairs)

    packed, own, chosen = call(
        pack_kernel,
        (
            in_hbm(hidden),
            in_hbm(loss_mask.reshape(1, tokens)),
            in_hbm(target_ids.reshape(1, tokens)),
            in_hbm(turn_ids.reshape(1, tokens)),
        ),
        [HBM] * 4,
        (
            shape((CAP, width + IDS), bf16),
            shape((CAP, width), bf16),
            shape((CAP, tokens), bf16),
        ),
        (VMEM,) * 3,
        [pltpu.VMEM((tokens, width), bf16)]
        + [pltpu.VMEM((1, tokens), i32)] * 3
        + [pltpu.SemaphoreType.DMA((4,))],
    )

    line_order = [0, *range(2, zs), 1]
    blocks = [send(packed, z=z) if z else packed for z in line_order[:-1]]
    corners = {x: send(own, y=1, x=x) for x in range(1, xs)}
    blocks.append(send(packed, z=1))
    line_rows = zs * CAP
    line, line_plain, far = call(
        functools.partial(join_kernel, line_order),
        (*blocks[:-1], *corners.values(), blocks[-1]),
        [VMEM] * (zs - 1) + [ANY] * len(corners) + [VMEM],
        (
            shape((line_rows, width + IDS), bf16),
            shape((line_rows, width), bf16),
            shape((line_rows - CAP, width), bf16),
        ),
        (VMEM,) * 3,
    )
    pieces = {(0, 1, 0): send(line, y=1)}
    for x in range(1, xs):
        pieces[2 * x, 0, 0] = send(line_plain, x=x)
        pieces[2 * x, 1, 0] = corners[x]
        pieces[2 * x, 1, 1] = send(far, y=1, x=x)
    held, away, same = call(
        functools.partial(stage_kernel, ranks),
        (line, in_hbm(weight)),
        [VMEM, HBM],
        (
            shape((depth, columns), bf16),
            shape((depth // 2, columns), bf16),
            shape(line.shape, bf16),
        ),
        (VMEM,) * 3,
        [pltpu.SemaphoreType.DMA((ranks + xs,))],
    )
    pieces[0, 0, 0] = same
    info = call(
        info_kernel,
        (same, pieces[0, 1, 0], advantages.reshape(1, -1)),
        [VMEM] * 3,
        shape((total_rows, 128), f32),
        VMEM,
    )

    def hold(value, after):
        like = shape(value.shape, value.dtype)
        return call(gate_kernel, (value, after), [ANY, ANY], like, ANY, aliases={0: 0})

    def part_logits(kernel, blocks, operands, out_shapes):
        parts = [[pieces[key] for key in sorted(pieces) if key[0] == b] for b in blocks]
        operands = (*operands, held, *(piece for part in parts for piece in part))
        return call(
            functools.partial(kernel, blocks, [len(part) for part in parts], ranks),
            operands,
            [VMEM] * len(operands),
            out_shapes,
            jax.tree.map(lambda _: VMEM, out_shapes),
            flops=flops * len(blocks) // ranks,
        )

    for x in range(1, xs):
        pieces[2 * x + 1, 1, 0] = send(pieces[2 * x, 1, 0], core=1)
        pieces[2 * x, 0, 0] = hold(pieces[2 * x, 0, 0], info)
        pieces[2 * x, 1, 1] = hold(pieces[2 * x, 1, 1], pieces[2 * x + 1, 1, 0])
    for b, y, part in list(pieces):
        if b % 2 == 0 and (b + 1, y, part) not in pieces:
            pieces[b + 1, y, part] = send(pieces[b, y, part], core=1)

    logits_shape = shape((total_rows, columns), f32)
    partial = part_logits(first_kernel, [*range(0, ranks, 2), 1], (), logits_shape)
    logits, stats = part_logits(
        lambda blocks, counts, ranks, *refs: logits_kernel(blocks, counts, ranks, dps, *refs),
        list(range(3, ranks, 2)),
        (info, partial),
        (logits_shape, shape((dps * ranks, 1, total_rows + LANES), f32)),
    )
    parted = [[pieces[key] for key in sorted(pieces) if key[0] == b] for b in range(ranks)]

    def rows_of(blocks):
        return [piece for b in blocks for piece in parted[b]]

    def counts_of(blocks):
        return [len(parted[b]) for b in blocks]

    other_logits = send(logits, core=1)
    other_held = send(hold(away, stats), core=1)
    stats = lax.all_to_all(stats, AXES, 0, 0)
    rows_part = total_rows // 4
    order = sorted(range(1, ranks), key=lambda place: (-(place % 2 + (place > 1)), place)) + [0]
    outs = (shape((rows_part, width), bf16),) * (ranks - 1) + (shape((rows_part, width), f32),)
    logit_grad, table, *going = call(
        functools.partial(grad_kernel, order, dps),
        (info, logits, other_logits, held, other_held, stats),
        [VMEM] * 6,
        (shape((total_rows, columns), bf16), shape((total_rows, 128), f32)) + outs * 2,
        (VMEM,) * (2 + 2 * ranks),
        flops=flops,
    )
    def weight_part(first, after, *extra):
        blocks = range(first, first + ranks // 2)
        chosen_rows = rows_of(blocks)
        return call(
            functools.partial(weight_kernel, blocks, counts_of(blocks), len(extra)),
            (after, logit_grad, *extra, *chosen_rows),
            [ANY, VMEM] + [HBM] * (len(extra) > 0)
            + [VMEM] * (max(len(extra) - 1, 0) + len(chosen_rows)),
            (shape((depth, columns), bf16), shape((8, 128), f32)),
            (HBM, VMEM),
            [
                pltpu.VMEM((depth // 2, columns), bf16),
                pltpu.SemaphoreType.DMA((ranks // 2,)),
            ],
            flops=flops // 2,
            aliases={2: 0} if extra else {},
        )

    far_values, near_values = list(going[:ranks]), list(going[ranks:])
    weight_grad, finished = weight_part(0, far_values[-1])
    near_values[:-1] = call(
        gate_kernel,
        (*near_values[:-1], finished),
        [ANY] * ranks,
        outs[:-1],
        (ANY,) * (ranks - 1),
        aliases={place: place for place in range(ranks - 1)},
    )
    ends, sums = [None] * zs, [None, None]
    for chunk, values in ((1, far_values), (0, near_values)):
        sums[chunk] = [values[-1]]
        for place, value in zip(order, values):
            if place:
                sums[chunk].append(send(value, y=place % 2, x=place // 2))
    for chunk in (1, 0):
        near = chunk * zs // 2
        parts_z = call(
            functools.partial(corner_kernel, ranks - 1),
            (table, *sums[chunk]),
            [ANY] + [VMEM] * ranks,
            tuple(shape((CAP, width), bf16 if near + z else f32) for z in range(zs // 2)),
            (VMEM,) * (zs // 2),
        )
        for z, value in enumerate(parts_z):
            ends[near + z] = send(value, z=near + z) if near + z else value
    weight_grad, last = weight_part(ranks // 2, parts_z[0], weight_grad, info, table, stats)
    hidden_grad, loss = call(
        unpack_kernel,
        (last, chosen, *ends),
        [VMEM] * (2 + len(ends)),
        (shape((tokens, width), bf16), shape((1, 1), f32)),
        (VMEM, SMEM),
    )
    return loss[0, 0], hidden_grad, weight_grad


def solution(mesh):
    return jax.shard_map(
        functools.partial(body, mesh.shape["dp"], mesh.shape["vocab"]),
        mesh=mesh,
        in_specs=(P("dp", "vocab"), P(None, AXES), P("dp"), P("dp"), P("dp"), P()),
        out_specs=(P(), P("dp", "vocab"), P(None, AXES)),
        check_vma=False,
    )
```

```python
import functools
import math

import jax
import jax.numpy as jnp
from jax import lax
from jax.experimental import pallas as pl
from jax.experimental.pallas import tpu as pltpu
from jax.sharding import PartitionSpec as P

CAP = 32
MOST_VMEM = 56 * 1024 * 1024
IDS = 128
LANES = 128
grad_scale = 16384.0
AXES = ("dp", "vocab")
SMEM = pl.BlockSpec(memory_space=pltpu.SMEM)
VMEM = pl.BlockSpec(memory_space=pltpu.VMEM)
HBM = pl.BlockSpec(memory_space=pltpu.HBM)
ANY = pl.BlockSpec(memory_space=pl.ANY)


def size_of(value):
    return math.prod(value.shape) * jnp.dtype(value.dtype).itemsize


def call(kernel, operands, in_specs, out_shape, out_specs, scratch=(), spare=4, flops=0, aliases={}):
    outs = jax.tree.leaves(out_shape)
    sized = [v for v, s in zip(operands, in_specs) if s is VMEM]
    sized += [v for v, s in zip(outs, jax.tree.leaves(out_specs)) if s is VMEM]
    held = [s for s in scratch if getattr(s, "memory_space", None) == pltpu.VMEM]
    total = sum(size_of(v) for v in sized) + sum(size_of(s) for s in held)
    return pl.pallas_call(
        kernel,
        out_shape=out_shape,
        in_specs=in_specs,
        out_specs=out_specs,
        scratch_shapes=scratch,
        input_output_aliases=aliases,
        compiler_params=pltpu.CompilerParams(vmem_limit_bytes=min(total + spare * 1024 * 1024, MOST_VMEM)),
        cost_estimate=pl.CostEstimate(
            flops=flops,
            bytes_accessed=sum(size_of(v) for v in list(operands) + outs),
            transcendentals=0,
        ),
    )(*operands)


def in_hbm(value):
    return pltpu.with_memory_space_constraint(value, pltpu.HBM)


def coordinates():
    group, rank = lax.axis_index("dp"), lax.axis_index("vocab")
    groups, ranks = lax.axis_size("dp"), lax.axis_size("vocab")
    position = group % 2 * (groups // 2) + group // 2
    return rank, position, group * ranks + rank


def choose(mask):
    tokens = mask.shape[1]
    wide = jnp.broadcast_to(mask.astype(jnp.float32), (8, tokens))
    before = lax.broadcasted_iota(jnp.int32, (tokens, tokens), 0)
    after = lax.broadcasted_iota(jnp.int32, (tokens, tokens), 1)
    upto = (before <= after).astype(jnp.float32)
    slot = jnp.dot(
        wide.astype(jnp.bfloat16), upto.astype(jnp.bfloat16), preferred_element_type=jnp.float32
    )[0:1]
    grid = lax.broadcasted_iota(jnp.int32, (CAP, tokens), 0) + 1
    return (slot.astype(jnp.int32) == grid) & (mask == 1)


def pack_kernel(hidden_hbm, mask_hbm, target_hbm, turn_hbm, rows, plain, chosen_out, *scratch):
    hidden, mask, target, turn, sems = scratch
    copies = []
    for place, (source, held) in enumerate(
        ((mask_hbm, mask), (target_hbm, target), (turn_hbm, turn), (hidden_hbm, hidden))
    ):
        copy = pltpu.make_async_copy(source, held, sems.at[place])
        copy.start()
        copies.append(copy)
    for copy in copies[:3]:
        copy.wait()
    width = hidden.shape[1]
    chosen = choose(mask[...])
    one_hot = chosen.astype(jnp.float32).astype(jnp.bfloat16)
    chosen_out[...] = one_hot
    turns, targets = turn[...], target[...]
    fields = (
        mask[...],
        turns & 255,
        turns >> 8,
        targets & 255,
        (targets >> 8) & 255,
        targets >> 16,
    )
    lane = lax.broadcasted_iota(jnp.int32, (CAP, IDS), 1)
    table = jnp.zeros((CAP, IDS), jnp.float32)
    for place, field in enumerate(fields):
        picked = jnp.where(chosen, field.astype(jnp.float32), 0.0)
        table = jnp.where(lane == place, jnp.sum(picked, axis=1, keepdims=True), table)
    rows[:, width:] = table.astype(jnp.bfloat16)
    copies[3].wait()
    packed = jnp.dot(one_hot, hidden[...], preferred_element_type=jnp.float32)
    packed = packed.astype(jnp.bfloat16)
    rows[:, :width] = packed
    plain[...] = packed


def join_kernel(order, *refs):
    blocks, (line, plain, far) = refs[:len(order) - 1] + refs[-4:-3], refs[-3:]
    width = plain.shape[1]
    for place, block in zip(order, blocks):
        rows = slice(place * CAP, (place + 1) * CAP)
        line[rows] = block[...]
        plain[rows] = block[:, :width]
        if place:
            far[(place - 1) * CAP:place * CAP] = block[:, :width]


def stage_kernel(blocks, line, weight, held, away, same, sems):
    rank = coordinates()[0]
    width = weight.shape[0] // blocks
    copies = []
    for block in list(range(1, blocks, 2)) + list(range(0, blocks, 2)):
        start = pl.multiple_of((rank ^ block) * width, width)
        targets = [held.at[pl.ds(start, width)]]
        if block % 2:
            targets.append(away.at[pl.ds(block // 2 * width, width)])
        for target in targets:
            copy = pltpu.make_async_copy(
                weight.at[pl.ds(start, width)], target, sems.at[len(copies)]
            )
            copy.start()
            copies.append(copy)
    same[...] = line[...]
    for copy in copies:
        copy.wait()


def gate_kernel(*refs):
    pass


def info_kernel(*refs):
    advantages, info = refs[-2:]
    start = refs[0].shape[1] - IDS
    table = jnp.concatenate([ref[:, start:] for ref in refs[:-2]], axis=0).astype(jnp.float32)
    valid = table[:, 0:1]
    turn = table[:, 1:2] + 256.0 * table[:, 2:3]
    target = table[:, 3:4] + 256.0 * table[:, 4:5] + 65536.0 * table[:, 5:6]
    turns = advantages.shape[1]
    spot = lax.broadcasted_iota(jnp.int32, (table.shape[0], turns), 1)
    gain = jnp.sum(
        jnp.where(spot == turn.astype(jnp.int32), advantages[...], 0.0), axis=1, keepdims=True
    )
    weight = valid * gain / jnp.sum(valid)
    lane = lax.broadcasted_iota(jnp.int32, info.shape, 1)
    info[...] = jnp.where(lane == 0, weight, jnp.where(lane == 1, target, 0.0))


def reorder(stats, position, groups):
    lanes = stats.shape[1]
    lane = lax.broadcasted_iota(jnp.int32, stats.shape, 1)
    bit = 1
    while bit < groups:
        size = CAP * bit
        swapped = jnp.where(
            (lane & size) != 0,
            pltpu.roll(stats, size, 1),
            pltpu.roll(stats, lanes - size, 1),
        )
        stats = jnp.where((position & bit) != 0, swapped, stats)
        bit *= 2
    return stats


def all_rows(pieces, counts, place, width):
    start = sum(counts[:place])
    return jnp.concatenate([ref[:, :width] for ref in pieces[start:start + counts[place]]], axis=0)


def some_logits(blocks, counts, ranks, pieces, weight):
    width = weight.shape[0] // ranks
    rank, total = coordinates()[0], None
    for place, block in enumerate(blocks):
        start = pl.multiple_of((rank ^ block) * width, width)
        part = jnp.dot(
            all_rows(pieces, counts, place, width),
            weight[pl.ds(start, width), :],
            preferred_element_type=jnp.float32,
        )
        total = part if total is None else total + part
    return total


def first_kernel(blocks, counts, ranks, weight, *refs):
    refs[-1][...] = some_logits(blocks, counts, ranks, refs[:-1], weight)


def logits_kernel(blocks, counts, ranks, groups, info, partial, weight, *refs):
    pieces, (logits, stats) = refs[:-2], refs[-2:]
    _, position, shard = coordinates()
    total = partial[...] + some_logits(blocks, counts, ranks, pieces, weight)
    logits[...] = total
    height, columns = total.shape
    target = info[:, 1:2].astype(jnp.int32) - shard * columns
    column = lax.broadcasted_iota(jnp.int32, total.shape, 1)
    hit = jnp.sum(jnp.where(column == target, total, 0.0), axis=1, keepdims=True)
    hit = jnp.sum(hit * info[:, 0:1])
    peak = jnp.max(total, axis=1, keepdims=True)
    mass = jnp.sum(jnp.exp(total - peak), axis=1, keepdims=True)
    lane = lax.broadcasted_iota(jnp.int32, (height, 128), 1)
    table = jnp.where(lane == 0, peak + jnp.log(mass), hit)
    table = reorder(jnp.transpose(table)[0:8], position, groups)
    line = jnp.concatenate([table[0:1], table[1:2, :LANES]], axis=1)
    stats[...] = jnp.broadcast_to(line[None], stats.shape)


def log_totals(groups, stats, height):
    parts = stats[:, :, :height]
    peak = jnp.max(parts, axis=0)
    line = peak + jnp.log(jnp.sum(jnp.exp(parts - peak[None]), axis=0))
    line = reorder(jnp.broadcast_to(line, (8, height)), coordinates()[1], groups)
    return jnp.transpose(jnp.concatenate([line] * 16, axis=0))


def grad_kernel(order, groups, info, mine, theirs, weight, other_weight, stats, *refs):
    logit_grad, table, outs = refs[0], refs[1], refs[2:]
    chunks = (outs[len(order):], outs[:len(order)])
    rank, _, shard = coordinates()
    height, columns = mine.shape
    part = height // 4
    table[...] = log_totals(groups, stats, height)
    log_total = table[:, 0:1]
    row_weight, target = info[:, 0:1], info[:, 1:2].astype(jnp.int32)

    def grad_of(logits, shard):
        column = lax.broadcasted_iota(jnp.int32, (height, columns), 1) + shard * columns
        probability = jnp.exp(logits[...] - log_total)
        return (
            grad_scale * row_weight * (probability - (column == target).astype(jnp.float32))
        ).astype(jnp.bfloat16)

    grad = grad_of(mine, shard)
    logit_grad[...] = grad
    grads = (grad, grad_of(theirs, shard ^ 1))
    width = outs[0].shape[1]
    for x in range(len(order) // 2):
        start = pl.multiple_of((rank ^ 2 * x) * width, width)
        weights = (weight[pl.ds(start, width), :], other_weight[x * width:(x + 1) * width, :])
        total = sum(
            lax.dot_general(g, w, (((1,), (1,)), ((), ())), preferred_element_type=jnp.float32)
            for g, w in zip(grads, weights)
        )
        for quarter in range(4):
            out = chunks[quarter % 2][order.index(2 * x + quarter // 2)]
            out[...] = total[quarter * part:(quarter + 1) * part].astype(out.dtype)


def weight_kernel(blocks, counts, skipped, after, logit_grad, *refs):
    results = 5 if skipped else 4
    pieces, (out, last, *loss, done, sems) = refs[skipped:-results], refs[-results:]
    rank = coordinates()[0]
    width = done.shape[0] // len(blocks)
    copies = []
    for place, block in enumerate(blocks):
        done[place * width:(place + 1) * width] = lax.dot_general(
            all_rows(pieces, counts, place, width),
            logit_grad[...],
            (((0,), (0,)), ((), ())),
            preferred_element_type=jnp.float32,
        ).astype(jnp.bfloat16)
        start = pl.multiple_of((rank ^ block) * width, width)
        copy = pltpu.make_async_copy(
            done.at[pl.ds(place * width, width)], out.at[pl.ds(start, width)], sems.at[place]
        )
        copy.start()
        copies.append(copy)
    if skipped:
        info, table, stats = refs[1:4]
        hits = jnp.sum(stats[:, :, info.shape[0]:], axis=0)
        loss[0][0, 0] = jnp.sum(info[:, 0:1] * table[:, 0:1]) - hits[0, 0]
    last[...] = jnp.zeros_like(last)
    for copy in copies:
        copy.wait()


def corner_kernel(count, after, kept, *refs):
    total = kept[...]
    for ref in refs[:count]:
        total = total + ref[...].astype(jnp.float32)
    for place, out in enumerate(refs[count:]):
        out[...] = total[place * CAP:(place + 1) * CAP].astype(out.dtype)


def unpack_kernel(after, chosen, *refs):
    ends, (out, held, sems) = refs[:-3], refs[-3:]
    half = held.shape[1] // 2
    copies = []
    for place in range(2):
        lanes = pl.ds(place * half, half)
        total = sum(ref[:, lanes].astype(jnp.float32) for ref in ends)
        held[:, lanes] = lax.dot_general(
            chosen[...],
            total.astype(jnp.bfloat16),
            (((0,), (0,)), ((), ())),
            preferred_element_type=jnp.float32,
        ).astype(jnp.bfloat16)
        copy = pltpu.make_async_copy(held.at[:, lanes], out.at[:, lanes], sems.at[place])
        copy.start()
        copies.append(copy)
    for copy in copies:
        copy.wait()


def body(dps, ranks, hidden, weight, loss_mask, target_ids, turn_ids, advantages):
    tokens, width = hidden.shape
    depth, columns = weight.shape
    zs, xs = dps // 2, ranks // 2
    total_rows = dps * CAP
    bf16, f32, i32 = jnp.bfloat16, jnp.float32, jnp.int32
    shape = jax.ShapeDtypeStruct
    flops = 2 * total_rows * depth * columns

    def send(value, z=0, y=0, x=0, core=0):
        far, near = 2 * z + y, 2 * x + core
        pairs = [
            (d * ranks + v, (d ^ far) * ranks + (v ^ near))
            for d in range(dps)
            for v in range(ranks)
        ]
        return lax.ppermute(value, AXES, pairs)

    packed, own, chosen = call(
        pack_kernel,
        (
            in_hbm(hidden),
            in_hbm(loss_mask.reshape(1, tokens)),
            in_hbm(target_ids.reshape(1, tokens)),
            in_hbm(turn_ids.reshape(1, tokens)),
        ),
        [HBM] * 4,
        (
            shape((CAP, width + IDS), bf16),
            shape((CAP, width), bf16),
            shape((CAP, tokens), bf16),
        ),
        (VMEM,) * 3,
        [pltpu.VMEM((tokens, width), bf16)]
        + [pltpu.VMEM((1, tokens), i32)] * 3
        + [pltpu.SemaphoreType.DMA((4,))],
    )

    line_order = [0, *range(2, zs), 1]
    blocks = [send(packed, z=z) if z else packed for z in line_order[:-1]]
    corners = {x: send(own, y=1, x=x) for x in range(1, xs)}
    blocks.append(send(packed, z=1))
    line_rows = zs * CAP
    line, line_plain, far = call(
        functools.partial(join_kernel, line_order),
        (*blocks[:-1], *corners.values(), blocks[-1]),
        [VMEM] * (zs - 1) + [ANY] * len(corners) + [VMEM],
        (
            shape((line_rows, width + IDS), bf16),
            shape((line_rows, width), bf16),
            shape((line_rows - CAP, width), bf16),
        ),
        (VMEM,) * 3,
    )
    pieces = {(0, 1, 0): send(line, y=1)}
    for x in range(1, xs):
        pieces[2 * x, 0, 0] = send(line_plain, x=x)
        pieces[2 * x, 1, 0] = corners[x]
        pieces[2 * x, 1, 1] = send(far, y=1, x=x)
    held, away, same = call(
        functools.partial(stage_kernel, ranks),
        (line, in_hbm(weight)),
        [VMEM, HBM],
        (
            shape((depth, columns), bf16),
            shape((depth // 2, columns), bf16),
            shape(line.shape, bf16),
        ),
        (VMEM,) * 3,
        [pltpu.SemaphoreType.DMA((ranks + xs,))],
    )
    pieces[0, 0, 0] = same
    info = call(
        info_kernel,
        (same, pieces[0, 1, 0], advantages.reshape(1, -1)),
        [VMEM] * 3,
        shape((total_rows, 128), f32),
        VMEM,
    )

    def hold(value, after):
        like = shape(value.shape, value.dtype)
        return call(gate_kernel, (value, after), [ANY, ANY], like, ANY, aliases={0: 0})

    def part_logits(kernel, blocks, operands, out_shapes):
        parts = [[pieces[key] for key in sorted(pieces) if key[0] == b] for b in blocks]
        operands = (*operands, held, *(piece for part in parts for piece in part))
        return call(
            functools.partial(kernel, blocks, [len(part) for part in parts], ranks),
            operands,
            [VMEM] * len(operands),
            out_shapes,
            jax.tree.map(lambda _: VMEM, out_shapes),
            flops=flops * len(blocks) // ranks,
        )

    for x in range(1, xs):
        pieces[2 * x + 1, 1, 0] = send(pieces[2 * x, 1, 0], core=1)
        pieces[2 * x, 0, 0] = hold(pieces[2 * x, 0, 0], info)
        pieces[2 * x, 1, 1] = hold(pieces[2 * x, 1, 1], pieces[2 * x + 1, 1, 0])
    for b, y, part in list(pieces):
        if b % 2 == 0 and (b + 1, y, part) not in pieces:
            pieces[b + 1, y, part] = send(pieces[b, y, part], core=1)

    logits_shape = shape((total_rows, columns), f32)
    partial = part_logits(first_kernel, [*range(0, ranks, 2), 1], (), logits_shape)
    logits, stats = part_logits(
        lambda blocks, counts, ranks, *refs: logits_kernel(blocks, counts, ranks, dps, *refs),
        list(range(3, ranks, 2)),
        (info, partial),
        (logits_shape, shape((dps * ranks, 1, total_rows + LANES), f32)),
    )
    parted = [[pieces[key] for key in sorted(pieces) if key[0] == b] for b in range(ranks)]

    def rows_of(blocks):
        return [piece for b in blocks for piece in parted[b]]

    def counts_of(blocks):
        return [len(parted[b]) for b in blocks]

    other_logits = send(logits, core=1)
    other_held = send(hold(away, stats), core=1)
    stats = lax.all_to_all(stats, AXES, 0, 0)
    rows_part = total_rows // 4
    order = sorted(range(1, ranks), key=lambda place: (-(place % 2 + (place > 1)), place)) + [0]
    outs = (shape((rows_part, width), bf16),) * (ranks - 1) + (shape((rows_part, width), f32),)
    logit_grad, table, *going = call(
        functools.partial(grad_kernel, order, dps),
        (info, logits, other_logits, held, other_held, stats),
        [VMEM] * 6,
        (shape((total_rows, columns), bf16), shape((total_rows, 128), f32)) + outs * 2,
        (VMEM,) * (2 + 2 * ranks),
        flops=flops,
    )
    def weight_part(first, after, *extra):
        blocks = range(first, first + ranks // 2)
        chosen_rows = rows_of(blocks)
        return call(
            functools.partial(weight_kernel, blocks, counts_of(blocks), len(extra)),
            (after, logit_grad, *extra, *chosen_rows),
            [ANY, VMEM] + [HBM] * (len(extra) > 0)
            + [VMEM] * (max(len(extra) - 1, 0) + len(chosen_rows)),
            (shape((depth, columns), bf16), shape((8, 128), f32))
            + (shape((1, 1), f32),) * (len(extra) > 0),
            (HBM, VMEM) + (SMEM,) * (len(extra) > 0),
            [
                pltpu.VMEM((depth // 2, columns), bf16),
                pltpu.SemaphoreType.DMA((ranks // 2,)),
            ],
            flops=flops // 2,
            aliases={2: 0} if extra else {},
        )

    far_values, near_values = list(going[:ranks]), list(going[ranks:])
    weight_grad, finished = weight_part(0, far_values[-1])
    near_values[:-1] = call(
        gate_kernel,
        (*near_values[:-1], finished),
        [ANY] * ranks,
        outs[:-1],
        (ANY,) * (ranks - 1),
        aliases={place: place for place in range(ranks - 1)},
    )
    ends, sums = [None] * zs, [None, None]
    for chunk, values in ((1, far_values), (0, near_values)):
        sums[chunk] = [values[-1]]
        for place, value in zip(order, values):
            if place:
                sums[chunk].append(send(value, y=place % 2, x=place // 2))
    for chunk in (1, 0):
        near = chunk * zs // 2
        parts_z = call(
            functools.partial(corner_kernel, ranks - 1),
            (table, *sums[chunk]),
            [ANY] + [VMEM] * ranks,
            tuple(shape((CAP, width), bf16 if near + z else f32) for z in range(zs // 2)),
            (VMEM,) * (zs // 2),
        )
        for z, value in enumerate(parts_z):
            ends[near + z] = send(value, z=near + z) if near + z else value
    weight_grad, last, loss = weight_part(ranks // 2, parts_z[0], weight_grad, info, table, stats)
    hidden_grad = call(
        unpack_kernel,
        (last, chosen, *ends),
        [ANY] + [VMEM] * (1 + len(ends)),
        shape((tokens, width), bf16),
        HBM,
        [pltpu.VMEM((tokens, width), bf16), pltpu.SemaphoreType.DMA((2,))],
    )
    return loss[0, 0], hidden_grad, weight_grad


def solution(mesh):
    return jax.shard_map(
        functools.partial(body, mesh.shape["dp"], mesh.shape["vocab"]),
        mesh=mesh,
        in_specs=(P("dp", "vocab"), P(None, AXES), P("dp"), P("dp"), P("dp"), P()),
        out_specs=(P(), P("dp", "vocab"), P(None, AXES)),
        check_vma=False,
    )
```

```python
import functools
import math

import jax
import jax.numpy as jnp
from jax import lax
from jax.experimental import pallas as pl
from jax.experimental.pallas import tpu as pltpu
from jax.sharding import PartitionSpec as P

CAP = 32
MOST_VMEM = 56 * 1024 * 1024
IDS = 128
LANES = 128
grad_scale = 16384.0
AXES = ("dp", "vocab")
SMEM = pl.BlockSpec(memory_space=pltpu.SMEM)
VMEM = pl.BlockSpec(memory_space=pltpu.VMEM)
HBM = pl.BlockSpec(memory_space=pltpu.HBM)
ANY = pl.BlockSpec(memory_space=pl.ANY)


def size_of(value):
    return math.prod(value.shape) * jnp.dtype(value.dtype).itemsize


def call(kernel, operands, in_specs, out_shape, out_specs, scratch=(), spare=4, flops=0, aliases={}):
    outs = jax.tree.leaves(out_shape)
    sized = [v for v, s in zip(operands, in_specs) if s is VMEM]
    sized += [v for v, s in zip(outs, jax.tree.leaves(out_specs)) if s is VMEM]
    held = [s for s in scratch if getattr(s, "memory_space", None) == pltpu.VMEM]
    total = sum(size_of(v) for v in sized) + sum(size_of(s) for s in held)
    return pl.pallas_call(
        kernel,
        out_shape=out_shape,
        in_specs=in_specs,
        out_specs=out_specs,
        scratch_shapes=scratch,
        input_output_aliases=aliases,
        compiler_params=pltpu.CompilerParams(vmem_limit_bytes=min(total + spare * 1024 * 1024, MOST_VMEM)),
        cost_estimate=pl.CostEstimate(
            flops=flops,
            bytes_accessed=sum(size_of(v) for v in list(operands) + outs),
            transcendentals=0,
        ),
    )(*operands)


def in_hbm(value):
    return pltpu.with_memory_space_constraint(value, pltpu.HBM)


def coordinates():
    group, rank = lax.axis_index("dp"), lax.axis_index("vocab")
    groups, ranks = lax.axis_size("dp"), lax.axis_size("vocab")
    position = group % 2 * (groups // 2) + group // 2
    return rank, position, group * ranks + rank


def choose(mask):
    tokens = mask.shape[1]
    wide = jnp.broadcast_to(mask.astype(jnp.float32), (8, tokens))
    before = lax.broadcasted_iota(jnp.int32, (tokens, tokens), 0)
    after = lax.broadcasted_iota(jnp.int32, (tokens, tokens), 1)
    upto = (before <= after).astype(jnp.float32)
    slot = jnp.dot(
        wide.astype(jnp.bfloat16), upto.astype(jnp.bfloat16), preferred_element_type=jnp.float32
    )[0:1]
    grid = lax.broadcasted_iota(jnp.int32, (CAP, tokens), 0) + 1
    return (slot.astype(jnp.int32) == grid) & (mask == 1)


def pack_kernel(hidden_hbm, mask_hbm, target_hbm, turn_hbm, rows, plain, chosen_out, *scratch):
    hidden, mask, target, turn, sems = scratch
    copies = []
    for place, (source, held) in enumerate(
        ((mask_hbm, mask), (target_hbm, target), (turn_hbm, turn), (hidden_hbm, hidden))
    ):
        copy = pltpu.make_async_copy(source, held, sems.at[place])
        copy.start()
        copies.append(copy)
    for copy in copies[:3]:
        copy.wait()
    width = hidden.shape[1]
    chosen = choose(mask[...])
    one_hot = chosen.astype(jnp.float32).astype(jnp.bfloat16)
    chosen_out[...] = one_hot
    turns, targets = turn[...], target[...]
    fields = (
        mask[...],
        turns & 255,
        turns >> 8,
        targets & 255,
        (targets >> 8) & 255,
        targets >> 16,
    )
    lane = lax.broadcasted_iota(jnp.int32, (CAP, IDS), 1)
    table = jnp.zeros((CAP, IDS), jnp.float32)
    for place, field in enumerate(fields):
        picked = jnp.where(chosen, field.astype(jnp.float32), 0.0)
        table = jnp.where(lane == place, jnp.sum(picked, axis=1, keepdims=True), table)
    rows[:, width:] = table.astype(jnp.bfloat16)
    copies[3].wait()
    packed = jnp.dot(one_hot, hidden[...], preferred_element_type=jnp.float32)
    packed = packed.astype(jnp.bfloat16)
    rows[:, :width] = packed
    plain[...] = packed


def join_kernel(order, *refs):
    blocks, (line, plain, far) = refs[:len(order) - 1] + refs[-4:-3], refs[-3:]
    width = plain.shape[1]
    for place, block in zip(order, blocks):
        rows = slice(place * CAP, (place + 1) * CAP)
        line[rows] = block[...]
        plain[rows] = block[:, :width]
        if place:
            far[(place - 1) * CAP:place * CAP] = block[:, :width]


def stage_kernel(blocks, line, weight, held, away, same, sems):
    rank = coordinates()[0]
    width = weight.shape[0] // blocks
    copies = []
    for block in list(range(1, blocks, 2)) + list(range(0, blocks, 2)):
        start = pl.multiple_of((rank ^ block) * width, width)
        targets = [held.at[pl.ds(start, width)]]
        if block % 2:
            targets.append(away.at[pl.ds(block // 2 * width, width)])
        for target in targets:
            copy = pltpu.make_async_copy(
                weight.at[pl.ds(start, width)], target, sems.at[len(copies)]
            )
            copy.start()
            copies.append(copy)
    same[...] = line[...]
    for copy in copies:
        copy.wait()


def gate_kernel(*refs):
    pass


def info_kernel(*refs):
    advantages, info = refs[-2:]
    start = refs[0].shape[1] - IDS
    table = jnp.concatenate([ref[:, start:] for ref in refs[:-2]], axis=0).astype(jnp.float32)
    valid = table[:, 0:1]
    turn = table[:, 1:2] + 256.0 * table[:, 2:3]
    target = table[:, 3:4] + 256.0 * table[:, 4:5] + 65536.0 * table[:, 5:6]
    turns = advantages.shape[1]
    spot = lax.broadcasted_iota(jnp.int32, (table.shape[0], turns), 1)
    gain = jnp.sum(
        jnp.where(spot == turn.astype(jnp.int32), advantages[...], 0.0), axis=1, keepdims=True
    )
    weight = valid * gain / jnp.sum(valid)
    lane = lax.broadcasted_iota(jnp.int32, info.shape, 1)
    info[...] = jnp.where(lane == 0, weight, jnp.where(lane == 1, target, 0.0))


def reorder(stats, position, groups):
    lanes = stats.shape[1]
    lane = lax.broadcasted_iota(jnp.int32, stats.shape, 1)
    bit = 1
    while bit < groups:
        size = CAP * bit
        swapped = jnp.where(
            (lane & size) != 0,
            pltpu.roll(stats, size, 1),
            pltpu.roll(stats, lanes - size, 1),
        )
        stats = jnp.where((position & bit) != 0, swapped, stats)
        bit *= 2
    return stats


def all_rows(pieces, counts, place, width):
    start = sum(counts[:place])
    return jnp.concatenate([ref[:, :width] for ref in pieces[start:start + counts[place]]], axis=0)


def some_logits(blocks, counts, ranks, pieces, weight):
    width = weight.shape[0] // ranks
    rank, total = coordinates()[0], None
    for place, block in enumerate(blocks):
        start = pl.multiple_of((rank ^ block) * width, width)
        part = jnp.dot(
            all_rows(pieces, counts, place, width),
            weight[pl.ds(start, width), :],
            preferred_element_type=jnp.float32,
        )
        total = part if total is None else total + part
    return total


def first_kernel(blocks, counts, ranks, weight, *refs):
    refs[-1][...] = some_logits(blocks, counts, ranks, refs[:-1], weight)


def logits_kernel(blocks, counts, ranks, groups, info, partial, weight, *refs):
    pieces, (logits, stats) = refs[:-2], refs[-2:]
    _, position, shard = coordinates()
    total = partial[...] + some_logits(blocks, counts, ranks, pieces, weight)
    logits[...] = total
    height, columns = total.shape
    target = info[:, 1:2].astype(jnp.int32) - shard * columns
    column = lax.broadcasted_iota(jnp.int32, total.shape, 1)
    hit = jnp.sum(jnp.where(column == target, total, 0.0), axis=1, keepdims=True)
    hit = jnp.sum(hit * info[:, 0:1])
    peak = jnp.max(total, axis=1, keepdims=True)
    mass = jnp.sum(jnp.exp(total - peak), axis=1, keepdims=True)
    lane = lax.broadcasted_iota(jnp.int32, (height, 128), 1)
    table = jnp.where(lane == 0, peak + jnp.log(mass), hit)
    table = reorder(jnp.transpose(table)[0:8], position, groups)
    line = jnp.concatenate([table[0:1], table[1:2, :LANES]], axis=1)
    stats[...] = jnp.broadcast_to(line[None], stats.shape)


def log_totals(groups, stats, height):
    parts = stats[:, :, :height]
    peak = jnp.max(parts, axis=0)
    line = peak + jnp.log(jnp.sum(jnp.exp(parts - peak[None]), axis=0))
    line = reorder(jnp.broadcast_to(line, (8, height)), coordinates()[1], groups)
    return jnp.transpose(jnp.concatenate([line] * 16, axis=0))


def grad_kernel(order, groups, info, mine, theirs, weight, other_weight, stats, *refs):
    logit_grad, table, outs = refs[0], refs[1], refs[2:]
    chunks = (outs[len(order):], outs[:len(order)])
    rank, _, shard = coordinates()
    height, columns = mine.shape
    part = height // 4
    table[...] = log_totals(groups, stats, height)
    log_total = table[:, 0:1]
    row_weight, target = info[:, 0:1], info[:, 1:2].astype(jnp.int32)

    def grad_of(logits, shard):
        column = lax.broadcasted_iota(jnp.int32, (height, columns), 1) + shard * columns
        probability = jnp.exp(logits[...] - log_total)
        return (
            grad_scale * row_weight * (probability - (column == target).astype(jnp.float32))
        ).astype(jnp.bfloat16)

    grad = grad_of(mine, shard)
    logit_grad[...] = grad
    grads = (grad, grad_of(theirs, shard ^ 1))
    width = outs[0].shape[1]
    for x in range(len(order) // 2):
        start = pl.multiple_of((rank ^ 2 * x) * width, width)
        weights = (weight[pl.ds(start, width), :], other_weight[x * width:(x + 1) * width, :])
        total = sum(
            lax.dot_general(g, w, (((1,), (1,)), ((), ())), preferred_element_type=jnp.float32)
            for g, w in zip(grads, weights)
        )
        for quarter in range(4):
            out = chunks[quarter % 2][order.index(2 * x + quarter // 2)]
            out[...] = total[quarter * part:(quarter + 1) * part].astype(out.dtype)


def weight_kernel(blocks, counts, skipped, after, logit_grad, *refs):
    pieces, (out, last, done, sems) = refs[skipped:-4], refs[-4:]
    rank = coordinates()[0]
    width = done.shape[0] // len(blocks)
    copies = []
    for place, block in enumerate(blocks):
        done[place * width:(place + 1) * width] = lax.dot_general(
            all_rows(pieces, counts, place, width),
            logit_grad[...],
            (((0,), (0,)), ((), ())),
            preferred_element_type=jnp.float32,
        ).astype(jnp.bfloat16)
        start = pl.multiple_of((rank ^ block) * width, width)
        copy = pltpu.make_async_copy(
            done.at[pl.ds(place * width, width)], out.at[pl.ds(start, width)], sems.at[place]
        )
        copy.start()
        copies.append(copy)
    if skipped:
        info, table, stats = refs[1:4]
        hits = jnp.sum(stats[:, :, info.shape[0]:], axis=0)
        loss = jnp.sum(info[:, 0:1] * table[:, 0:1]) - hits[0, 0]
        last[...] = jnp.full(last.shape, loss, jnp.float32)
    else:
        last[...] = jnp.zeros_like(last)
    for copy in copies:
        copy.wait()


def corner_kernel(count, after, kept, *refs):
    total = kept[...]
    for ref in refs[:count]:
        total = total + ref[...].astype(jnp.float32)
    for place, out in enumerate(refs[count:]):
        out[...] = total[place * CAP:(place + 1) * CAP].astype(out.dtype)


def unpack_kernel(last, chosen, *refs):
    out, loss = refs[-2:]
    loss[0, 0] = last[0, 0]
    total = sum(ref[...].astype(jnp.float32) for ref in refs[:-2])
    out[...] = lax.dot_general(
        chosen[...],
        total.astype(jnp.bfloat16),
        (((0,), (0,)), ((), ())),
        preferred_element_type=jnp.float32,
    ).astype(jnp.bfloat16)


def body(dps, ranks, hidden, weight, loss_mask, target_ids, turn_ids, advantages):
    tokens, width = hidden.shape
    depth, columns = weight.shape
    zs, xs = dps // 2, ranks // 2
    total_rows = dps * CAP
    bf16, f32, i32 = jnp.bfloat16, jnp.float32, jnp.int32
    shape = jax.ShapeDtypeStruct
    flops = 2 * total_rows * depth * columns

    def send(value, z=0, y=0, x=0, core=0):
        far, near = 2 * z + y, 2 * x + core
        pairs = [
            (d * ranks + v, (d ^ far) * ranks + (v ^ near))
            for d in range(dps)
            for v in range(ranks)
        ]
        return lax.ppermute(value, AXES, pairs)

    packed, own, chosen = call(
        pack_kernel,
        (
            in_hbm(hidden),
            in_hbm(loss_mask.reshape(1, tokens)),
            in_hbm(target_ids.reshape(1, tokens)),
            in_hbm(turn_ids.reshape(1, tokens)),
        ),
        [HBM] * 4,
        (
            shape((CAP, width + IDS), bf16),
            shape((CAP, width), bf16),
            shape((CAP, tokens), bf16),
        ),
        (VMEM,) * 3,
        [pltpu.VMEM((tokens, width), bf16)]
        + [pltpu.VMEM((1, tokens), i32)] * 3
        + [pltpu.SemaphoreType.DMA((4,))],
    )

    line_order = [0, *range(2, zs), 1]
    blocks = [send(packed, z=z) if z else packed for z in line_order[:-1]]
    corners = {x: send(own, y=1, x=x) for x in range(1, xs)}
    blocks.append(send(packed, z=1))
    line_rows = zs * CAP
    line, line_plain, far = call(
        functools.partial(join_kernel, line_order),
        (*blocks[:-1], *corners.values(), blocks[-1]),
        [VMEM] * (zs - 1) + [ANY] * len(corners) + [VMEM],
        (
            shape((line_rows, width + IDS), bf16),
            shape((line_rows, width), bf16),
            shape((line_rows - CAP, width), bf16),
        ),
        (VMEM,) * 3,
    )
    pieces = {(0, 1, 0): send(line, y=1)}
    for x in range(1, xs):
        pieces[2 * x, 0, 0] = send(line_plain, x=x)
        pieces[2 * x, 1, 0] = corners[x]
        pieces[2 * x, 1, 1] = send(far, y=1, x=x)
    held, away, same = call(
        functools.partial(stage_kernel, ranks),
        (line, in_hbm(weight)),
        [VMEM, HBM],
        (
            shape((depth, columns), bf16),
            shape((depth // 2, columns), bf16),
            shape(line.shape, bf16),
        ),
        (VMEM,) * 3,
        [pltpu.SemaphoreType.DMA((ranks + xs,))],
    )
    pieces[0, 0, 0] = same
    info = call(
        info_kernel,
        (same, pieces[0, 1, 0], advantages.reshape(1, -1)),
        [VMEM] * 3,
        shape((total_rows, 128), f32),
        VMEM,
    )

    def hold(value, after):
        like = shape(value.shape, value.dtype)
        return call(gate_kernel, (value, after), [ANY, ANY], like, ANY, aliases={0: 0})

    def part_logits(kernel, blocks, operands, out_shapes):
        parts = [[pieces[key] for key in sorted(pieces) if key[0] == b] for b in blocks]
        operands = (*operands, held, *(piece for part in parts for piece in part))
        return call(
            functools.partial(kernel, blocks, [len(part) for part in parts], ranks),
            operands,
            [VMEM] * len(operands),
            out_shapes,
            jax.tree.map(lambda _: VMEM, out_shapes),
            flops=flops * len(blocks) // ranks,
        )

    for x in range(1, xs):
        pieces[2 * x + 1, 1, 0] = send(pieces[2 * x, 1, 0], core=1)
        pieces[2 * x, 0, 0] = hold(pieces[2 * x, 0, 0], info)
        pieces[2 * x, 1, 1] = hold(pieces[2 * x, 1, 1], pieces[2 * x + 1, 1, 0])
    for b, y, part in list(pieces):
        if b % 2 == 0 and (b + 1, y, part) not in pieces:
            pieces[b + 1, y, part] = send(pieces[b, y, part], core=1)

    logits_shape = shape((total_rows, columns), f32)
    partial = part_logits(first_kernel, [*range(0, ranks, 2), 1], (), logits_shape)
    logits, stats = part_logits(
        lambda blocks, counts, ranks, *refs: logits_kernel(blocks, counts, ranks, dps, *refs),
        list(range(3, ranks, 2)),
        (info, partial),
        (logits_shape, shape((dps * ranks, 1, total_rows + LANES), f32)),
    )
    parted = [[pieces[key] for key in sorted(pieces) if key[0] == b] for b in range(ranks)]

    def rows_of(blocks):
        return [piece for b in blocks for piece in parted[b]]

    def counts_of(blocks):
        return [len(parted[b]) for b in blocks]

    other_logits = send(logits, core=1)
    other_held = send(hold(away, stats), core=1)
    stats = lax.all_to_all(stats, AXES, 0, 0)
    rows_part = total_rows // 4
    order = sorted(range(1, ranks), key=lambda place: (-(place % 2 + (place > 1)), place)) + [0]
    outs = (shape((rows_part, width), bf16),) * (ranks - 1) + (shape((rows_part, width), f32),)
    logit_grad, table, *going = call(
        functools.partial(grad_kernel, order, dps),
        (info, logits, other_logits, held, other_held, stats),
        [VMEM] * 6,
        (shape((total_rows, columns), bf16), shape((total_rows, 128), f32)) + outs * 2,
        (VMEM,) * (2 + 2 * ranks),
        flops=flops,
    )
    def weight_part(blocks, after, *extra):
        chosen_rows = rows_of(blocks)
        return call(
            functools.partial(weight_kernel, blocks, counts_of(blocks), len(extra)),
            (after, logit_grad, *extra, *chosen_rows),
            [ANY, VMEM] + [HBM] * (len(extra) > 0)
            + [VMEM] * (max(len(extra) - 1, 0) + len(chosen_rows)),
            (shape((depth, columns), bf16), shape((8, 128), f32)),
            (HBM, VMEM),
            [
                pltpu.VMEM((len(blocks) * width, columns), bf16),
                pltpu.SemaphoreType.DMA((len(blocks),)),
            ],
            flops=flops * len(blocks) // ranks,
            aliases={2: 0} if extra else {},
        )

    far_values, near_values = list(going[:ranks]), list(going[ranks:])
    weight_grad, finished = weight_part(range(ranks // 4), far_values[-1])
    near_values[:-1] = call(
        gate_kernel,
        (*near_values[:-1], finished),
        [ANY] * ranks,
        outs[:-1],
        (ANY,) * (ranks - 1),
        aliases={place: place for place in range(ranks - 1)},
    )
    ends, sums = [None] * zs, [None, None]
    for chunk, values in ((1, far_values), (0, near_values)):
        sums[chunk] = [values[-1]]
        for place, value in zip(order, values):
            if place:
                sums[chunk].append(send(value, y=place % 2, x=place // 2))
    for chunk in (1, 0):
        near = chunk * zs // 2
        parts_z = call(
            functools.partial(corner_kernel, ranks - 1),
            (table, *sums[chunk]),
            [ANY] + [VMEM] * ranks,
            tuple(shape((CAP, width), bf16 if near + z else f32) for z in range(zs // 2)),
            (VMEM,) * (zs // 2),
        )
        for z, value in enumerate(parts_z):
            ends[near + z] = send(value, z=near + z) if near + z else value
    weight_grad, last = weight_part(
        range(ranks // 4, ranks), parts_z[0], weight_grad, info, table, stats
    )
    hidden_grad, loss = call(
        unpack_kernel,
        (last, chosen, *ends),
        [VMEM] * (2 + len(ends)),
        (shape((tokens, width), bf16), shape((1, 1), f32)),
        (VMEM, SMEM),
    )
    return loss[0, 0], hidden_grad, weight_grad


def solution(mesh):
    return jax.shard_map(
        functools.partial(body, mesh.shape["dp"], mesh.shape["vocab"]),
        mesh=mesh,
        in_specs=(P("dp", "vocab"), P(None, AXES), P("dp"), P("dp"), P("dp"), P()),
        out_specs=(P(), P("dp", "vocab"), P(None, AXES)),
        check_vma=False,
    )
```

```python
import functools
import math

import jax
import jax.numpy as jnp
from jax import lax
from jax.experimental import pallas as pl
from jax.experimental.pallas import tpu as pltpu
from jax.sharding import PartitionSpec as P

CAP = 32
MOST_VMEM = 56 * 1024 * 1024
IDS = 128
LANES = 128
grad_scale = 16384.0
AXES = ("dp", "vocab")
SMEM = pl.BlockSpec(memory_space=pltpu.SMEM)
VMEM = pl.BlockSpec(memory_space=pltpu.VMEM)
HBM = pl.BlockSpec(memory_space=pltpu.HBM)
ANY = pl.BlockSpec(memory_space=pl.ANY)


def size_of(value):
    return math.prod(value.shape) * jnp.dtype(value.dtype).itemsize


def call(kernel, operands, in_specs, out_shape, out_specs, scratch=(), spare=4, flops=0, aliases={}):
    outs = jax.tree.leaves(out_shape)
    sized = [v for v, s in zip(operands, in_specs) if s is VMEM]
    sized += [v for v, s in zip(outs, jax.tree.leaves(out_specs)) if s is VMEM]
    held = [s for s in scratch if getattr(s, "memory_space", None) == pltpu.VMEM]
    total = sum(size_of(v) for v in sized) + sum(size_of(s) for s in held)
    return pl.pallas_call(
        kernel,
        out_shape=out_shape,
        in_specs=in_specs,
        out_specs=out_specs,
        scratch_shapes=scratch,
        input_output_aliases=aliases,
        compiler_params=pltpu.CompilerParams(vmem_limit_bytes=min(total + spare * 1024 * 1024, MOST_VMEM)),
        cost_estimate=pl.CostEstimate(
            flops=flops,
            bytes_accessed=sum(size_of(v) for v in list(operands) + outs),
            transcendentals=0,
        ),
    )(*operands)


def in_hbm(value):
    return pltpu.with_memory_space_constraint(value, pltpu.HBM)


def coordinates():
    group, rank = lax.axis_index("dp"), lax.axis_index("vocab")
    groups, ranks = lax.axis_size("dp"), lax.axis_size("vocab")
    position = group % 2 * (groups // 2) + group // 2
    return rank, position, group * ranks + rank


def choose(mask):
    tokens = mask.shape[1]
    wide = jnp.broadcast_to(mask.astype(jnp.float32), (8, tokens))
    before = lax.broadcasted_iota(jnp.int32, (tokens, tokens), 0)
    after = lax.broadcasted_iota(jnp.int32, (tokens, tokens), 1)
    upto = (before <= after).astype(jnp.float32)
    slot = jnp.dot(
        wide.astype(jnp.bfloat16), upto.astype(jnp.bfloat16), preferred_element_type=jnp.float32
    )[0:1]
    grid = lax.broadcasted_iota(jnp.int32, (CAP, tokens), 0) + 1
    return (slot.astype(jnp.int32) == grid) & (mask == 1)


def pack_kernel(hidden_hbm, mask_hbm, target_hbm, turn_hbm, rows, plain, chosen_out, *scratch):
    hidden, mask, target, turn, sems = scratch
    copies = []
    for place, (source, held) in enumerate(
        ((mask_hbm, mask), (target_hbm, target), (turn_hbm, turn), (hidden_hbm, hidden))
    ):
        copy = pltpu.make_async_copy(source, held, sems.at[place])
        copy.start()
        copies.append(copy)
    for copy in copies[:3]:
        copy.wait()
    width = hidden.shape[1]
    chosen = choose(mask[...])
    one_hot = chosen.astype(jnp.float32).astype(jnp.bfloat16)
    chosen_out[...] = one_hot
    turns, targets = turn[...], target[...]
    fields = (
        mask[...],
        turns & 255,
        turns >> 8,
        targets & 255,
        (targets >> 8) & 255,
        targets >> 16,
    )
    lane = lax.broadcasted_iota(jnp.int32, (CAP, IDS), 1)
    table = jnp.zeros((CAP, IDS), jnp.float32)
    for place, field in enumerate(fields):
        picked = jnp.where(chosen, field.astype(jnp.float32), 0.0)
        table = jnp.where(lane == place, jnp.sum(picked, axis=1, keepdims=True), table)
    rows[:, width:] = table.astype(jnp.bfloat16)
    copies[3].wait()
    packed = jnp.dot(one_hot, hidden[...], preferred_element_type=jnp.float32)
    packed = packed.astype(jnp.bfloat16)
    rows[:, :width] = packed
    plain[...] = packed


def join_kernel(order, *refs):
    blocks, (line, plain, far) = refs[:len(order) - 1] + refs[-4:-3], refs[-3:]
    width = plain.shape[1]
    for place, block in zip(order, blocks):
        rows = slice(place * CAP, (place + 1) * CAP)
        line[rows] = block[...]
        plain[rows] = block[:, :width]
        if place:
            far[(place - 1) * CAP:place * CAP] = block[:, :width]


def stage_kernel(blocks, line, weight, held, away, same, sems):
    rank = coordinates()[0]
    width = weight.shape[0] // blocks
    copies = []
    for block in list(range(1, blocks, 2)) + list(range(0, blocks, 2)):
        start = pl.multiple_of((rank ^ block) * width, width)
        targets = [held.at[pl.ds(start, width)]]
        if block % 2:
            targets.append(away.at[pl.ds(block // 2 * width, width)])
        for target in targets:
            copy = pltpu.make_async_copy(
                weight.at[pl.ds(start, width)], target, sems.at[len(copies)]
            )
            copy.start()
            copies.append(copy)
    same[...] = line[...]
    for copy in copies:
        copy.wait()


def gate_kernel(*refs):
    pass


def info_kernel(*refs):
    advantages, info = refs[-2:]
    start = refs[0].shape[1] - IDS
    table = jnp.concatenate([ref[:, start:] for ref in refs[:-2]], axis=0).astype(jnp.float32)
    valid = table[:, 0:1]
    turn = table[:, 1:2] + 256.0 * table[:, 2:3]
    target = table[:, 3:4] + 256.0 * table[:, 4:5] + 65536.0 * table[:, 5:6]
    turns = advantages.shape[1]
    spot = lax.broadcasted_iota(jnp.int32, (table.shape[0], turns), 1)
    gain = jnp.sum(
        jnp.where(spot == turn.astype(jnp.int32), advantages[...], 0.0), axis=1, keepdims=True
    )
    weight = valid * gain / jnp.sum(valid)
    lane = lax.broadcasted_iota(jnp.int32, info.shape, 1)
    info[...] = jnp.where(lane == 0, weight, jnp.where(lane == 1, target, 0.0))


def reorder(stats, position, groups):
    lanes = stats.shape[1]
    lane = lax.broadcasted_iota(jnp.int32, stats.shape, 1)
    bit = 1
    while bit < groups:
        size = CAP * bit
        swapped = jnp.where(
            (lane & size) != 0,
            pltpu.roll(stats, size, 1),
            pltpu.roll(stats, lanes - size, 1),
        )
        stats = jnp.where((position & bit) != 0, swapped, stats)
        bit *= 2
    return stats


def all_rows(pieces, counts, place, width):
    start = sum(counts[:place])
    return jnp.concatenate([ref[:, :width] for ref in pieces[start:start + counts[place]]], axis=0)


def some_logits(blocks, counts, ranks, pieces, weight):
    width = weight.shape[0] // ranks
    rank, total = coordinates()[0], None
    for place, block in enumerate(blocks):
        start = pl.multiple_of((rank ^ block) * width, width)
        part = jnp.dot(
            all_rows(pieces, counts, place, width),
            weight[pl.ds(start, width), :],
            preferred_element_type=jnp.float32,
        )
        total = part if total is None else total + part
    return total


def first_kernel(blocks, counts, ranks, weight, *refs):
    refs[-1][...] = some_logits(blocks, counts, ranks, refs[:-1], weight)


def logits_kernel(blocks, counts, ranks, groups, info, partial, weight, *refs):
    pieces, (logits, stats) = refs[:-2], refs[-2:]
    _, position, shard = coordinates()
    total = partial[...] + some_logits(blocks, counts, ranks, pieces, weight)
    logits[...] = total
    height, columns = total.shape
    target = info[:, 1:2].astype(jnp.int32) - shard * columns
    column = lax.broadcasted_iota(jnp.int32, total.shape, 1)
    hit = jnp.sum(jnp.where(column == target, total, 0.0), axis=1, keepdims=True)
    hit = jnp.sum(hit * info[:, 0:1])
    peak = jnp.max(total, axis=1, keepdims=True)
    mass = jnp.sum(jnp.exp(total - peak), axis=1, keepdims=True)
    lane = lax.broadcasted_iota(jnp.int32, (height, 128), 1)
    table = jnp.where(lane == 0, peak + jnp.log(mass), hit)
    table = reorder(jnp.transpose(table)[0:8], position, groups)
    line = jnp.concatenate([table[0:1], table[1:2, :LANES]], axis=1)
    stats[...] = jnp.broadcast_to(line[None], stats.shape)


def log_totals(groups, stats, height):
    parts = stats[:, :, :height]
    peak = jnp.max(parts, axis=0)
    line = peak + jnp.log(jnp.sum(jnp.exp(parts - peak[None]), axis=0))
    line = reorder(jnp.broadcast_to(line, (8, height)), coordinates()[1], groups)
    return jnp.transpose(jnp.concatenate([line] * 16, axis=0))


def grad_kernel(order, groups, info, mine, theirs, weight, other_weight, stats, *refs):
    logit_grad, table, outs = refs[0], refs[1], refs[2:]
    chunks = (outs[len(order):], outs[:len(order)])
    rank, _, shard = coordinates()
    height, columns = mine.shape
    part = height // 4
    table[...] = log_totals(groups, stats, height)
    log_total = table[:, 0:1]
    row_weight, target = info[:, 0:1], info[:, 1:2].astype(jnp.int32)

    def grad_of(logits, shard):
        column = lax.broadcasted_iota(jnp.int32, (height, columns), 1) + shard * columns
        probability = jnp.exp(logits[...] - log_total)
        return (
            grad_scale * row_weight * (probability - (column == target).astype(jnp.float32))
        ).astype(jnp.bfloat16)

    grad = grad_of(mine, shard)
    logit_grad[...] = grad
    grads = (grad, grad_of(theirs, shard ^ 1))
    width = outs[0].shape[1]
    for x in range(len(order) // 2):
        start = pl.multiple_of((rank ^ 2 * x) * width, width)
        weights = (weight[pl.ds(start, width), :], other_weight[x * width:(x + 1) * width, :])
        total = sum(
            lax.dot_general(g, w, (((1,), (1,)), ((), ())), preferred_element_type=jnp.float32)
            for g, w in zip(grads, weights)
        )
        for quarter in range(4):
            out = chunks[quarter % 2][order.index(2 * x + quarter // 2)]
            out[...] = total[quarter * part:(quarter + 1) * part].astype(out.dtype)


def weight_kernel(blocks, counts, skipped, after, logit_grad, *refs):
    pieces, (out, last, done, sems) = refs[skipped:-4], refs[-4:]
    rank = coordinates()[0]
    width = done.shape[0] // len(blocks)
    copies = []
    for place, block in enumerate(blocks):
        done[place * width:(place + 1) * width] = lax.dot_general(
            all_rows(pieces, counts, place, width),
            logit_grad[...],
            (((0,), (0,)), ((), ())),
            preferred_element_type=jnp.float32,
        ).astype(jnp.bfloat16)
        start = pl.multiple_of((rank ^ block) * width, width)
        copy = pltpu.make_async_copy(
            done.at[pl.ds(place * width, width)], out.at[pl.ds(start, width)], sems.at[place]
        )
        copy.start()
        copies.append(copy)
    if skipped:
        info, table, stats = refs[1:4]
        hits = jnp.sum(stats[:, :, info.shape[0]:], axis=0)
        loss = jnp.sum(info[:, 0:1] * table[:, 0:1]) - hits[0, 0]
        last[...] = jnp.full(last.shape, loss, jnp.float32)
    else:
        last[...] = jnp.zeros_like(last)
    for copy in copies:
        copy.wait()


def corner_kernel(count, after, kept, *refs):
    total = kept[...]
    for ref in refs[:count]:
        total = total + ref[...].astype(jnp.float32)
    for place, out in enumerate(refs[count:]):
        out[...] = total[place * CAP:(place + 1) * CAP].astype(out.dtype)


def unpack_kernel(last, chosen, *refs):
    out, loss = refs[-2:]
    loss[0, 0] = last[0, 0]
    total = sum(ref[...].astype(jnp.float32) for ref in refs[:-2])
    out[...] = lax.dot_general(
        chosen[...],
        total.astype(jnp.bfloat16),
        (((0,), (0,)), ((), ())),
        preferred_element_type=jnp.float32,
    ).astype(jnp.bfloat16)


def body(dps, ranks, hidden, weight, loss_mask, target_ids, turn_ids, advantages):
    tokens, width = hidden.shape
    depth, columns = weight.shape
    zs, xs = dps // 2, ranks // 2
    total_rows = dps * CAP
    bf16, f32, i32 = jnp.bfloat16, jnp.float32, jnp.int32
    shape = jax.ShapeDtypeStruct
    flops = 2 * total_rows * depth * columns

    def send(value, z=0, y=0, x=0, core=0):
        far, near = 2 * z + y, 2 * x + core
        pairs = [
            (d * ranks + v, (d ^ far) * ranks + (v ^ near))
            for d in range(dps)
            for v in range(ranks)
        ]
        return lax.ppermute(value, AXES, pairs)

    packed, own, chosen = call(
        pack_kernel,
        (
            in_hbm(hidden),
            in_hbm(loss_mask.reshape(1, tokens)),
            in_hbm(target_ids.reshape(1, tokens)),
            in_hbm(turn_ids.reshape(1, tokens)),
        ),
        [HBM] * 4,
        (
            shape((CAP, width + IDS), bf16),
            shape((CAP, width), bf16),
            shape((CAP, tokens), bf16),
        ),
        (VMEM,) * 3,
        [pltpu.VMEM((tokens, width), bf16)]
        + [pltpu.VMEM((1, tokens), i32)] * 3
        + [pltpu.SemaphoreType.DMA((4,))],
    )

    line_order = [0, *range(2, zs), 1]
    blocks = [send(packed, z=z) if z else packed for z in line_order[:-1]]
    corners = {x: send(own, y=1, x=x) for x in range(1, xs)}
    blocks.append(send(packed, z=1))
    line_rows = zs * CAP
    line, line_plain, far = call(
        functools.partial(join_kernel, line_order),
        (*blocks[:-1], *corners.values(), blocks[-1]),
        [VMEM] * (zs - 1) + [ANY] * len(corners) + [VMEM],
        (
            shape((line_rows, width + IDS), bf16),
            shape((line_rows, width), bf16),
            shape((line_rows - CAP, width), bf16),
        ),
        (VMEM,) * 3,
    )
    pieces = {(0, 1, 0): send(line, y=1)}
    for x in range(1, xs):
        pieces[2 * x, 0, 0] = send(line_plain, x=x)
        pieces[2 * x, 1, 0] = corners[x]
        pieces[2 * x, 1, 1] = send(far, y=1, x=x)
    held, away, same = call(
        functools.partial(stage_kernel, ranks),
        (line, in_hbm(weight)),
        [VMEM, HBM],
        (
            shape((depth, columns), bf16),
            shape((depth // 2, columns), bf16),
            shape(line.shape, bf16),
        ),
        (VMEM,) * 3,
        [pltpu.SemaphoreType.DMA((ranks + xs,))],
    )
    pieces[0, 0, 0] = same
    info = call(
        info_kernel,
        (same, pieces[0, 1, 0], advantages.reshape(1, -1)),
        [VMEM] * 3,
        shape((total_rows, 128), f32),
        VMEM,
    )

    def hold(value, after):
        like = shape(value.shape, value.dtype)
        return call(gate_kernel, (value, after), [ANY, ANY], like, ANY, aliases={0: 0})

    def part_logits(kernel, blocks, operands, out_shapes):
        parts = [[pieces[key] for key in sorted(pieces) if key[0] == b] for b in blocks]
        operands = (*operands, held, *(piece for part in parts for piece in part))
        return call(
            functools.partial(kernel, blocks, [len(part) for part in parts], ranks),
            operands,
            [VMEM] * len(operands),
            out_shapes,
            jax.tree.map(lambda _: VMEM, out_shapes),
            flops=flops * len(blocks) // ranks,
        )

    for x in range(1, xs):
        pieces[2 * x + 1, 1, 0] = send(pieces[2 * x, 1, 0], core=1)
        pieces[2 * x, 0, 0] = hold(pieces[2 * x, 0, 0], info)
        pieces[2 * x, 1, 1] = hold(pieces[2 * x, 1, 1], pieces[2 * x + 1, 1, 0])
    for b, y, part in list(pieces):
        if b % 2 == 0 and (b + 1, y, part) not in pieces:
            pieces[b + 1, y, part] = send(pieces[b, y, part], core=1)

    logits_shape = shape((total_rows, columns), f32)
    partial = part_logits(first_kernel, [*range(0, ranks, 2), 1], (), logits_shape)
    logits, stats = part_logits(
        lambda blocks, counts, ranks, *refs: logits_kernel(blocks, counts, ranks, dps, *refs),
        list(range(3, ranks, 2)),
        (info, partial),
        (logits_shape, shape((dps * ranks, 1, total_rows + LANES), f32)),
    )
    parted = [[pieces[key] for key in sorted(pieces) if key[0] == b] for b in range(ranks)]

    def rows_of(blocks):
        return [piece for b in blocks for piece in parted[b]]

    def counts_of(blocks):
        return [len(parted[b]) for b in blocks]

    other_logits = send(logits, core=1)
    other_held = send(hold(away, stats), core=1)
    stats = lax.all_to_all(stats, AXES, 0, 0)
    rows_part = total_rows // 4
    order = sorted(range(1, ranks), key=lambda place: (place > 1, -(place % 2), place)) + [0]
    outs = (shape((rows_part, width), bf16),) * (ranks - 1) + (shape((rows_part, width), f32),)
    logit_grad, table, *going = call(
        functools.partial(grad_kernel, order, dps),
        (info, logits, other_logits, held, other_held, stats),
        [VMEM] * 6,
        (shape((total_rows, columns), bf16), shape((total_rows, 128), f32)) + outs * 2,
        (VMEM,) * (2 + 2 * ranks),
        flops=flops,
    )
    def weight_part(first, after, *extra):
        blocks = range(first, first + ranks // 2)
        chosen_rows = rows_of(blocks)
        return call(
            functools.partial(weight_kernel, blocks, counts_of(blocks), len(extra)),
            (after, logit_grad, *extra, *chosen_rows),
            [ANY, VMEM] + [HBM] * (len(extra) > 0)
            + [VMEM] * (max(len(extra) - 1, 0) + len(chosen_rows)),
            (shape((depth, columns), bf16), shape((8, 128), f32)),
            (HBM, VMEM),
            [
                pltpu.VMEM((depth // 2, columns), bf16),
                pltpu.SemaphoreType.DMA((ranks // 2,)),
            ],
            flops=flops // 2,
            aliases={2: 0} if extra else {},
        )

    far_values, near_values = list(going[:ranks]), list(going[ranks:])
    weight_grad, finished = weight_part(0, far_values[-1])
    near_values[:-1] = call(
        gate_kernel,
        (*near_values[:-1], finished),
        [ANY] * ranks,
        outs[:-1],
        (ANY,) * (ranks - 1),
        aliases={place: place for place in range(ranks - 1)},
    )
    ends, sums = [None] * zs, [None, None]
    for chunk, values in ((1, far_values), (0, near_values)):
        sums[chunk] = [values[-1]]
        for place, value in zip(order, values):
            if place:
                sums[chunk].append(send(value, y=place % 2, x=place // 2))
    for chunk in (1, 0):
        near = chunk * zs // 2
        parts_z = call(
            functools.partial(corner_kernel, ranks - 1),
            (table, *sums[chunk]),
            [ANY] + [VMEM] * ranks,
            tuple(shape((CAP, width), bf16 if near + z else f32) for z in range(zs // 2)),
            (VMEM,) * (zs // 2),
        )
        for z, value in enumerate(parts_z):
            ends[near + z] = send(value, z=near + z) if near + z else value
    weight_grad, last = weight_part(ranks // 2, parts_z[0], weight_grad, info, table, stats)
    hidden_grad, loss = call(
        unpack_kernel,
        (last, chosen, *ends),
        [VMEM] * (2 + len(ends)),
        (shape((tokens, width), bf16), shape((1, 1), f32)),
        (VMEM, SMEM),
    )
    return loss[0, 0], hidden_grad, weight_grad


def solution(mesh):
    return jax.shard_map(
        functools.partial(body, mesh.shape["dp"], mesh.shape["vocab"]),
        mesh=mesh,
        in_specs=(P("dp", "vocab"), P(None, AXES), P("dp"), P("dp"), P("dp"), P()),
        out_specs=(P(), P("dp", "vocab"), P(None, AXES)),
        check_vma=False,
    )
```

```python
import functools
import math

import jax
import jax.numpy as jnp
from jax import lax
from jax.experimental import pallas as pl
from jax.experimental.pallas import tpu as pltpu
from jax.sharding import PartitionSpec as P

CAP = 32
MOST_VMEM = 56 * 1024 * 1024
IDS = 128
LANES = 128
grad_scale = 16384.0
AXES = ("dp", "vocab")
SMEM = pl.BlockSpec(memory_space=pltpu.SMEM)
VMEM = pl.BlockSpec(memory_space=pltpu.VMEM)
HBM = pl.BlockSpec(memory_space=pltpu.HBM)
ANY = pl.BlockSpec(memory_space=pl.ANY)


def size_of(value):
    return math.prod(value.shape) * jnp.dtype(value.dtype).itemsize


def call(kernel, operands, in_specs, out_shape, out_specs, scratch=(), spare=4, flops=0, aliases={}):
    outs = jax.tree.leaves(out_shape)
    sized = [v for v, s in zip(operands, in_specs) if s is VMEM]
    sized += [v for v, s in zip(outs, jax.tree.leaves(out_specs)) if s is VMEM]
    held = [s for s in scratch if getattr(s, "memory_space", None) == pltpu.VMEM]
    total = sum(size_of(v) for v in sized) + sum(size_of(s) for s in held)
    return pl.pallas_call(
        kernel,
        out_shape=out_shape,
        in_specs=in_specs,
        out_specs=out_specs,
        scratch_shapes=scratch,
        input_output_aliases=aliases,
        compiler_params=pltpu.CompilerParams(vmem_limit_bytes=min(total + spare * 1024 * 1024, MOST_VMEM)),
        cost_estimate=pl.CostEstimate(
            flops=flops,
            bytes_accessed=sum(size_of(v) for v in list(operands) + outs),
            transcendentals=0,
        ),
    )(*operands)


def in_hbm(value):
    return pltpu.with_memory_space_constraint(value, pltpu.HBM)


def coordinates():
    group, rank = lax.axis_index("dp"), lax.axis_index("vocab")
    groups, ranks = lax.axis_size("dp"), lax.axis_size("vocab")
    position = group % 2 * (groups // 2) + group // 2
    return rank, position, group * ranks + rank


def choose(mask):
    tokens = mask.shape[1]
    wide = jnp.broadcast_to(mask.astype(jnp.float32), (8, tokens))
    before = lax.broadcasted_iota(jnp.int32, (tokens, tokens), 0)
    after = lax.broadcasted_iota(jnp.int32, (tokens, tokens), 1)
    upto = (before <= after).astype(jnp.float32)
    slot = jnp.dot(
        wide.astype(jnp.bfloat16), upto.astype(jnp.bfloat16), preferred_element_type=jnp.float32
    )[0:1]
    grid = lax.broadcasted_iota(jnp.int32, (CAP, tokens), 0) + 1
    return (slot.astype(jnp.int32) == grid) & (mask == 1)


def pack_kernel(hidden_hbm, mask_hbm, target_hbm, turn_hbm, rows, plain, chosen_out, *scratch):
    hidden, mask, target, turn, sems = scratch
    copies = []
    for place, (source, held) in enumerate(
        ((mask_hbm, mask), (target_hbm, target), (turn_hbm, turn), (hidden_hbm, hidden))
    ):
        copy = pltpu.make_async_copy(source, held, sems.at[place])
        copy.start()
        copies.append(copy)
    for copy in copies[:3]:
        copy.wait()
    width = hidden.shape[1]
    chosen = choose(mask[...])
    one_hot = chosen.astype(jnp.float32).astype(jnp.bfloat16)
    chosen_out[...] = one_hot
    turns, targets = turn[...], target[...]
    fields = (
        mask[...],
        turns & 255,
        turns >> 8,
        targets & 255,
        (targets >> 8) & 255,
        targets >> 16,
    )
    lane = lax.broadcasted_iota(jnp.int32, (CAP, IDS), 1)
    table = jnp.zeros((CAP, IDS), jnp.float32)
    for place, field in enumerate(fields):
        picked = jnp.where(chosen, field.astype(jnp.float32), 0.0)
        table = jnp.where(lane == place, jnp.sum(picked, axis=1, keepdims=True), table)
    rows[:, width:] = table.astype(jnp.bfloat16)
    copies[3].wait()
    packed = jnp.dot(one_hot, hidden[...], preferred_element_type=jnp.float32)
    packed = packed.astype(jnp.bfloat16)
    rows[:, :width] = packed
    plain[...] = packed


def join_kernel(order, *refs):
    blocks, (line, plain, far) = refs[:len(order) - 1] + refs[-4:-3], refs[-3:]
    width = plain.shape[1]
    for place, block in zip(order, blocks):
        rows = slice(place * CAP, (place + 1) * CAP)
        line[rows] = block[...]
        plain[rows] = block[:, :width]
        if place:
            far[(place - 1) * CAP:place * CAP] = block[:, :width]


def stage_kernel(blocks, line, weight, held, away, same, sems):
    rank = coordinates()[0]
    width = weight.shape[0] // blocks
    copies = []
    for block in list(range(1, blocks, 2)) + list(range(0, blocks, 2)):
        start = pl.multiple_of((rank ^ block) * width, width)
        targets = [held.at[pl.ds(start, width)]]
        if block % 2:
            targets.append(away.at[pl.ds(block // 2 * width, width)])
        for target in targets:
            copy = pltpu.make_async_copy(
                weight.at[pl.ds(start, width)], target, sems.at[len(copies)]
            )
            copy.start()
            copies.append(copy)
    same[...] = line[...]
    for copy in copies:
        copy.wait()


def gate_kernel(*refs):
    pass


def info_kernel(*refs):
    advantages, info = refs[-2:]
    start = refs[0].shape[1] - IDS
    table = jnp.concatenate([ref[:, start:] for ref in refs[:-2]], axis=0).astype(jnp.float32)
    valid = table[:, 0:1]
    turn = table[:, 1:2] + 256.0 * table[:, 2:3]
    target = table[:, 3:4] + 256.0 * table[:, 4:5] + 65536.0 * table[:, 5:6]
    turns = advantages.shape[1]
    spot = lax.broadcasted_iota(jnp.int32, (table.shape[0], turns), 1)
    gain = jnp.sum(
        jnp.where(spot == turn.astype(jnp.int32), advantages[...], 0.0), axis=1, keepdims=True
    )
    weight = valid * gain / jnp.sum(valid)
    lane = lax.broadcasted_iota(jnp.int32, info.shape, 1)
    info[...] = jnp.where(lane == 0, weight, jnp.where(lane == 1, target, 0.0))


def reorder(stats, position, groups):
    lanes = stats.shape[1]
    lane = lax.broadcasted_iota(jnp.int32, stats.shape, 1)
    bit = 1
    while bit < groups:
        size = CAP * bit
        swapped = jnp.where(
            (lane & size) != 0,
            pltpu.roll(stats, size, 1),
            pltpu.roll(stats, lanes - size, 1),
        )
        stats = jnp.where((position & bit) != 0, swapped, stats)
        bit *= 2
    return stats


def all_rows(pieces, counts, place, width):
    start = sum(counts[:place])
    return jnp.concatenate([ref[:, :width] for ref in pieces[start:start + counts[place]]], axis=0)


def some_logits(blocks, counts, ranks, pieces, weight):
    width = weight.shape[0] // ranks
    rank, total = coordinates()[0], None
    for place, block in enumerate(blocks):
        start = pl.multiple_of((rank ^ block) * width, width)
        part = jnp.dot(
            all_rows(pieces, counts, place, width),
            weight[pl.ds(start, width), :],
            preferred_element_type=jnp.float32,
        )
        total = part if total is None else total + part
    return total


def first_kernel(blocks, counts, ranks, weight, *refs):
    refs[-1][...] = some_logits(blocks, counts, ranks, refs[:-1], weight)


def logits_kernel(blocks, counts, ranks, groups, info, partial, weight, *refs):
    pieces, (logits, stats) = refs[:-2], refs[-2:]
    _, position, shard = coordinates()
    total = partial[...] + some_logits(blocks, counts, ranks, pieces, weight)
    logits[...] = total
    height, columns = total.shape
    target = info[:, 1:2].astype(jnp.int32) - shard * columns
    column = lax.broadcasted_iota(jnp.int32, total.shape, 1)
    hit = jnp.sum(jnp.where(column == target, total, 0.0), axis=1, keepdims=True)
    hit = jnp.sum(hit * info[:, 0:1])
    peak = jnp.max(total, axis=1, keepdims=True)
    mass = jnp.sum(jnp.exp(total - peak), axis=1, keepdims=True)
    lane = lax.broadcasted_iota(jnp.int32, (height, 128), 1)
    table = jnp.where(lane == 0, peak + jnp.log(mass), hit)
    table = reorder(jnp.transpose(table)[0:8], position, groups)
    line = jnp.concatenate([table[0:1], table[1:2, :LANES]], axis=1)
    stats[...] = jnp.broadcast_to(line[None], stats.shape)


def log_totals(groups, stats, height):
    parts = stats[:, :, :height]
    peak = jnp.max(parts, axis=0)
    line = peak + jnp.log(jnp.sum(jnp.exp(parts - peak[None]), axis=0))
    line = reorder(jnp.broadcast_to(line, (8, height)), coordinates()[1], groups)
    return jnp.transpose(jnp.concatenate([line] * 16, axis=0))


def grad_kernel(order, groups, info, mine, theirs, weight, other_weight, stats, *refs):
    logit_grad, table, outs = refs[0], refs[1], refs[2:]
    chunks = (outs[len(order):], outs[:len(order)])
    rank, _, shard = coordinates()
    height, columns = mine.shape
    part = height // 4
    table[...] = log_totals(groups, stats, height)
    log_total = table[:, 0:1]
    row_weight, target = info[:, 0:1], info[:, 1:2].astype(jnp.int32)

    def grad_of(logits, shard):
        column = lax.broadcasted_iota(jnp.int32, (height, columns), 1) + shard * columns
        probability = jnp.exp(logits[...] - log_total)
        return (
            grad_scale * row_weight * (probability - (column == target).astype(jnp.float32))
        ).astype(jnp.bfloat16)

    grad = grad_of(mine, shard)
    logit_grad[...] = grad
    grads = (grad, grad_of(theirs, shard ^ 1))
    width = outs[0].shape[1]
    for x in range(len(order) // 2):
        start = pl.multiple_of((rank ^ 2 * x) * width, width)
        weights = (weight[pl.ds(start, width), :], other_weight[x * width:(x + 1) * width, :])
        total = sum(
            lax.dot_general(g, w, (((1,), (1,)), ((), ())), preferred_element_type=jnp.float32)
            for g, w in zip(grads, weights)
        )
        for quarter in range(4):
            out = chunks[quarter % 2][order.index(2 * x + quarter // 2)]
            out[...] = total[quarter * part:(quarter + 1) * part].astype(out.dtype)


def weight_kernel(blocks, counts, skipped, after, logit_grad, *refs):
    pieces, (out, last, done, sems) = refs[skipped:-4], refs[-4:]
    rank = coordinates()[0]
    width = done.shape[0] // len(blocks)
    copies = []
    for place, block in enumerate(blocks):
        done[place * width:(place + 1) * width] = lax.dot_general(
            all_rows(pieces, counts, place, width),
            logit_grad[...],
            (((0,), (0,)), ((), ())),
            preferred_element_type=jnp.float32,
        ).astype(jnp.bfloat16)
        start = pl.multiple_of((rank ^ block) * width, width)
        copy = pltpu.make_async_copy(
            done.at[pl.ds(place * width, width)], out.at[pl.ds(start, width)], sems.at[place]
        )
        copy.start()
        copies.append(copy)
    if skipped:
        info, table, stats = refs[1:4]
        hits = jnp.sum(stats[:, :, info.shape[0]:], axis=0)
        loss = jnp.sum(info[:, 0:1] * table[:, 0:1]) - hits[0, 0]
        last[...] = jnp.full(last.shape, loss, jnp.float32)
    else:
        last[...] = jnp.zeros_like(last)
    for copy in copies:
        copy.wait()


def corner_kernel(count, after, kept, *refs):
    total = kept[...]
    for ref in refs[:count]:
        total = total + ref[...].astype(jnp.float32)
    for place, out in enumerate(refs[count:]):
        out[...] = total[place * CAP:(place + 1) * CAP].astype(out.dtype)


def unpack_kernel(last, chosen, *refs):
    out, loss = refs[-2:]
    loss[0, 0] = last[0, 0]
    total = sum(ref[...].astype(jnp.float32) for ref in refs[:-2])
    out[...] = lax.dot_general(
        chosen[...],
        total.astype(jnp.bfloat16),
        (((0,), (0,)), ((), ())),
        preferred_element_type=jnp.float32,
    ).astype(jnp.bfloat16)


def body(dps, ranks, hidden, weight, loss_mask, target_ids, turn_ids, advantages):
    tokens, width = hidden.shape
    depth, columns = weight.shape
    zs, xs = dps // 2, ranks // 2
    total_rows = dps * CAP
    bf16, f32, i32 = jnp.bfloat16, jnp.float32, jnp.int32
    shape = jax.ShapeDtypeStruct
    flops = 2 * total_rows * depth * columns

    def send(value, z=0, y=0, x=0, core=0):
        far, near = 2 * z + y, 2 * x + core
        pairs = [
            (d * ranks + v, (d ^ far) * ranks + (v ^ near))
            for d in range(dps)
            for v in range(ranks)
        ]
        return lax.ppermute(value, AXES, pairs)

    packed, own, chosen = call(
        pack_kernel,
        (
            in_hbm(hidden),
            in_hbm(loss_mask.reshape(1, tokens)),
            in_hbm(target_ids.reshape(1, tokens)),
            in_hbm(turn_ids.reshape(1, tokens)),
        ),
        [HBM] * 4,
        (
            shape((CAP, width + IDS), bf16),
            shape((CAP, width), bf16),
            shape((CAP, tokens), bf16),
        ),
        (VMEM,) * 3,
        [pltpu.VMEM((tokens, width), bf16)]
        + [pltpu.VMEM((1, tokens), i32)] * 3
        + [pltpu.SemaphoreType.DMA((4,))],
    )

    line_order = [0, *range(2, zs), 1]
    blocks = [send(packed, z=z) if z else packed for z in line_order[:-1]]
    corners = {x: send(own, y=1, x=x) for x in range(1, xs)}
    blocks.append(send(packed, z=1))
    line_rows = zs * CAP
    line, line_plain, far = call(
        functools.partial(join_kernel, line_order),
        (*blocks[:-1], *corners.values(), blocks[-1]),
        [VMEM] * (zs - 1) + [ANY] * len(corners) + [VMEM],
        (
            shape((line_rows, width + IDS), bf16),
            shape((line_rows, width), bf16),
            shape((line_rows - CAP, width), bf16),
        ),
        (VMEM,) * 3,
    )
    pieces = {(0, 1, 0): send(line, y=1)}
    for x in range(1, xs):
        pieces[2 * x, 0, 0] = send(line_plain, x=x)
        pieces[2 * x, 1, 0] = corners[x]
        pieces[2 * x, 1, 1] = send(far, y=1, x=x)
    held, away, same = call(
        functools.partial(stage_kernel, ranks),
        (line, in_hbm(weight)),
        [VMEM, HBM],
        (
            shape((depth, columns), bf16),
            shape((depth // 2, columns), bf16),
            shape(line.shape, bf16),
        ),
        (VMEM,) * 3,
        [pltpu.SemaphoreType.DMA((ranks + xs,))],
    )
    pieces[0, 0, 0] = same
    info = call(
        info_kernel,
        (same, pieces[0, 1, 0], advantages.reshape(1, -1)),
        [VMEM] * 3,
        shape((total_rows, 128), f32),
        VMEM,
    )

    def hold(value, after):
        like = shape(value.shape, value.dtype)
        return call(gate_kernel, (value, after), [ANY, ANY], like, ANY, aliases={0: 0})

    def part_logits(kernel, blocks, operands, out_shapes):
        parts = [[pieces[key] for key in sorted(pieces) if key[0] == b] for b in blocks]
        operands = (*operands, held, *(piece for part in parts for piece in part))
        return call(
            functools.partial(kernel, blocks, [len(part) for part in parts], ranks),
            operands,
            [VMEM] * len(operands),
            out_shapes,
            jax.tree.map(lambda _: VMEM, out_shapes),
            flops=flops * len(blocks) // ranks,
        )

    for x in range(1, xs):
        pieces[2 * x + 1, 1, 0] = send(pieces[2 * x, 1, 0], core=1)
        pieces[2 * x, 0, 0] = hold(pieces[2 * x, 0, 0], info)
        pieces[2 * x, 1, 1] = hold(pieces[2 * x, 1, 1], pieces[2 * x + 1, 1, 0])
    for b, y, part in list(pieces):
        if b % 2 == 0 and (b + 1, y, part) not in pieces:
            pieces[b + 1, y, part] = send(pieces[b, y, part], core=1)

    logits_shape = shape((total_rows, columns), f32)
    partial = part_logits(first_kernel, [*range(0, ranks, 2), 1], (), logits_shape)
    logits, stats = part_logits(
        lambda blocks, counts, ranks, *refs: logits_kernel(blocks, counts, ranks, dps, *refs),
        list(range(3, ranks, 2)),
        (info, partial),
        (logits_shape, shape((dps * ranks, 1, total_rows + LANES), f32)),
    )
    parted = [[pieces[key] for key in sorted(pieces) if key[0] == b] for b in range(ranks)]

    def rows_of(blocks):
        return [piece for b in blocks for piece in parted[b]]

    def counts_of(blocks):
        return [len(parted[b]) for b in blocks]

    other_logits = send(logits, core=1)
    other_held = send(hold(away, stats), core=1)
    stats = lax.all_to_all(stats, AXES, 0, 0)
    rows_part = total_rows // 4
    order = sorted(range(1, ranks), key=lambda place: (-(place % 2 + (place > 1)), place)) + [0]
    outs = (shape((rows_part, width), bf16),) * (ranks - 1) + (shape((rows_part, width), f32),)
    logit_grad, table, *going = call(
        functools.partial(grad_kernel, order, dps),
        (info, logits, other_logits, held, other_held, stats),
        [VMEM] * 6,
        (shape((total_rows, columns), bf16), shape((total_rows, 128), f32)) + outs * 2,
        (VMEM,) * (2 + 2 * ranks),
        flops=flops,
    )
    def weight_part(first, after, *extra):
        blocks = range(first, first + ranks // 2)
        chosen_rows = rows_of(blocks)
        return call(
            functools.partial(weight_kernel, blocks, counts_of(blocks), len(extra)),
            (after, logit_grad, *extra, *chosen_rows),
            [ANY, VMEM] + [HBM] * (len(extra) > 0)
            + [VMEM] * (max(len(extra) - 1, 0) + len(chosen_rows)),
            (shape((depth, columns), bf16), shape((8, 128), f32)),
            (HBM, VMEM),
            [
                pltpu.VMEM((depth // 2, columns), bf16),
                pltpu.SemaphoreType.DMA((ranks // 2,)),
            ],
            flops=flops // 2,
            aliases={2: 0} if extra else {},
        )

    far_values, near_values = list(going[:ranks]), list(going[ranks:])
    weight_grad, finished = weight_part(0, far_values[-1])
    near_values[:-1] = call(
        gate_kernel,
        (*near_values[:-1], finished),
        [ANY] * ranks,
        outs[:-1],
        (ANY,) * (ranks - 1),
        aliases={place: place for place in range(ranks - 1)},
    )
    ends, sums = [None] * zs, [None, None]
    for chunk, values in ((1, far_values), (0, near_values)):
        sums[chunk] = [values[-1]]
        for place, value in zip(order, values):
            if place:
                sums[chunk].append(send(value, y=place % 2, x=place // 2))
    for chunk in (1, 0):
        near = chunk * zs // 2
        parts_z = call(
            functools.partial(corner_kernel, ranks - 1),
            (table, *sums[chunk]),
            [ANY] + [VMEM] * ranks,
            tuple(shape((CAP, width), bf16 if near + z else f32) for z in range(zs // 2)),
            (VMEM,) * (zs // 2),
        )
        for z, value in enumerate(parts_z):
            ends[near + z] = send(value, z=near + z) if near + z else value
    weight_grad, last = weight_part(ranks // 2, parts_z[0], weight_grad, info, table, stats)
    hidden_grad, loss = call(
        unpack_kernel,
        (last, chosen, *ends[:zs // 2], *reversed(ends[zs // 2:])),
        [VMEM] * (2 + len(ends)),
        (shape((tokens, width), bf16), shape((1, 1), f32)),
        (VMEM, SMEM),
    )
    return loss[0, 0], hidden_grad, weight_grad


def solution(mesh):
    return jax.shard_map(
        functools.partial(body, mesh.shape["dp"], mesh.shape["vocab"]),
        mesh=mesh,
        in_specs=(P("dp", "vocab"), P(None, AXES), P("dp"), P("dp"), P("dp"), P()),
        out_specs=(P(), P("dp", "vocab"), P(None, AXES)),
        check_vma=False,
    )
```

```python
import functools
import math

import jax
import jax.numpy as jnp
from jax import lax
from jax.experimental import pallas as pl
from jax.experimental.pallas import tpu as pltpu
from jax.sharding import PartitionSpec as P

CAP = 32
MOST_VMEM = 56 * 1024 * 1024
IDS = 128
LANES = 128
grad_scale = 16384.0
AXES = ("dp", "vocab")
SMEM = pl.BlockSpec(memory_space=pltpu.SMEM)
VMEM = pl.BlockSpec(memory_space=pltpu.VMEM)
HBM = pl.BlockSpec(memory_space=pltpu.HBM)
ANY = pl.BlockSpec(memory_space=pl.ANY)


def size_of(value):
    return math.prod(value.shape) * jnp.dtype(value.dtype).itemsize


def call(kernel, operands, in_specs, out_shape, out_specs, scratch=(), spare=4, flops=0, aliases={}):
    outs = jax.tree.leaves(out_shape)
    sized = [v for v, s in zip(operands, in_specs) if s is VMEM]
    sized += [v for v, s in zip(outs, jax.tree.leaves(out_specs)) if s is VMEM]
    held = [s for s in scratch if getattr(s, "memory_space", None) == pltpu.VMEM]
    total = sum(size_of(v) for v in sized) + sum(size_of(s) for s in held)
    return pl.pallas_call(
        kernel,
        out_shape=out_shape,
        in_specs=in_specs,
        out_specs=out_specs,
        scratch_shapes=scratch,
        input_output_aliases=aliases,
        compiler_params=pltpu.CompilerParams(vmem_limit_bytes=min(total + spare * 1024 * 1024, MOST_VMEM)),
        cost_estimate=pl.CostEstimate(
            flops=flops,
            bytes_accessed=sum(size_of(v) for v in list(operands) + outs),
            transcendentals=0,
        ),
    )(*operands)


def in_hbm(value):
    return pltpu.with_memory_space_constraint(value, pltpu.HBM)


def coordinates():
    group, rank = lax.axis_index("dp"), lax.axis_index("vocab")
    groups, ranks = lax.axis_size("dp"), lax.axis_size("vocab")
    position = group % 2 * (groups // 2) + group // 2
    return rank, position, group * ranks + rank


def choose(mask):
    tokens = mask.shape[1]
    wide = jnp.broadcast_to(mask.astype(jnp.float32), (8, tokens))
    before = lax.broadcasted_iota(jnp.int32, (tokens, tokens), 0)
    after = lax.broadcasted_iota(jnp.int32, (tokens, tokens), 1)
    upto = (before <= after).astype(jnp.float32)
    slot = jnp.dot(
        wide.astype(jnp.bfloat16), upto.astype(jnp.bfloat16), preferred_element_type=jnp.float32
    )[0:1]
    grid = lax.broadcasted_iota(jnp.int32, (CAP, tokens), 0) + 1
    return (slot.astype(jnp.int32) == grid) & (mask == 1)


def pack_kernel(hidden_hbm, mask_hbm, target_hbm, turn_hbm, rows, plain, chosen_out, *scratch):
    hidden, mask, target, turn, sems = scratch
    copies = []
    for place, (source, held) in enumerate(
        ((mask_hbm, mask), (target_hbm, target), (turn_hbm, turn), (hidden_hbm, hidden))
    ):
        copy = pltpu.make_async_copy(source, held, sems.at[place])
        copy.start()
        copies.append(copy)
    for copy in copies[:3]:
        copy.wait()
    width = hidden.shape[1]
    chosen = choose(mask[...])
    one_hot = chosen.astype(jnp.float32).astype(jnp.bfloat16)
    chosen_out[...] = one_hot
    turns, targets = turn[...], target[...]
    fields = (
        mask[...],
        turns & 255,
        turns >> 8,
        targets & 255,
        (targets >> 8) & 255,
        targets >> 16,
    )
    lane = lax.broadcasted_iota(jnp.int32, (CAP, IDS), 1)
    table = jnp.zeros((CAP, IDS), jnp.float32)
    for place, field in enumerate(fields):
        picked = jnp.where(chosen, field.astype(jnp.float32), 0.0)
        table = jnp.where(lane == place, jnp.sum(picked, axis=1, keepdims=True), table)
    rows[:, width:] = table.astype(jnp.bfloat16)
    copies[3].wait()
    packed = jnp.dot(one_hot, hidden[...], preferred_element_type=jnp.float32)
    packed = packed.astype(jnp.bfloat16)
    rows[:, :width] = packed
    plain[...] = packed


def join_kernel(order, *refs):
    blocks, (line, plain, far) = refs[:len(order) - 1] + refs[-4:-3], refs[-3:]
    width = plain.shape[1]
    for place, block in zip(order, blocks):
        rows = slice(place * CAP, (place + 1) * CAP)
        line[rows] = block[...]
        plain[rows] = block[:, :width]
        if place:
            far[(place - 1) * CAP:place * CAP] = block[:, :width]


def stage_kernel(blocks, line, weight, held, away, same, sems):
    rank = coordinates()[0]
    width = weight.shape[0] // blocks
    copies = []
    for block in list(range(1, blocks, 2)) + list(range(0, blocks, 2)):
        start = pl.multiple_of((rank ^ block) * width, width)
        targets = [held.at[pl.ds(start, width)]]
        if block % 2:
            targets.append(away.at[pl.ds(block // 2 * width, width)])
        for target in targets:
            copy = pltpu.make_async_copy(
                weight.at[pl.ds(start, width)], target, sems.at[len(copies)]
            )
            copy.start()
            copies.append(copy)
    same[...] = line[...]
    for copy in copies:
        copy.wait()


def gate_kernel(*refs):
    pass


def info_kernel(*refs):
    advantages, info = refs[-2:]
    start = refs[0].shape[1] - IDS
    table = jnp.concatenate([ref[:, start:] for ref in refs[:-2]], axis=0).astype(jnp.float32)
    valid = table[:, 0:1]
    turn = table[:, 1:2] + 256.0 * table[:, 2:3]
    target = table[:, 3:4] + 256.0 * table[:, 4:5] + 65536.0 * table[:, 5:6]
    turns = advantages.shape[1]
    spot = lax.broadcasted_iota(jnp.int32, (table.shape[0], turns), 1)
    gain = jnp.sum(
        jnp.where(spot == turn.astype(jnp.int32), advantages[...], 0.0), axis=1, keepdims=True
    )
    weight = valid * gain / jnp.sum(valid)
    lane = lax.broadcasted_iota(jnp.int32, info.shape, 1)
    info[...] = jnp.where(lane == 0, weight, jnp.where(lane == 1, target, 0.0))


def reorder(stats, position, groups):
    lanes = stats.shape[1]
    lane = lax.broadcasted_iota(jnp.int32, stats.shape, 1)
    bit = 1
    while bit < groups:
        size = CAP * bit
        swapped = jnp.where(
            (lane & size) != 0,
            pltpu.roll(stats, size, 1),
            pltpu.roll(stats, lanes - size, 1),
        )
        stats = jnp.where((position & bit) != 0, swapped, stats)
        bit *= 2
    return stats


def all_rows(pieces, counts, place, width):
    start = sum(counts[:place])
    return jnp.concatenate([ref[:, :width] for ref in pieces[start:start + counts[place]]], axis=0)


def some_logits(blocks, counts, ranks, pieces, weight):
    width = weight.shape[0] // ranks
    rank, total = coordinates()[0], None
    for place, block in enumerate(blocks):
        start = pl.multiple_of((rank ^ block) * width, width)
        part = jnp.dot(
            all_rows(pieces, counts, place, width),
            weight[pl.ds(start, width), :],
            preferred_element_type=jnp.float32,
        )
        total = part if total is None else total + part
    return total


def first_kernel(blocks, counts, ranks, weight, *refs):
    refs[-1][...] = some_logits(blocks, counts, ranks, refs[:-1], weight)


def logits_kernel(blocks, counts, ranks, groups, info, partial, weight, *refs):
    pieces, (logits, stats) = refs[:-2], refs[-2:]
    _, position, shard = coordinates()
    total = partial[...] + some_logits(blocks, counts, ranks, pieces, weight)
    logits[...] = total
    height, columns = total.shape
    target = info[:, 1:2].astype(jnp.int32) - shard * columns
    column = lax.broadcasted_iota(jnp.int32, total.shape, 1)
    hit = jnp.sum(jnp.where(column == target, total, 0.0), axis=1, keepdims=True)
    hit = jnp.sum(hit * info[:, 0:1])
    peak = jnp.max(total, axis=1, keepdims=True)
    mass = jnp.sum(jnp.exp(total - peak), axis=1, keepdims=True)
    lane = lax.broadcasted_iota(jnp.int32, (height, 128), 1)
    table = jnp.where(lane == 0, peak + jnp.log(mass), hit)
    table = reorder(jnp.transpose(table)[0:8], position, groups)
    line = jnp.concatenate([table[0:1], table[1:2, :LANES]], axis=1)
    stats[...] = jnp.broadcast_to(line[None], stats.shape)


def log_totals(groups, stats, height):
    parts = stats[:, :, :height]
    peak = jnp.max(parts, axis=0)
    line = peak + jnp.log(jnp.sum(jnp.exp(parts - peak[None]), axis=0))
    line = reorder(jnp.broadcast_to(line, (8, height)), coordinates()[1], groups)
    return jnp.transpose(jnp.concatenate([line] * 16, axis=0))


def grad_kernel(order, groups, info, mine, theirs, weight, other_weight, stats, *refs):
    logit_grad, table, outs = refs[0], refs[1], refs[2:]
    chunks = (outs[len(order):], outs[:len(order)])
    rank, _, shard = coordinates()
    height, columns = mine.shape
    part = height // 4
    table[...] = log_totals(groups, stats, height)
    log_total = table[:, 0:1]
    row_weight, target = info[:, 0:1], info[:, 1:2].astype(jnp.int32)

    def grad_of(logits, shard):
        column = lax.broadcasted_iota(jnp.int32, (height, columns), 1) + shard * columns
        probability = jnp.exp(logits[...] - log_total)
        return (
            grad_scale * row_weight * (probability - (column == target).astype(jnp.float32))
        ).astype(jnp.bfloat16)

    grad = grad_of(mine, shard)
    logit_grad[...] = grad
    grads = (grad, grad_of(theirs, shard ^ 1))
    width = outs[0].shape[1]
    for x in range(len(order) // 2):
        start = pl.multiple_of((rank ^ 2 * x) * width, width)
        weights = (weight[pl.ds(start, width), :], other_weight[x * width:(x + 1) * width, :])
        total = sum(
            lax.dot_general(g, w, (((1,), (1,)), ((), ())), preferred_element_type=jnp.float32)
            for g, w in zip(grads, weights)
        )
        for quarter in range(4):
            out = chunks[quarter % 2][order.index(2 * x + quarter // 2)]
            out[...] = total[quarter * part:(quarter + 1) * part].astype(out.dtype)


def weight_kernel(blocks, counts, skipped, after, logit_grad, *refs):
    pieces, (out, last, done, sems) = refs[skipped:-4], refs[-4:]
    rank = coordinates()[0]
    width = done.shape[0] // len(blocks)
    copies = []
    for place, block in enumerate(blocks):
        done[place * width:(place + 1) * width] = lax.dot_general(
            all_rows(pieces, counts, place, width),
            logit_grad[...],
            (((0,), (0,)), ((), ())),
            preferred_element_type=jnp.float32,
        ).astype(jnp.bfloat16)
        start = pl.multiple_of((rank ^ block) * width, width)
        copy = pltpu.make_async_copy(
            done.at[pl.ds(place * width, width)], out.at[pl.ds(start, width)], sems.at[place]
        )
        copy.start()
        copies.append(copy)
    if skipped:
        info, table, stats = refs[1:4]
        hits = jnp.sum(stats[:, :, info.shape[0]:], axis=0)
        loss = jnp.sum(info[:, 0:1] * table[:, 0:1]) - hits[0, 0]
        last[...] = jnp.full(last.shape, loss, jnp.float32)
    else:
        last[...] = jnp.zeros_like(last)
    for copy in copies:
        copy.wait()


def corner_kernel(count, after, kept, *refs):
    total = kept[...]
    for ref in refs[:count]:
        total = total + ref[...].astype(jnp.float32)
    for place, out in enumerate(refs[count:]):
        out[...] = total[place * CAP:(place + 1) * CAP].astype(out.dtype)


def unpack_kernel(last, chosen, *refs):
    out, loss = refs[-2:]
    loss[0, 0] = last[0, 0]
    total = sum(ref[...].astype(jnp.float32) for ref in refs[:-2])
    out[...] = lax.dot_general(
        chosen[...],
        total.astype(jnp.bfloat16),
        (((0,), (0,)), ((), ())),
        preferred_element_type=jnp.float32,
    ).astype(jnp.bfloat16)


def body(dps, ranks, hidden, weight, loss_mask, target_ids, turn_ids, advantages):
    tokens, width = hidden.shape
    depth, columns = weight.shape
    zs, xs = dps // 2, ranks // 2
    total_rows = dps * CAP
    bf16, f32, i32 = jnp.bfloat16, jnp.float32, jnp.int32
    shape = jax.ShapeDtypeStruct
    flops = 2 * total_rows * depth * columns

    def send(value, z=0, y=0, x=0, core=0):
        far, near = 2 * z + y, 2 * x + core
        pairs = [
            (d * ranks + v, (d ^ far) * ranks + (v ^ near))
            for d in range(dps)
            for v in range(ranks)
        ]
        return lax.ppermute(value, AXES, pairs)

    packed, own, chosen = call(
        pack_kernel,
        (
            in_hbm(hidden),
            in_hbm(loss_mask.reshape(1, tokens)),
            in_hbm(target_ids.reshape(1, tokens)),
            in_hbm(turn_ids.reshape(1, tokens)),
        ),
        [HBM] * 4,
        (
            shape((CAP, width + IDS), bf16),
            shape((CAP, width), bf16),
            shape((CAP, tokens), bf16),
        ),
        (VMEM,) * 3,
        [pltpu.VMEM((tokens, width), bf16)]
        + [pltpu.VMEM((1, tokens), i32)] * 3
        + [pltpu.SemaphoreType.DMA((4,))],
    )

    line_order = [0, *range(2, zs), 1]
    blocks = [send(packed, z=z) if z else packed for z in line_order[:-1]]
    corners = {x: send(own, y=1, x=x) for x in range(1, xs)}
    blocks.append(send(packed, z=1))
    line_rows = zs * CAP
    line, line_plain, far = call(
        functools.partial(join_kernel, line_order),
        (*blocks[:-1], *corners.values(), blocks[-1]),
        [VMEM] * (zs - 1) + [ANY] * len(corners) + [VMEM],
        (
            shape((line_rows, width + IDS), bf16),
            shape((line_rows, width), bf16),
            shape((line_rows - CAP, width), bf16),
        ),
        (VMEM,) * 3,
    )
    pieces = {(0, 1, 0): send(line, y=1)}
    for x in range(1, xs):
        pieces[2 * x, 0, 0] = send(line_plain, x=x)
        pieces[2 * x, 1, 0] = corners[x]
        pieces[2 * x, 1, 1] = send(far, y=1, x=x)
    held, away, same = call(
        functools.partial(stage_kernel, ranks),
        (line, in_hbm(weight)),
        [VMEM, HBM],
        (
            shape((depth, columns), bf16),
            shape((depth // 2, columns), bf16),
            shape(line.shape, bf16),
        ),
        (VMEM,) * 3,
        [pltpu.SemaphoreType.DMA((ranks + xs,))],
    )
    pieces[0, 0, 0] = same
    info = call(
        info_kernel,
        (same, pieces[0, 1, 0], advantages.reshape(1, -1)),
        [VMEM] * 3,
        shape((total_rows, 128), f32),
        VMEM,
    )

    def hold(value, after):
        like = shape(value.shape, value.dtype)
        return call(gate_kernel, (value, after), [ANY, ANY], like, ANY, aliases={0: 0})

    def part_logits(kernel, blocks, operands, out_shapes):
        parts = [[pieces[key] for key in sorted(pieces) if key[0] == b] for b in blocks]
        operands = (*operands, held, *(piece for part in parts for piece in part))
        return call(
            functools.partial(kernel, blocks, [len(part) for part in parts], ranks),
            operands,
            [VMEM] * len(operands),
            out_shapes,
            jax.tree.map(lambda _: VMEM, out_shapes),
            flops=flops * len(blocks) // ranks,
        )

    for x in range(1, xs):
        pieces[2 * x + 1, 1, 0] = send(pieces[2 * x, 1, 0], core=1)
        pieces[2 * x, 0, 0] = hold(pieces[2 * x, 0, 0], info)
        pieces[2 * x, 1, 1] = hold(pieces[2 * x, 1, 1], pieces[2 * x + 1, 1, 0])
    for b, y, part in list(pieces):
        if b % 2 == 0 and (b + 1, y, part) not in pieces:
            pieces[b + 1, y, part] = send(pieces[b, y, part], core=1)

    logits_shape = shape((total_rows, columns), f32)
    partial = part_logits(first_kernel, [*range(0, ranks, 2), 1], (), logits_shape)
    logits, stats = part_logits(
        lambda blocks, counts, ranks, *refs: logits_kernel(blocks, counts, ranks, dps, *refs),
        list(range(3, ranks, 2)),
        (info, partial),
        (logits_shape, shape((dps * ranks, 1, total_rows + LANES), f32)),
    )
    parted = [[pieces[key] for key in sorted(pieces) if key[0] == b] for b in range(ranks)]

    def rows_of(blocks):
        return [piece for b in blocks for piece in parted[b]]

    def counts_of(blocks):
        return [len(parted[b]) for b in blocks]

    other_logits = send(logits, core=1)
    other_held = send(hold(away, stats), core=1)
    stats = lax.all_to_all(stats, AXES, 0, 0)
    rows_part = total_rows // 4
    order = sorted(range(1, ranks), key=lambda place: (-(place % 2 + (place > 1)), place)) + [0]
    outs = (shape((rows_part, width), bf16),) * (ranks - 1) + (shape((rows_part, width), f32),)
    logit_grad, table, *going = call(
        functools.partial(grad_kernel, order, dps),
        (info, logits, other_logits, held, other_held, stats),
        [VMEM] * 6,
        (shape((total_rows, columns), bf16), shape((total_rows, 128), f32)) + outs * 2,
        (VMEM,) * (2 + 2 * ranks),
        flops=flops,
    )
    def weight_part(first, after, *extra):
        blocks = range(first, first + ranks // 2)
        chosen_rows = rows_of(blocks)
        return call(
            functools.partial(weight_kernel, blocks, counts_of(blocks), len(extra)),
            (after, logit_grad, *extra, *chosen_rows),
            [ANY, VMEM] + [HBM] * (len(extra) > 0)
            + [VMEM] * (max(len(extra) - 1, 0) + len(chosen_rows)),
            (shape((depth, columns), bf16), shape((8, 128), f32)),
            (HBM, VMEM),
            [
                pltpu.VMEM((depth // 2, columns), bf16),
                pltpu.SemaphoreType.DMA((ranks // 2,)),
            ],
            flops=flops // 2,
            aliases={2: 0} if extra else {},
        )

    far_values, near_values = list(going[:ranks]), list(going[ranks:])
    weight_grad, finished = weight_part(0, near_values[-1])
    ends, sums = [None] * zs, [None, None]
    for chunk, values in ((1, far_values), (0, near_values)):
        sums[chunk] = [values[-1]]
        for place, value in zip(order, values):
            if place:
                sums[chunk].append(send(value, y=place % 2, x=place // 2))
    for chunk in (1, 0):
        near = chunk * zs // 2
        parts_z = call(
            functools.partial(corner_kernel, ranks - 1),
            (table if chunk else finished, *sums[chunk]),
            [ANY] + [VMEM] * ranks,
            tuple(shape((CAP, width), bf16 if near + z else f32) for z in range(zs // 2)),
            (VMEM,) * (zs // 2),
        )
        for z, value in enumerate(parts_z):
            ends[near + z] = send(value, z=near + z) if near + z else value
    weight_grad, last = weight_part(ranks // 2, parts_z[0], weight_grad, info, table, stats)
    hidden_grad, loss = call(
        unpack_kernel,
        (last, chosen, *ends),
        [VMEM] * (2 + len(ends)),
        (shape((tokens, width), bf16), shape((1, 1), f32)),
        (VMEM, SMEM),
    )
    return loss[0, 0], hidden_grad, weight_grad


def solution(mesh):
    return jax.shard_map(
        functools.partial(body, mesh.shape["dp"], mesh.shape["vocab"]),
        mesh=mesh,
        in_specs=(P("dp", "vocab"), P(None, AXES), P("dp"), P("dp"), P("dp"), P()),
        out_specs=(P(), P("dp", "vocab"), P(None, AXES)),
        check_vma=False,
    )
```
